32 devices in a mesh: section: 2 (over core), tensor: 4 (over y, x), dp: 4 (over z).
Axes of the slice: x: 2, y: 2, z: 4, core: 2. Of those that a mesh axis runs over, the one named last changes fastest.
Arguments:
- activations: bfloat16 [2, 1, 1024, 1024], P(None, None, ('dp', 'tensor')), may hold values from -6 to 6
- lengths: int32 [2, 1, 8], replicated, may hold values from 1 to 768, as said below
- projection: bfloat16 [2, 1024, 3, 1024], P('section', None, None, 'tensor'), may hold values from -0.1875 to 0.1875
- output_weight: bfloat16 [2, 1024, 1024], P('section', 'tensor'), may hold values from -0.1875 to 0.1875
- expansion: bfloat16 [2, 1024, 2, 4096], P('section', None, None, 'tensor'), may hold values from -0.1875 to 0.1875
- reduction: bfloat16 [2, 4096, 1024], P('section', 'tensor'), may hold values from -0.09375 to 0.09375
- query_scale: float32 [2, 1024], P('section', 'tensor'), may hold values from 0.7 to 1.6
- unit_scales: float32 [2, 2, 4096], P('section', None, 'tensor'), may hold values from 0.5 to 2
- alphas: float32 [2, 2, 1024], P('section'), may hold values from 0.2 to 0.8
- cotangent: bfloat16 [2, 1, 1024, 1024], P(None, None, ('dp', 'tensor')), may hold values from -6 to 6
Outputs:
- layer_output: bfloat16 [2, 2, 1, 1024, 1024], P('section', None, None, ('dp', 'tensor'))
- input_gradient: bfloat16 [2, 2, 1, 1024, 1024], P('section', None, None, ('dp', 'tensor'))
- projection_gradient: float32 [2, 1024, 3, 1024], P('section', None, None, 'tensor')
- output_gradient: float32 [2, 1024, 1024], P('section', 'tensor')
- expansion_gradient: float32 [2, 1024, 2, 4096], P('section', None, None, 'tensor')
- reduction_gradient: float32 [2, 4096, 1024], P('section', 'tensor')
- query_scale_gradient: float32 [2, 1024], P('section', 'tensor')
- unit_scales_gradient: float32 [2, 2, 4096], P('section', None, 'tensor')
- alphas_gradient: float32 [2, 2, 1024], P('section')
The draws below stay inside these ranges and needn't reach their ends.
Inputs may be any that keep to these rules, and one draw needn't show every extreme that they name: `lengths`: the sequences of a row lie in order from slot 0; the slots after the last one are padding.
All inputs are finite; a program needn't handle non-finite values.
Results may differ from the reference program's by a relative error of at most 0.04.
Values may be sent and summed in bfloat16 or wider, within the bound.
A program may use at most 192 MiB of HBM per device.

```python
import math
import jax
import jax.numpy as jnp
from jax import lax

D = 1024
HEADS = 16
HDIM = 64
FF = 4096
SLOT_DEV = 256
ROWS_MB = 1
MB = 2
NSEG = 8
SLOTS = 1024
N_SECTION = 2


def draw_lengths(key, part):
    key = jax.random.fold_in(key, 7)
    keys = jax.random.split(key, 5)
    count = MB * ROWS_MB
    weights = 2 ** jax.random.randint(keys[0], (count, NSEG), 0, 4)
    padding = jax.random.randint(keys[1], (count, 1), 0, SLOT_DEV // 2 + 1)
    base = SLOTS - padding
    share = 1 + weights * (base - NSEG) // jnp.sum(weights, axis=1, keepdims=True)
    share = jnp.concatenate([share[:, :-1], share[:, -1:] + base - jnp.sum(share, axis=1, keepdims=True)], axis=1)
    lead = jax.random.randint(keys[2], (1,), 1, SLOT_DEV - NSEG + 3)
    rest = SLOT_DEV - lead
    small = 2 ** jax.random.randint(keys[3], (NSEG - 2,), 0, 4)
    pieces = 1 + small * (rest - (NSEG - 2)) // jnp.sum(small)
    pieces = jnp.concatenate([pieces[:-1], pieces[-1:] + rest - jnp.sum(pieces)])
    special = jnp.concatenate([lead, jnp.full((1,), SLOTS - SLOT_DEV, jnp.int32), pieces])
    chosen = jax.random.randint(keys[4], (), 0, count)
    table = jnp.where(jnp.arange(count)[:, None] == chosen, special[None, :], share)
    return table.reshape(MB, ROWS_MB, NSEG).astype(jnp.int32)


def shard_levels(own_key, dims, shards, smallest, largest):
    loudness, own = 1.0, jax.random.fold_in(own_key, 6)
    for dim, parts in shards:
        draws = jnp.exp(jax.random.uniform(jax.random.fold_in(own, dim), (parts,), jnp.float32, smallest / len(shards), largest / len(shards)))
        loudness = loudness * jnp.repeat(draws, dims[dim] // parts).reshape([-1 if axis == dim else 1 for axis in range(len(dims))])
    return loudness


def scatter_about(key, extent, deviation, most, shards=(), kind=jnp.bfloat16):
    array = deviation * jax.random.normal(key, extent, jnp.float32)
    if shards:
        array = array * shard_levels(key, extent, shards, -0.22, 0.18)
    return jnp.clip(array, -most, most).astype(kind)


def setup_inputs(seed: int = 0) -> dict:
    arg_keys = jax.random.split(jax.random.key(seed), 11)
    activations = scatter_about(arg_keys[0], (MB, ROWS_MB, SLOTS, D), 1.0, 6.0, ((2, 16),))
    lengths = draw_lengths(jax.random.fold_in(arg_keys[10], 71), 0)
    projection = scatter_about(arg_keys[2], (N_SECTION, D, 3, HEADS * HDIM), D ** -0.5, 0.1875, ((0, 2), (3, 4)))
    output_weight = scatter_about(arg_keys[3], (N_SECTION, HEADS * HDIM, D), (HEADS * HDIM) ** -0.5, 0.1875, ((0, 2), (1, 4)))
    expansion = scatter_about(arg_keys[4], (N_SECTION, D, 2, FF), D ** -0.5, 0.1875, ((0, 2), (3, 4)))
    reduction = scatter_about(arg_keys[5], (N_SECTION, FF, D), FF ** -0.5, 0.09375, ((0, 2), (1, 4)))
    query_scale = jnp.clip(jnp.exp(math.log(1.6) - 0.82667861 * jax.random.uniform(arg_keys[6], (N_SECTION, HEADS * HDIM), jnp.float32) ** shard_levels(arg_keys[6], (N_SECTION, HEADS * HDIM), ((0, 2), (1, 4)), -0.2, 0.2)), 0.7, 1.6)
    unit_scales = jnp.clip(jnp.exp(math.log(2.0) - 1.3862944 * jax.random.uniform(arg_keys[7], (N_SECTION, 2, FF), jnp.float32) ** shard_levels(arg_keys[7], (N_SECTION, 2, FF), ((0, 2), (2, 4)), -0.2, 0.2)), 0.5, 2.0)
    alphas = jnp.clip(0.2 + 0.6 * jax.random.uniform(arg_keys[8], (N_SECTION, 2, D), jnp.float32) ** shard_levels(arg_keys[8], (N_SECTION, 2, D), ((0, 2),), -0.2, 0.2), 0.2, 0.8)
    cotangent = scatter_about(arg_keys[9], (MB, ROWS_MB, SLOTS, D), 1.0, 6.0, ((2, 16),))
    return dict(activations=activations, lengths=lengths, projection=projection, output_weight=output_weight, expansion=expansion, reduction=reduction, query_scale=query_scale, unit_scales=unit_scales, alphas=alphas, cotangent=cotangent)


HIGHEST = lax.Precision.HIGHEST

@jax.custom_vjp
def low(v):
    return lax.optimization_barrier(v.astype(jnp.bfloat16)).astype(jnp.float32)

@jax.custom_vjp
def low_back(v):
    return v

def low_keep(v):
    return (low(v), None)

def low_pass(kept, grad):
    return (grad,)

def back_keep(v):
    return (v, None)

def back_low(kept, grad):
    return (low(grad),)
low.defvjp(low_keep, low_pass)
low_back.defvjp(back_keep, back_low)

def normed(v):
    return v * lax.rsqrt(lax.optimization_barrier(jnp.mean(v * v, axis=-1, keepdims=True)) + 1e-06)

def unit_heads(v):
    return v * lax.rsqrt(lax.optimization_barrier(jnp.sum(v * v, axis=-1, keepdims=True)) + 1e-06)

def frequencies(half):
    return jnp.exp(jnp.arange(half, dtype=jnp.float32) * (-2.0 * math.log(10000.0) / (2 * half)))

def rotate(view, angle):
    half = view.shape[-1] // 2
    cosine = jnp.cos(angle)[..., None, :]
    sine = jnp.sin(angle)[..., None, :]
    front = view[..., :half]
    back = view[..., half:]
    return jnp.concatenate([front * cosine - back * sine, back * cosine + front * sine], axis=-1)

def shaped(projected, scale, angle, heads):
    inner = projected.shape[-1] // 3
    lead = projected.shape[:-1]

    def turned(piece):
        view = piece.reshape(lead + (heads, inner // heads))
        return unit_heads(rotate(view, angle)).reshape(lead + (inner,)) * scale
    return (turned(projected[..., :inner]), turned(projected[..., inner:2 * inner]), projected[..., 2 * inner:])

def layout(lengths_row, slots):
    ends = jnp.cumsum(lengths_row, dtype=jnp.int32)
    index = jnp.arange(slots, dtype=jnp.int32)
    after = index[:, None] >= ends[None, :]
    segment = lax.optimization_barrier(jnp.sum(after.astype(jnp.int32), axis=1, dtype=jnp.int32))
    begin = lax.optimization_barrier(jnp.sum(jnp.where(after, lengths_row[None, :], 0), axis=1, dtype=jnp.int32))
    inside = index < ends[-1]
    segment = jnp.where(inside, segment, lengths_row.shape[0] + index)
    position = jnp.where(inside, index - begin, 0)
    return (segment, position)

def blend(base, branch, alpha):
    return normed(base + alpha * (normed(branch) - base))

def activate(expanded, scales):
    half = expanded.shape[-1] // 2
    return expanded[..., :half] * scales[0] * jax.nn.silu(expanded[..., half:] * scales[1])

def attention(query, key, value, segment, heads):
    slots, inner = query.shape
    depth = inner // heads
    key_heads = key.reshape(slots, heads, depth)
    value_heads = value.reshape(slots, heads, depth)
    index = jnp.arange(slots, dtype=jnp.int32)
    block = min(512, slots)
    count = slots // block

    def attend(pieces):
        query_block, segment_block, index_block = pieces
        scores = low_back(jnp.einsum('qhe,khe->hqk', query_block, key_heads, precision=HIGHEST) * math.sqrt(depth))
        allowed = (segment_block[:, None] == segment[None, :]) & (index[None, :] <= index_block[:, None])
        scores = jnp.where(allowed[None], scores, -1e+30)
        highest = lax.optimization_barrier(jnp.max(scores, axis=-1, keepdims=True))
        lifted = jnp.exp(scores - highest)
        probs = lifted / lax.optimization_barrier(jnp.sum(lifted, axis=-1, keepdims=True))
        mixed = jnp.einsum('hqk,khe->qhe', low(probs), value_heads, precision=HIGHEST)
        return mixed.reshape(block, inner)
    mixed = lax.map(jax.checkpoint(attend), (query.reshape(count, block, heads, depth), segment.reshape(count, block), index.reshape(count, block)))
    return mixed.reshape(slots, inner)

def layer(stream, segment, position, weights):
    projection, output_weight, expansion, reduction, query_scale, unit_scales, alphas = weights
    slots, width = stream.shape
    inner = output_weight.shape[0]
    heads = inner // HDIM
    hidden_width = reduction.shape[0]
    projected = low_back(jnp.dot(stream, projection.reshape(width, 3 * inner), precision=HIGHEST))
    angle = position.astype(jnp.float32)[:, None] * frequencies(HDIM // 2)
    query, key, value = shaped(projected, query_scale, angle, heads)
    mixed = attention(low(query), low(key), low(value), segment, heads)
    attended = low(low_back(mixed))
    branch = low_back(jnp.dot(attended, output_weight, precision=HIGHEST))
    middle = blend(stream, branch, alphas[0])
    expanded = low_back(jnp.dot(low(middle), expansion.reshape(width, 2 * hidden_width), precision=HIGHEST))
    hidden = low(activate(expanded, unit_scales))
    feed = low_back(jnp.dot(hidden, reduction, precision=HIGHEST))
    return blend(middle, feed, alphas[1])

def reference(activations, lengths, projection, output_weight, expansion, reduction, query_scale, unit_scales, alphas, cotangent):
    params = tuple((piece.astype(jnp.float32) for piece in (projection, output_weight, expansion, reduction, query_scale, unit_scales, alphas)))
    micro, rows_mb, slots, width = activations.shape
    rows = micro * rows_mb
    streams = activations.astype(jnp.float32).reshape(rows, slots, width)
    layouts = lax.map(lambda row: layout(row, slots), lengths.reshape(rows, -1))
    delta = jnp.zeros_like(streams)

    def whole(params, streams, delta):

        def one_row(pieces):
            stream, shift_in, segment, position = pieces
            first = layer(stream, segment, position, tuple((piece[0] for piece in params)))
            passed = low_back(low(first)) + shift_in
            second = layer(passed, segment, position, tuple((piece[1] for piece in params)))
            return (first, second)
        return lax.map(jax.checkpoint(one_row), (streams, delta, layouts[0], layouts[1]))
    (first, second), pullback = jax.vjp(whole, params, streams, delta)
    grads, stream_grad, passed_grad = pullback((jnp.zeros_like(first), cotangent.astype(jnp.float32).reshape(rows, slots, width)))
    full = (2, micro, rows_mb, slots, width)
    layer_output = jnp.stack([first, second]).reshape(full).astype(jnp.bfloat16)
    input_gradient = jnp.stack([stream_grad, passed_grad]).reshape(full).astype(jnp.bfloat16)
    return (layer_output, input_gradient, grads[0], grads[1], grads[2], grads[3], grads[4], grads[5], grads[6])
```

```python
import functools
import math

import jax
import jax.numpy as jnp
from jax import lax
from jax.experimental import pallas as pl
from jax.experimental.pallas import tpu as pltpu
from jax.sharding import PartitionSpec as P

HDIM = 64


def from_behind(value, axis, steps):
    count = lax.axis_size(axis)
    initial, last = (max(0, -steps), min(count, count - steps))
    return lax.ppermute(value, axis, [(source, source + steps) for source in range(initial, last)])


def normed(v):
    return v * lax.rsqrt(jnp.mean(v * v, axis=-1, keepdims=True) + 1e-06)


def unit_heads(v):
    return v * lax.rsqrt(jnp.sum(v * v, axis=-1, keepdims=True) + 1e-06)


def frequencies(half):
    return jnp.exp(jnp.arange(half, dtype=jnp.float32) * (-2.0 * math.log(10000.0) / (2 * half)))


def rotate(view, angle):
    half = view.shape[-1] // 2
    cosine = jnp.cos(angle)[..., None, :]
    sine = jnp.sin(angle)[..., None, :]
    front = view[..., :half]
    back = view[..., half:]
    return jnp.concatenate([front * cosine - back * sine, back * cosine + front * sine], axis=-1)


def shaped(projected, scale, angle, heads):
    inner = projected.shape[-1] // 3
    lead = projected.shape[:-1]

    def turned(piece):
        view = piece.reshape(lead + (heads, inner // heads))
        return unit_heads(rotate(view, angle)).reshape(lead + (inner,)) * scale

    return (
        turned(projected[..., :inner]),
        turned(projected[..., inner : 2 * inner]),
        projected[..., 2 * inner :],
    )


def layout(lengths_row, slots):
    ends = jnp.cumsum(lengths_row, dtype=jnp.int32)
    index = jnp.arange(slots, dtype=jnp.int32)
    after = index[:, None] >= ends[None, :]
    segment = jnp.sum(after.astype(jnp.int32), axis=1, dtype=jnp.int32)
    begin = jnp.sum(jnp.where(after, lengths_row[None, :], 0), axis=1, dtype=jnp.int32)
    inside = index < ends[-1]
    segment = jnp.where(inside, segment, lengths_row.shape[0] + index)
    position = jnp.where(inside, index - begin, 0)
    return (segment, position)


def blend(base, branch, alpha):
    return normed(base + alpha * (normed(branch) - base))


def activate(expanded, scales):
    half = expanded.shape[-1] // 2
    return expanded[..., :half] * scales[0] * jax.nn.silu(expanded[..., half:] * scales[1])


def placing(lengths_now, local):
    slots = local * lax.axis_size("dp")
    start_here = lax.axis_index("dp") * local
    segment_all, position_all = jax.vmap(lambda row: layout(row, slots))(lengths_now)
    segment_here = lax.dynamic_slice_in_dim(segment_all, start_here, local, 1)
    position_here = lax.dynamic_slice_in_dim(position_all, start_here, local, 1)
    index_here = start_here + jnp.arange(local, dtype=jnp.int32)
    every = jnp.arange(slots, dtype=jnp.int32)
    allowed = (segment_here[:, :, None] == segment_all[:, None, :]) & (
        every[None, None, :] <= index_here[None, :, None]
    )
    angle = position_here.astype(jnp.float32)[..., None] * frequencies(HDIM // 2)
    return (allowed, angle)


def scored(query, key_all, allowed, heads):
    rows, local, inner = query.shape
    depth = inner // heads
    query_heads = query.reshape(rows, local, heads, depth)
    key_heads = key_all.reshape(rows, key_all.shape[1], heads, depth)
    raw = jnp.einsum(
        "rqhe,rkhe->rhqk", query_heads, key_heads, preferred_element_type=jnp.float32
    ) * math.sqrt(depth)
    return jnp.where(allowed[:, None], raw, -1e30)


def forward(stream, lengths_now, weights):
    projection, output_weight, expansion, reduction, query_scale, unit_scales, alphas = weights
    rows, part, width = stream.shape
    inner = output_weight.shape[0]
    heads = inner // HDIM
    hidden_width = reduction.shape[0]
    gathered = lax.all_gather(stream.astype(jnp.bfloat16), "tensor", axis=1, tiled=True)
    local = gathered.shape[1]
    allowed, angle = placing(lengths_now, local)
    projected = jnp.einsum(
        "rsd,dc->rsc",
        gathered,
        projection.reshape(width, 3 * inner),
        preferred_element_type=jnp.float32,
    )
    query, key, value = shaped(projected, query_scale, angle, heads)
    query_low = query.astype(jnp.bfloat16)
    key_low = key.astype(jnp.bfloat16)
    value_low = value.astype(jnp.bfloat16)
    key_all, value_all = (
        lax.all_gather(key_low, "dp", axis=1, tiled=True),
        lax.all_gather(value_low, "dp", axis=1, tiled=True),
    )
    scores = scored(query_low, key_all, allowed, heads)
    highest = jnp.max(scores, axis=-1, keepdims=True)
    lifted = jnp.exp(scores - highest)
    total = jnp.sum(lifted, axis=-1, keepdims=True)
    log_total = highest + jnp.log(total)
    probs_low = (lifted / total).astype(jnp.bfloat16)
    value_heads = value_all.reshape(rows, value_all.shape[1], heads, HDIM)
    mixed = jnp.einsum(
        "rhqk,rkhe->rqhe", probs_low, value_heads, preferred_element_type=jnp.float32
    )
    attended = mixed.reshape(rows, local, inner).astype(jnp.bfloat16)
    partial_branch = jnp.einsum(
        "rsc,cd->rsd", attended, output_weight, preferred_element_type=jnp.float32
    )
    branch = lax.psum_scatter(partial_branch, "tensor", scatter_dimension=1, tiled=True)
    middle = blend(stream, branch, alphas[0])
    middle_all = lax.all_gather(middle.astype(jnp.bfloat16), "tensor", axis=1, tiled=True)
    expanded = jnp.einsum(
        "rsd,dc->rsc",
        middle_all,
        expansion.reshape(width, 2 * hidden_width),
        preferred_element_type=jnp.float32,
    )
    hidden = activate(expanded, unit_scales).astype(jnp.bfloat16)
    partial_feed = jnp.einsum("rsf,fd->rsd", hidden, reduction, preferred_element_type=jnp.float32)
    feed = lax.psum_scatter(partial_feed, "tensor", scatter_dimension=1, tiled=True)
    result = blend(middle, feed, alphas[1])
    kept = dict(
        stream=stream,
        gathered=gathered,
        projected=projected,
        query=query_low,
        key=key_low,
        value=value_low,
        log_total=log_total,
        attended=attended,
        branch=branch,
        middle=middle,
        middle_all=middle_all,
        expanded=expanded,
        hidden=hidden,
        feed=feed,
        lengths=lengths_now,
    )
    kept = dict(kept, key_all=key_all, value_all=value_all)
    return (result, kept)


def backward(slope, kept, weights):
    projection, output_weight, expansion, reduction, query_scale, unit_scales, alphas = weights
    rows, part, width = slope.shape
    inner = output_weight.shape[0]
    heads = inner // HDIM
    hidden_width = reduction.shape[0]
    _, pull_feed = jax.vjp(blend, kept["middle"], kept["feed"], alphas[1])
    middle_slope, feed_slope, alpha_feed = pull_feed(slope)
    feed_all = lax.all_gather(feed_slope.astype(jnp.bfloat16), "tensor", axis=1, tiled=True)
    reduction_grad = jnp.einsum(
        "rsf,rsd->fd", kept["hidden"], feed_all, preferred_element_type=jnp.float32
    )
    hidden_slope = jnp.einsum(
        "rsd,fd->rsf", feed_all, reduction, preferred_element_type=jnp.float32
    )
    _, pull_active = jax.vjp(activate, kept["expanded"], unit_scales)
    expanded_slope, unit_grad = pull_active(hidden_slope)
    expanded_low = expanded_slope.astype(jnp.bfloat16)
    expansion_grad = jnp.einsum(
        "rsd,rsc->dc", kept["middle_all"], expanded_low, preferred_element_type=jnp.float32
    ).reshape(width, 2, hidden_width)
    partial_middle = jnp.einsum(
        "rsc,dc->rsd",
        expanded_low,
        expansion.reshape(width, 2 * hidden_width),
        preferred_element_type=jnp.float32,
    )
    middle_total = middle_slope + lax.psum_scatter(
        partial_middle, "tensor", scatter_dimension=1, tiled=True
    )
    _, pull_branch = jax.vjp(blend, kept["stream"], kept["branch"], alphas[0])
    stream_slope, branch_slope, alpha_branch = pull_branch(middle_total)
    branch_all = lax.all_gather(branch_slope.astype(jnp.bfloat16), "tensor", axis=1, tiled=True)
    output_grad = jnp.einsum(
        "rsc,rsd->cd", kept["attended"], branch_all, preferred_element_type=jnp.float32
    )
    attended_low = jnp.einsum(
        "rsd,cd->rsc", branch_all, output_weight, preferred_element_type=jnp.float32
    ).astype(jnp.bfloat16)
    local = attended_low.shape[1]
    key_all = kept["key_all"]
    value_all = kept["value_all"]
    slots = key_all.shape[1]
    allowed, angle = placing(kept["lengths"], local)
    scores = scored(kept["query"], key_all, allowed, heads)
    probs = jnp.exp(scores - kept["log_total"])
    scale = math.sqrt(HDIM)
    back_heads = attended_low.reshape(rows, local, heads, HDIM)
    query_heads = kept["query"].reshape(rows, local, heads, HDIM)
    key_heads = key_all.reshape(rows, slots, heads, HDIM)
    value_heads = value_all.reshape(rows, slots, heads, HDIM)
    probs_slope = jnp.einsum(
        "rqhe,rkhe->rhqk", back_heads, value_heads, preferred_element_type=jnp.float32
    )
    row_term = jnp.sum(probs * probs_slope, axis=-1, keepdims=True)
    scores_low = (probs * (probs_slope - row_term)).astype(jnp.bfloat16)
    query_slope = (
        jnp.einsum("rhqk,rkhe->rqhe", scores_low, key_heads, preferred_element_type=jnp.float32)
        * scale
    )
    value_grad_all = jnp.einsum(
        "rhqk,rqhe->rkhe",
        probs.astype(jnp.bfloat16),
        back_heads,
        preferred_element_type=jnp.float32,
    )
    key_grad_all = (
        jnp.einsum("rhqk,rqhe->rkhe", scores_low, query_heads, preferred_element_type=jnp.float32)
        * scale
    )
    key_slope, value_slope = (
        lax.psum_scatter(
            key_grad_all.reshape(rows, slots, inner), "dp", scatter_dimension=1, tiled=True
        ),
        lax.psum_scatter(
            value_grad_all.reshape(rows, slots, inner), "dp", scatter_dimension=1, tiled=True
        ),
    )
    _, pull_shape = jax.vjp(
        lambda source, scale_now: shaped(source, scale_now, angle, heads),
        kept["projected"],
        query_scale,
    )
    projected_slope, query_scale_grad = pull_shape(
        (query_slope.reshape(rows, local, inner), key_slope, value_slope)
    )
    projected_low = projected_slope.astype(jnp.bfloat16)
    projection_grad = jnp.einsum(
        "rsd,rsc->dc", kept["gathered"], projected_low, preferred_element_type=jnp.float32
    ).reshape(width, 3, inner)
    partial_stream = jnp.einsum(
        "rsc,dc->rsd",
        projected_low,
        projection.reshape(width, 3 * inner),
        preferred_element_type=jnp.float32,
    )
    spread = jnp.broadcast_to(
        jnp.stack([alpha_branch, alpha_feed])[:, None, :], (2, lax.axis_size("tensor"), width)
    )
    stream_part, alpha_sum = (
        lax.psum_scatter(partial_stream, "tensor", scatter_dimension=1, tiled=True),
        lax.psum_scatter(spread, "tensor", scatter_dimension=1, tiled=True),
    )
    stream_total = stream_slope + stream_part
    return (
        stream_total,
        (
            projection_grad,
            output_grad,
            expansion_grad,
            reduction_grad,
            query_scale_grad,
            unit_grad,
            alpha_sum[:, 0],
        ),
    )


def body(
    activations,
    lengths,
    projection,
    output_weight,
    expansion,
    reduction,
    query_scale,
    unit_scales,
    alphas,
    cotangent,
):
    micro, rows, part, width = activations.shape
    section = lax.axis_index("section")
    first = section == 0
    weights = (
        projection[0],
        output_weight[0],
        expansion[0],
        reduction[0],
        query_scale[0],
        unit_scales[0],
        alphas[0],
    )
    steps = micro + 1
    received = jnp.zeros((rows, part, width), jnp.bfloat16)
    outputs = []
    keeps = []
    for step in range(steps):
        index_now = jnp.clip(step - section, 0, micro - 1)
        lengths_now = lax.dynamic_index_in_dim(lengths, index_now, 0, keepdims=False)
        stream = jnp.where(first, activations[min(step, micro - 1)], received).astype(jnp.float32)
        result, kept = forward(stream, lengths_now, weights)
        result_low = result.astype(jnp.bfloat16)
        outputs.append(result_low)
        keeps.append(kept)
        if step + 1 < steps:
            received = from_behind(result_low, "section", 1)
    stacked = jnp.stack(outputs)
    layer_output = jnp.where(first, stacked[:micro], stacked[1:])[None]
    back_received = jnp.zeros((rows, part, width), jnp.bfloat16)
    slopes = []
    summed = None
    for step in range(steps):
        batch_now = step - 1 + section
        valid = (batch_now >= 0) & (batch_now < micro)
        slope = jnp.where(first, back_received, cotangent[min(step, micro - 1)]).astype(jnp.float32)
        earlier = keeps[max(step - 1, 0)]
        later = keeps[min(step + 1, micro)]
        kept = jax.tree.map(lambda left, right: jnp.where(first, left, right), earlier, later)
        stream_total, layer_grads = backward(slope, kept, weights)
        stream_low = stream_total.astype(jnp.bfloat16)
        slopes.append(stream_low)
        masked = tuple((jnp.where(valid, piece, 0.0) for piece in layer_grads))
        summed = (
            masked
            if summed is None
            else tuple((left + right for left, right in zip(summed, masked)))
        )
        if step + 1 < steps:
            back_received = from_behind(stream_low, "section", -1)
    stacked_slopes = jnp.stack(slopes)
    input_gradient = jnp.where(first, stacked_slopes[1:], stacked_slopes[:micro])[None]
    (
        projection_grad,
        output_grad,
        expansion_grad,
        reduction_grad,
        query_scale_grad,
        unit_grad,
        alpha_grad,
    ) = summed
    totals = lax.psum(
        (
            projection_grad,
            output_grad,
            expansion_grad,
            reduction_grad,
            query_scale_grad,
            unit_grad,
            alpha_grad,
        ),
        "dp",
    )
    return (
        layer_output,
        input_gradient,
        totals[0][None],
        totals[1][None],
        totals[2][None],
        totals[3][None],
        totals[4][None],
        totals[5][None],
        totals[6][None],
    )


MESH_IDS = pl.DeviceIdType.MESH
F32, BF16 = jnp.float32, jnp.bfloat16
NN = ((1,), (0,))
NT = ((1,), (1,))
TN = ((0,), (0,))


def dot(left, right, dims):
    return lax.dot_general(left, right, (dims, ((), ())), preferred_element_type=F32)


def norm_parts(v):
    rate = lax.rsqrt(jnp.mean(v * v, axis=-1, keepdims=True) + 1e-06)
    return v * rate, rate


def norm_back(slope, unit, rate):
    return rate * (slope - unit * jnp.mean(unit * slope, axis=-1, keepdims=True))


def blend_back(slope, base, branch, alpha):
    unit_branch, rate_branch = norm_parts(branch)
    toward = unit_branch - base
    unit, rate = norm_parts(base + alpha * toward)
    inner_slope = norm_back(slope, unit, rate)
    alpha_slope = jnp.sum(inner_slope * toward, axis=0, keepdims=True)
    scaled = alpha * inner_slope
    return inner_slope - scaled, norm_back(scaled, unit_branch, rate_branch), alpha_slope


def sequence_starts(lengths_ref, row, index):
    begin = jnp.zeros_like(index)
    end = jnp.int32(0)
    for sequence in range(lengths_ref.shape[2]):
        end = end + lengths_ref[row, 0, sequence]
        begin = jnp.where(index >= end, end, begin)
    return jnp.where(index < end, begin, index)


class Sizes:
    def __init__(self, tensors, places, part, width, inner, units, sequences):
        self.tensors, self.places, self.part, self.width = tensors, places, part, width
        self.inner, self.units, self.sequences = inner, units, sequences
        self.local = part * tensors
        self.heads = inner // HDIM


PHASES = ("stream", "heads", "mixed", "branch", "middle", "feed", "feed_low", "middle_back", "branch_low", "mixed_back", "heads_back", "stream_back")


def relay_kernel(
    sizes,
    lengths_ref, acts_ref, cot_ref, qs_ref, us_ref, al_ref, wp_ref, wo_ref, we_ref, wr_ref,
    lo_ref, ig_ref, small_ref, gp_ref, go_ref, ge_ref, gr_ref,
    wp, wo, we, wr, qs, us, al,
    stream, turned, rate, heads_in, probs, mixed_in, sums_in, middles, branch_f, middle_f, feed_f,
    up_f, gate_f, hidden, feed_low, branch_low, back_in, heads_back_in,
    heads_out, mixed_out, back_out, heads_back_out, sums_out, expanded_low,
    outs, outs_in, grads, grad_out, key_rows, value_rows, key_grad, value_grad,
    gp, go, ge, gr,
    weight_sem, weight_send, send_sem, recv_sem, out_send, out_recv, grad_sem,
):
    T, Z, S, part = sizes.tensors, sizes.places, sizes.local, sizes.part
    H, inner, units, D = sizes.heads, sizes.inner, sizes.units, sizes.width
    core, t, z = lax.axis_index("section"), lax.axis_index("tensor"), lax.axis_index("dp")
    sibling = (1 - core, t, z)
    tensor_peers = [lax.rem(t + k, T) for k in range(1, T)]
    place_peers = [lax.rem(z + k, Z) for k in range(1, Z)]
    tensor_ids = [(core, peer, z) for peer in tensor_peers]
    place_ids = [(core, t, peer) for peer in place_peers]
    pending = []

    own_weights = [(wp_ref, wp), (wo_ref, wo), (we_ref, we), (wr_ref, wr)]
    for piece, (source, target) in enumerate(own_weights):
        pltpu.make_async_copy(source, target.at[core], weight_sem.at[core, piece]).start()
    small_weights = [(qs_ref, qs), (us_ref, us), (al_ref, al)]
    for piece, (source, target) in enumerate(small_weights):
        pltpu.make_async_copy(source, target.at[core], weight_sem.at[core, 4 + piece]).start()

    barrier = pltpu.get_barrier_semaphore()
    partners = [sibling] + tensor_ids + place_ids
    for partner in partners:
        pl.semaphore_signal(barrier, inc=1, device_id=partner, device_id_type=MESH_IDS)
    pl.semaphore_wait(barrier, len(partners))

    for piece, (source, target) in list(enumerate(small_weights, 4)) + list(enumerate(own_weights)):
        copy = pltpu.make_async_remote_copy(
            source, target.at[core], weight_send.at[piece], weight_sem.at[core, piece], device_id=sibling, device_id_type=MESH_IDS
        )
        copy.start()
        pending.append(copy)

    def await_weight(layer, piece):
        source, target = (own_weights + small_weights)[piece]
        pltpu.make_async_copy(source, target.at[layer], weight_sem.at[layer, piece]).wait()

    def exchange(layer, phase, ids, sources, targets):
        number = layer * len(PHASES) + PHASES.index(phase)
        copies = []
        for k, device in enumerate(ids):
            copy = pltpu.make_async_remote_copy(
                sources[k], targets[k], send_sem.at[number, k], recv_sem.at[number, k], device_id=device, device_id_type=MESH_IDS
            )
            copy.start()
            copies.append(copy)
        pending.extend(copies)
        return copies

    def arrive(copies):
        for copy in copies:
            copy.wait_recv()

    my_rows = pl.ds(pl.multiple_of(t * part, part), part)

    def gather(layer, phase, target, value):
        target[layer, my_rows, :] = value
        mine = target.at[layer, my_rows, :]
        return exchange(layer, phase, tensor_ids, [mine] * (T - 1), [mine] * (T - 1))

    def scatter(layer, phase, number):
        return exchange(
            layer, phase, tensor_ids, [sums_out.at[layer, number, peer] for peer in tensor_peers], [sums_in.at[layer, number, k] for k in range(T - 1)]
        )

    def scattered(layer, number, copies):
        arrive(copies)
        total = sums_out[layer, number, t].astype(F32)
        for k in range(T - 1):
            total = total + sums_in[layer, number, k].astype(F32)
        return total

    def spread(layer, phase, source, target):
        target[layer, z] = source[layer, z]
        return exchange(layer, phase, place_ids, [source.at[layer, peer] for peer in place_peers], [target.at[layer, z]] * (Z - 1))

    index_all = lax.broadcasted_iota(jnp.int32, (1, S * Z), 1)
    index_here = lax.broadcasted_iota(jnp.int32, (1, S), 1) + z * S
    starts = sequence_starts(lengths_ref, core, index_all)
    position = (index_here - sequence_starts(lengths_ref, core, index_here)).astype(F32)
    half = HDIM // 2
    rates = jnp.exp(lax.broadcasted_iota(jnp.int32, (half, 1), 0).astype(F32) * (-2.0 * math.log(10000.0) / HDIM))
    angle = rates * position
    cosine, sine = jnp.cos(angle)[None], jnp.sin(angle)[None]
    key_index = lax.broadcasted_iota(jnp.int32, (S * Z, S), 0)

    def rotate_heads(v):
        front, back = v[:, :half], v[:, half:]
        return jnp.concatenate([front * cosine - back * sine, back * cosine + front * sine], axis=1)

    def rotate_back(v):
        front, back = v[:, :half], v[:, half:]
        return jnp.concatenate([front * cosine + back * sine, back * cosine - front * sine], axis=1)

    def column(row):
        return jnp.broadcast_to(row, (8, row.shape[1])).T[:, :1]

    def block(query, key):
        return query * (query + 1) // 2 + key

    def forward(layer, base_low):
        copies = gather(layer, "stream", stream, base_low)
        await_weight(layer, 0)
        await_weight(layer, 4)
        await_weight(layer, 5)
        await_weight(layer, 6)
        scale = column(qs[layer]).reshape(H, HDIM, 1)
        base = base_low.astype(F32)
        arrive(copies)
        gathered = stream[layer]
        for third in range(3):
            piece = dot(gathered, wp[layer, third], NN).T.reshape(H, HDIM, S)
            if third < 2:
                piece = rotate_heads(piece)
                speed = lax.rsqrt(jnp.sum(piece * piece, axis=1, keepdims=True) + 1e-06)
                piece = piece * speed
                turned[layer, third] = piece
                rate[layer, third] = speed
                piece = piece * scale
            heads_out[layer, :, third] = piece.astype(BF16)
        copies = spread(layer, "heads", heads_out, heads_in)
        arrive(copies)
        for place in range(Z):
            key_rows[place] = heads_in[layer, place, 1].T
        for query in range(Z):
            count = (query + 1) * S
            raw = [
                dot(key_rows[key], heads_in[layer, query, 0], NN) * math.sqrt(HDIM) for key in range(query + 1)
            ]
            first = starts[:, query * S : count]
            last = index_all[:, query * S : count]
            scores = []
            for key in range(query + 1):
                keys = key_index[key * S : (key + 1) * S]
                allowed = keys >= first
                if key == query:
                    allowed = allowed & (keys <= last)
                scores.append(jnp.where(allowed, raw[key], -1e30))
            highest = scores[0].max(axis=0, keepdims=True)
            for piece in scores[1:]:
                highest = jnp.maximum(highest, piece.max(axis=0, keepdims=True))
            lifted = [jnp.exp(piece - highest) for piece in scores]
            total = lifted[0].sum(axis=0, keepdims=True)
            for piece in lifted[1:]:
                total = total + piece.sum(axis=0, keepdims=True)
            shrink = 1.0 / total
            mixed = None
            for key in range(query + 1):
                low = (lifted[key] * shrink).astype(BF16)
                probs[layer, block(query, key)] = low
                term = dot(heads_in[layer, key, 2], low, NN)
                mixed = term if mixed is None else mixed + term
            mixed_out[layer, query] = mixed.astype(BF16)
        copies = spread(layer, "mixed", mixed_out, mixed_in)
        await_weight(layer, 1)
        arrive(copies)
        attended = mixed_in[layer].reshape(inner, S).T
        partial = dot(attended, wo[layer], NN)
        sums_out[layer, 0] = partial.astype(BF16).reshape(T, part, D)
        branch = scattered(layer, 0, scatter(layer, "branch", 0))
        branch_f[layer] = branch
        alpha = al[layer]
        middle = norm_parts(base + alpha[0:1] * (norm_parts(branch)[0] - base))[0]
        middle_f[layer] = middle
        copies = gather(layer, "middle", middles, middle.astype(BF16))
        await_weight(layer, 2)
        arrive(copies)
        middle_all = middles[layer]
        step = 256
        for begin in range(0, units, step):
            cols = slice(begin, begin + step)
            up = dot(middle_all, we[layer, 0, :, cols], NN)
            gate = dot(middle_all, we[layer, 1, :, cols], NN)
            up_f[layer, :, cols] = up
            gate_f[layer, :, cols] = gate
            inside = us[layer, 1:2, cols] * gate
            hidden[layer, :, cols] = (us[layer, 0:1, cols] * up * (inside / (1.0 + jnp.exp(-inside)))).astype(BF16)
        await_weight(layer, 3)
        acted = hidden[layer]
        for begin in range(0, D, step):
            cols = slice(begin, begin + step)
            sums_out[layer, 1, :, :, cols] = dot(acted, wr[layer, :, cols], NN).astype(BF16).reshape(T, part, step)
        feed = scattered(layer, 1, scatter(layer, "feed", 1))
        feed_f[layer] = feed
        result = norm_parts(middle + alpha[1:2] * (norm_parts(feed)[0] - middle))[0].astype(BF16)
        outs[0, layer] = result
        return result

    def backward(layer, base_low, slope):
        alpha = al[layer]
        middle_slope, feed_slope, alpha_m = blend_back(slope, middle_f[layer], feed_f[layer], alpha[1:2])
        arrive(gather(layer, "feed_low", feed_low, feed_slope.astype(BF16)))
        small_ref[layer, 1:2] = alpha_m
        feed_all = feed_low[layer]
        step = 256
        for begin in range(0, units, step):
            cols = slice(begin, begin + step)
            slope_hidden = dot(feed_all, wr[layer, cols, :], NT)
            up, gate = up_f[layer, :, cols], gate_f[layer, :, cols]
            scale_up, scale_gate = us[layer, 0:1, cols], us[layer, 1:2, cols]
            inside = scale_gate * gate
            sigmoid = 1.0 / (1.0 + jnp.exp(-inside))
            silu = inside * sigmoid
            silu_slope = sigmoid + silu * (1.0 - sigmoid)
            by_up = silu * slope_hidden
            by_gate = scale_up * up * silu_slope * slope_hidden
            small_ref[layer, 2:3, cols] = jnp.sum(by_up * up, axis=0, keepdims=True)
            small_ref[layer, 3:4, cols] = jnp.sum(by_gate * gate, axis=0, keepdims=True)
            expanded_low[layer, 0, :, cols] = (by_up * scale_up).astype(BF16)
            expanded_low[layer, 1, :, cols] = (by_gate * scale_gate).astype(BF16)
        for begin in range(0, D, step):
            rows = slice(begin, begin + step)
            partial = dot(expanded_low[layer, 0], we[layer, 0, rows, :], NT) + dot(expanded_low[layer, 1], we[layer, 1, rows, :], NT)
            sums_out[layer, 2, :, :, rows] = partial.astype(BF16).reshape(T, part, step)
        copies = scatter(layer, "middle_back", 2)
        middle_cols = middles[layer].T
        hidden_cols = hidden[layer].T
        slot = lax.rem(core + layer, 2)
        for begin in range(0, units, step):
            cols = slice(begin, begin + step)
            for side in range(2):
                ge[side, :, cols] = dot(middle_cols, expanded_low[layer, side, :, cols], NN).astype(BF16)
            gr[:, cols] = dot(hidden_cols, feed_all[:, cols], NN).astype(BF16)
        started = [
            pltpu.make_async_copy(ge, ge_ref.at[slot], grad_sem.at[layer, 0]),
            pltpu.make_async_copy(gr, gr_ref.at[slot], grad_sem.at[layer, 1]),
        ]
        for copy in started:
            copy.start()
        middle_total = middle_slope + scattered(layer, 2, copies)
        stream_slope, branch_slope, alpha_a = blend_back(middle_total, base_low.astype(F32), branch_f[layer], alpha[0:1])
        arrive(gather(layer, "branch_low", branch_low, branch_slope.astype(BF16)))
        small_ref[layer, 0:1] = alpha_a
        branch_all = branch_low[layer]
        back_out[layer] = dot(wo[layer], branch_all, NT).astype(BF16).reshape(H, HDIM, S)
        copies = spread(layer, "mixed_back", back_out, back_in)
        go[...] = dot(mixed_in[layer].reshape(inner, S), branch_all, NN).astype(BF16)
        copy = pltpu.make_async_copy(go, go_ref.at[slot], grad_sem.at[layer, 2])
        copy.start()
        started.append(copy)
        for place in range(Z):
            value_rows[place] = heads_in[layer, place, 2].T
        arrive(copies)
        for query in range(Z):
            slope_mixed = back_in[layer, query]
            lows = [probs[layer, block(query, key)] for key in range(query + 1)]
            probs_slope = [dot(value_rows[key], slope_mixed, NN) for key in range(query + 1)]
            row_term = None
            for low, piece in zip(lows, probs_slope):
                term = jnp.sum(low.astype(F32) * piece, axis=0, keepdims=True)
                row_term = term if row_term is None else row_term + term
            query_slope = None
            for key in range(query + 1):
                low = lows[key]
                scores_low = (low.astype(F32) * (probs_slope[key] - row_term)).astype(BF16)
                term = dot(heads_in[layer, key, 1], scores_low, NN)
                query_slope = term if query_slope is None else query_slope + term
                key_term = dot(heads_in[layer, query, 0], scores_low, NT)
                value_term = dot(slope_mixed, low, NT)
                if key == query:
                    key_grad[key] = key_term
                    value_grad[key] = value_term
                else:
                    key_grad[key] += key_term
                    value_grad[key] += value_term
            heads_back_out[layer, query, 0] = (query_slope * math.sqrt(HDIM)).astype(BF16)
        for place in range(Z):
            heads_back_out[layer, place, 1] = (key_grad[place] * math.sqrt(HDIM)).astype(BF16)
            heads_back_out[layer, place, 2] = value_grad[place].astype(BF16)
        copies = spread(layer, "heads_back", heads_back_out, heads_back_in)
        scale = column(qs[layer]).reshape(H, HDIM, 1)
        stream_cols = stream[layer].T
        arrive(copies)
        scale_slope = None
        lows = []
        for third in range(3):
            piece = heads_back_in[layer, :, third]
            if third < 2:
                piece = piece.astype(F32)
                unit = turned[layer, third]
                term = jnp.sum(piece * unit, axis=2, keepdims=True)
                scale_slope = term if scale_slope is None else scale_slope + term
                piece = piece * scale
                piece = rate[layer, third] * (piece - unit * jnp.sum(unit * piece, axis=1, keepdims=True))
                piece = rotate_back(piece).astype(BF16)
            lows.append(piece.reshape(inner, S).T)
        partial = None
        for third in range(3):
            term = dot(lows[third], wp[layer, third], NT)
            partial = term if partial is None else partial + term
        sums_out[layer, 3] = partial.astype(BF16).reshape(T, part, D)
        copies = scatter(layer, "stream_back", 3)
        small_ref[layer, 4:5, :inner] = jnp.broadcast_to(scale_slope.reshape(inner, 1), (inner, 128)).T[:1]
        for third in range(3):
            gp[third] = dot(stream_cols, lows[third], NN).astype(BF16)
        copy = pltpu.make_async_copy(gp, gp_ref.at[slot], grad_sem.at[layer, 3])
        copy.start()
        started.append(copy)
        result = (stream_slope + scattered(layer, 3, copies)).astype(BF16)
        outs[1, layer] = result
        for copy in started:
            copy.wait()
        return result

    small_ref[...] = jnp.zeros_like(small_ref)
    base_first = acts_ref[core, 0]
    first = forward(0, base_first)
    forward(1, first)
    slope = backward(1, outs[0, 0], cot_ref[core, 0].astype(F32))
    backward(0, acts_ref[core, 0], slope.astype(F32))

    other = 1 - core
    copy = pltpu.make_async_remote_copy(
        outs.at[:, other], outs_in, out_send, out_recv, device_id=sibling, device_id_type=MESH_IDS
    )
    copy.start()
    for kind, target in enumerate((lo_ref, ig_ref)):
        target[core] = outs[kind, core]
    copy.wait_recv()
    for kind, target in enumerate((lo_ref, ig_ref)):
        target[other] = outs_in[kind]
    copy.wait_send()
    for copy in pending:
        copy.wait_send()


def relay(sizes, lengths, acts, cot, qs, us, al, wp, wo, we, wr):
    T, Z, S, part = sizes.tensors, sizes.places, sizes.local, sizes.part
    H, inner, units, D = sizes.heads, sizes.inner, sizes.units, sizes.width
    blocks = Z * (Z + 1) // 2
    vmem = pl.BlockSpec(memory_space=pltpu.VMEM)
    hbm = pl.BlockSpec(memory_space=pl.ANY)
    out_shape = (
        jax.ShapeDtypeStruct((2, part, D), BF16),
        jax.ShapeDtypeStruct((2, part, D), BF16),
        jax.ShapeDtypeStruct((2, 8, D), F32),
        jax.ShapeDtypeStruct((2, 3, D, inner), BF16),
        jax.ShapeDtypeStruct((2, inner, D), BF16),
        jax.ShapeDtypeStruct((2, 2, D, units), BF16),
        jax.ShapeDtypeStruct((2, units, D), BF16),
    )
    DMA = pltpu.SemaphoreType.DMA
    V = pltpu.VMEM
    scratch = [
        V((2, 3, D, inner), BF16), V((2, inner, D), BF16), V((2, 2, D, units), BF16), V((2, units, D), BF16),
        V((2, 1, inner), F32), V((2, 2, units), F32), V((2, 2, D), F32),
        V((2, S, D), BF16),
        V((2, 2, H, HDIM, S), F32),
        V((2, 2, H, 1, S), F32),
        V((2, Z, 3, HDIM, S), BF16),
        V((2, blocks, S, S), BF16),
        V((2, H, HDIM, S), BF16),
        V((2, 4, T - 1, part, D), BF16),
        V((2, S, D), BF16),
        V((2, part, D), F32), V((2, part, D), F32), V((2, part, D), F32),
        V((2, S, units), F32), V((2, S, units), F32),
        V((2, S, units), BF16),
        V((2, S, D), BF16), V((2, S, D), BF16),
        V((2, Z, HDIM, S), BF16),
        V((2, H, 3, HDIM, S), BF16),
        V((2, H, 3, HDIM, S), BF16),
        V((2, Z, HDIM, S), BF16),
        V((2, H, HDIM, S), BF16),
        V((2, Z, 3, HDIM, S), BF16),
        V((2, 4, T, part, D), BF16),
        V((2, 2, S, units), BF16),
        V((2, 2, part, D), BF16), V((2, part, D), BF16),
        V((8, 128), F32), V((8, 128), F32),
        V((Z, S, HDIM), BF16), V((Z, S, HDIM), BF16),
        V((Z, HDIM, S), F32), V((Z, HDIM, S), F32),
        V((3, D, inner), BF16), V((inner, D), BF16), V((2, D, units), BF16), V((units, D), BF16),
        DMA((2, 7)), DMA((7,)), DMA((2 * len(PHASES), 3)), DMA((2 * len(PHASES), 3)), DMA, DMA, DMA((2, 4)),
    ]
    return pl.pallas_call(
        functools.partial(relay_kernel, sizes),
        out_shape=out_shape,
        in_specs=[pl.BlockSpec(memory_space=pltpu.SMEM), vmem, vmem, vmem, vmem, vmem, hbm, hbm, hbm, hbm],
        out_specs=(vmem, vmem, vmem, hbm, hbm, hbm, hbm),
        scratch_shapes=scratch,
        compiler_params=pltpu.CompilerParams(collective_id=0, has_side_effects=True, vmem_limit_bytes=60 * 2**20),
        name="relay",
    )(lengths, acts, cot, qs, us, al, wp, wo, we, wr)


def fast_body(
    activations, lengths, projection, output_weight, expansion, reduction, query_scale, unit_scales, alphas, cotangent
):
    _, _, part, width = activations.shape
    inner, units = output_weight.shape[1], reduction.shape[1]
    sizes = Sizes(lax.axis_size("tensor"), lax.axis_size("dp"), part, width, inner, units, lengths.shape[2])
    core = lax.axis_index("section")
    lo, ig, small, gp, go, ge, gr = relay(
        sizes, lengths, activations, cotangent, query_scale, unit_scales[0], alphas[0],
        projection[0].transpose(1, 0, 2), output_weight[0], expansion[0].transpose(1, 0, 2), reduction[0],
    )

    def total(pair):
        got = lax.ppermute(pair[1], "section", [(0, 1), (1, 0)])
        return lax.psum((pair[0].astype(F32) + got.astype(F32)).astype(BF16), "dp").astype(F32)

    small = lax.psum(small, ("section", "dp"))
    small = lax.dynamic_index_in_dim(small, core, 0, keepdims=False)
    alpha_grad = lax.psum(small[0:2], "tensor")
    return (
        lo[None, :, None],
        ig[None, :, None],
        total(gp).transpose(1, 0, 2)[None],
        total(go)[None],
        total(ge).transpose(1, 0, 2)[None],
        total(gr)[None],
        small[4:5, :inner],
        small[None, 2:4, :units],
        alpha_grad[None],
    )


def solution(mesh):
    in_specs = (
        P(None, None, ("dp", "tensor"), None),
        P(),
        P("section", None, None, "tensor"),
        P("section", "tensor", None),
        P("section", None, None, "tensor"),
        P("section", "tensor", None),
        P("section", "tensor"),
        P("section", None, "tensor"),
        P("section", None, None),
        P(None, None, ("dp", "tensor"), None),
    )
    out_specs = (
        P("section", None, None, ("dp", "tensor"), None),
        P("section", None, None, ("dp", "tensor"), None),
        P("section", None, None, "tensor"),
        P("section", "tensor", None),
        P("section", None, None, "tensor"),
        P("section", "tensor", None),
        P("section", "tensor"),
        P("section", None, "tensor"),
        P("section", None, None),
    )
    def chosen(*arrays):
        activations, output_weight = arrays[0], arrays[3]
        heads = output_weight.shape[1] // HDIM
        fits = (
            mesh.shape["section"] == 2
            and mesh.shape["tensor"] == 4
            and mesh.shape["dp"] == heads
            and activations.shape[:2] == (2, 1)
            and activations.shape[2] * mesh.shape["tensor"] == 256
        )
        return (fast_body if fits else body)(*arrays)

    return jax.shard_map(chosen, mesh=mesh, in_specs=in_specs, out_specs=out_specs, check_vma=False)
```

```python
import functools
import math

import jax
import jax.numpy as jnp
from jax import lax
from jax.experimental import pallas as pl
from jax.experimental.pallas import tpu as pltpu
from jax.sharding import PartitionSpec as P

HDIM = 64


def from_behind(value, axis, steps):
    count = lax.axis_size(axis)
    initial, last = (max(0, -steps), min(count, count - steps))
    return lax.ppermute(value, axis, [(source, source + steps) for source in range(initial, last)])


def normed(v):
    return v * lax.rsqrt(jnp.mean(v * v, axis=-1, keepdims=True) + 1e-06)


def unit_heads(v):
    return v * lax.rsqrt(jnp.sum(v * v, axis=-1, keepdims=True) + 1e-06)


def frequencies(half):
    return jnp.exp(jnp.arange(half, dtype=jnp.float32) * (-2.0 * math.log(10000.0) / (2 * half)))


def rotate(view, angle):
    half = view.shape[-1] // 2
    cosine = jnp.cos(angle)[..., None, :]
    sine = jnp.sin(angle)[..., None, :]
    front = view[..., :half]
    back = view[..., half:]
    return jnp.concatenate([front * cosine - back * sine, back * cosine + front * sine], axis=-1)


def shaped(projected, scale, angle, heads):
    inner = projected.shape[-1] // 3
    lead = projected.shape[:-1]

    def turned(piece):
        view = piece.reshape(lead + (heads, inner // heads))
        return unit_heads(rotate(view, angle)).reshape(lead + (inner,)) * scale

    return (
        turned(projected[..., :inner]),
        turned(projected[..., inner : 2 * inner]),
        projected[..., 2 * inner :],
    )


def layout(lengths_row, slots):
    ends = jnp.cumsum(lengths_row, dtype=jnp.int32)
    index = jnp.arange(slots, dtype=jnp.int32)
    after = index[:, None] >= ends[None, :]
    segment = jnp.sum(after.astype(jnp.int32), axis=1, dtype=jnp.int32)
    begin = jnp.sum(jnp.where(after, lengths_row[None, :], 0), axis=1, dtype=jnp.int32)
    inside = index < ends[-1]
    segment = jnp.where(inside, segment, lengths_row.shape[0] + index)
    position = jnp.where(inside, index - begin, 0)
    return (segment, position)


def blend(base, branch, alpha):
    return normed(base + alpha * (normed(branch) - base))


def activate(expanded, scales):
    half = expanded.shape[-1] // 2
    return expanded[..., :half] * scales[0] * jax.nn.silu(expanded[..., half:] * scales[1])


def placing(lengths_now, local):
    slots = local * lax.axis_size("dp")
    start_here = lax.axis_index("dp") * local
    segment_all, position_all = jax.vmap(lambda row: layout(row, slots))(lengths_now)
    segment_here = lax.dynamic_slice_in_dim(segment_all, start_here, local, 1)
    position_here = lax.dynamic_slice_in_dim(position_all, start_here, local, 1)
    index_here = start_here + jnp.arange(local, dtype=jnp.int32)
    every = jnp.arange(slots, dtype=jnp.int32)
    allowed = (segment_here[:, :, None] == segment_all[:, None, :]) & (
        every[None, None, :] <= index_here[None, :, None]
    )
    angle = position_here.astype(jnp.float32)[..., None] * frequencies(HDIM // 2)
    return (allowed, angle)


def scored(query, key_all, allowed, heads):
    rows, local, inner = query.shape
    depth = inner // heads
    query_heads = query.reshape(rows, local, heads, depth)
    key_heads = key_all.reshape(rows, key_all.shape[1], heads, depth)
    raw = jnp.einsum(
        "rqhe,rkhe->rhqk", query_heads, key_heads, preferred_element_type=jnp.float32
    ) * math.sqrt(depth)
    return jnp.where(allowed[:, None], raw, -1e30)


def forward(stream, lengths_now, weights):
    projection, output_weight, expansion, reduction, query_scale, unit_scales, alphas = weights
    rows, part, width = stream.shape
    inner = output_weight.shape[0]
    heads = inner // HDIM
    hidden_width = reduction.shape[0]
    gathered = lax.all_gather(stream.astype(jnp.bfloat16), "tensor", axis=1, tiled=True)
    local = gathered.shape[1]
    allowed, angle = placing(lengths_now, local)
    projected = jnp.einsum(
        "rsd,dc->rsc",
        gathered,
        projection.reshape(width, 3 * inner),
        preferred_element_type=jnp.float32,
    )
    query, key, value = shaped(projected, query_scale, angle, heads)
    query_low = query.astype(jnp.bfloat16)
    key_low = key.astype(jnp.bfloat16)
    value_low = value.astype(jnp.bfloat16)
    key_all, value_all = (
        lax.all_gather(key_low, "dp", axis=1, tiled=True),
        lax.all_gather(value_low, "dp", axis=1, tiled=True),
    )
    scores = scored(query_low, key_all, allowed, heads)
    highest = jnp.max(scores, axis=-1, keepdims=True)
    lifted = jnp.exp(scores - highest)
    total = jnp.sum(lifted, axis=-1, keepdims=True)
    log_total = highest + jnp.log(total)
    probs_low = (lifted / total).astype(jnp.bfloat16)
    value_heads = value_all.reshape(rows, value_all.shape[1], heads, HDIM)
    mixed = jnp.einsum(
        "rhqk,rkhe->rqhe", probs_low, value_heads, preferred_element_type=jnp.float32
    )
    attended = mixed.reshape(rows, local, inner).astype(jnp.bfloat16)
    partial_branch = jnp.einsum(
        "rsc,cd->rsd", attended, output_weight, preferred_element_type=jnp.float32
    )
    branch = lax.psum_scatter(partial_branch, "tensor", scatter_dimension=1, tiled=True)
    middle = blend(stream, branch, alphas[0])
    middle_all = lax.all_gather(middle.astype(jnp.bfloat16), "tensor", axis=1, tiled=True)
    expanded = jnp.einsum(
        "rsd,dc->rsc",
        middle_all,
        expansion.reshape(width, 2 * hidden_width),
        preferred_element_type=jnp.float32,
    )
    hidden = activate(expanded, unit_scales).astype(jnp.bfloat16)
    partial_feed = jnp.einsum("rsf,fd->rsd", hidden, reduction, preferred_element_type=jnp.float32)
    feed = lax.psum_scatter(partial_feed, "tensor", scatter_dimension=1, tiled=True)
    result = blend(middle, feed, alphas[1])
    kept = dict(
        stream=stream,
        gathered=gathered,
        projected=projected,
        query=query_low,
        key=key_low,
        value=value_low,
        log_total=log_total,
        attended=attended,
        branch=branch,
        middle=middle,
        middle_all=middle_all,
        expanded=expanded,
        hidden=hidden,
        feed=feed,
        lengths=lengths_now,
    )
    kept = dict(kept, key_all=key_all, value_all=value_all)
    return (result, kept)


def backward(slope, kept, weights):
    projection, output_weight, expansion, reduction, query_scale, unit_scales, alphas = weights
    rows, part, width = slope.shape
    inner = output_weight.shape[0]
    heads = inner // HDIM
    hidden_width = reduction.shape[0]
    _, pull_feed = jax.vjp(blend, kept["middle"], kept["feed"], alphas[1])
    middle_slope, feed_slope, alpha_feed = pull_feed(slope)
    feed_all = lax.all_gather(feed_slope.astype(jnp.bfloat16), "tensor", axis=1, tiled=True)
    reduction_grad = jnp.einsum(
        "rsf,rsd->fd", kept["hidden"], feed_all, preferred_element_type=jnp.float32
    )
    hidden_slope = jnp.einsum(
        "rsd,fd->rsf", feed_all, reduction, preferred_element_type=jnp.float32
    )
    _, pull_active = jax.vjp(activate, kept["expanded"], unit_scales)
    expanded_slope, unit_grad = pull_active(hidden_slope)
    expanded_low = expanded_slope.astype(jnp.bfloat16)
    expansion_grad = jnp.einsum(
        "rsd,rsc->dc", kept["middle_all"], expanded_low, preferred_element_type=jnp.float32
    ).reshape(width, 2, hidden_width)
    partial_middle = jnp.einsum(
        "rsc,dc->rsd",
        expanded_low,
        expansion.reshape(width, 2 * hidden_width),
        preferred_element_type=jnp.float32,
    )
    middle_total = middle_slope + lax.psum_scatter(
        partial_middle, "tensor", scatter_dimension=1, tiled=True
    )
    _, pull_branch = jax.vjp(blend, kept["stream"], kept["branch"], alphas[0])
    stream_slope, branch_slope, alpha_branch = pull_branch(middle_total)
    branch_all = lax.all_gather(branch_slope.astype(jnp.bfloat16), "tensor", axis=1, tiled=True)
    output_grad = jnp.einsum(
        "rsc,rsd->cd", kept["attended"], branch_all, preferred_element_type=jnp.float32
    )
    attended_low = jnp.einsum(
        "rsd,cd->rsc", branch_all, output_weight, preferred_element_type=jnp.float32
    ).astype(jnp.bfloat16)
    local = attended_low.shape[1]
    key_all = kept["key_all"]
    value_all = kept["value_all"]
    slots = key_all.shape[1]
    allowed, angle = placing(kept["lengths"], local)
    scores = scored(kept["query"], key_all, allowed, heads)
    probs = jnp.exp(scores - kept["log_total"])
    scale = math.sqrt(HDIM)
    back_heads = attended_low.reshape(rows, local, heads, HDIM)
    query_heads = kept["query"].reshape(rows, local, heads, HDIM)
    key_heads = key_all.reshape(rows, slots, heads, HDIM)
    value_heads = value_all.reshape(rows, slots, heads, HDIM)
    probs_slope = jnp.einsum(
        "rqhe,rkhe->rhqk", back_heads, value_heads, preferred_element_type=jnp.float32
    )
    row_term = jnp.sum(probs * probs_slope, axis=-1, keepdims=True)
    scores_low = (probs * (probs_slope - row_term)).astype(jnp.bfloat16)
    query_slope = (
        jnp.einsum("rhqk,rkhe->rqhe", scores_low, key_heads, preferred_element_type=jnp.float32)
        * scale
    )
    value_grad_all = jnp.einsum(
        "rhqk,rqhe->rkhe",
        probs.astype(jnp.bfloat16),
        back_heads,
        preferred_element_type=jnp.float32,
    )
    key_grad_all = (
        jnp.einsum("rhqk,rqhe->rkhe", scores_low, query_heads, preferred_element_type=jnp.float32)
        * scale
    )
    key_slope, value_slope = (
        lax.psum_scatter(
            key_grad_all.reshape(rows, slots, inner), "dp", scatter_dimension=1, tiled=True
        ),
        lax.psum_scatter(
            value_grad_all.reshape(rows, slots, inner), "dp", scatter_dimension=1, tiled=True
        ),
    )
    _, pull_shape = jax.vjp(
        lambda source, scale_now: shaped(source, scale_now, angle, heads),
        kept["projected"],
        query_scale,
    )
    projected_slope, query_scale_grad = pull_shape(
        (query_slope.reshape(rows, local, inner), key_slope, value_slope)
    )
    projected_low = projected_slope.astype(jnp.bfloat16)
    projection_grad = jnp.einsum(
        "rsd,rsc->dc", kept["gathered"], projected_low, preferred_element_type=jnp.float32
    ).reshape(width, 3, inner)
    partial_stream = jnp.einsum(
        "rsc,dc->rsd",
        projected_low,
        projection.reshape(width, 3 * inner),
        preferred_element_type=jnp.float32,
    )
    spread = jnp.broadcast_to(
        jnp.stack([alpha_branch, alpha_feed])[:, None, :], (2, lax.axis_size("tensor"), width)
    )
    stream_part, alpha_sum = (
        lax.psum_scatter(partial_stream, "tensor", scatter_dimension=1, tiled=True),
        lax.psum_scatter(spread, "tensor", scatter_dimension=1, tiled=True),
    )
    stream_total = stream_slope + stream_part
    return (
        stream_total,
        (
            projection_grad,
            output_grad,
            expansion_grad,
            reduction_grad,
            query_scale_grad,
            unit_grad,
            alpha_sum[:, 0],
        ),
    )


def body(
    activations,
    lengths,
    projection,
    output_weight,
    expansion,
    reduction,
    query_scale,
    unit_scales,
    alphas,
    cotangent,
):
    micro, rows, part, width = activations.shape
    section = lax.axis_index("section")
    first = section == 0
    weights = (
        projection[0],
        output_weight[0],
        expansion[0],
        reduction[0],
        query_scale[0],
        unit_scales[0],
        alphas[0],
    )
    steps = micro + 1
    received = jnp.zeros((rows, part, width), jnp.bfloat16)
    outputs = []
    keeps = []
    for step in range(steps):
        index_now = jnp.clip(step - section, 0, micro - 1)
        lengths_now = lax.dynamic_index_in_dim(lengths, index_now, 0, keepdims=False)
        stream = jnp.where(first, activations[min(step, micro - 1)], received).astype(jnp.float32)
        result, kept = forward(stream, lengths_now, weights)
        result_low = result.astype(jnp.bfloat16)
        outputs.append(result_low)
        keeps.append(kept)
        if step + 1 < steps:
            received = from_behind(result_low, "section", 1)
    stacked = jnp.stack(outputs)
    layer_output = jnp.where(first, stacked[:micro], stacked[1:])[None]
    back_received = jnp.zeros((rows, part, width), jnp.bfloat16)
    slopes = []
    summed = None
    for step in range(steps):
        batch_now = step - 1 + section
        valid = (batch_now >= 0) & (batch_now < micro)
        slope = jnp.where(first, back_received, cotangent[min(step, micro - 1)]).astype(jnp.float32)
        earlier = keeps[max(step - 1, 0)]
        later = keeps[min(step + 1, micro)]
        kept = jax.tree.map(lambda left, right: jnp.where(first, left, right), earlier, later)
        stream_total, layer_grads = backward(slope, kept, weights)
        stream_low = stream_total.astype(jnp.bfloat16)
        slopes.append(stream_low)
        masked = tuple((jnp.where(valid, piece, 0.0) for piece in layer_grads))
        summed = (
            masked
            if summed is None
            else tuple((left + right for left, right in zip(summed, masked)))
        )
        if step + 1 < steps:
            back_received = from_behind(stream_low, "section", -1)
    stacked_slopes = jnp.stack(slopes)
    input_gradient = jnp.where(first, stacked_slopes[1:], stacked_slopes[:micro])[None]
    (
        projection_grad,
        output_grad,
        expansion_grad,
        reduction_grad,
        query_scale_grad,
        unit_grad,
        alpha_grad,
    ) = summed
    totals = lax.psum(
        (
            projection_grad,
            output_grad,
            expansion_grad,
            reduction_grad,
            query_scale_grad,
            unit_grad,
            alpha_grad,
        ),
        "dp",
    )
    return (
        layer_output,
        input_gradient,
        totals[0][None],
        totals[1][None],
        totals[2][None],
        totals[3][None],
        totals[4][None],
        totals[5][None],
        totals[6][None],
    )


MESH_IDS = pl.DeviceIdType.MESH
F32, BF16 = jnp.float32, jnp.bfloat16
CHUNK = 256
NN = ((1,), (0,))
NT = ((1,), (1,))


def dot(left, right, dims):
    return lax.dot_general(left, right, (dims, ((), ())), preferred_element_type=F32)


def norm_parts(v):
    rate = lax.rsqrt(jnp.mean(v * v, axis=-1, keepdims=True) + 1e-06)
    return v * rate, rate


def norm_back(slope, unit, rate):
    return rate * (slope - unit * jnp.mean(unit * slope, axis=-1, keepdims=True))


def blend_back(slope, base, branch, alpha):
    unit_branch, rate_branch = norm_parts(branch)
    toward = unit_branch - base
    unit, rate = norm_parts(base + alpha * toward)
    inner_slope = norm_back(slope, unit, rate)
    alpha_slope = jnp.sum(inner_slope * toward, axis=0, keepdims=True)
    scaled = alpha * inner_slope
    return inner_slope - scaled, norm_back(scaled, unit_branch, rate_branch), alpha_slope


def sequence_starts(lengths_ref, row, index):
    begin = jnp.zeros_like(index)
    end = jnp.int32(0)
    for sequence in range(lengths_ref.shape[2]):
        end = end + lengths_ref[row, 0, sequence]
        begin = jnp.where(index >= end, end, begin)
    return jnp.where(index < end, begin, index)


class Sizes:
    def __init__(self, tensors, places, part, width, inner, units):
        self.tensors, self.places, self.part, self.width = tensors, places, part, width
        self.inner, self.units = inner, units
        self.local = part * tensors
        self.heads = inner // HDIM


class Slots:
    def __init__(self, send, recv):
        self.send, self.recv, self.used = send, recv, 0

    def copy(self, source, target, device):
        number = self.used
        self.used += 1
        return pltpu.make_async_remote_copy(
            source, target, self.send.at[number], self.recv.at[number], device_id=device, device_id_type=MESH_IDS
        )


COPIES = 224


def relay_kernel(
    sizes,
    lengths_ref, acts_ref, cot_ref, qs_ref, us_ref, al_ref, wp_ref, wo_ref, we_ref, wr_ref,
    lo_ref, ig_ref, small_ref, attn_ref, ge_ref, gr_ref,
    wp, wo, we, wr, qs, us, al,
    stream, middles, feed_low, branch_low,
    cosines, sines, scales,
    heads_in, rates_in, probs, mixed_in, sums_in, branch_f, middle_f, feed_f, ups, gates,
    hidden, expanded_low, back_in, heads_back_in,
    heads_out, rates_out, mixed_out, back_out, heads_back_out, sums_out, go_out, go_in,
    outs, outs_in, key_rows, value_rows, query_grad, key_grad, value_grad,
    attn_own, attn_sib, attn_all, scale_own, scale_sib, scale_all,
    alpha_own, alpha_in, finals, finals_in,
    middle_cols, hidden_part, up_part, gate_part, stage_e, stage_r,
    weight_sem, weight_send, send_sem, recv_sem, stage_sem,
):
    T, Z, S, part = sizes.tensors, sizes.places, sizes.local, sizes.part
    H, inner, units, D = sizes.heads, sizes.inner, sizes.units, sizes.width
    core, t, z = lax.axis_index("section"), lax.axis_index("tensor"), lax.axis_index("dp")
    sibling = (1 - core, t, z)
    side, row = lax.rem(t, 2), t // 2
    tensor_peers = [row * 2 + (1 - side), (1 - row) * 2 + side, (1 - row) * 2 + (1 - side)]
    place_peers = [lax.rem(z + k, Z) for k in range(1, Z)]
    place_sources = [lax.rem(z + Z - k, Z) for k in range(1, Z)]
    tensor_ids = [(core, peer, z) for peer in tensor_peers]
    place_ids = [(core, t, peer) for peer in place_peers]
    slots = Slots(send_sem, recv_sem)
    pending = []

    own_weights = [(wp_ref, wp), (wo_ref, wo), (we_ref, we), (wr_ref, wr)]
    for piece, (source, target) in enumerate(own_weights):
        pltpu.make_async_copy(source, target.at[core], weight_sem.at[core, piece]).start()
    small_weights = [(qs_ref, qs), (us_ref, us), (al_ref, al)]
    for piece, (source, target) in enumerate(small_weights):
        pltpu.make_async_copy(source, target.at[core], weight_sem.at[core, 4 + piece]).start()

    barrier = pltpu.get_barrier_semaphore()
    partners = [sibling] + tensor_ids + place_ids
    for partner in partners:
        pl.semaphore_signal(barrier, inc=1, device_id=partner, device_id_type=MESH_IDS)
    pl.semaphore_wait(barrier, len(partners))

    for piece, (source, target) in list(enumerate(small_weights, 4)) + list(enumerate(own_weights)):
        copy = pltpu.make_async_remote_copy(
            source, target.at[core], weight_send.at[piece], weight_sem.at[core, piece], device_id=sibling, device_id_type=MESH_IDS
        )
        copy.start()
        pending.append(copy)

    def await_weight(layer, piece):
        source, target = (own_weights + small_weights)[piece]
        pltpu.make_async_copy(source, target.at[layer], weight_sem.at[layer, piece]).wait()

    def send(source, target, device):
        copy = slots.copy(source, target, device)
        copy.start()
        pending.append(copy)
        return copy

    def arrive(copies):
        for copy in copies:
            copy.wait_recv()

    def rows_of(index):
        return pl.ds(pl.multiple_of(index * part, part), part)

    my_rows, far_rows = rows_of(t), rows_of(tensor_peers[2])

    def gather(layer, target, value):
        target[layer, z, my_rows, :] = value
        mine = target.at[layer, z, my_rows, :]
        return [send(mine, mine, device) for device in tensor_ids]

    def to_places(layer, target, rows):
        mine = target.at[layer, z, rows, :]
        return [send(mine, mine, device) for device in place_ids]

    def pass_on(layer, target, copies):
        passed = []
        for copy, place in zip(copies, place_sources):
            copy.wait_recv()
            got = target.at[layer, place, my_rows, :]
            passed += [send(got, got, device) for device in tensor_ids[:2]]
        return passed

    def scatter(number):
        return [
            send(sums_out.at[number, peer], sums_in.at[number, k], device)
            for k, (peer, device) in enumerate(zip(tensor_peers, tensor_ids))
        ]

    def scattered(number, copies):
        arrive(copies)
        total = sums_out[number, t].astype(F32)
        for k in range(T - 1):
            total = total + sums_in[number, k].astype(F32)
        return total

    def retire(copies):
        for copy in copies:
            copy.wait_send()
        pending[:] = [copy for copy in pending if not any(copy is done for done in copies)]

    def spread(source, target):
        target[z] = source[z]
        return [send(source.at[peer], target.at[z], device) for peer, device in zip(place_peers, place_ids)]

    half = HDIM // 2
    index_all = lax.broadcasted_iota(jnp.int32, (1, S * Z), 1)
    starts = sequence_starts(lengths_ref, core, index_all)
    rates = jnp.exp(lax.broadcasted_iota(jnp.int32, (half, 1), 0).astype(F32) * (-2.0 * math.log(10000.0) / HDIM))
    angle = rates * (index_all - starts).astype(F32)
    cosine, sine = jnp.cos(angle), jnp.sin(angle)
    for place in range(Z):
        cosines[place] = cosine[:, place * S : (place + 1) * S]
        sines[place] = sine[:, place * S : (place + 1) * S]
    key_index = lax.broadcasted_iota(jnp.int32, (S * Z, S), 0)

    def block(query, key):
        return query * (query + 1) // 2 + key

    used, waiting = {}, {}

    def free(name):
        retire(used.pop(name, []))

    def forward(layer, base_low):
        stream_copies = gather(layer, stream, base_low)
        stream_places = to_places(layer, stream, my_rows)
        await_weight(layer, 0)
        for piece in (4, 5, 6):
            await_weight(layer, piece)
        scale = jnp.broadcast_to(jnp.broadcast_to(qs[layer], (8, inner)).T[:, :1], (inner, 128)).reshape(H, HDIM, 128)
        scales[layer] = scale
        base = base_low.astype(F32)
        cosine_here, sine_here = cosines[z][None], sines[z][None]
        arrive(stream_copies)
        free("heads")
        gathered = stream[layer, z]
        for third in range(3):
            piece = dot(gathered, wp[layer, third], NN).T.reshape(H, HDIM, S)
            if third < 2:
                front, back = piece[:, :half], piece[:, half:]
                piece = jnp.concatenate([front * cosine_here - back * sine_here, back * cosine_here + front * sine_here], axis=1)
                speed = lax.rsqrt(jnp.sum(piece * piece, axis=1, keepdims=True) + 1e-06)
                piece = piece * speed * scale[:, :, :1]
                for head in range(H):
                    rates_out[head, third : third + 1] = speed[head]
            heads_out[:, third] = piece.astype(BF16)
        copies = spread(heads_out, heads_in.at[layer])
        rate_copies = spread(rates_out, rates_in.at[layer])
        used["heads"] = copies + rate_copies
        stream_places += to_places(layer, stream, far_rows)
        stream_passed = pass_on(layer, stream, stream_places[: Z - 1])
        if layer:
            waiting["middle", 0] = pass_on(0, middles, waiting["middle", 0])
        arrive(copies + rate_copies)
        for place in range(Z):
            key_rows[place] = heads_in[layer, place, 1].T
        free("mixed")
        for query in range(Z):
            raw = [dot(key_rows[key], heads_in[layer, query, 0], NN) * math.sqrt(HDIM) for key in range(query + 1)]
            first = starts[:, query * S : (query + 1) * S]
            last = index_all[:, query * S : (query + 1) * S]
            scores = []
            for key in range(query + 1):
                keys = key_index[key * S : (key + 1) * S]
                allowed = keys >= first
                if key == query:
                    allowed = allowed & (keys <= last)
                scores.append(jnp.where(allowed, raw[key], -1e30))
            highest = scores[0].max(axis=0, keepdims=True)
            for piece in scores[1:]:
                highest = jnp.maximum(highest, piece.max(axis=0, keepdims=True))
            lifted = [jnp.exp(piece - highest) for piece in scores]
            total = lifted[0].sum(axis=0, keepdims=True)
            for piece in lifted[1:]:
                total = total + piece.sum(axis=0, keepdims=True)
            shrink = 1.0 / total
            mixed = None
            for key in range(query + 1):
                low = (lifted[key] * shrink).astype(BF16)
                probs[layer, block(query, key)] = low
                term = dot(heads_in[layer, key, 2], low, NN)
                mixed = term if mixed is None else mixed + term
            mixed_out[query] = mixed.astype(BF16)
        copies = spread(mixed_out, mixed_in.at[layer])
        used["mixed"] = copies
        await_weight(layer, 1)
        arrive(copies)
        attended = mixed_in[layer].reshape(inner, S).T
        free("branch")
        sums_out[0] = dot(attended, wo[layer], NN).astype(BF16).reshape(T, part, D)
        copies = scatter(0)
        branch = scattered(0, copies)
        used["branch"] = copies
        branch_f[layer] = branch
        alpha = al[layer]
        middle = norm_parts(base + alpha[0:1] * (norm_parts(branch)[0] - base))[0]
        middle_f[layer] = middle
        copies = gather(layer, middles, middle.astype(BF16))
        middle_places = to_places(layer, middles, my_rows)
        await_weight(layer, 2)
        arrive(copies)
        middle_far = to_places(layer, middles, far_rows)
        middle_all = middles[layer, z]
        for begin in range(0, units, CHUNK):
            cols = slice(begin, begin + CHUNK)
            up = dot(middle_all, we[layer, 0, :, cols], NN)
            gate = dot(middle_all, we[layer, 1, :, cols], NN)
            ups[layer, :, cols] = up.astype(BF16)
            gates[layer, :, cols] = gate.astype(BF16)
            inside = us[layer, 1:2, cols] * gate
            hidden[:, cols] = (us[layer, 0:1, cols] * up * (inside / (1.0 + jnp.exp(-inside)))).astype(BF16)
        await_weight(layer, 3)
        free("feed")
        acted = hidden[...]
        for begin in range(0, D, CHUNK):
            cols = slice(begin, begin + CHUNK)
            sums_out[1, :, :, cols] = dot(acted, wr[layer, :, cols], NN).astype(BF16).reshape(T, part, CHUNK)
        copies = scatter(1)
        feed = scattered(1, copies)
        used["feed"] = copies
        feed_f[layer] = feed
        result = norm_parts(middle + alpha[1:2] * (norm_parts(feed)[0] - middle))[0].astype(BF16)
        outs[0, layer] = result
        waiting["stream", layer] = stream_passed + stream_places[Z - 1 :]
        waiting["middle", layer] = middle_places
        waiting["middle far", layer] = middle_far
        return result

    def act_back(layer, cols, up, gate, slope_hidden):
        scale_up, scale_gate = us[layer, 0:1, cols], us[layer, 1:2, cols]
        inside = scale_gate * gate
        sigmoid = 1.0 / (1.0 + jnp.exp(-inside))
        silu = inside * sigmoid
        by_up = silu * slope_hidden
        by_gate = scale_up * up * (sigmoid + silu * (1.0 - sigmoid)) * slope_hidden
        return silu, by_up, by_gate

    def stage_copy(layer, chunk, which):
        buffer = (stage_e, stage_r)[which].at[chunk % 2]
        target = (ge_ref.at[0, chunk], gr_ref.at[0, chunk])[which]
        return pltpu.make_async_copy(buffer, target, stage_sem.at[layer, chunk, which])

    stage_slots = {}

    def stage_send(layer, chunk, which):
        buffer = (stage_e, stage_r)[which].at[chunk % 2]
        target = (ge_ref.at[1, chunk], gr_ref.at[1, chunk])[which]
        if (chunk, which) not in stage_slots:
            stage_slots[chunk, which] = slots.used
            slots.used += 1
        number = stage_slots[chunk, which]
        return pltpu.make_async_remote_copy(
            buffer, target, send_sem.at[number], recv_sem.at[number], device_id=sibling, device_id_type=MESH_IDS
        )

    def stage_wait(layer, chunk):
        @pl.when(core == layer)
        def _():
            for which in range(2):
                stage_copy(layer, chunk, which).wait()

        @pl.when(core != layer)
        def _():
            for which in range(2):
                stage_send(layer, chunk, which).wait_send()

    staged = []

    def feed_grads(layer, chunk):
        if chunk == 0:
            for place in range(Z):
                middle_cols[:, place * S : (place + 1) * S] = middles[layer, place].T
        cols = slice(chunk * CHUNK, (chunk + 1) * CHUNK)
        scale_up, scale_gate = us[layer, 0:1, cols], us[layer, 1:2, cols]
        sum_up = sum_gate = None
        for place in range(Z):
            rows = slice(place * S, (place + 1) * S)
            up = dot(middles[layer, place], we[layer, 0, :, cols], NN)
            gate = dot(middles[layer, place], we[layer, 1, :, cols], NN)
            slope_hidden = dot(feed_low[layer, place], wr[layer, cols, :], NT)
            silu, by_up, by_gate = act_back(layer, cols, up, gate, slope_hidden)
            hidden_part[:, rows] = (scale_up * up * silu).astype(BF16).T
            up_part[rows] = (by_up * scale_up).astype(BF16)
            gate_part[rows] = (by_gate * scale_gate).astype(BF16)
            term_up = jnp.sum(by_up * up, axis=0, keepdims=True)
            term_gate = jnp.sum(by_gate * gate, axis=0, keepdims=True)
            sum_up = term_up if sum_up is None else sum_up + term_up
            sum_gate = term_gate if sum_gate is None else sum_gate + term_gate
        finals[layer, 2:3, cols] = sum_up
        finals[layer, 3:4, cols] = sum_gate
        if len(staged) >= 2:
            stage_wait(*staged[-2])
        buffer = chunk % 2
        stage_e[buffer, 0] = dot(middle_cols[...], up_part[...], NN).astype(BF16)
        stage_e[buffer, 1] = dot(middle_cols[...], gate_part[...], NN).astype(BF16)
        stage_r[buffer] = dot(hidden_part[...], feed_low[layer].reshape(Z * S, D), NN).astype(BF16)

        @pl.when(core == layer)
        def _():
            for which in range(2):
                stage_copy(layer, chunk, which).start()

        @pl.when(core != layer)
        def _():
            for which in range(2):
                stage_send(layer, chunk, which).start()

        staged.append((layer, chunk))

    chunks = units // CHUNK
    attn_slot = [slots.used + k for k in range(2 + 2 * (Z - 1))]
    slots.used += len(attn_slot)

    def pair(number, source, target, device):
        return pltpu.make_async_remote_copy(
            source, target, send_sem.at[attn_slot[number]], recv_sem.at[attn_slot[number]], device_id=device, device_id_type=MESH_IDS
        )

    def attn_pair():
        return [pair(0, attn_own, attn_sib, sibling), pair(1, scale_own, scale_sib, sibling)]

    def attn_spread():
        return [pair(2 + 2 * k, attn_all.at[z], attn_all.at[z], device) for k, device in enumerate(place_ids)] + [
            pair(3 + 2 * k, scale_all.at[z], scale_all.at[z], device) for k, device in enumerate(place_ids)
        ]

    def attn_offer(layer):
        @pl.when(core != layer)
        def _():
            for copy in attn_pair():
                copy.start()

    def attn_join(layer):
        @pl.when(core == layer)
        def _():
            for copy in attn_pair():
                copy.wait_recv()
            attn_all[z] = (attn_own[...].astype(F32) + attn_sib[...].astype(F32)).astype(BF16)
            scale_all[z] = scale_own[...] + scale_sib[...]
            for copy in attn_spread():
                copy.start()

        @pl.when(core != layer)
        def _():
            for copy in attn_pair():
                copy.wait_send()

    def backward(layer, base_low, slope):
        alpha = al[layer]
        middle_slope, feed_slope, alpha_m = blend_back(slope, middle_f[layer], feed_f[layer], alpha[1:2])
        copies = gather(layer, feed_low, feed_slope.astype(BF16))
        feed_places = to_places(layer, feed_low, my_rows)
        alpha_own[layer, 1:2] = alpha_m
        if layer == 0:
            feed_grads(1, chunks - 1)
        arrive(copies)
        feed_far = to_places(layer, feed_low, far_rows)
        feed_all = feed_low[layer, z]
        for begin in range(0, units, CHUNK):
            cols = slice(begin, begin + CHUNK)
            slope_hidden = dot(feed_all, wr[layer, cols, :], NT)
            up, gate = ups[layer, :, cols].astype(F32), gates[layer, :, cols].astype(F32)
            _, by_up, by_gate = act_back(layer, cols, up, gate, slope_hidden)
            expanded_low[0, :, cols] = (by_up * us[layer, 0:1, cols]).astype(BF16)
            expanded_low[1, :, cols] = (by_gate * us[layer, 1:2, cols]).astype(BF16)
        free("middle_back")
        for begin in range(0, D, CHUNK):
            rows = slice(begin, begin + CHUNK)
            partial = dot(expanded_low[0], we[layer, 0, rows, :], NT) + dot(expanded_low[1], we[layer, 1, rows, :], NT)
            sums_out[2, :, :, rows] = partial.astype(BF16).reshape(T, part, CHUNK)
        copies = scatter(2)
        middle_total = middle_slope + scattered(2, copies)
        used["middle_back"] = copies
        stream_slope, branch_slope, alpha_a = blend_back(middle_total, base_low.astype(F32), branch_f[layer], alpha[0:1])
        free("branch_low")
        branch_low[my_rows, :] = branch_slope.astype(BF16)
        mine = branch_low.at[my_rows, :]
        copies = [send(mine, mine, device) for device in tensor_ids]
        used["branch_low"] = copies
        alpha_own[layer, 0:1] = alpha_a
        if layer == 0:
            alpha_copies = [send(alpha_own, alpha_in.at[k], device) for k, device in enumerate(tensor_ids)]
        arrive(copies)
        feed_passed = pass_on(layer, feed_low, feed_places)
        branch_all = branch_low[...]
        free("mixed_back")
        back_out[...] = dot(wo[layer], branch_all, NT).astype(BF16).reshape(H, HDIM, S)
        copies = spread(back_out, back_in)
        used["mixed_back"] = copies
        free("go")
        go_out[...] = dot(mixed_in[layer].reshape(inner, S), branch_all, NN).astype(BF16).reshape(H, HDIM, D)
        go_copies = [send(go_out.at[peer], go_in.at[layer, k], device) for k, (peer, device) in enumerate(zip(place_peers, place_ids))]
        used["go"] = go_copies
        if layer:
            waiting["middle", 1] = pass_on(1, middles, waiting["middle", 1])
        for place in range(Z):
            value_rows[place] = heads_in[layer, place, 2].T
        if layer == 0:
            arrive(alpha_copies)
            retire(alpha_copies)
            total = alpha_own[...]
            for k in range(T - 1):
                total = total + alpha_in[k]
            alpha_own[...] = total
            alpha_copies = [send(alpha_own, alpha_in.at[T - 1 + k], device) for k, device in enumerate(place_ids)]
        arrive(copies)
        for query in range(Z):
            slope_mixed = back_in[query]
            lows = [probs[layer, block(query, key)] for key in range(query + 1)]
            probs_slope = [dot(value_rows[key], slope_mixed, NN) for key in range(query + 1)]
            row_term = None
            for low, piece in zip(lows, probs_slope):
                term = jnp.sum(low.astype(F32) * piece, axis=0, keepdims=True)
                row_term = term if row_term is None else row_term + term
            query_slope = None
            for key in range(query + 1):
                low = lows[key]
                scores_low = (low.astype(F32) * (probs_slope[key] - row_term)).astype(BF16)
                term = dot(heads_in[layer, key, 1], scores_low, NN)
                query_slope = term if query_slope is None else query_slope + term
                key_term = dot(heads_in[layer, query, 0], scores_low, NT)
                value_term = dot(slope_mixed, low, NT)
                if key == query:
                    key_grad[key] = key_term
                    value_grad[key] = value_term
                else:
                    key_grad[key] += key_term
                    value_grad[key] += value_term
            query_grad[query] = query_slope
        free("heads_back")
        scale = scales[layer, z][:, :1]
        inverse = 1.0 / scale
        scale_slope = None
        for place in range(Z):
            cosine_there, sine_there = cosines[place], sines[place]
            for third, source in ((0, query_grad), (1, key_grad)):
                piece = source[place] * math.sqrt(HDIM)
                unit = heads_in[layer, place, third].astype(F32) * inverse
                term = jnp.sum(piece * unit, axis=1, keepdims=True)
                scale_slope = term if scale_slope is None else scale_slope + term
                piece = piece * scale
                piece = rates_in[layer, place, third : third + 1] * (piece - unit * jnp.sum(unit * piece, axis=0, keepdims=True))
                front, back = piece[:half], piece[half:]
                piece = jnp.concatenate([front * cosine_there + back * sine_there, back * cosine_there - front * sine_there], axis=0)
                heads_back_out[place, third] = piece.astype(BF16)
            heads_back_out[place, 2] = value_grad[place].astype(BF16)
        copies = spread(heads_back_out, heads_back_in)
        used["heads_back"] = copies
        arrive(waiting["stream", layer])
        grad = None
        for place in range(Z):
            term = dot(heads_back_out[place].reshape(3 * HDIM, S), stream[layer, place], NN)
            grad = term if grad is None else grad + term
        attn_own[: 3 * HDIM] = grad.astype(BF16)
        arrive(go_copies)
        total = go_out[z].astype(F32)
        for k in range(Z - 1):
            total = total + go_in[layer, k].astype(F32)
        attn_own[3 * HDIM :] = total.astype(BF16)
        scale_rows = jnp.broadcast_to(scale_slope, (HDIM, 128)).T[:8]
        scale_own[...] = jnp.concatenate([scale_rows, scale_rows], axis=1)
        attn_offer(layer)
        arrive(feed_passed + feed_far)
        if layer:
            arrive(waiting["middle", 1] + waiting["middle far", 1])
        else:
            arrive(waiting["middle", 0] + waiting["middle far", 0])
        for chunk in range(2):
            feed_grads(layer, chunk)
        if layer == 0:
            arrive(alpha_copies)
            total = alpha_own[...]
            for k in range(Z - 1):
                total = total + alpha_in[T - 1 + k]
            finals[0, 0:2] = total[0]
            finals[1, 0:2] = total[1]
        arrive(copies)
        partial = None
        for third in range(3):
            term = dot(heads_back_in[:, third].reshape(inner, S).T, wp[layer, third], NT)
            partial = term if partial is None else partial + term
        free("stream_back")
        sums_out[3] = partial.astype(BF16).reshape(T, part, D)
        copies = scatter(3)
        attn_join(layer)
        for chunk in range(2, chunks if layer == 0 else chunks - 1):
            feed_grads(layer, chunk)
        result = (stream_slope + scattered(3, copies)).astype(BF16)
        used["stream_back"] = copies
        outs[1, layer] = result
        return result

    forward(1, forward(0, acts_ref[core, 0]))
    slope = backward(1, outs[0, 0], cot_ref[core, 0].astype(F32))
    backward(0, acts_ref[core, 0], slope.astype(F32))

    other = 1 - core
    last = [send(outs.at[:, other], outs_in, sibling), send(finals.at[other], finals_in, sibling)]
    for kind, target in enumerate((lo_ref, ig_ref)):
        target[core] = outs[kind, core]
    arrive(last)
    for kind, target in enumerate((lo_ref, ig_ref)):
        target[other] = outs_in[kind]
    small_ref[0:4] = finals[core] + finals_in[...]
    for layer, chunk in staged[-2:]:
        stage_wait(layer, chunk)
    for chunk in range(chunks):
        for which in range(2):
            stage_send(0, chunk, which).wait_recv()
    for copy in attn_spread():
        copy.wait_recv()
    attn_copy = pltpu.make_async_copy(attn_all, attn_ref, stage_sem.at[0, 0, 0])
    attn_copy.start()
    for place in range(Z):
        small_ref[4 + place : 5 + place, :128] = scale_all[place, :1]
    for copy in attn_spread() + pending:
        copy.wait_send()
    attn_copy.wait()
    assert slots.used <= COPIES, slots.used


def relay(sizes, lengths, acts, cot, qs, us, al, wp, wo, we, wr):
    T, Z, S, part = sizes.tensors, sizes.places, sizes.local, sizes.part
    H, inner, units, D = sizes.heads, sizes.inner, sizes.units, sizes.width
    blocks, chunks = Z * (Z + 1) // 2, units // CHUNK
    vmem = pl.BlockSpec(memory_space=pltpu.VMEM)
    hbm = pl.BlockSpec(memory_space=pl.ANY)
    out_shape = (
        jax.ShapeDtypeStruct((2, part, D), BF16),
        jax.ShapeDtypeStruct((2, part, D), BF16),
        jax.ShapeDtypeStruct((4 + Z, D), F32),
        jax.ShapeDtypeStruct((Z, 4 * HDIM, D), BF16),
        jax.ShapeDtypeStruct((2, chunks, 2, D, CHUNK), BF16),
        jax.ShapeDtypeStruct((2, chunks, CHUNK, D), BF16),
    )
    DMA = pltpu.SemaphoreType.DMA
    V = pltpu.VMEM
    scratch = [
        V((2, 3, D, inner), BF16), V((2, inner, D), BF16), V((2, 2, D, units), BF16), V((2, units, D), BF16),
        V((2, 1, inner), F32), V((2, 2, units), F32), V((2, 2, D), F32),
        V((2, Z, S, D), BF16), V((2, Z, S, D), BF16), V((2, Z, S, D), BF16), V((S, D), BF16),
        V((Z, HDIM // 2, S), F32), V((Z, HDIM // 2, S), F32), V((2, H, HDIM, 128), F32),
        V((2, Z, 3, HDIM, S), BF16), V((2, Z, 2, S), F32),
        V((2, blocks, S, S), BF16), V((2, H, HDIM, S), BF16),
        V((4, T - 1, part, D), BF16),
        V((2, part, D), F32), V((2, part, D), F32), V((2, part, D), F32),
        V((2, S, units), BF16), V((2, S, units), BF16),
        V((S, units), BF16), V((2, S, units), BF16),
        V((Z, HDIM, S), BF16), V((H, 3, HDIM, S), BF16),
        V((H, 3, HDIM, S), BF16), V((H, 2, S), F32),
        V((Z, HDIM, S), BF16), V((H, HDIM, S), BF16), V((Z, 3, HDIM, S), BF16),
        V((4, T, part, D), BF16), V((H, HDIM, D), BF16), V((2, Z - 1, HDIM, D), BF16),
        V((2, 2, part, D), BF16), V((2, part, D), BF16),
        V((Z, S, HDIM), BF16), V((Z, S, HDIM), BF16),
        V((Z, HDIM, S), F32), V((Z, HDIM, S), F32), V((Z, HDIM, S), F32),
        V((4 * HDIM, D), BF16), V((4 * HDIM, D), BF16), V((Z, 4 * HDIM, D), BF16),
        V((8, 128), F32), V((8, 128), F32), V((Z, 8, 128), F32),
        V((2, 2, D), F32), V((T + Z - 2, 2, 2, D), F32), V((2, 4, D), F32), V((4, D), F32),
        V((D, Z * S), BF16), V((CHUNK, Z * S), BF16), V((Z * S, CHUNK), BF16), V((Z * S, CHUNK), BF16),
        V((2, 2, D, CHUNK), BF16), V((2, CHUNK, D), BF16),
        DMA((2, 7)), DMA((7,)), DMA((COPIES,)), DMA((COPIES,)), DMA((2, chunks, 2)),
    ]
    return pl.pallas_call(
        functools.partial(relay_kernel, sizes),
        out_shape=out_shape,
        in_specs=[pl.BlockSpec(memory_space=pltpu.SMEM), vmem, vmem, vmem, vmem, vmem, hbm, hbm, hbm, hbm],
        out_specs=(vmem, vmem, vmem, hbm, hbm, hbm),
        scratch_shapes=scratch,
        compiler_params=pltpu.CompilerParams(collective_id=0, has_side_effects=True, vmem_limit_bytes=62 * 2**20),
        name="relay",
    )(lengths, acts, cot, qs, us, al, wp, wo, we, wr)


def fast_body(
    activations, lengths, projection, output_weight, expansion, reduction, query_scale, unit_scales, alphas, cotangent
):
    _, _, part, width = activations.shape
    inner, units = output_weight.shape[1], reduction.shape[1]
    places = lax.axis_size("dp")
    sizes = Sizes(lax.axis_size("tensor"), places, part, width, inner, units)
    lo, ig, small, attn, ge, gr = relay(
        sizes, lengths, activations, cotangent, query_scale, unit_scales[0], alphas[0],
        projection[0].transpose(1, 0, 2), output_weight[0], expansion[0].transpose(1, 0, 2), reduction[0],
    )
    attn = attn.astype(F32)
    projection_grad = attn[:, : 3 * HDIM].reshape(places, 3, HDIM, width).transpose(3, 1, 0, 2).reshape(width, 3, inner)
    output_grad = attn[:, 3 * HDIM :].reshape(inner, width)
    expansion_grad = (ge[0].astype(F32) + ge[1].astype(F32)).transpose(2, 1, 0, 3).reshape(width, 2, units)
    reduction_grad = (gr[0].astype(F32) + gr[1].astype(F32)).reshape(units, width)
    return (
        lo[None, :, None],
        ig[None, :, None],
        projection_grad[None],
        output_grad[None],
        expansion_grad[None],
        reduction_grad[None],
        small[4:, :HDIM].reshape(1, inner),
        small[None, 2:4, :units],
        small[None, 0:2],
    )


def solution(mesh):
    in_specs = (
        P(None, None, ("dp", "tensor"), None),
        P(),
        P("section", None, None, "tensor"),
        P("section", "tensor", None),
        P("section", None, None, "tensor"),
        P("section", "tensor", None),
        P("section", "tensor"),
        P("section", None, "tensor"),
        P("section", None, None),
        P(None, None, ("dp", "tensor"), None),
    )
    out_specs = (
        P("section", None, None, ("dp", "tensor"), None),
        P("section", None, None, ("dp", "tensor"), None),
        P("section", None, None, "tensor"),
        P("section", "tensor", None),
        P("section", None, None, "tensor"),
        P("section", "tensor", None),
        P("section", "tensor"),
        P("section", None, "tensor"),
        P("section", None, None),
    )
    def chosen(*arrays):
        activations, output_weight = arrays[0], arrays[3]
        heads = output_weight.shape[1] // HDIM
        fits = (
            mesh.shape["section"] == 2
            and mesh.shape["tensor"] == 4
            and mesh.shape["dp"] == heads
            and activations.shape[:2] == (2, 1)
            and activations.shape[2] * mesh.shape["tensor"] == 256
        )
        return (fast_body if fits else body)(*arrays)

    return jax.shard_map(chosen, mesh=mesh, in_specs=in_specs, out_specs=out_specs, check_vma=False)
```

```python
import functools
import math

import jax
import jax.numpy as jnp
from jax import lax
from jax.experimental import pallas as pl
from jax.experimental.pallas import tpu as pltpu
from jax.sharding import PartitionSpec as P

HDIM = 64


def from_behind(value, axis, steps):
    count = lax.axis_size(axis)
    initial, last = (max(0, -steps), min(count, count - steps))
    return lax.ppermute(value, axis, [(source, source + steps) for source in range(initial, last)])


def normed(v):
    return v * lax.rsqrt(jnp.mean(v * v, axis=-1, keepdims=True) + 1e-06)


def unit_heads(v):
    return v * lax.rsqrt(jnp.sum(v * v, axis=-1, keepdims=True) + 1e-06)


def frequencies(half):
    return jnp.exp(jnp.arange(half, dtype=jnp.float32) * (-2.0 * math.log(10000.0) / (2 * half)))


def rotate(view, angle):
    half = view.shape[-1] // 2
    cosine = jnp.cos(angle)[..., None, :]
    sine = jnp.sin(angle)[..., None, :]
    front = view[..., :half]
    back = view[..., half:]
    return jnp.concatenate([front * cosine - back * sine, back * cosine + front * sine], axis=-1)


def shaped(projected, scale, angle, heads):
    inner = projected.shape[-1] // 3
    lead = projected.shape[:-1]

    def turned(piece):
        view = piece.reshape(lead + (heads, inner // heads))
        return unit_heads(rotate(view, angle)).reshape(lead + (inner,)) * scale

    return (
        turned(projected[..., :inner]),
        turned(projected[..., inner : 2 * inner]),
        projected[..., 2 * inner :],
    )


def layout(lengths_row, slots):
    ends = jnp.cumsum(lengths_row, dtype=jnp.int32)
    index = jnp.arange(slots, dtype=jnp.int32)
    after = index[:, None] >= ends[None, :]
    segment = jnp.sum(after.astype(jnp.int32), axis=1, dtype=jnp.int32)
    begin = jnp.sum(jnp.where(after, lengths_row[None, :], 0), axis=1, dtype=jnp.int32)
    inside = index < ends[-1]
    segment = jnp.where(inside, segment, lengths_row.shape[0] + index)
    position = jnp.where(inside, index - begin, 0)
    return (segment, position)


def blend(base, branch, alpha):
    return normed(base + alpha * (normed(branch) - base))


def activate(expanded, scales):
    half = expanded.shape[-1] // 2
    return expanded[..., :half] * scales[0] * jax.nn.silu(expanded[..., half:] * scales[1])


def placing(lengths_now, local):
    slots = local * lax.axis_size("dp")
    start_here = lax.axis_index("dp") * local
    segment_all, position_all = jax.vmap(lambda row: layout(row, slots))(lengths_now)
    segment_here = lax.dynamic_slice_in_dim(segment_all, start_here, local, 1)
    position_here = lax.dynamic_slice_in_dim(position_all, start_here, local, 1)
    index_here = start_here + jnp.arange(local, dtype=jnp.int32)
    every = jnp.arange(slots, dtype=jnp.int32)
    allowed = (segment_here[:, :, None] == segment_all[:, None, :]) & (
        every[None, None, :] <= index_here[None, :, None]
    )
    angle = position_here.astype(jnp.float32)[..., None] * frequencies(HDIM // 2)
    return (allowed, angle)


def scored(query, key_all, allowed, heads):
    rows, local, inner = query.shape
    depth = inner // heads
    query_heads = query.reshape(rows, local, heads, depth)
    key_heads = key_all.reshape(rows, key_all.shape[1], heads, depth)
    raw = jnp.einsum(
        "rqhe,rkhe->rhqk", query_heads, key_heads, preferred_element_type=jnp.float32
    ) * math.sqrt(depth)
    return jnp.where(allowed[:, None], raw, -1e30)


def forward(stream, lengths_now, weights):
    projection, output_weight, expansion, reduction, query_scale, unit_scales, alphas = weights
    rows, part, width = stream.shape
    inner = output_weight.shape[0]
    heads = inner // HDIM
    hidden_width = reduction.shape[0]
    gathered = lax.all_gather(stream.astype(jnp.bfloat16), "tensor", axis=1, tiled=True)
    local = gathered.shape[1]
    allowed, angle = placing(lengths_now, local)
    projected = jnp.einsum(
        "rsd,dc->rsc",
        gathered,
        projection.reshape(width, 3 * inner),
        preferred_element_type=jnp.float32,
    )
    query, key, value = shaped(projected, query_scale, angle, heads)
    query_low = query.astype(jnp.bfloat16)
    key_low = key.astype(jnp.bfloat16)
    value_low = value.astype(jnp.bfloat16)
    key_all, value_all = (
        lax.all_gather(key_low, "dp", axis=1, tiled=True),
        lax.all_gather(value_low, "dp", axis=1, tiled=True),
    )
    scores = scored(query_low, key_all, allowed, heads)
    highest = jnp.max(scores, axis=-1, keepdims=True)
    lifted = jnp.exp(scores - highest)
    total = jnp.sum(lifted, axis=-1, keepdims=True)
    log_total = highest + jnp.log(total)
    probs_low = (lifted / total).astype(jnp.bfloat16)
    value_heads = value_all.reshape(rows, value_all.shape[1], heads, HDIM)
    mixed = jnp.einsum(
        "rhqk,rkhe->rqhe", probs_low, value_heads, preferred_element_type=jnp.float32
    )
    attended = mixed.reshape(rows, local, inner).astype(jnp.bfloat16)
    partial_branch = jnp.einsum(
        "rsc,cd->rsd", attended, output_weight, preferred_element_type=jnp.float32
    )
    branch = lax.psum_scatter(partial_branch, "tensor", scatter_dimension=1, tiled=True)
    middle = blend(stream, branch, alphas[0])
    middle_all = lax.all_gather(middle.astype(jnp.bfloat16), "tensor", axis=1, tiled=True)
    expanded = jnp.einsum(
        "rsd,dc->rsc",
        middle_all,
        expansion.reshape(width, 2 * hidden_width),
        preferred_element_type=jnp.float32,
    )
    hidden = activate(expanded, unit_scales).astype(jnp.bfloat16)
    partial_feed = jnp.einsum("rsf,fd->rsd", hidden, reduction, preferred_element_type=jnp.float32)
    feed = lax.psum_scatter(partial_feed, "tensor", scatter_dimension=1, tiled=True)
    result = blend(middle, feed, alphas[1])
    kept = dict(
        stream=stream,
        gathered=gathered,
        projected=projected,
        query=query_low,
        key=key_low,
        value=value_low,
        log_total=log_total,
        attended=attended,
        branch=branch,
        middle=middle,
        middle_all=middle_all,
        expanded=expanded,
        hidden=hidden,
        feed=feed,
        lengths=lengths_now,
    )
    kept = dict(kept, key_all=key_all, value_all=value_all)
    return (result, kept)


def backward(slope, kept, weights):
    projection, output_weight, expansion, reduction, query_scale, unit_scales, alphas = weights
    rows, part, width = slope.shape
    inner = output_weight.shape[0]
    heads = inner // HDIM
    hidden_width = reduction.shape[0]
    _, pull_feed = jax.vjp(blend, kept["middle"], kept["feed"], alphas[1])
    middle_slope, feed_slope, alpha_feed = pull_feed(slope)
    feed_all = lax.all_gather(feed_slope.astype(jnp.bfloat16), "tensor", axis=1, tiled=True)
    reduction_grad = jnp.einsum(
        "rsf,rsd->fd", kept["hidden"], feed_all, preferred_element_type=jnp.float32
    )
    hidden_slope = jnp.einsum(
        "rsd,fd->rsf", feed_all, reduction, preferred_element_type=jnp.float32
    )
    _, pull_active = jax.vjp(activate, kept["expanded"], unit_scales)
    expanded_slope, unit_grad = pull_active(hidden_slope)
    expanded_low = expanded_slope.astype(jnp.bfloat16)
    expansion_grad = jnp.einsum(
        "rsd,rsc->dc", kept["middle_all"], expanded_low, preferred_element_type=jnp.float32
    ).reshape(width, 2, hidden_width)
    partial_middle = jnp.einsum(
        "rsc,dc->rsd",
        expanded_low,
        expansion.reshape(width, 2 * hidden_width),
        preferred_element_type=jnp.float32,
    )
    middle_total = middle_slope + lax.psum_scatter(
        partial_middle, "tensor", scatter_dimension=1, tiled=True
    )
    _, pull_branch = jax.vjp(blend, kept["stream"], kept["branch"], alphas[0])
    stream_slope, branch_slope, alpha_branch = pull_branch(middle_total)
    branch_all = lax.all_gather(branch_slope.astype(jnp.bfloat16), "tensor", axis=1, tiled=True)
    output_grad = jnp.einsum(
        "rsc,rsd->cd", kept["attended"], branch_all, preferred_element_type=jnp.float32
    )
    attended_low = jnp.einsum(
        "rsd,cd->rsc", branch_all, output_weight, preferred_element_type=jnp.float32
    ).astype(jnp.bfloat16)
    local = attended_low.shape[1]
    key_all = kept["key_all"]
    value_all = kept["value_all"]
    slots = key_all.shape[1]
    allowed, angle = placing(kept["lengths"], local)
    scores = scored(kept["query"], key_all, allowed, heads)
    probs = jnp.exp(scores - kept["log_total"])
    scale = math.sqrt(HDIM)
    back_heads = attended_low.reshape(rows, local, heads, HDIM)
    query_heads = kept["query"].reshape(rows, local, heads, HDIM)
    key_heads = key_all.reshape(rows, slots, heads, HDIM)
    value_heads = value_all.reshape(rows, slots, heads, HDIM)
    probs_slope = jnp.einsum(
        "rqhe,rkhe->rhqk", back_heads, value_heads, preferred_element_type=jnp.float32
    )
    row_term = jnp.sum(probs * probs_slope, axis=-1, keepdims=True)
    scores_low = (probs * (probs_slope - row_term)).astype(jnp.bfloat16)
    query_slope = (
        jnp.einsum("rhqk,rkhe->rqhe", scores_low, key_heads, preferred_element_type=jnp.float32)
        * scale
    )
    value_grad_all = jnp.einsum(
        "rhqk,rqhe->rkhe",
        probs.astype(jnp.bfloat16),
        back_heads,
        preferred_element_type=jnp.float32,
    )
    key_grad_all = (
        jnp.einsum("rhqk,rqhe->rkhe", scores_low, query_heads, preferred_element_type=jnp.float32)
        * scale
    )
    key_slope, value_slope = (
        lax.psum_scatter(
            key_grad_all.reshape(rows, slots, inner), "dp", scatter_dimension=1, tiled=True
        ),
        lax.psum_scatter(
            value_grad_all.reshape(rows, slots, inner), "dp", scatter_dimension=1, tiled=True
        ),
    )
    _, pull_shape = jax.vjp(
        lambda source, scale_now: shaped(source, scale_now, angle, heads),
        kept["projected"],
        query_scale,
    )
    projected_slope, query_scale_grad = pull_shape(
        (query_slope.reshape(rows, local, inner), key_slope, value_slope)
    )
    projected_low = projected_slope.astype(jnp.bfloat16)
    projection_grad = jnp.einsum(
        "rsd,rsc->dc", kept["gathered"], projected_low, preferred_element_type=jnp.float32
    ).reshape(width, 3, inner)
    partial_stream = jnp.einsum(
        "rsc,dc->rsd",
        projected_low,
        projection.reshape(width, 3 * inner),
        preferred_element_type=jnp.float32,
    )
    spread = jnp.broadcast_to(
        jnp.stack([alpha_branch, alpha_feed])[:, None, :], (2, lax.axis_size("tensor"), width)
    )
    stream_part, alpha_sum = (
        lax.psum_scatter(partial_stream, "tensor", scatter_dimension=1, tiled=True),
        lax.psum_scatter(spread, "tensor", scatter_dimension=1, tiled=True),
    )
    stream_total = stream_slope + stream_part
    return (
        stream_total,
        (
            projection_grad,
            output_grad,
            expansion_grad,
            reduction_grad,
            query_scale_grad,
            unit_grad,
            alpha_sum[:, 0],
        ),
    )


def body(
    activations,
    lengths,
    projection,
    output_weight,
    expansion,
    reduction,
    query_scale,
    unit_scales,
    alphas,
    cotangent,
):
    micro, rows, part, width = activations.shape
    section = lax.axis_index("section")
    first = section == 0
    weights = (
        projection[0],
        output_weight[0],
        expansion[0],
        reduction[0],
        query_scale[0],
        unit_scales[0],
        alphas[0],
    )
    steps = micro + 1
    received = jnp.zeros((rows, part, width), jnp.bfloat16)
    outputs = []
    keeps = []
    for step in range(steps):
        index_now = jnp.clip(step - section, 0, micro - 1)
        lengths_now = lax.dynamic_index_in_dim(lengths, index_now, 0, keepdims=False)
        stream = jnp.where(first, activations[min(step, micro - 1)], received).astype(jnp.float32)
        result, kept = forward(stream, lengths_now, weights)
        result_low = result.astype(jnp.bfloat16)
        outputs.append(result_low)
        keeps.append(kept)
        if step + 1 < steps:
            received = from_behind(result_low, "section", 1)
    stacked = jnp.stack(outputs)
    layer_output = jnp.where(first, stacked[:micro], stacked[1:])[None]
    back_received = jnp.zeros((rows, part, width), jnp.bfloat16)
    slopes = []
    summed = None
    for step in range(steps):
        batch_now = step - 1 + section
        valid = (batch_now >= 0) & (batch_now < micro)
        slope = jnp.where(first, back_received, cotangent[min(step, micro - 1)]).astype(jnp.float32)
        earlier = keeps[max(step - 1, 0)]
        later = keeps[min(step + 1, micro)]
        kept = jax.tree.map(lambda left, right: jnp.where(first, left, right), earlier, later)
        stream_total, layer_grads = backward(slope, kept, weights)
        stream_low = stream_total.astype(jnp.bfloat16)
        slopes.append(stream_low)
        masked = tuple((jnp.where(valid, piece, 0.0) for piece in layer_grads))
        summed = (
            masked
            if summed is None
            else tuple((left + right for left, right in zip(summed, masked)))
        )
        if step + 1 < steps:
            back_received = from_behind(stream_low, "section", -1)
    stacked_slopes = jnp.stack(slopes)
    input_gradient = jnp.where(first, stacked_slopes[1:], stacked_slopes[:micro])[None]
    (
        projection_grad,
        output_grad,
        expansion_grad,
        reduction_grad,
        query_scale_grad,
        unit_grad,
        alpha_grad,
    ) = summed
    totals = lax.psum(
        (
            projection_grad,
            output_grad,
            expansion_grad,
            reduction_grad,
            query_scale_grad,
            unit_grad,
            alpha_grad,
        ),
        "dp",
    )
    return (
        layer_output,
        input_gradient,
        totals[0][None],
        totals[1][None],
        totals[2][None],
        totals[3][None],
        totals[4][None],
        totals[5][None],
        totals[6][None],
    )


MESH_IDS = pl.DeviceIdType.MESH
F32, BF16 = jnp.float32, jnp.bfloat16
CHUNK = 256
NN = ((1,), (0,))
NT = ((1,), (1,))


def dot(left, right, dims):
    return lax.dot_general(left, right, (dims, ((), ())), preferred_element_type=F32)


def norm_parts(v):
    rate = lax.rsqrt(jnp.mean(v * v, axis=-1, keepdims=True) + 1e-06)
    return v * rate, rate


def norm_back(slope, unit, rate):
    return rate * (slope - unit * jnp.mean(unit * slope, axis=-1, keepdims=True))


def blend_back(slope, base, branch, alpha):
    unit_branch, rate_branch = norm_parts(branch)
    toward = unit_branch - base
    unit, rate = norm_parts(base + alpha * toward)
    inner_slope = norm_back(slope, unit, rate)
    alpha_slope = jnp.sum(inner_slope * toward, axis=0, keepdims=True)
    scaled = alpha * inner_slope
    return inner_slope - scaled, norm_back(scaled, unit_branch, rate_branch), alpha_slope


def sequence_starts(lengths_ref, row, index):
    begin = jnp.zeros_like(index)
    end = jnp.int32(0)
    for sequence in range(lengths_ref.shape[2]):
        end = end + lengths_ref[row, 0, sequence]
        begin = jnp.where(index >= end, end, begin)
    return jnp.where(index < end, begin, index)


class Sizes:
    def __init__(self, tensors, places, part, width, inner, units):
        self.tensors, self.places, self.part, self.width = tensors, places, part, width
        self.inner, self.units = inner, units
        self.local = part * tensors
        self.heads = inner // HDIM


class Slots:
    def __init__(self, send, recv):
        self.send, self.recv, self.used = send, recv, 0

    def copy(self, source, target, device):
        number = self.used
        self.used += 1
        return pltpu.make_async_remote_copy(
            source, target, self.send.at[number], self.recv.at[number], device_id=device, device_id_type=MESH_IDS
        )


COPIES = 288


def relay_kernel(
    sizes,
    lengths_ref, acts_ref, cot_ref, qs_ref, us_ref, al_ref, wp_ref, wo_ref, we_ref, wr_ref,
    lo_ref, ig_ref, small_ref, attn_ref, ge_ref, gr_ref,
    wp, wo, we, wr, qs, us, al,
    stream, middles, feed_low, branch_low,
    cosines, sines, scales,
    heads_in, rates_in, probs, mixed_in, sums_in, branch_f, middle_f, feed_f, ups, gates,
    hidden, expanded_low, back_in, heads_back_in,
    heads_out, rates_out, mixed_out, back_out, heads_back_out, sums_out, go_out, go_sib, go_in,
    outs, outs_in, key_rows, value_rows, query_grad, key_grad, value_grad,
    attn_own, attn_sib, attn_all, scale_own, scale_sib, scale_all,
    alpha_own, alpha_in, finals, finals_in,
    middle_cols, hidden_part, up_part, gate_part, stage_e, stage_r,
    weight_sem, weight_send, send_sem, recv_sem, stage_sem,
):
    T, Z, S, part = sizes.tensors, sizes.places, sizes.local, sizes.part
    H, inner, units, D = sizes.heads, sizes.inner, sizes.units, sizes.width
    core, t, z = lax.axis_index("section"), lax.axis_index("tensor"), lax.axis_index("dp")
    sibling = (1 - core, t, z)
    side, row = lax.rem(t, 2), t // 2
    tensor_peers = [row * 2 + (1 - side), (1 - row) * 2 + side, (1 - row) * 2 + (1 - side)]
    place_peers = [lax.rem(z + k, Z) for k in range(1, Z)]
    tensor_ids = [(core, peer, z) for peer in tensor_peers]
    place_ids = [(core, t, peer) for peer in place_peers]
    slots = Slots(send_sem, recv_sem)
    pending = []

    own_weights = [(wp_ref, wp), (wo_ref, wo), (we_ref, we), (wr_ref, wr)]
    for piece, (source, target) in enumerate(own_weights):
        pltpu.make_async_copy(source, target.at[core], weight_sem.at[core, piece]).start()
    small_weights = [(qs_ref, qs), (us_ref, us), (al_ref, al)]
    for piece, (source, target) in enumerate(small_weights):
        pltpu.make_async_copy(source, target.at[core], weight_sem.at[core, 4 + piece]).start()

    barrier = pltpu.get_barrier_semaphore()
    partners = [sibling] + tensor_ids + place_ids
    for partner in partners:
        pl.semaphore_signal(barrier, inc=1, device_id=partner, device_id_type=MESH_IDS)
    pl.semaphore_wait(barrier, len(partners))

    def weight_copy(piece):
        source, target = (own_weights + small_weights)[piece]
        return pltpu.make_async_remote_copy(
            source, target.at[core], weight_send.at[piece], weight_sem.at[core, piece], device_id=sibling, device_id_type=MESH_IDS
        )

    def lend_weights(layer, pieces):
        @pl.when(core == layer)
        def _():
            for piece in pieces:
                weight_copy(piece).start()

    for piece in (4, 5, 6):
        weight_copy(piece).start()
    lend_weights(0, (0,))

    def await_weight(layer, piece):
        source, target = (own_weights + small_weights)[piece]
        pltpu.make_async_copy(source, target.at[layer], weight_sem.at[layer, piece]).wait()

    def send(source, target, device):
        copy = slots.copy(source, target, device)
        copy.start()
        pending.append(copy)
        return copy

    def arrive(copies):
        for copy in copies:
            copy.wait_recv()

    def rows_of(index):
        return pl.ds(pl.multiple_of(index * part, part), part)

    my_rows, far_rows = rows_of(t), rows_of(tensor_peers[2])

    def gather(layer, target, value):
        target[layer, z, my_rows, :] = value
        mine = target.at[layer, z, my_rows, :]
        return [send(mine, mine, device) for device in tensor_ids]

    class Line:
        def __init__(self, views, guard=None):
            self.views, self.guard = views, guard
            self.first = slots.used
            self.width = len(views(0))
            slots.used += 2 * (Z - 1) * self.width
            lines.append(self)

        def copies(self, way, step, origin):
            device = (core, t, z + 1) if way == 0 else (core, t, z - 1)
            first = self.first + (way * (Z - 1) + step) * self.width
            return [
                pltpu.make_async_remote_copy(
                    view, view, send_sem.at[first + k], recv_sem.at[first + k], device_id=device, device_id_type=MESH_IDS
                )
                for k, view in enumerate(self.views(origin))
            ]

        def when(self, condition):
            return pl.when(condition if self.guard is None else condition & self.guard)

        def origin(self, way, step):
            return z - step if way == 0 else z + step

        def sends(self, way, step):
            return (z >= step) & (z + 1 < Z) if way == 0 else (z + step < Z) & (z >= 1)

        def step(self, step):
            for way in range(2):
                if step > 0:
                    @self.when(z >= step if way == 0 else z + step < Z)
                    def _():
                        for copy in self.copies(way, step - 1, self.origin(way, step)):
                            copy.wait_recv()

                if step < Z - 1:
                    @self.when(self.sends(way, step))
                    def _():
                        for copy in self.copies(way, step, self.origin(way, step)):
                            copy.start()

        def finish(self):
            for way in range(2):
                for step in range(Z - 1):
                    @self.when(self.sends(way, step))
                    def _():
                        for copy in self.copies(way, step, self.origin(way, step)):
                            copy.wait_send()

    lines = []

    def row_line(layer, target):
        return Line(lambda place: [target.at[layer, place, my_rows, :], target.at[layer, place, far_rows, :]])

    def pass_on(layer, target):
        passed = []
        for place in place_peers:
            got = target.at[layer, place, my_rows, :]
            passed += [send(got, got, device) for device in tensor_ids[:2]]
        return passed

    def scatter(number):
        return [
            send(sums_out.at[number, peer], sums_in.at[number, k], device)
            for k, (peer, device) in enumerate(zip(tensor_peers, tensor_ids))
        ]

    def scattered(number, copies):
        arrive(copies)
        total = sums_out[number, t].astype(F32)
        for k in range(T - 1):
            total = total + sums_in[number, k].astype(F32)
        return total

    def retire(copies):
        for copy in copies:
            copy.wait_send()
        pending[:] = [copy for copy in pending if not any(copy is done for done in copies)]

    def spread(source, target):
        target[z] = source[z]
        return [send(source.at[peer], target.at[z], device) for peer, device in zip(place_peers, place_ids)]

    half = HDIM // 2
    index_all = lax.broadcasted_iota(jnp.int32, (1, S * Z), 1)
    starts = sequence_starts(lengths_ref, core, index_all)
    rates = jnp.exp(lax.broadcasted_iota(jnp.int32, (half, 1), 0).astype(F32) * (-2.0 * math.log(10000.0) / HDIM))
    angle = rates * (index_all - starts).astype(F32)
    cosine, sine = jnp.cos(angle), jnp.sin(angle)
    for place in range(Z):
        cosines[place] = cosine[:, place * S : (place + 1) * S]
        sines[place] = sine[:, place * S : (place + 1) * S]
    key_index = lax.broadcasted_iota(jnp.int32, (S * Z, S), 0)

    def block(query, key):
        return query * (query + 1) // 2 + key

    used, waiting = {}, {}
    stream_lines = [row_line(layer, stream) for layer in range(2)]
    middle_lines = [row_line(layer, middles) for layer in range(2)]
    feed_lines = [row_line(layer, feed_low) for layer in range(2)]

    def free(name):
        retire(used.pop(name, []))

    def forward(layer, base_low):
        stream_copies = gather(layer, stream, base_low)
        await_weight(layer, 0)
        for piece in (4, 5, 6):
            await_weight(layer, piece)
        scale = jnp.broadcast_to(jnp.broadcast_to(qs[layer], (8, inner)).T[:, :1], (inner, 128)).reshape(H, HDIM, 128)
        scales[layer] = scale
        base = base_low.astype(F32)
        cosine_here, sine_here = cosines[z][None], sines[z][None]
        arrive(stream_copies)
        lend_weights(layer, (1,) if layer == 0 else (3,))
        if layer:
            middle_lines[0].step(2)
        free("heads")
        gathered = stream[layer, z]
        for third in range(3):
            piece = dot(gathered, wp[layer, third], NN).T.reshape(H, HDIM, S)
            if third < 2:
                front, back = piece[:, :half], piece[:, half:]
                piece = jnp.concatenate([front * cosine_here - back * sine_here, back * cosine_here + front * sine_here], axis=1)
                speed = lax.rsqrt(jnp.sum(piece * piece, axis=1, keepdims=True) + 1e-06)
                piece = piece * speed * scale[:, :, :1]
                for head in range(H):
                    rates_out[head, third : third + 1] = speed[head]
            heads_out[:, third] = piece.astype(BF16)
        copies = spread(heads_out, heads_in.at[layer])
        rate_copies = spread(rates_out, rates_in.at[layer])
        used["heads"] = copies + rate_copies
        if layer:
            stream_lines[0].step(3)
            waiting["stream", 0] = pass_on(0, stream)
        arrive(copies + rate_copies)
        if layer:
            middle_lines[0].step(3)
            waiting["middle", 0] = pass_on(0, middles)
        else:
            lend_weights(0, (2, 3))
        for place in range(Z):
            key_rows[place] = heads_in[layer, place, 1].T
        free("mixed")
        for query in range(Z):
            raw = [dot(key_rows[key], heads_in[layer, query, 0], NN) * math.sqrt(HDIM) for key in range(query + 1)]
            first = starts[:, query * S : (query + 1) * S]
            last = index_all[:, query * S : (query + 1) * S]
            scores = []
            for key in range(query + 1):
                keys = key_index[key * S : (key + 1) * S]
                allowed = keys >= first
                if key == query:
                    allowed = allowed & (keys <= last)
                scores.append(jnp.where(allowed, raw[key], -1e30))
            highest = scores[0].max(axis=0, keepdims=True)
            for piece in scores[1:]:
                highest = jnp.maximum(highest, piece.max(axis=0, keepdims=True))
            lifted = [jnp.exp(piece - highest) for piece in scores]
            total = lifted[0].sum(axis=0, keepdims=True)
            for piece in lifted[1:]:
                total = total + piece.sum(axis=0, keepdims=True)
            shrink = 1.0 / total
            mixed = None
            for key in range(query + 1):
                low = (lifted[key] * shrink).astype(BF16)
                probs[layer, block(query, key)] = low
                term = dot(heads_in[layer, key, 2], low, NN)
                mixed = term if mixed is None else mixed + term
            mixed_out[query] = mixed.astype(BF16)
        copies = spread(mixed_out, mixed_in.at[layer])
        used["mixed"] = copies
        await_weight(layer, 1)
        arrive(copies)
        stream_lines[layer].step(0)
        attended = mixed_in[layer].reshape(inner, S).T
        free("branch")
        sums_out[0] = dot(attended, wo[layer], NN).astype(BF16).reshape(T, part, D)
        copies = scatter(0)
        branch = scattered(0, copies)
        stream_lines[layer].step(1)
        if layer == 0:
            lend_weights(1, (0, 1))
        used["branch"] = copies
        branch_f[layer] = branch
        alpha = al[layer]
        middle = norm_parts(base + alpha[0:1] * (norm_parts(branch)[0] - base))[0]
        middle_f[layer] = middle
        copies = gather(layer, middles, middle.astype(BF16))
        await_weight(layer, 2)
        arrive(copies)
        stream_lines[layer].step(2)
        middle_lines[layer].step(0)
        middle_all = middles[layer, z]
        for begin in range(0, units, CHUNK):
            cols = slice(begin, begin + CHUNK)
            up = dot(middle_all, we[layer, 0, :, cols], NN)
            gate = dot(middle_all, we[layer, 1, :, cols], NN)
            ups[layer, :, cols] = up.astype(BF16)
            gates[layer, :, cols] = gate.astype(BF16)
            inside = us[layer, 1:2, cols] * gate
            hidden[:, cols] = (us[layer, 0:1, cols] * up * (inside / (1.0 + jnp.exp(-inside)))).astype(BF16)
        await_weight(layer, 3)
        free("feed")
        acted = hidden[...]
        for begin in range(0, D, CHUNK):
            cols = slice(begin, begin + CHUNK)
            sums_out[1, :, :, cols] = dot(acted, wr[layer, :, cols], NN).astype(BF16).reshape(T, part, CHUNK)
        copies = scatter(1)
        feed = scattered(1, copies)
        middle_lines[layer].step(1)
        if layer == 0:
            lend_weights(1, (2,))
        used["feed"] = copies
        feed_f[layer] = feed
        result = norm_parts(middle + alpha[1:2] * (norm_parts(feed)[0] - middle))[0].astype(BF16)
        outs[0, layer] = result
        return result

    def act_back(layer, cols, up, gate, slope_hidden):
        scale_up, scale_gate = us[layer, 0:1, cols], us[layer, 1:2, cols]
        inside = scale_gate * gate
        sigmoid = 1.0 / (1.0 + jnp.exp(-inside))
        silu = inside * sigmoid
        by_up = silu * slope_hidden
        by_gate = scale_up * up * (sigmoid + silu * (1.0 - sigmoid)) * slope_hidden
        return silu, by_up, by_gate

    def stage_copy(layer, chunk, which):
        buffer = (stage_e, stage_r)[which].at[chunk % 2]
        target = (ge_ref.at[0, chunk], gr_ref.at[0, chunk])[which]
        return pltpu.make_async_copy(buffer, target, stage_sem.at[layer, chunk, which])

    stage_slots = {}

    def stage_send(layer, chunk, which):
        buffer = (stage_e, stage_r)[which].at[chunk % 2]
        target = (ge_ref.at[1, chunk], gr_ref.at[1, chunk])[which]
        if (chunk, which) not in stage_slots:
            stage_slots[chunk, which] = slots.used
            slots.used += 1
        number = stage_slots[chunk, which]
        return pltpu.make_async_remote_copy(
            buffer, target, send_sem.at[number], recv_sem.at[number], device_id=sibling, device_id_type=MESH_IDS
        )

    def stage_wait(layer, chunk):
        @pl.when(core == layer)
        def _():
            for which in range(2):
                stage_copy(layer, chunk, which).wait()

        @pl.when(core != layer)
        def _():
            for which in range(2):
                stage_send(layer, chunk, which).wait_send()

    staged = []

    def feed_grads(layer, chunk):
        if chunk == 0:
            for place in range(Z):
                middle_cols[:, place * S : (place + 1) * S] = middles[layer, place].T
        cols = slice(chunk * CHUNK, (chunk + 1) * CHUNK)
        scale_up, scale_gate = us[layer, 0:1, cols], us[layer, 1:2, cols]
        sum_up = sum_gate = None
        for place in range(Z):
            rows = slice(place * S, (place + 1) * S)
            up = dot(middles[layer, place], we[layer, 0, :, cols], NN)
            gate = dot(middles[layer, place], we[layer, 1, :, cols], NN)
            slope_hidden = dot(feed_low[layer, place], wr[layer, cols, :], NT)
            silu, by_up, by_gate = act_back(layer, cols, up, gate, slope_hidden)
            hidden_part[:, rows] = (scale_up * up * silu).astype(BF16).T
            up_part[rows] = (by_up * scale_up).astype(BF16)
            gate_part[rows] = (by_gate * scale_gate).astype(BF16)
            term_up = jnp.sum(by_up * up, axis=0, keepdims=True)
            term_gate = jnp.sum(by_gate * gate, axis=0, keepdims=True)
            sum_up = term_up if sum_up is None else sum_up + term_up
            sum_gate = term_gate if sum_gate is None else sum_gate + term_gate
        finals[layer, 2:3, cols] = sum_up
        finals[layer, 3:4, cols] = sum_gate
        if len(staged) >= 2:
            stage_wait(*staged[-2])
        buffer = chunk % 2
        stage_e[buffer, 0] = dot(middle_cols[...], up_part[...], NN).astype(BF16)
        stage_e[buffer, 1] = dot(middle_cols[...], gate_part[...], NN).astype(BF16)
        stage_r[buffer] = dot(hidden_part[...], feed_low[layer].reshape(Z * S, D), NN).astype(BF16)

        @pl.when(core == layer)
        def _():
            for which in range(2):
                stage_copy(layer, chunk, which).start()

        @pl.when(core != layer)
        def _():
            for which in range(2):
                stage_send(layer, chunk, which).start()

        staged.append((layer, chunk))

    chunks = units // CHUNK
    projected = 3 * HDIM
    attn_slot = slots.used
    slots.used += 3 + 3 * (Z - 1)

    def attn_copy(number, source, target, device):
        number = attn_slot + number
        return pltpu.make_async_remote_copy(
            source, target, send_sem.at[number], recv_sem.at[number], device_id=device, device_id_type=MESH_IDS
        )

    def attn_pair():
        return [attn_copy(0, attn_own, attn_sib, sibling), attn_copy(1, scale_own, scale_sib, sibling)]

    def go_pair():
        return [attn_copy(2, go_out, go_sib, sibling)]

    def go_spread():
        return [
            attn_copy(3 + k, go_out.at[peer], go_in.at[k], device) for k, (peer, device) in enumerate(zip(place_peers, place_ids))
        ]

    def attn_spread():
        first = 3 + Z - 1
        return [attn_copy(first + 2 * k, attn_all.at[z], attn_all.at[z], device) for k, device in enumerate(place_ids)] + [
            attn_copy(first + 2 * k + 1, scale_all.at[z], scale_all.at[z], device) for k, device in enumerate(place_ids)
        ]

    def offer(layer, pair):
        @pl.when(core != layer)
        def _():
            for copy in pair():
                copy.start()

    def go_join(layer):
        @pl.when(core == layer)
        def _():
            for copy in go_pair():
                copy.wait_recv()
            go_out[...] = (go_out[...].astype(F32) + go_sib[...].astype(F32)).astype(BF16)
            for copy in go_spread():
                copy.start()

        @pl.when(core != layer)
        def _():
            for copy in go_pair():
                copy.wait_send()

    attn_line = Line(lambda place: [attn_all.at[place], scale_all.at[place]], core == 1)

    def attn_join(layer):
        @pl.when(core == layer)
        def _():
            for copy in go_spread():
                copy.wait_recv()
            total = go_out[z].astype(F32)
            for k in range(Z - 1):
                total = total + go_in[k].astype(F32)
            attn_all[z, projected:] = total.astype(BF16)
            for copy in attn_pair():
                copy.wait_recv()
            attn_all[z, :projected] = (attn_own[...].astype(F32) + attn_sib[...].astype(F32)).astype(BF16)
            scale_all[z] = scale_own[...] + scale_sib[...]
            for copy in go_spread():
                copy.wait_send()
            if layer == 0:
                for copy in attn_spread():
                    copy.start()

        @pl.when(core != layer)
        def _():
            for copy in attn_pair():
                copy.wait_send()

        if layer == 1:
            attn_line.step(0)

    def backward(layer, base_low, slope):
        alpha = al[layer]
        middle_slope, feed_slope, alpha_m = blend_back(slope, middle_f[layer], feed_f[layer], alpha[1:2])
        copies = gather(layer, feed_low, feed_slope.astype(BF16))
        alpha_own[layer, 1:2] = alpha_m
        if layer == 0:
            feed_grads(1, 1)
        arrive(copies)
        if layer:
            middle_lines[1].step(2)
        feed_lines[layer].step(0)
        if layer == 0:
            attn_join(1)
        feed_all = feed_low[layer, z]
        for begin in range(0, units, CHUNK):
            cols = slice(begin, begin + CHUNK)
            slope_hidden = dot(feed_all, wr[layer, cols, :], NT)
            up, gate = ups[layer, :, cols].astype(F32), gates[layer, :, cols].astype(F32)
            _, by_up, by_gate = act_back(layer, cols, up, gate, slope_hidden)
            expanded_low[0, :, cols] = (by_up * us[layer, 0:1, cols]).astype(BF16)
            expanded_low[1, :, cols] = (by_gate * us[layer, 1:2, cols]).astype(BF16)
        free("middle_back")
        for begin in range(0, D, CHUNK):
            rows = slice(begin, begin + CHUNK)
            partial = dot(expanded_low[0], we[layer, 0, rows, :], NT) + dot(expanded_low[1], we[layer, 1, rows, :], NT)
            sums_out[2, :, :, rows] = partial.astype(BF16).reshape(T, part, CHUNK)
        copies = scatter(2)
        if layer == 0:
            feed_grads(1, 2)
        middle_total = middle_slope + scattered(2, copies)
        feed_lines[layer].step(1)
        if layer == 0:
            attn_line.step(1)
        used["middle_back"] = copies
        stream_slope, branch_slope, alpha_a = blend_back(middle_total, base_low.astype(F32), branch_f[layer], alpha[0:1])
        free("branch_low")
        branch_low[my_rows, :] = branch_slope.astype(BF16)
        mine = branch_low.at[my_rows, :]
        copies = [send(mine, mine, device) for device in tensor_ids]
        used["branch_low"] = copies
        alpha_own[layer, 0:1] = alpha_a
        if layer == 0:
            alpha_copies = [send(alpha_own, alpha_in.at[k], device) for k, device in enumerate(tensor_ids)]
            feed_grads(1, 3)
        arrive(copies)
        branch_all = branch_low[...]
        free("mixed_back")
        back_out[...] = dot(wo[layer], branch_all, NT).astype(BF16).reshape(H, HDIM, S)
        copies = spread(back_out, back_in)
        used["mixed_back"] = copies
        go_out[...] = dot(mixed_in[layer].reshape(inner, S), branch_all, NN).astype(BF16).reshape(H, HDIM, D)
        offer(layer, go_pair)
        feed_lines[layer].step(2)
        if layer:
            stream_lines[1].step(3)
            waiting["stream", 1] = pass_on(1, stream)
            middle_lines[1].step(3)
            waiting["middle", 1] = pass_on(1, middles)
        else:
            attn_line.step(2)
        for place in range(Z):
            value_rows[place] = heads_in[layer, place, 2].T
        if layer == 0:
            arrive(alpha_copies)
            retire(alpha_copies)
            total = alpha_own[...]
            for k in range(T - 1):
                total = total + alpha_in[k]
            alpha_own[...] = total
            alpha_copies = [send(alpha_own, alpha_in.at[T - 1 + k], device) for k, device in enumerate(place_ids)]
        arrive(copies)
        if layer == 0:
            go_join(0)
            feed_lines[0].step(3)
            feed_passed = pass_on(0, feed_low)
        for query in range(Z):
            slope_mixed = back_in[query]
            lows = [probs[layer, block(query, key)] for key in range(query + 1)]
            probs_slope = [dot(value_rows[key], slope_mixed, NN) for key in range(query + 1)]
            row_term = None
            for low, piece in zip(lows, probs_slope):
                term = jnp.sum(low.astype(F32) * piece, axis=0, keepdims=True)
                row_term = term if row_term is None else row_term + term
            query_slope = None
            for key in range(query + 1):
                low = lows[key]
                scores_low = (low.astype(F32) * (probs_slope[key] - row_term)).astype(BF16)
                term = dot(heads_in[layer, key, 1], scores_low, NN)
                query_slope = term if query_slope is None else query_slope + term
                key_term = dot(heads_in[layer, query, 0], scores_low, NT)
                value_term = dot(slope_mixed, low, NT)
                if key == query:
                    key_grad[key] = key_term
                    value_grad[key] = value_term
                else:
                    key_grad[key] += key_term
                    value_grad[key] += value_term
            query_grad[query] = query_slope
        free("heads_back")
        scale = scales[layer, z][:, :1]
        inverse = 1.0 / scale
        scale_slope = None
        for place in range(Z):
            cosine_there, sine_there = cosines[place], sines[place]
            for third, source in ((0, query_grad), (1, key_grad)):
                piece = source[place] * math.sqrt(HDIM)
                unit = heads_in[layer, place, third].astype(F32) * inverse
                term = jnp.sum(piece * unit, axis=1, keepdims=True)
                scale_slope = term if scale_slope is None else scale_slope + term
                piece = piece * scale
                piece = rates_in[layer, place, third : third + 1] * (piece - unit * jnp.sum(unit * piece, axis=0, keepdims=True))
                front, back = piece[:half], piece[half:]
                piece = jnp.concatenate([front * cosine_there + back * sine_there, back * cosine_there - front * sine_there], axis=0)
                heads_back_out[place, third] = piece.astype(BF16)
            heads_back_out[place, 2] = value_grad[place].astype(BF16)
        copies = spread(heads_back_out, heads_back_in)
        used["heads_back"] = copies
        arrive(waiting["stream", layer])
        grad = None
        for place in range(Z):
            term = dot(heads_back_out[place].reshape(3 * HDIM, S), stream[layer, place], NN)
            grad = term if grad is None else grad + term
        attn_own[...] = grad.astype(BF16)
        scale_rows = jnp.broadcast_to(scale_slope, (HDIM, 128)).T[:8]
        scale_own[...] = jnp.concatenate([scale_rows, scale_rows], axis=1)
        offer(layer, attn_pair)
        if layer:
            feed_lines[1].step(3)
            waiting["feed", 1] = pass_on(1, feed_low)
        else:
            arrive(alpha_copies)
            total = alpha_own[...]
            for k in range(Z - 1):
                total = total + alpha_in[T - 1 + k]
            finals[0, 0:2] = total[0]
            finals[1, 0:2] = total[1]
            arrive(feed_passed + waiting["middle", 0])
            feed_grads(0, 0)
            attn_join(0)
            feed_grads(0, 1)
        arrive(copies)
        partial = None
        for third in range(3):
            term = dot(heads_back_in[:, third].reshape(inner, S).T, wp[layer, third], NT)
            partial = term if partial is None else partial + term
        free("stream_back")
        sums_out[3] = partial.astype(BF16).reshape(T, part, D)
        copies = scatter(3)
        if layer:
            go_join(1)
            arrive(waiting["feed", 1] + waiting["middle", 1])
            feed_grads(1, 0)
        else:
            feed_grads(0, 2)
        result = (stream_slope + scattered(3, copies)).astype(BF16)
        used["stream_back"] = copies
        outs[1, layer] = result
        return result

    forward(1, forward(0, acts_ref[core, 0]))
    slope = backward(1, outs[0, 0], cot_ref[core, 0].astype(F32))
    backward(0, acts_ref[core, 0], slope.astype(F32))

    other = 1 - core
    last = [send(outs.at[:, other], outs_in, sibling)]
    feed_grads(0, 3)
    last += [send(finals.at[other], finals_in, sibling)]
    for kind, target in enumerate((lo_ref, ig_ref)):
        target[core] = outs[kind, core]
    arrive(last)
    for kind, target in enumerate((lo_ref, ig_ref)):
        target[other] = outs_in[kind]
    small_ref[0:4] = finals[core] + finals_in[...]
    for layer, chunk in staged[-2:]:
        stage_wait(layer, chunk)
    for chunk in range(chunks):
        for which in range(2):
            stage_send(0, chunk, which).wait_recv()
    @pl.when(core == 0)
    def _():
        for copy in attn_spread():
            copy.wait_recv()
            copy.wait_send()

    attn_line.step(3)
    attn_out = pltpu.make_async_copy(attn_all, attn_ref, stage_sem.at[0, 0, 0])
    attn_out.start()
    for place in range(Z):
        small_ref[4 + place : 5 + place, :128] = scale_all[place, :1]
    for copy in pending + [weight_copy(piece) for piece in range(7)]:
        copy.wait_send()
    for line in lines:
        line.finish()
    attn_out.wait()
    assert slots.used <= COPIES, slots.used


def relay(sizes, lengths, acts, cot, qs, us, al, wp, wo, we, wr):
    T, Z, S, part = sizes.tensors, sizes.places, sizes.local, sizes.part
    H, inner, units, D = sizes.heads, sizes.inner, sizes.units, sizes.width
    blocks, chunks = Z * (Z + 1) // 2, units // CHUNK
    vmem = pl.BlockSpec(memory_space=pltpu.VMEM)
    hbm = pl.BlockSpec(memory_space=pl.ANY)
    out_shape = (
        jax.ShapeDtypeStruct((2, part, D), BF16),
        jax.ShapeDtypeStruct((2, part, D), BF16),
        jax.ShapeDtypeStruct((4 + Z, D), F32),
        jax.ShapeDtypeStruct((Z, 4 * HDIM, D), BF16),
        jax.ShapeDtypeStruct((2, chunks, 2, D, CHUNK), BF16),
        jax.ShapeDtypeStruct((2, chunks, CHUNK, D), BF16),
    )
    DMA = pltpu.SemaphoreType.DMA
    V = pltpu.VMEM
    scratch = [
        V((2, 3, D, inner), BF16), V((2, inner, D), BF16), V((2, 2, D, units), BF16), V((2, units, D), BF16),
        V((2, 1, inner), F32), V((2, 2, units), F32), V((2, 2, D), F32),
        V((2, Z, S, D), BF16), V((2, Z, S, D), BF16), V((2, Z, S, D), BF16), V((S, D), BF16),
        V((Z, HDIM // 2, S), F32), V((Z, HDIM // 2, S), F32), V((2, H, HDIM, 128), F32),
        V((2, Z, 3, HDIM, S), BF16), V((2, Z, 2, S), F32),
        V((2, blocks, S, S), BF16), V((2, H, HDIM, S), BF16),
        V((4, T - 1, part, D), BF16),
        V((2, part, D), F32), V((2, part, D), F32), V((2, part, D), F32),
        V((2, S, units), BF16), V((2, S, units), BF16),
        V((S, units), BF16), V((2, S, units), BF16),
        V((Z, HDIM, S), BF16), V((H, 3, HDIM, S), BF16),
        V((H, 3, HDIM, S), BF16), V((H, 2, S), F32),
        V((Z, HDIM, S), BF16), V((H, HDIM, S), BF16), V((Z, 3, HDIM, S), BF16),
        V((4, T, part, D), BF16), V((H, HDIM, D), BF16), V((H, HDIM, D), BF16), V((Z - 1, HDIM, D), BF16),
        V((2, 2, part, D), BF16), V((2, part, D), BF16),
        V((Z, S, HDIM), BF16), V((Z, S, HDIM), BF16),
        V((Z, HDIM, S), F32), V((Z, HDIM, S), F32), V((Z, HDIM, S), F32),
        V((3 * HDIM, D), BF16), V((3 * HDIM, D), BF16), V((Z, 4 * HDIM, D), BF16),
        V((8, 128), F32), V((8, 128), F32), V((Z, 8, 128), F32),
        V((2, 2, D), F32), V((T + Z - 2, 2, 2, D), F32), V((2, 4, D), F32), V((4, D), F32),
        V((D, Z * S), BF16), V((CHUNK, Z * S), BF16), V((Z * S, CHUNK), BF16), V((Z * S, CHUNK), BF16),
        V((2, 2, D, CHUNK), BF16), V((2, CHUNK, D), BF16),
        DMA((2, 7)), DMA((7,)), DMA((COPIES,)), DMA((COPIES,)), DMA((2, chunks, 2)),
    ]
    return pl.pallas_call(
        functools.partial(relay_kernel, sizes),
        out_shape=out_shape,
        in_specs=[pl.BlockSpec(memory_space=pltpu.SMEM), vmem, vmem, vmem, vmem, vmem, hbm, hbm, hbm, hbm],
        out_specs=(vmem, vmem, vmem, hbm, hbm, hbm),
        scratch_shapes=scratch,
        compiler_params=pltpu.CompilerParams(collective_id=0, has_side_effects=True, vmem_limit_bytes=62 * 2**20),
        name="relay",
    )(lengths, acts, cot, qs, us, al, wp, wo, we, wr)


def fast_body(
    activations, lengths, projection, output_weight, expansion, reduction, query_scale, unit_scales, alphas, cotangent
):
    _, _, part, width = activations.shape
    inner, units = output_weight.shape[1], reduction.shape[1]
    places = lax.axis_size("dp")
    sizes = Sizes(lax.axis_size("tensor"), places, part, width, inner, units)
    lo, ig, small, attn, ge, gr = relay(
        sizes, lengths, activations, cotangent, query_scale, unit_scales[0], alphas[0],
        projection[0].transpose(1, 0, 2), output_weight[0], expansion[0].transpose(1, 0, 2), reduction[0],
    )
    attn = attn.astype(F32)
    projection_grad = attn[:, : 3 * HDIM].reshape(places, 3, HDIM, width).transpose(3, 1, 0, 2).reshape(width, 3, inner)
    output_grad = attn[:, 3 * HDIM :].reshape(inner, width)
    expansion_grad = (ge[0].astype(F32) + ge[1].astype(F32)).transpose(2, 1, 0, 3).reshape(width, 2, units)
    reduction_grad = (gr[0].astype(F32) + gr[1].astype(F32)).reshape(units, width)
    return (
        lo[None, :, None],
        ig[None, :, None],
        projection_grad[None],
        output_grad[None],
        expansion_grad[None],
        reduction_grad[None],
        small[4:, :HDIM].reshape(1, inner),
        small[None, 2:4, :units],
        small[None, 0:2],
    )


def solution(mesh):
    in_specs = (
        P(None, None, ("dp", "tensor"), None),
        P(),
        P("section", None, None, "tensor"),
        P("section", "tensor", None),
        P("section", None, None, "tensor"),
        P("section", "tensor", None),
        P("section", "tensor"),
        P("section", None, "tensor"),
        P("section", None, None),
        P(None, None, ("dp", "tensor"), None),
    )
    out_specs = (
        P("section", None, None, ("dp", "tensor"), None),
        P("section", None, None, ("dp", "tensor"), None),
        P("section", None, None, "tensor"),
        P("section", "tensor", None),
        P("section", None, None, "tensor"),
        P("section", "tensor", None),
        P("section", "tensor"),
        P("section", None, "tensor"),
        P("section", None, None),
    )
    def chosen(*arrays):
        activations, output_weight = arrays[0], arrays[3]
        heads = output_weight.shape[1] // HDIM
        fits = (
            mesh.shape["section"] == 2
            and mesh.shape["tensor"] == 4
            and mesh.shape["dp"] == heads
            and activations.shape[:2] == (2, 1)
            and activations.shape[2] * mesh.shape["tensor"] == 256
        )
        return (fast_body if fits else body)(*arrays)

    return jax.shard_map(chosen, mesh=mesh, in_specs=in_specs, out_specs=out_specs, check_vma=False)
```

```python
import functools
import math

import jax
import jax.numpy as jnp
from jax import lax
from jax.experimental import pallas as pl
from jax.experimental.pallas import tpu as pltpu
from jax.sharding import PartitionSpec as P

HDIM = 64


def from_behind(value, axis, steps):
    count = lax.axis_size(axis)
    initial, last = (max(0, -steps), min(count, count - steps))
    return lax.ppermute(value, axis, [(source, source + steps) for source in range(initial, last)])


def normed(v):
    return v * lax.rsqrt(jnp.mean(v * v, axis=-1, keepdims=True) + 1e-06)


def unit_heads(v):
    return v * lax.rsqrt(jnp.sum(v * v, axis=-1, keepdims=True) + 1e-06)


def frequencies(half):
    return jnp.exp(jnp.arange(half, dtype=jnp.float32) * (-2.0 * math.log(10000.0) / (2 * half)))


def rotate(view, angle):
    half = view.shape[-1] // 2
    cosine = jnp.cos(angle)[..., None, :]
    sine = jnp.sin(angle)[..., None, :]
    front = view[..., :half]
    back = view[..., half:]
    return jnp.concatenate([front * cosine - back * sine, back * cosine + front * sine], axis=-1)


def shaped(projected, scale, angle, heads):
    inner = projected.shape[-1] // 3
    lead = projected.shape[:-1]

    def turned(piece):
        view = piece.reshape(lead + (heads, inner // heads))
        return unit_heads(rotate(view, angle)).reshape(lead + (inner,)) * scale

    return (
        turned(projected[..., :inner]),
        turned(projected[..., inner : 2 * inner]),
        projected[..., 2 * inner :],
    )


def layout(lengths_row, slots):
    ends = jnp.cumsum(lengths_row, dtype=jnp.int32)
    index = jnp.arange(slots, dtype=jnp.int32)
    after = index[:, None] >= ends[None, :]
    segment = jnp.sum(after.astype(jnp.int32), axis=1, dtype=jnp.int32)
    begin = jnp.sum(jnp.where(after, lengths_row[None, :], 0), axis=1, dtype=jnp.int32)
    inside = index < ends[-1]
    segment = jnp.where(inside, segment, lengths_row.shape[0] + index)
    position = jnp.where(inside, index - begin, 0)
    return (segment, position)


def blend(base, branch, alpha):
    return normed(base + alpha * (normed(branch) - base))


def activate(expanded, scales):
    half = expanded.shape[-1] // 2
    return expanded[..., :half] * scales[0] * jax.nn.silu(expanded[..., half:] * scales[1])


def placing(lengths_now, local):
    slots = local * lax.axis_size("dp")
    start_here = lax.axis_index("dp") * local
    segment_all, position_all = jax.vmap(lambda row: layout(row, slots))(lengths_now)
    segment_here = lax.dynamic_slice_in_dim(segment_all, start_here, local, 1)
    position_here = lax.dynamic_slice_in_dim(position_all, start_here, local, 1)
    index_here = start_here + jnp.arange(local, dtype=jnp.int32)
    every = jnp.arange(slots, dtype=jnp.int32)
    allowed = (segment_here[:, :, None] == segment_all[:, None, :]) & (
        every[None, None, :] <= index_here[None, :, None]
    )
    angle = position_here.astype(jnp.float32)[..., None] * frequencies(HDIM // 2)
    return (allowed, angle)


def scored(query, key_all, allowed, heads):
    rows, local, inner = query.shape
    depth = inner // heads
    query_heads = query.reshape(rows, local, heads, depth)
    key_heads = key_all.reshape(rows, key_all.shape[1], heads, depth)
    raw = jnp.einsum(
        "rqhe,rkhe->rhqk", query_heads, key_heads, preferred_element_type=jnp.float32
    ) * math.sqrt(depth)
    return jnp.where(allowed[:, None], raw, -1e30)


def forward(stream, lengths_now, weights):
    projection, output_weight, expansion, reduction, query_scale, unit_scales, alphas = weights
    rows, part, width = stream.shape
    inner = output_weight.shape[0]
    heads = inner // HDIM
    hidden_width = reduction.shape[0]
    gathered = lax.all_gather(stream.astype(jnp.bfloat16), "tensor", axis=1, tiled=True)
    local = gathered.shape[1]
    allowed, angle = placing(lengths_now, local)
    projected = jnp.einsum(
        "rsd,dc->rsc",
        gathered,
        projection.reshape(width, 3 * inner),
        preferred_element_type=jnp.float32,
    )
    query, key, value = shaped(projected, query_scale, angle, heads)
    query_low = query.astype(jnp.bfloat16)
    key_low = key.astype(jnp.bfloat16)
    value_low = value.astype(jnp.bfloat16)
    key_all, value_all = (
        lax.all_gather(key_low, "dp", axis=1, tiled=True),
        lax.all_gather(value_low, "dp", axis=1, tiled=True),
    )
    scores = scored(query_low, key_all, allowed, heads)
    highest = jnp.max(scores, axis=-1, keepdims=True)
    lifted = jnp.exp(scores - highest)
    total = jnp.sum(lifted, axis=-1, keepdims=True)
    log_total = highest + jnp.log(total)
    probs_low = (lifted / total).astype(jnp.bfloat16)
    value_heads = value_all.reshape(rows, value_all.shape[1], heads, HDIM)
    mixed = jnp.einsum(
        "rhqk,rkhe->rqhe", probs_low, value_heads, preferred_element_type=jnp.float32
    )
    attended = mixed.reshape(rows, local, inner).astype(jnp.bfloat16)
    partial_branch = jnp.einsum(
        "rsc,cd->rsd", attended, output_weight, preferred_element_type=jnp.float32
    )
    branch = lax.psum_scatter(partial_branch, "tensor", scatter_dimension=1, tiled=True)
    middle = blend(stream, branch, alphas[0])
    middle_all = lax.all_gather(middle.astype(jnp.bfloat16), "tensor", axis=1, tiled=True)
    expanded = jnp.einsum(
        "rsd,dc->rsc",
        middle_all,
        expansion.reshape(width, 2 * hidden_width),
        preferred_element_type=jnp.float32,
    )
    hidden = activate(expanded, unit_scales).astype(jnp.bfloat16)
    partial_feed = jnp.einsum("rsf,fd->rsd", hidden, reduction, preferred_element_type=jnp.float32)
    feed = lax.psum_scatter(partial_feed, "tensor", scatter_dimension=1, tiled=True)
    result = blend(middle, feed, alphas[1])
    kept = dict(
        stream=stream,
        gathered=gathered,
        projected=projected,
        query=query_low,
        key=key_low,
        value=value_low,
        log_total=log_total,
        attended=attended,
        branch=branch,
        middle=middle,
        middle_all=middle_all,
        expanded=expanded,
        hidden=hidden,
        feed=feed,
        lengths=lengths_now,
    )
    kept = dict(kept, key_all=key_all, value_all=value_all)
    return (result, kept)


def backward(slope, kept, weights):
    projection, output_weight, expansion, reduction, query_scale, unit_scales, alphas = weights
    rows, part, width = slope.shape
    inner = output_weight.shape[0]
    heads = inner // HDIM
    hidden_width = reduction.shape[0]
    _, pull_feed = jax.vjp(blend, kept["middle"], kept["feed"], alphas[1])
    middle_slope, feed_slope, alpha_feed = pull_feed(slope)
    feed_all = lax.all_gather(feed_slope.astype(jnp.bfloat16), "tensor", axis=1, tiled=True)
    reduction_grad = jnp.einsum(
        "rsf,rsd->fd", kept["hidden"], feed_all, preferred_element_type=jnp.float32
    )
    hidden_slope = jnp.einsum(
        "rsd,fd->rsf", feed_all, reduction, preferred_element_type=jnp.float32
    )
    _, pull_active = jax.vjp(activate, kept["expanded"], unit_scales)
    expanded_slope, unit_grad = pull_active(hidden_slope)
    expanded_low = expanded_slope.astype(jnp.bfloat16)
    expansion_grad = jnp.einsum(
        "rsd,rsc->dc", kept["middle_all"], expanded_low, preferred_element_type=jnp.float32
    ).reshape(width, 2, hidden_width)
    partial_middle = jnp.einsum(
        "rsc,dc->rsd",
        expanded_low,
        expansion.reshape(width, 2 * hidden_width),
        preferred_element_type=jnp.float32,
    )
    middle_total = middle_slope + lax.psum_scatter(
        partial_middle, "tensor", scatter_dimension=1, tiled=True
    )
    _, pull_branch = jax.vjp(blend, kept["stream"], kept["branch"], alphas[0])
    stream_slope, branch_slope, alpha_branch = pull_branch(middle_total)
    branch_all = lax.all_gather(branch_slope.astype(jnp.bfloat16), "tensor", axis=1, tiled=True)
    output_grad = jnp.einsum(
        "rsc,rsd->cd", kept["attended"], branch_all, preferred_element_type=jnp.float32
    )
    attended_low = jnp.einsum(
        "rsd,cd->rsc", branch_all, output_weight, preferred_element_type=jnp.float32
    ).astype(jnp.bfloat16)
    local = attended_low.shape[1]
    key_all = kept["key_all"]
    value_all = kept["value_all"]
    slots = key_all.shape[1]
    allowed, angle = placing(kept["lengths"], local)
    scores = scored(kept["query"], key_all, allowed, heads)
    probs = jnp.exp(scores - kept["log_total"])
    scale = math.sqrt(HDIM)
    back_heads = attended_low.reshape(rows, local, heads, HDIM)
    query_heads = kept["query"].reshape(rows, local, heads, HDIM)
    key_heads = key_all.reshape(rows, slots, heads, HDIM)
    value_heads = value_all.reshape(rows, slots, heads, HDIM)
    probs_slope = jnp.einsum(
        "rqhe,rkhe->rhqk", back_heads, value_heads, preferred_element_type=jnp.float32
    )
    row_term = jnp.sum(probs * probs_slope, axis=-1, keepdims=True)
    scores_low = (probs * (probs_slope - row_term)).astype(jnp.bfloat16)
    query_slope = (
        jnp.einsum("rhqk,rkhe->rqhe", scores_low, key_heads, preferred_element_type=jnp.float32)
        * scale
    )
    value_grad_all = jnp.einsum(
        "rhqk,rqhe->rkhe",
        probs.astype(jnp.bfloat16),
        back_heads,
        preferred_element_type=jnp.float32,
    )
    key_grad_all = (
        jnp.einsum("rhqk,rqhe->rkhe", scores_low, query_heads, preferred_element_type=jnp.float32)
        * scale
    )
    key_slope, value_slope = (
        lax.psum_scatter(
            key_grad_all.reshape(rows, slots, inner), "dp", scatter_dimension=1, tiled=True
        ),
        lax.psum_scatter(
            value_grad_all.reshape(rows, slots, inner), "dp", scatter_dimension=1, tiled=True
        ),
    )
    _, pull_shape = jax.vjp(
        lambda source, scale_now: shaped(source, scale_now, angle, heads),
        kept["projected"],
        query_scale,
    )
    projected_slope, query_scale_grad = pull_shape(
        (query_slope.reshape(rows, local, inner), key_slope, value_slope)
    )
    projected_low = projected_slope.astype(jnp.bfloat16)
    projection_grad = jnp.einsum(
        "rsd,rsc->dc", kept["gathered"], projected_low, preferred_element_type=jnp.float32
    ).reshape(width, 3, inner)
    partial_stream = jnp.einsum(
        "rsc,dc->rsd",
        projected_low,
        projection.reshape(width, 3 * inner),
        preferred_element_type=jnp.float32,
    )
    spread = jnp.broadcast_to(
        jnp.stack([alpha_branch, alpha_feed])[:, None, :], (2, lax.axis_size("tensor"), width)
    )
    stream_part, alpha_sum = (
        lax.psum_scatter(partial_stream, "tensor", scatter_dimension=1, tiled=True),
        lax.psum_scatter(spread, "tensor", scatter_dimension=1, tiled=True),
    )
    stream_total = stream_slope + stream_part
    return (
        stream_total,
        (
            projection_grad,
            output_grad,
            expansion_grad,
            reduction_grad,
            query_scale_grad,
            unit_grad,
            alpha_sum[:, 0],
        ),
    )


def body(
    activations,
    lengths,
    projection,
    output_weight,
    expansion,
    reduction,
    query_scale,
    unit_scales,
    alphas,
    cotangent,
):
    micro, rows, part, width = activations.shape
    section = lax.axis_index("section")
    first = section == 0
    weights = (
        projection[0],
        output_weight[0],
        expansion[0],
        reduction[0],
        query_scale[0],
        unit_scales[0],
        alphas[0],
    )
    steps = micro + 1
    received = jnp.zeros((rows, part, width), jnp.bfloat16)
    outputs = []
    keeps = []
    for step in range(steps):
        index_now = jnp.clip(step - section, 0, micro - 1)
        lengths_now = lax.dynamic_index_in_dim(lengths, index_now, 0, keepdims=False)
        stream = jnp.where(first, activations[min(step, micro - 1)], received).astype(jnp.float32)
        result, kept = forward(stream, lengths_now, weights)
        result_low = result.astype(jnp.bfloat16)
        outputs.append(result_low)
        keeps.append(kept)
        if step + 1 < steps:
            received = from_behind(result_low, "section", 1)
    stacked = jnp.stack(outputs)
    layer_output = jnp.where(first, stacked[:micro], stacked[1:])[None]
    back_received = jnp.zeros((rows, part, width), jnp.bfloat16)
    slopes = []
    summed = None
    for step in range(steps):
        batch_now = step - 1 + section
        valid = (batch_now >= 0) & (batch_now < micro)
        slope = jnp.where(first, back_received, cotangent[min(step, micro - 1)]).astype(jnp.float32)
        earlier = keeps[max(step - 1, 0)]
        later = keeps[min(step + 1, micro)]
        kept = jax.tree.map(lambda left, right: jnp.where(first, left, right), earlier, later)
        stream_total, layer_grads = backward(slope, kept, weights)
        stream_low = stream_total.astype(jnp.bfloat16)
        slopes.append(stream_low)
        masked = tuple((jnp.where(valid, piece, 0.0) for piece in layer_grads))
        summed = (
            masked
            if summed is None
            else tuple((left + right for left, right in zip(summed, masked)))
        )
        if step + 1 < steps:
            back_received = from_behind(stream_low, "section", -1)
    stacked_slopes = jnp.stack(slopes)
    input_gradient = jnp.where(first, stacked_slopes[1:], stacked_slopes[:micro])[None]
    (
        projection_grad,
        output_grad,
        expansion_grad,
        reduction_grad,
        query_scale_grad,
        unit_grad,
        alpha_grad,
    ) = summed
    totals = lax.psum(
        (
            projection_grad,
            output_grad,
            expansion_grad,
            reduction_grad,
            query_scale_grad,
            unit_grad,
            alpha_grad,
        ),
        "dp",
    )
    return (
        layer_output,
        input_gradient,
        totals[0][None],
        totals[1][None],
        totals[2][None],
        totals[3][None],
        totals[4][None],
        totals[5][None],
        totals[6][None],
    )


MESH_IDS = pl.DeviceIdType.MESH
F32, BF16 = jnp.float32, jnp.bfloat16
CHUNK = 256
NN = ((1,), (0,))
NT = ((1,), (1,))


def dot(left, right, dims):
    return lax.dot_general(left, right, (dims, ((), ())), preferred_element_type=F32)


def norm_parts(v):
    rate = lax.rsqrt(jnp.mean(v * v, axis=-1, keepdims=True) + 1e-06)
    return v * rate, rate


def norm_back(slope, unit, rate):
    return rate * (slope - unit * jnp.mean(unit * slope, axis=-1, keepdims=True))


def blend_back(slope, base, branch, alpha):
    unit_branch, rate_branch = norm_parts(branch)
    toward = unit_branch - base
    unit, rate = norm_parts(base + alpha * toward)
    inner_slope = norm_back(slope, unit, rate)
    alpha_slope = jnp.sum(inner_slope * toward, axis=0, keepdims=True)
    scaled = alpha * inner_slope
    return inner_slope - scaled, norm_back(scaled, unit_branch, rate_branch), alpha_slope


def sequence_starts(lengths_ref, row, index):
    begin = jnp.zeros_like(index)
    end = jnp.int32(0)
    for sequence in range(lengths_ref.shape[2]):
        end = end + lengths_ref[row, 0, sequence]
        begin = jnp.where(index >= end, end, begin)
    return jnp.where(index < end, begin, index)


class Sizes:
    def __init__(self, tensors, places, part, width, inner, units):
        self.tensors, self.places, self.part, self.width = tensors, places, part, width
        self.inner, self.units = inner, units
        self.local = part * tensors
        self.heads = inner // HDIM


class Slots:
    def __init__(self, send, recv):
        self.send, self.recv, self.used = send, recv, 0

    def copy(self, source, target, device):
        number = self.used
        self.used += 1
        return pltpu.make_async_remote_copy(
            source, target, self.send.at[number], self.recv.at[number], device_id=device, device_id_type=MESH_IDS
        )


COPIES = 232


def relay_kernel(
    sizes,
    lengths_ref, acts_ref, cot_ref, qs_ref, us_ref, al_ref, wp_ref, wo_ref, we_ref, wr_ref,
    lo_ref, ig_ref, small_ref, attn_ref, ge_ref, gr_ref,
    wp, wo, we, wr, qs, us, al,
    stream, middles, feed_low, branch_low,
    cosines, sines, scales,
    heads_in, rates_in, probs, mixed_in, sums_in, branch_f, middle_f, feed_f, ups, gates,
    hidden, expanded_low, back_in, heads_back_in,
    heads_out, rates_out, mixed_out, back_out, heads_back_out, sums_out, go_out, go_sib, go_in,
    outs, outs_in, key_rows, value_rows, query_grad, key_grad, value_grad,
    attn_own, attn_sib, attn_all, scale_own, scale_sib, scale_all,
    alpha_own, alpha_in, finals, finals_in,
    middle_cols, hidden_part, up_part, gate_part, stage_e, stage_r,
    weight_sem, weight_send, send_sem, recv_sem, stage_sem,
):
    T, Z, S, part = sizes.tensors, sizes.places, sizes.local, sizes.part
    H, inner, units, D = sizes.heads, sizes.inner, sizes.units, sizes.width
    core, t, z = lax.axis_index("section"), lax.axis_index("tensor"), lax.axis_index("dp")
    sibling = (1 - core, t, z)
    side, row = lax.rem(t, 2), t // 2
    tensor_peers = [row * 2 + (1 - side), (1 - row) * 2 + side, (1 - row) * 2 + (1 - side)]
    place_peers = [lax.rem(z + k, Z) for k in range(1, Z)]
    tensor_ids = [(core, peer, z) for peer in tensor_peers]
    place_ids = [(core, t, peer) for peer in place_peers]
    slots = Slots(send_sem, recv_sem)
    pending = [[]]

    weights = [
        (wp_ref, lambda layer: wp.at[layer]),
        (wo_ref, lambda layer: wo.at[layer]),
        (we_ref.at[0], lambda layer: we.at[layer, 0]),
        (we_ref.at[1], lambda layer: we.at[layer, 1]),
        (wr_ref, lambda layer: wr.at[layer]),
        (qs_ref, lambda layer: qs.at[layer]),
        (us_ref, lambda layer: us.at[layer]),
        (al_ref, lambda layer: al.at[layer]),
    ]

    def weight_load(layer, piece):
        source, target = weights[piece]
        return pltpu.make_async_copy(source, target(layer), weight_sem.at[layer, piece])

    for piece in range(len(weights)):
        weight_load(core, piece).start()

    barrier = pltpu.get_barrier_semaphore()
    partners = [sibling] + tensor_ids + place_ids
    for partner in partners:
        pl.semaphore_signal(barrier, inc=1, device_id=partner, device_id_type=MESH_IDS)
    pl.semaphore_wait(barrier, len(partners))

    def weight_copy(piece):
        source, target = weights[piece]
        return pltpu.make_async_remote_copy(
            source, target(core), weight_send.at[piece], weight_sem.at[core, piece], device_id=sibling, device_id_type=MESH_IDS
        )

    def lend_weights(layer, pieces):
        @pl.when(core == layer)
        def _():
            for piece in pieces:
                weight_copy(piece).start()

    for piece in (5, 6, 7):
        weight_copy(piece).start()

    def await_weight(layer, piece):
        weight_load(layer, piece).wait()

    def send(source, target, device):
        copy = slots.copy(source, target, device)
        copy.start()
        pending[-1].append(copy)
        return copy

    def settle(keep=4):
        pending.append([])
        while len(pending) > keep:
            for copy in pending.pop(0):
                copy.wait_send()

    def arrive(copies):
        for copy in copies:
            copy.wait_recv()

    def rows_of(index):
        return pl.ds(pl.multiple_of(index * part, part), part)

    my_rows, far_rows = rows_of(t), rows_of(tensor_peers[2])

    def gather(layer, target, value):
        target[layer, z, my_rows, :] = value
        mine = target.at[layer, z, my_rows, :]
        return [send(mine, mine, device) for device in tensor_ids]

    class Line:
        def __init__(self, views, guard=None):
            self.views, self.guard = views, guard
            self.first = slots.used
            self.width = len(views(0))
            slots.used += 2 * (Z - 1) * self.width

        def copies(self, way, step, origin):
            device = (core, t, z + 1) if way == 0 else (core, t, z - 1)
            first = self.first + (way * (Z - 1) + step) * self.width
            return [
                pltpu.make_async_remote_copy(
                    view, view, send_sem.at[first + k], recv_sem.at[first + k], device_id=device, device_id_type=MESH_IDS
                )
                for k, view in enumerate(self.views(origin))
            ]

        def when(self, condition):
            return pl.when(condition if self.guard is None else condition & self.guard)

        def origin(self, way, step):
            return z - step if way == 0 else z + step

        def sends(self, way, step):
            return (z >= step) & (z + 1 < Z) if way == 0 else (z + step < Z) & (z >= 1)

        def step(self, step):
            for way in range(2):
                if step > 0:
                    @self.when(z >= step if way == 0 else z + step < Z)
                    def _():
                        for copy in self.copies(way, step - 1, self.origin(way, step)):
                            copy.wait_recv()

                if step < Z - 1:
                    @self.when(self.sends(way, step))
                    def _():
                        for copy in self.copies(way, step, self.origin(way, step)):
                            copy.start()

        def finish(self):
            for way in range(2):
                for step in range(Z - 1):
                    @self.when(self.sends(way, step))
                    def _():
                        for copy in self.copies(way, step, self.origin(way, step)):
                            copy.wait_send()

    def row_line(layer, target):
        return Line(lambda place: [target.at[layer, place, my_rows, :], target.at[layer, place, far_rows, :]])

    def pass_on(layer, target):
        passed = []
        for place in place_peers:
            got = target.at[layer, place, my_rows, :]
            passed += [send(got, got, device) for device in tensor_ids[:2]]
        return passed

    def scatter(number):
        return [
            send(sums_out.at[number, peer], sums_in.at[number, k], device)
            for k, (peer, device) in enumerate(zip(tensor_peers, tensor_ids))
        ]

    def scattered(number, copies):
        arrive(copies)
        total = sums_out[number, t].astype(F32)
        for k in range(T - 1):
            total = total + sums_in[number, k].astype(F32)
        return total

    def retire(copies):
        for copy in copies:
            for group in pending:
                if any(copy is other for other in group):
                    copy.wait_send()
                    group[:] = [other for other in group if other is not copy]

    def spread(source, target):
        target[z] = source[z]
        return [send(source.at[peer], target.at[z], device) for peer, device in zip(place_peers, place_ids)]

    half = HDIM // 2
    index_all = lax.broadcasted_iota(jnp.int32, (1, S * Z), 1)
    starts = sequence_starts(lengths_ref, core, index_all)
    rates = jnp.exp(lax.broadcasted_iota(jnp.int32, (half, 1), 0).astype(F32) * (-2.0 * math.log(10000.0) / HDIM))
    angle = rates * (index_all - starts).astype(F32)
    cosine, sine = jnp.cos(angle), jnp.sin(angle)
    for place in range(Z):
        cosines[place] = cosine[:, place * S : (place + 1) * S]
        sines[place] = sine[:, place * S : (place + 1) * S]
    key_index = lax.broadcasted_iota(jnp.int32, (S * Z, S), 0)

    def block(query, key):
        return query * (query + 1) // 2 + key

    used, waiting = {}, {}
    stream_lines = [row_line(layer, stream) for layer in range(2)]
    middle_lines = [row_line(layer, middles) for layer in range(2)]
    feed_lines = [row_line(layer, feed_low) for layer in range(2)]

    def free(name):
        retire(used.pop(name, []))

    def forward(layer, base_low):
        stream_copies = gather(layer, stream, base_low)
        lend_weights(layer, (0,))
        await_weight(layer, 0)
        for piece in (5, 6, 7):
            await_weight(layer, piece)
        scale = jnp.broadcast_to(jnp.broadcast_to(qs[layer], (8, inner)).T[:, :1], (inner, 128)).reshape(H, HDIM, 128)
        scales[layer] = scale
        base = base_low.astype(F32)
        cosine_here, sine_here = cosines[z][None], sines[z][None]
        arrive(stream_copies)
        if layer:
            middle_lines[0].step(2)
        free("heads")
        gathered = stream[layer, z]
        for third in range(3):
            piece = dot(gathered, wp[layer, third], NN).T.reshape(H, HDIM, S)
            if third < 2:
                front, back = piece[:, :half], piece[:, half:]
                piece = jnp.concatenate([front * cosine_here - back * sine_here, back * cosine_here + front * sine_here], axis=1)
                speed = lax.rsqrt(jnp.sum(piece * piece, axis=1, keepdims=True) + 1e-06)
                piece = piece * speed * scale[:, :, :1]
                for head in range(H):
                    rates_out[head, third : third + 1] = speed[head]
            heads_out[:, third] = piece.astype(BF16)
        copies = spread(heads_out, heads_in.at[layer])
        rate_copies = spread(rates_out, rates_in.at[layer])
        used["heads"] = copies + rate_copies
        lend_weights(layer, (1, 2))
        settle()
        if layer:
            stream_lines[0].step(3)
            waiting["stream", 0] = pass_on(0, stream)
        arrive(copies + rate_copies)
        if layer:
            middle_lines[0].step(3)
            waiting["middle", 0] = pass_on(0, middles)
        for place in range(Z):
            key_rows[place] = heads_in[layer, place, 1].T
        free("mixed")
        for query in range(Z):
            raw = [dot(key_rows[key], heads_in[layer, query, 0], NN) * math.sqrt(HDIM) for key in range(query + 1)]
            first = starts[:, query * S : (query + 1) * S]
            last = index_all[:, query * S : (query + 1) * S]
            scores = []
            for key in range(query + 1):
                keys = key_index[key * S : (key + 1) * S]
                allowed = keys >= first
                if key == query:
                    allowed = allowed & (keys <= last)
                scores.append(jnp.where(allowed, raw[key], -1e30))
            highest = scores[0].max(axis=0, keepdims=True)
            for piece in scores[1:]:
                highest = jnp.maximum(highest, piece.max(axis=0, keepdims=True))
            lifted = [jnp.exp(piece - highest) for piece in scores]
            total = lifted[0].sum(axis=0, keepdims=True)
            for piece in lifted[1:]:
                total = total + piece.sum(axis=0, keepdims=True)
            shrink = 1.0 / total
            mixed = None
            for key in range(query + 1):
                low = (lifted[key] * shrink).astype(BF16)
                probs[layer, block(query, key)] = low
                term = dot(heads_in[layer, key, 2], low, NN)
                mixed = term if mixed is None else mixed + term
            mixed_out[query] = mixed.astype(BF16)
        copies = spread(mixed_out, mixed_in.at[layer])
        used["mixed"] = copies
        settle()
        await_weight(layer, 1)
        arrive(copies)
        attended = mixed_in[layer].reshape(inner, S).T
        free("branch")
        sums_out[0] = dot(attended, wo[layer], NN).astype(BF16).reshape(T, part, D)
        copies = scatter(0)
        stream_lines[layer].step(0)
        lend_weights(layer, (3,))
        settle()
        branch = scattered(0, copies)
        used["branch"] = copies
        branch_f[layer] = branch
        alpha = al[layer]
        middle = norm_parts(base + alpha[0:1] * (norm_parts(branch)[0] - base))[0]
        middle_f[layer] = middle
        copies = gather(layer, middles, middle.astype(BF16))
        stream_lines[layer].step(1)
        lend_weights(layer, (4,))
        settle()
        await_weight(layer, 2)
        await_weight(layer, 3)
        arrive(copies)
        stream_lines[layer].step(2)
        middle_lines[layer].step(0)
        middle_all = middles[layer, z]
        for begin in range(0, units, CHUNK):
            cols = slice(begin, begin + CHUNK)
            up = dot(middle_all, we[layer, 0, :, cols], NN)
            gate = dot(middle_all, we[layer, 1, :, cols], NN)
            ups[layer, :, cols] = up.astype(BF16)
            gates[layer, :, cols] = gate.astype(BF16)
            inside = us[layer, 1:2, cols] * gate
            hidden[:, cols] = (us[layer, 0:1, cols] * up * (inside / (1.0 + jnp.exp(-inside)))).astype(BF16)
        await_weight(layer, 4)
        free("feed")
        acted = hidden[...]
        for begin in range(0, D, CHUNK):
            cols = slice(begin, begin + CHUNK)
            sums_out[1, :, :, cols] = dot(acted, wr[layer, :, cols], NN).astype(BF16).reshape(T, part, CHUNK)
        copies = scatter(1)
        settle()
        feed = scattered(1, copies)
        middle_lines[layer].step(1)
        used["feed"] = copies
        feed_f[layer] = feed
        result = norm_parts(middle + alpha[1:2] * (norm_parts(feed)[0] - middle))[0].astype(BF16)
        outs[0, layer] = result
        return result

    def act_back(layer, cols, up, gate, slope_hidden):
        scale_up, scale_gate = us[layer, 0:1, cols], us[layer, 1:2, cols]
        inside = scale_gate * gate
        sigmoid = 1.0 / (1.0 + jnp.exp(-inside))
        silu = inside * sigmoid
        by_up = silu * slope_hidden
        by_gate = scale_up * up * (sigmoid + silu * (1.0 - sigmoid)) * slope_hidden
        return silu, by_up, by_gate

    def stage_copy(layer, chunk, which):
        buffer = (stage_e, stage_r)[which].at[chunk % 2]
        target = (ge_ref.at[0, chunk], gr_ref.at[0, chunk])[which]
        return pltpu.make_async_copy(buffer, target, stage_sem.at[layer, chunk, which])

    stage_slots = {}

    def stage_send(layer, chunk, which):
        buffer = (stage_e, stage_r)[which].at[chunk % 2]
        target = (ge_ref.at[1, chunk], gr_ref.at[1, chunk])[which]
        if (chunk, which) not in stage_slots:
            stage_slots[chunk, which] = slots.used
            slots.used += 1
        number = stage_slots[chunk, which]
        return pltpu.make_async_remote_copy(
            buffer, target, send_sem.at[number], recv_sem.at[number], device_id=sibling, device_id_type=MESH_IDS
        )

    def stage_wait(layer, chunk):
        @pl.when(core == layer)
        def _():
            for which in range(2):
                stage_copy(layer, chunk, which).wait()

        @pl.when(core != layer)
        def _():
            for which in range(2):
                stage_send(layer, chunk, which).wait_send()

    staged = []

    def feed_grads(layer, chunk):
        if chunk == 0:
            for place in range(Z):
                middle_cols[:, place * S : (place + 1) * S] = middles[layer, place].T
        cols = slice(chunk * CHUNK, (chunk + 1) * CHUNK)
        scale_up, scale_gate = us[layer, 0:1, cols], us[layer, 1:2, cols]
        sum_up = sum_gate = None
        for place in range(Z):
            rows = slice(place * S, (place + 1) * S)
            up = dot(middles[layer, place], we[layer, 0, :, cols], NN)
            gate = dot(middles[layer, place], we[layer, 1, :, cols], NN)
            slope_hidden = dot(feed_low[layer, place], wr[layer, cols, :], NT)
            silu, by_up, by_gate = act_back(layer, cols, up, gate, slope_hidden)
            hidden_part[:, rows] = (scale_up * up * silu).astype(BF16).T
            up_part[rows] = (by_up * scale_up).astype(BF16)
            gate_part[rows] = (by_gate * scale_gate).astype(BF16)
            term_up = jnp.sum(by_up * up, axis=0, keepdims=True)
            term_gate = jnp.sum(by_gate * gate, axis=0, keepdims=True)
            sum_up = term_up if sum_up is None else sum_up + term_up
            sum_gate = term_gate if sum_gate is None else sum_gate + term_gate
        finals[layer, 2:3, cols] = sum_up
        finals[layer, 3:4, cols] = sum_gate
        if len(staged) >= 2:
            stage_wait(*staged[-2])
        buffer = chunk % 2
        stage_e[buffer, 0] = dot(middle_cols[...], up_part[...], NN).astype(BF16)
        stage_e[buffer, 1] = dot(middle_cols[...], gate_part[...], NN).astype(BF16)
        stage_r[buffer] = dot(hidden_part[...], feed_low[layer].reshape(Z * S, D), NN).astype(BF16)

        @pl.when(core == layer)
        def _():
            for which in range(2):
                stage_copy(layer, chunk, which).start()

        @pl.when(core != layer)
        def _():
            for which in range(2):
                stage_send(layer, chunk, which).start()

        staged.append((layer, chunk))

    chunks = units // CHUNK
    projected = 3 * HDIM
    attn_slot = slots.used
    slots.used += 3 + Z - 1

    def attn_copy(number, source, target, device):
        number = attn_slot + number
        return pltpu.make_async_remote_copy(
            source, target, send_sem.at[number], recv_sem.at[number], device_id=device, device_id_type=MESH_IDS
        )

    def attn_pair():
        return [attn_copy(0, attn_own, attn_sib, sibling), attn_copy(1, scale_own, scale_sib, sibling)]

    def go_pair():
        return [attn_copy(2, go_out, go_sib, sibling)]

    def go_spread():
        return [
            attn_copy(3 + k, go_out.at[peer], go_in.at[k], device) for k, (peer, device) in enumerate(zip(place_peers, place_ids))
        ]

    def offer(layer, pair):
        @pl.when(core != layer)
        def _():
            for copy in pair():
                copy.start()

    def go_join(layer):
        @pl.when(core == layer)
        def _():
            for copy in go_pair():
                copy.wait_recv()
            go_out[...] = (go_out[...].astype(F32) + go_sib[...].astype(F32)).astype(BF16)
            for copy in go_spread():
                copy.start()

        @pl.when(core != layer)
        def _():
            for copy in go_pair():
                copy.wait_send()

    attn_lines = [Line(lambda place: [attn_all.at[place], scale_all.at[place]], core == layer) for layer in range(2)]

    def attn_join(layer):
        @pl.when(core == layer)
        def _():
            for copy in go_spread():
                copy.wait_recv()
            total = go_out[z].astype(F32)
            for k in range(Z - 1):
                total = total + go_in[k].astype(F32)
            attn_all[z, projected:] = total.astype(BF16)
            for copy in attn_pair():
                copy.wait_recv()
            attn_all[z, :projected] = (attn_own[...].astype(F32) + attn_sib[...].astype(F32)).astype(BF16)
            scale_all[z] = scale_own[...] + scale_sib[...]
            for copy in go_spread():
                copy.wait_send()

        @pl.when(core != layer)
        def _():
            for copy in attn_pair():
                copy.wait_send()

        attn_lines[layer].step(0)

    def head_grads(layer, scale_slope):
        arrive(waiting["stream", layer])
        grad = None
        for place in range(Z):
            term = dot(heads_back_out[place].reshape(3 * HDIM, S), stream[layer, place], NN)
            grad = term if grad is None else grad + term
        attn_own[...] = grad.astype(BF16)
        scale_rows = jnp.broadcast_to(scale_slope, (HDIM, 128)).T[:8]
        scale_own[...] = jnp.concatenate([scale_rows, scale_rows], axis=1)
        offer(layer, attn_pair)

    def backward(layer, base_low, slope):
        alpha = al[layer]
        middle_slope, feed_slope, alpha_m = blend_back(slope, middle_f[layer], feed_f[layer], alpha[1:2])
        copies = gather(layer, feed_low, feed_slope.astype(BF16))
        alpha_own[layer, 1:2] = alpha_m
        settle()
        if layer == 0:
            arrive(waiting["feed", 1] + waiting["middle", 1])
            feed_grads(1, 0)
        else:
            stream_lines[0].finish()
            middle_lines[0].finish()
        arrive(copies)
        if layer:
            middle_lines[1].step(2)
        feed_lines[layer].step(0)
        if layer == 0:
            attn_join(1)
        feed_all = feed_low[layer, z]
        for begin in range(0, units, CHUNK):
            cols = slice(begin, begin + CHUNK)
            slope_hidden = dot(feed_all, wr[layer, cols, :], NT)
            up, gate = ups[layer, :, cols].astype(F32), gates[layer, :, cols].astype(F32)
            _, by_up, by_gate = act_back(layer, cols, up, gate, slope_hidden)
            expanded_low[0, :, cols] = (by_up * us[layer, 0:1, cols]).astype(BF16)
            expanded_low[1, :, cols] = (by_gate * us[layer, 1:2, cols]).astype(BF16)
        free("middle_back")
        for begin in range(0, D, CHUNK):
            rows = slice(begin, begin + CHUNK)
            partial = dot(expanded_low[0], we[layer, 0, rows, :], NT) + dot(expanded_low[1], we[layer, 1, rows, :], NT)
            sums_out[2, :, :, rows] = partial.astype(BF16).reshape(T, part, CHUNK)
        copies = scatter(2)
        settle()
        if layer == 0:
            feed_grads(1, 1)
        middle_total = middle_slope + scattered(2, copies)
        feed_lines[layer].step(1)
        if layer == 0:
            attn_lines[1].step(1)
        used["middle_back"] = copies
        stream_slope, branch_slope, alpha_a = blend_back(middle_total, base_low.astype(F32), branch_f[layer], alpha[0:1])
        free("branch_low")
        branch_low[my_rows, :] = branch_slope.astype(BF16)
        mine = branch_low.at[my_rows, :]
        copies = [send(mine, mine, device) for device in tensor_ids]
        used["branch_low"] = copies
        alpha_own[layer, 0:1] = alpha_a
        if layer == 0:
            alpha_copies = [send(alpha_own, alpha_in.at[k], device) for k, device in enumerate(tensor_ids)]
            feed_grads(1, 2)
        settle()
        arrive(copies)
        branch_all = branch_low[...]
        free("mixed_back")
        back_out[...] = dot(wo[layer], branch_all, NT).astype(BF16).reshape(H, HDIM, S)
        copies = spread(back_out, back_in)
        used["mixed_back"] = copies
        go_out[...] = dot(mixed_in[layer].reshape(inner, S), branch_all, NN).astype(BF16).reshape(H, HDIM, D)
        offer(layer, go_pair)
        feed_lines[layer].step(2)
        if layer:
            stream_lines[1].step(3)
            waiting["stream", 1] = pass_on(1, stream)
            middle_lines[1].step(3)
            waiting["middle", 1] = pass_on(1, middles)
        else:
            attn_lines[1].step(2)
            stream_lines[1].finish()
            middle_lines[1].finish()
        settle()
        for place in range(Z):
            value_rows[place] = heads_in[layer, place, 2].T
        if layer == 0:
            arrive(alpha_copies)
            retire(alpha_copies)
            total = alpha_own[...]
            for k in range(T - 1):
                total = total + alpha_in[k]
            alpha_own[...] = total
            alpha_copies = [send(alpha_own, alpha_in.at[T - 1 + k], device) for k, device in enumerate(place_ids)]
        arrive(copies)
        if layer == 0:
            go_join(0)
            feed_lines[0].step(3)
            feed_passed = pass_on(0, feed_low)
        for query in range(Z):
            slope_mixed = back_in[query]
            lows = [probs[layer, block(query, key)] for key in range(query + 1)]
            probs_slope = [dot(value_rows[key], slope_mixed, NN) for key in range(query + 1)]
            row_term = None
            for low, piece in zip(lows, probs_slope):
                term = jnp.sum(low.astype(F32) * piece, axis=0, keepdims=True)
                row_term = term if row_term is None else row_term + term
            query_slope = None
            for key in range(query + 1):
                low = lows[key]
                scores_low = (low.astype(F32) * (probs_slope[key] - row_term)).astype(BF16)
                term = dot(heads_in[layer, key, 1], scores_low, NN)
                query_slope = term if query_slope is None else query_slope + term
                key_term = dot(heads_in[layer, query, 0], scores_low, NT)
                value_term = dot(slope_mixed, low, NT)
                if key == query:
                    key_grad[key] = key_term
                    value_grad[key] = value_term
                else:
                    key_grad[key] += key_term
                    value_grad[key] += value_term
            query_grad[query] = query_slope
        free("heads_back")
        scale = scales[layer, z][:, :1]
        inverse = 1.0 / scale
        scale_slope = None
        for place in range(Z):
            cosine_there, sine_there = cosines[place], sines[place]
            for third, source in ((0, query_grad), (1, key_grad)):
                piece = source[place] * math.sqrt(HDIM)
                unit = heads_in[layer, place, third].astype(F32) * inverse
                term = jnp.sum(piece * unit, axis=1, keepdims=True)
                scale_slope = term if scale_slope is None else scale_slope + term
                piece = piece * scale
                piece = rates_in[layer, place, third : third + 1] * (piece - unit * jnp.sum(unit * piece, axis=0, keepdims=True))
                front, back = piece[:half], piece[half:]
                piece = jnp.concatenate([front * cosine_there + back * sine_there, back * cosine_there - front * sine_there], axis=0)
                heads_back_out[place, third] = piece.astype(BF16)
            heads_back_out[place, 2] = value_grad[place].astype(BF16)
        copies = spread(heads_back_out, heads_back_in)
        used["heads_back"] = copies
        settle()
        if layer:
            feed_lines[1].step(3)
            waiting["feed", 1] = pass_on(1, feed_low)
        else:
            head_grads(layer, scale_slope)
            attn_join(0)
            feed_grads(1, 3)
            arrive(feed_passed + waiting["middle", 0])
            feed_grads(0, 0)
        arrive(copies)
        partial = None
        for third in range(3):
            term = dot(heads_back_in[:, third].reshape(inner, S).T, wp[layer, third], NT)
            partial = term if partial is None else partial + term
        free("stream_back")
        sums_out[3] = partial.astype(BF16).reshape(T, part, D)
        copies = scatter(3)
        settle()
        if layer:
            head_grads(layer, scale_slope)
            go_join(1)
        else:
            attn_lines[0].step(1)
            feed_grads(0, 1)
            attn_lines[0].step(2)
        result = (stream_slope + scattered(3, copies)).astype(BF16)
        used["stream_back"] = copies
        outs[1, layer] = result
        if layer == 0:
            total = alpha_own[...]
            arrive(alpha_copies)
            for k in range(Z - 1):
                total = total + alpha_in[T - 1 + k]
            finals[0, 0:2] = total[0]
            finals[1, 0:2] = total[1]
        return result

    forward(1, forward(0, acts_ref[core, 0]))
    slope = backward(1, outs[0, 0], cot_ref[core, 0].astype(F32))
    backward(0, acts_ref[core, 0], slope.astype(F32))

    other = 1 - core
    last = [send(outs.at[:, other], outs_in, sibling)]
    feed_grads(0, 2)
    for line in feed_lines:
        line.finish()
    attn_lines[1].step(3)
    attn_lines[1].finish()
    settle(2)
    feed_grads(0, 3)
    last += [send(finals.at[other], finals_in, sibling)]
    for kind, target in enumerate((lo_ref, ig_ref)):
        target[core] = outs[kind, core]
    arrive(last)
    for kind, target in enumerate((lo_ref, ig_ref)):
        target[other] = outs_in[kind]
    small_ref[0:4] = finals[core] + finals_in[...]
    for layer, chunk in staged[-2:]:
        stage_wait(layer, chunk)
    for chunk in range(chunks):
        for which in range(2):
            stage_send(0, chunk, which).wait_recv()
    attn_lines[0].step(3)
    attn_out = pltpu.make_async_copy(attn_all, attn_ref, stage_sem.at[0, 0, 0])
    attn_out.start()
    for place in range(Z):
        small_ref[4:5, place * HDIM : (place + 1) * HDIM] = scale_all[place, :1, :HDIM]
    settle(0)
    for copy in [weight_copy(piece) for piece in range(len(weights))]:
        copy.wait_send()
    attn_lines[0].finish()
    attn_out.wait()
    assert slots.used <= COPIES, slots.used


def relay(sizes, lengths, acts, cot, qs, us, al, wp, wo, we, wr):
    T, Z, S, part = sizes.tensors, sizes.places, sizes.local, sizes.part
    H, inner, units, D = sizes.heads, sizes.inner, sizes.units, sizes.width
    blocks, chunks = Z * (Z + 1) // 2, units // CHUNK
    vmem = pl.BlockSpec(memory_space=pltpu.VMEM)
    hbm = pl.BlockSpec(memory_space=pl.ANY)
    out_shape = (
        jax.ShapeDtypeStruct((2, part, D), BF16),
        jax.ShapeDtypeStruct((2, part, D), BF16),
        jax.ShapeDtypeStruct((8, D), F32),
        jax.ShapeDtypeStruct((Z, 4 * HDIM, D), BF16),
        jax.ShapeDtypeStruct((2, chunks, 2, D, CHUNK), BF16),
        jax.ShapeDtypeStruct((2, chunks, CHUNK, D), BF16),
    )
    DMA = pltpu.SemaphoreType.DMA
    V = pltpu.VMEM
    scratch = [
        V((2, 3, D, inner), BF16), V((2, inner, D), BF16), V((2, 2, D, units), BF16), V((2, units, D), BF16),
        V((2, 1, inner), F32), V((2, 2, units), F32), V((2, 2, D), F32),
        V((2, Z, S, D), BF16), V((2, Z, S, D), BF16), V((2, Z, S, D), BF16), V((S, D), BF16),
        V((Z, HDIM // 2, S), F32), V((Z, HDIM // 2, S), F32), V((2, H, HDIM, 128), F32),
        V((2, Z, 3, HDIM, S), BF16), V((2, Z, 2, S), F32),
        V((2, blocks, S, S), BF16), V((2, H, HDIM, S), BF16),
        V((4, T - 1, part, D), BF16),
        V((2, part, D), F32), V((2, part, D), F32), V((2, part, D), F32),
        V((2, S, units), BF16), V((2, S, units), BF16),
        V((S, units), BF16), V((2, S, units), BF16),
        V((Z, HDIM, S), BF16), V((H, 3, HDIM, S), BF16),
        V((H, 3, HDIM, S), BF16), V((H, 2, S), F32),
        V((Z, HDIM, S), BF16), V((H, HDIM, S), BF16), V((Z, 3, HDIM, S), BF16),
        V((4, T, part, D), BF16), V((H, HDIM, D), BF16), V((H, HDIM, D), BF16), V((Z - 1, HDIM, D), BF16),
        V((2, 2, part, D), BF16), V((2, part, D), BF16),
        V((Z, S, HDIM), BF16), V((Z, S, HDIM), BF16),
        V((Z, HDIM, S), F32), V((Z, HDIM, S), F32), V((Z, HDIM, S), F32),
        V((3 * HDIM, D), BF16), V((3 * HDIM, D), BF16), V((Z, 4 * HDIM, D), BF16),
        V((8, 128), F32), V((8, 128), F32), V((Z, 8, 128), F32),
        V((2, 2, D), F32), V((T + Z - 2, 2, 2, D), F32), V((2, 4, D), F32), V((4, D), F32),
        V((D, Z * S), BF16), V((CHUNK, Z * S), BF16), V((Z * S, CHUNK), BF16), V((Z * S, CHUNK), BF16),
        V((2, 2, D, CHUNK), BF16), V((2, CHUNK, D), BF16),
        DMA((2, 8)), DMA((8,)), DMA((COPIES,)), DMA((COPIES,)), DMA((2, chunks, 2)),
    ]
    return pl.pallas_call(
        functools.partial(relay_kernel, sizes),
        out_shape=out_shape,
        in_specs=[pl.BlockSpec(memory_space=pltpu.SMEM), vmem, vmem, vmem, vmem, vmem, hbm, hbm, hbm, hbm],
        out_specs=(vmem, vmem, vmem, hbm, hbm, hbm),
        scratch_shapes=scratch,
        compiler_params=pltpu.CompilerParams(collective_id=0, has_side_effects=True, vmem_limit_bytes=62 * 2**20),
        name="relay",
    )(lengths, acts, cot, qs, us, al, wp, wo, we, wr)


def finish_kernel(
    attn_ref, ge_ref, gr_ref, lo_in, ig_in, small_ref,
    projection_ref, output_ref, expansion_ref, reduction_ref, lo_ref, ig_ref, scale_ref, units_ref, alphas_ref,
):
    @pl.when(pl.program_id(0) == 0)
    def _():
        lo_ref[...] = lo_in[...]
        ig_ref[...] = ig_in[...]
        alphas_ref[...] = small_ref[0:2]
        units_ref[...] = small_ref[2:4, : units_ref.shape[1]]
        scale_ref[...] = small_ref[4:5, : scale_ref.shape[1]]

    places, chunks = attn_ref.shape[0], ge_ref.shape[1]
    for chunk in range(chunks):
        for side in range(2):
            for part in range(CHUNK // 128):
                lanes = slice(part * 128, (part + 1) * 128)
                total = ge_ref[0, chunk, side, :, lanes].astype(F32) + ge_ref[1, chunk, side, :, lanes].astype(F32)
                expansion_ref[:, 2 * (chunk * (CHUNK // 128) + part) + side, :] = total
    reduction_ref[...] = gr_ref[0].astype(F32) + gr_ref[1].astype(F32)
    for third in range(3):
        rows = attn_ref[:, third * HDIM : (third + 1) * HDIM, :].astype(F32)
        projection_ref[third] = rows.reshape(places * HDIM, rows.shape[2]).T
    output_ref[...] = attn_ref[:, 3 * HDIM :, :].astype(F32).reshape(output_ref.shape)


def finish(attn, ge, gr, lo, ig, small):
    places, _, D = attn.shape
    chunks, units, inner = ge.shape[1], ge.shape[1] * CHUNK, places * HDIM
    steps = D // 128
    rows = units // steps

    def whole(shape):
        return pl.BlockSpec(shape, lambda i: (0,) * len(shape))

    return pl.pallas_call(
        finish_kernel,
        grid=(steps,),
        in_specs=[
            pl.BlockSpec((places, 4 * HDIM, 128), lambda i: (0, 0, i)),
            pl.BlockSpec((2, chunks, 2, 128, CHUNK), lambda i: (0, 0, 0, i, 0)),
            pl.BlockSpec((2, rows, D), lambda i: (0, i, 0)),
            whole(lo.shape),
            whole(ig.shape),
            whole(small.shape),
        ],
        out_specs=(
            pl.BlockSpec((3, 128, inner), lambda i: (0, i, 0)),
            pl.BlockSpec((inner, 128), lambda i: (0, i)),
            pl.BlockSpec((128, units // 64, 128), lambda i: (i, 0, 0)),
            pl.BlockSpec((rows, D), lambda i: (i, 0)),
            whole(lo.shape),
            whole(ig.shape),
            whole((1, inner)),
            whole((2, units)),
            whole((2, D)),
        ),
        out_shape=(
            jax.ShapeDtypeStruct((3, D, inner), F32),
            jax.ShapeDtypeStruct((inner, D), F32),
            jax.ShapeDtypeStruct((D, units // 64, 128), F32),
            jax.ShapeDtypeStruct((units, D), F32),
            jax.ShapeDtypeStruct(lo.shape, BF16),
            jax.ShapeDtypeStruct(ig.shape, BF16),
            jax.ShapeDtypeStruct((1, inner), F32),
            jax.ShapeDtypeStruct((2, units), F32),
            jax.ShapeDtypeStruct((2, D), F32),
        ),
        compiler_params=pltpu.CompilerParams(vmem_limit_bytes=60 * 2**20),
        name="finish",
    )(attn, ge, gr.reshape(2, units, D), lo, ig, small)


def fast_body(
    activations, lengths, projection, output_weight, expansion, reduction, query_scale, unit_scales, alphas, cotangent
):
    _, _, part, width = activations.shape
    inner, units = output_weight.shape[1], reduction.shape[1]
    places = lax.axis_size("dp")
    sizes = Sizes(lax.axis_size("tensor"), places, part, width, inner, units)
    lo, ig, small, attn, ge, gr = relay(
        sizes, lengths, activations, cotangent, query_scale, unit_scales[0], alphas[0],
        projection[0].transpose(1, 0, 2), output_weight[0], expansion[0].transpose(1, 0, 2), reduction[0],
    )
    projection_grad, output_grad, expansion_grad, reduction_grad, lo, ig, scale_grad, unit_grad, alpha_grad = finish(
        attn, ge, gr, lo, ig, small
    )
    columns = units // 128
    expansion_grad = expansion_grad.reshape(width, columns, 2, 128).transpose(0, 2, 1, 3).reshape(width, 2, units)
    projection_grad = projection_grad.transpose(1, 0, 2)
    return (
        lo[None, :, None],
        ig[None, :, None],
        projection_grad[None],
        output_grad[None],
        expansion_grad[None],
        reduction_grad[None],
        scale_grad,
        unit_grad[None],
        alpha_grad[None],
    )


def solution(mesh):
    in_specs = (
        P(None, None, ("dp", "tensor"), None),
        P(),
        P("section", None, None, "tensor"),
        P("section", "tensor", None),
        P("section", None, None, "tensor"),
        P("section", "tensor", None),
        P("section", "tensor"),
        P("section", None, "tensor"),
        P("section", None, None),
        P(None, None, ("dp", "tensor"), None),
    )
    out_specs = (
        P("section", None, None, ("dp", "tensor"), None),
        P("section", None, None, ("dp", "tensor"), None),
        P("section", None, None, "tensor"),
        P("section", "tensor", None),
        P("section", None, None, "tensor"),
        P("section", "tensor", None),
        P("section", "tensor"),
        P("section", None, "tensor"),
        P("section", None, None),
    )
    def chosen(*arrays):
        activations, output_weight = arrays[0], arrays[3]
        heads = output_weight.shape[1] // HDIM
        fits = (
            mesh.shape["section"] == 2
            and mesh.shape["tensor"] == 4
            and mesh.shape["dp"] == heads
            and activations.shape[:2] == (2, 1)
            and activations.shape[2] * mesh.shape["tensor"] == 256
        )
        return (fast_body if fits else body)(*arrays)

    return jax.shard_map(chosen, mesh=mesh, in_specs=in_specs, out_specs=out_specs, check_vma=False)
```

```python
import functools
import math

import jax
import jax.numpy as jnp
from jax import lax
from jax.experimental import pallas as pl
from jax.experimental.pallas import tpu as pltpu
from jax.sharding import PartitionSpec as P

HDIM = 64


def from_behind(value, axis, steps):
    count = lax.axis_size(axis)
    initial, last = (max(0, -steps), min(count, count - steps))
    return lax.ppermute(value, axis, [(source, source + steps) for source in range(initial, last)])


def normed(v):
    return v * lax.rsqrt(jnp.mean(v * v, axis=-1, keepdims=True) + 1e-06)


def unit_heads(v):
    return v * lax.rsqrt(jnp.sum(v * v, axis=-1, keepdims=True) + 1e-06)


def frequencies(half):
    return jnp.exp(jnp.arange(half, dtype=jnp.float32) * (-2.0 * math.log(10000.0) / (2 * half)))


def rotate(view, angle):
    half = view.shape[-1] // 2
    cosine = jnp.cos(angle)[..., None, :]
    sine = jnp.sin(angle)[..., None, :]
    front = view[..., :half]
    back = view[..., half:]
    return jnp.concatenate([front * cosine - back * sine, back * cosine + front * sine], axis=-1)


def shaped(projected, scale, angle, heads):
    inner = projected.shape[-1] // 3
    lead = projected.shape[:-1]

    def turned(piece):
        view = piece.reshape(lead + (heads, inner // heads))
        return unit_heads(rotate(view, angle)).reshape(lead + (inner,)) * scale

    return (
        turned(projected[..., :inner]),
        turned(projected[..., inner : 2 * inner]),
        projected[..., 2 * inner :],
    )


def layout(lengths_row, slots):
    ends = jnp.cumsum(lengths_row, dtype=jnp.int32)
    index = jnp.arange(slots, dtype=jnp.int32)
    after = index[:, None] >= ends[None, :]
    segment = jnp.sum(after.astype(jnp.int32), axis=1, dtype=jnp.int32)
    begin = jnp.sum(jnp.where(after, lengths_row[None, :], 0), axis=1, dtype=jnp.int32)
    inside = index < ends[-1]
    segment = jnp.where(inside, segment, lengths_row.shape[0] + index)
    position = jnp.where(inside, index - begin, 0)
    return (segment, position)


def blend(base, branch, alpha):
    return normed(base + alpha * (normed(branch) - base))


def activate(expanded, scales):
    half = expanded.shape[-1] // 2
    return expanded[..., :half] * scales[0] * jax.nn.silu(expanded[..., half:] * scales[1])


def placing(lengths_now, local):
    slots = local * lax.axis_size("dp")
    start_here = lax.axis_index("dp") * local
    segment_all, position_all = jax.vmap(lambda row: layout(row, slots))(lengths_now)
    segment_here = lax.dynamic_slice_in_dim(segment_all, start_here, local, 1)
    position_here = lax.dynamic_slice_in_dim(position_all, start_here, local, 1)
    index_here = start_here + jnp.arange(local, dtype=jnp.int32)
    every = jnp.arange(slots, dtype=jnp.int32)
    allowed = (segment_here[:, :, None] == segment_all[:, None, :]) & (
        every[None, None, :] <= index_here[None, :, None]
    )
    angle = position_here.astype(jnp.float32)[..., None] * frequencies(HDIM // 2)
    return (allowed, angle)


def scored(query, key_all, allowed, heads):
    rows, local, inner = query.shape
    depth = inner // heads
    query_heads = query.reshape(rows, local, heads, depth)
    key_heads = key_all.reshape(rows, key_all.shape[1], heads, depth)
    raw = jnp.einsum(
        "rqhe,rkhe->rhqk", query_heads, key_heads, preferred_element_type=jnp.float32
    ) * math.sqrt(depth)
    return jnp.where(allowed[:, None], raw, -1e30)


def forward(stream, lengths_now, weights):
    projection, output_weight, expansion, reduction, query_scale, unit_scales, alphas = weights
    rows, part, width = stream.shape
    inner = output_weight.shape[0]
    heads = inner // HDIM
    hidden_width = reduction.shape[0]
    gathered = lax.all_gather(stream.astype(jnp.bfloat16), "tensor", axis=1, tiled=True)
    local = gathered.shape[1]
    allowed, angle = placing(lengths_now, local)
    projected = jnp.einsum(
        "rsd,dc->rsc",
        gathered,
        projection.reshape(width, 3 * inner),
        preferred_element_type=jnp.float32,
    )
    query, key, value = shaped(projected, query_scale, angle, heads)
    query_low = query.astype(jnp.bfloat16)
    key_low = key.astype(jnp.bfloat16)
    value_low = value.astype(jnp.bfloat16)
    key_all, value_all = (
        lax.all_gather(key_low, "dp", axis=1, tiled=True),
        lax.all_gather(value_low, "dp", axis=1, tiled=True),
    )
    scores = scored(query_low, key_all, allowed, heads)
    highest = jnp.max(scores, axis=-1, keepdims=True)
    lifted = jnp.exp(scores - highest)
    total = jnp.sum(lifted, axis=-1, keepdims=True)
    log_total = highest + jnp.log(total)
    probs_low = (lifted / total).astype(jnp.bfloat16)
    value_heads = value_all.reshape(rows, value_all.shape[1], heads, HDIM)
    mixed = jnp.einsum(
        "rhqk,rkhe->rqhe", probs_low, value_heads, preferred_element_type=jnp.float32
    )
    attended = mixed.reshape(rows, local, inner).astype(jnp.bfloat16)
    partial_branch = jnp.einsum(
        "rsc,cd->rsd", attended, output_weight, preferred_element_type=jnp.float32
    )
    branch = lax.psum_scatter(partial_branch, "tensor", scatter_dimension=1, tiled=True)
    middle = blend(stream, branch, alphas[0])
    middle_all = lax.all_gather(middle.astype(jnp.bfloat16), "tensor", axis=1, tiled=True)
    expanded = jnp.einsum(
        "rsd,dc->rsc",
        middle_all,
        expansion.reshape(width, 2 * hidden_width),
        preferred_element_type=jnp.float32,
    )
    hidden = activate(expanded, unit_scales).astype(jnp.bfloat16)
    partial_feed = jnp.einsum("rsf,fd->rsd", hidden, reduction, preferred_element_type=jnp.float32)
    feed = lax.psum_scatter(partial_feed, "tensor", scatter_dimension=1, tiled=True)
    result = blend(middle, feed, alphas[1])
    kept = dict(
        stream=stream,
        gathered=gathered,
        projected=projected,
        query=query_low,
        key=key_low,
        value=value_low,
        log_total=log_total,
        attended=attended,
        branch=branch,
        middle=middle,
        middle_all=middle_all,
        expanded=expanded,
        hidden=hidden,
        feed=feed,
        lengths=lengths_now,
    )
    kept = dict(kept, key_all=key_all, value_all=value_all)
    return (result, kept)


def backward(slope, kept, weights):
    projection, output_weight, expansion, reduction, query_scale, unit_scales, alphas = weights
    rows, part, width = slope.shape
    inner = output_weight.shape[0]
    heads = inner // HDIM
    hidden_width = reduction.shape[0]
    _, pull_feed = jax.vjp(blend, kept["middle"], kept["feed"], alphas[1])
    middle_slope, feed_slope, alpha_feed = pull_feed(slope)
    feed_all = lax.all_gather(feed_slope.astype(jnp.bfloat16), "tensor", axis=1, tiled=True)
    reduction_grad = jnp.einsum(
        "rsf,rsd->fd", kept["hidden"], feed_all, preferred_element_type=jnp.float32
    )
    hidden_slope = jnp.einsum(
        "rsd,fd->rsf", feed_all, reduction, preferred_element_type=jnp.float32
    )
    _, pull_active = jax.vjp(activate, kept["expanded"], unit_scales)
    expanded_slope, unit_grad = pull_active(hidden_slope)
    expanded_low = expanded_slope.astype(jnp.bfloat16)
    expansion_grad = jnp.einsum(
        "rsd,rsc->dc", kept["middle_all"], expanded_low, preferred_element_type=jnp.float32
    ).reshape(width, 2, hidden_width)
    partial_middle = jnp.einsum(
        "rsc,dc->rsd",
        expanded_low,
        expansion.reshape(width, 2 * hidden_width),
        preferred_element_type=jnp.float32,
    )
    middle_total = middle_slope + lax.psum_scatter(
        partial_middle, "tensor", scatter_dimension=1, tiled=True
    )
    _, pull_branch = jax.vjp(blend, kept["stream"], kept["branch"], alphas[0])
    stream_slope, branch_slope, alpha_branch = pull_branch(middle_total)
    branch_all = lax.all_gather(branch_slope.astype(jnp.bfloat16), "tensor", axis=1, tiled=True)
    output_grad = jnp.einsum(
        "rsc,rsd->cd", kept["attended"], branch_all, preferred_element_type=jnp.float32
    )
    attended_low = jnp.einsum(
        "rsd,cd->rsc", branch_all, output_weight, preferred_element_type=jnp.float32
    ).astype(jnp.bfloat16)
    local = attended_low.shape[1]
    key_all = kept["key_all"]
    value_all = kept["value_all"]
    slots = key_all.shape[1]
    allowed, angle = placing(kept["lengths"], local)
    scores = scored(kept["query"], key_all, allowed, heads)
    probs = jnp.exp(scores - kept["log_total"])
    scale = math.sqrt(HDIM)
    back_heads = attended_low.reshape(rows, local, heads, HDIM)
    query_heads = kept["query"].reshape(rows, local, heads, HDIM)
    key_heads = key_all.reshape(rows, slots, heads, HDIM)
    value_heads = value_all.reshape(rows, slots, heads, HDIM)
    probs_slope = jnp.einsum(
        "rqhe,rkhe->rhqk", back_heads, value_heads, preferred_element_type=jnp.float32
    )
    row_term = jnp.sum(probs * probs_slope, axis=-1, keepdims=True)
    scores_low = (probs * (probs_slope - row_term)).astype(jnp.bfloat16)
    query_slope = (
        jnp.einsum("rhqk,rkhe->rqhe", scores_low, key_heads, preferred_element_type=jnp.float32)
        * scale
    )
    value_grad_all = jnp.einsum(
        "rhqk,rqhe->rkhe",
        probs.astype(jnp.bfloat16),
        back_heads,
        preferred_element_type=jnp.float32,
    )
    key_grad_all = (
        jnp.einsum("rhqk,rqhe->rkhe", scores_low, query_heads, preferred_element_type=jnp.float32)
        * scale
    )
    key_slope, value_slope = (
        lax.psum_scatter(
            key_grad_all.reshape(rows, slots, inner), "dp", scatter_dimension=1, tiled=True
        ),
        lax.psum_scatter(
            value_grad_all.reshape(rows, slots, inner), "dp", scatter_dimension=1, tiled=True
        ),
    )
    _, pull_shape = jax.vjp(
        lambda source, scale_now: shaped(source, scale_now, angle, heads),
        kept["projected"],
        query_scale,
    )
    projected_slope, query_scale_grad = pull_shape(
        (query_slope.reshape(rows, local, inner), key_slope, value_slope)
    )
    projected_low = projected_slope.astype(jnp.bfloat16)
    projection_grad = jnp.einsum(
        "rsd,rsc->dc", kept["gathered"], projected_low, preferred_element_type=jnp.float32
    ).reshape(width, 3, inner)
    partial_stream = jnp.einsum(
        "rsc,dc->rsd",
        projected_low,
        projection.reshape(width, 3 * inner),
        preferred_element_type=jnp.float32,
    )
    spread = jnp.broadcast_to(
        jnp.stack([alpha_branch, alpha_feed])[:, None, :], (2, lax.axis_size("tensor"), width)
    )
    stream_part, alpha_sum = (
        lax.psum_scatter(partial_stream, "tensor", scatter_dimension=1, tiled=True),
        lax.psum_scatter(spread, "tensor", scatter_dimension=1, tiled=True),
    )
    stream_total = stream_slope + stream_part
    return (
        stream_total,
        (
            projection_grad,
            output_grad,
            expansion_grad,
            reduction_grad,
            query_scale_grad,
            unit_grad,
            alpha_sum[:, 0],
        ),
    )


def body(
    activations,
    lengths,
    projection,
    output_weight,
    expansion,
    reduction,
    query_scale,
    unit_scales,
    alphas,
    cotangent,
):
    micro, rows, part, width = activations.shape
    section = lax.axis_index("section")
    first = section == 0
    weights = (
        projection[0],
        output_weight[0],
        expansion[0],
        reduction[0],
        query_scale[0],
        unit_scales[0],
        alphas[0],
    )
    steps = micro + 1
    received = jnp.zeros((rows, part, width), jnp.bfloat16)
    outputs = []
    keeps = []
    for step in range(steps):
        index_now = jnp.clip(step - section, 0, micro - 1)
        lengths_now = lax.dynamic_index_in_dim(lengths, index_now, 0, keepdims=False)
        stream = jnp.where(first, activations[min(step, micro - 1)], received).astype(jnp.float32)
        result, kept = forward(stream, lengths_now, weights)
        result_low = result.astype(jnp.bfloat16)
        outputs.append(result_low)
        keeps.append(kept)
        if step + 1 < steps:
            received = from_behind(result_low, "section", 1)
    stacked = jnp.stack(outputs)
    layer_output = jnp.where(first, stacked[:micro], stacked[1:])[None]
    back_received = jnp.zeros((rows, part, width), jnp.bfloat16)
    slopes = []
    summed = None
    for step in range(steps):
        batch_now = step - 1 + section
        valid = (batch_now >= 0) & (batch_now < micro)
        slope = jnp.where(first, back_received, cotangent[min(step, micro - 1)]).astype(jnp.float32)
        earlier = keeps[max(step - 1, 0)]
        later = keeps[min(step + 1, micro)]
        kept = jax.tree.map(lambda left, right: jnp.where(first, left, right), earlier, later)
        stream_total, layer_grads = backward(slope, kept, weights)
        stream_low = stream_total.astype(jnp.bfloat16)
        slopes.append(stream_low)
        masked = tuple((jnp.where(valid, piece, 0.0) for piece in layer_grads))
        summed = (
            masked
            if summed is None
            else tuple((left + right for left, right in zip(summed, masked)))
        )
        if step + 1 < steps:
            back_received = from_behind(stream_low, "section", -1)
    stacked_slopes = jnp.stack(slopes)
    input_gradient = jnp.where(first, stacked_slopes[1:], stacked_slopes[:micro])[None]
    (
        projection_grad,
        output_grad,
        expansion_grad,
        reduction_grad,
        query_scale_grad,
        unit_grad,
        alpha_grad,
    ) = summed
    totals = lax.psum(
        (
            projection_grad,
            output_grad,
            expansion_grad,
            reduction_grad,
            query_scale_grad,
            unit_grad,
            alpha_grad,
        ),
        "dp",
    )
    return (
        layer_output,
        input_gradient,
        totals[0][None],
        totals[1][None],
        totals[2][None],
        totals[3][None],
        totals[4][None],
        totals[5][None],
        totals[6][None],
    )


MESH_IDS = pl.DeviceIdType.MESH
F32, BF16 = jnp.float32, jnp.bfloat16
CHUNK = 256
NN = ((1,), (0,))
NT = ((1,), (1,))


def dot(left, right, dims):
    return lax.dot_general(left, right, (dims, ((), ())), preferred_element_type=F32)


def norm_parts(v):
    rate = lax.rsqrt(jnp.mean(v * v, axis=-1, keepdims=True) + 1e-06)
    return v * rate, rate


def norm_back(slope, unit, rate):
    return rate * (slope - unit * jnp.mean(unit * slope, axis=-1, keepdims=True))


def blend_back(slope, base, branch, alpha):
    unit_branch, rate_branch = norm_parts(branch)
    toward = unit_branch - base
    unit, rate = norm_parts(base + alpha * toward)
    inner_slope = norm_back(slope, unit, rate)
    alpha_slope = jnp.sum(inner_slope * toward, axis=0, keepdims=True)
    scaled = alpha * inner_slope
    return inner_slope - scaled, norm_back(scaled, unit_branch, rate_branch), alpha_slope


def sequence_starts(lengths_ref, row, index):
    begin = jnp.zeros_like(index)
    end = jnp.int32(0)
    for sequence in range(lengths_ref.shape[2]):
        end = end + lengths_ref[row, 0, sequence]
        begin = jnp.where(index >= end, end, begin)
    return jnp.where(index < end, begin, index)


class Sizes:
    def __init__(self, tensors, places, part, width, inner, units):
        self.tensors, self.places, self.part, self.width = tensors, places, part, width
        self.inner, self.units = inner, units
        self.local = part * tensors
        self.heads = inner // HDIM


class Slots:
    def __init__(self, send, recv):
        self.send, self.recv, self.names = send, recv, {}

    def copy(self, name, source, target, device):
        number = self.names.setdefault(name, len(self.names))
        return pltpu.make_async_remote_copy(
            source, target, self.send.at[number], self.recv.at[number], device_id=device, device_id_type=MESH_IDS
        )


HALVES = 2
COPIES = 166


def relay_kernel(
    sizes,
    lengths_ref, acts_ref, cot_ref, qs_ref, us_ref, al_ref, wp_ref, wo_ref, we_ref, wr_ref,
    lo_ref, ig_ref, small_ref, attn_ref, ge_ref, gr_ref,
    wp, wo, we, wr, qs, us, al,
    stream, middles, feed_low, branch_low,
    cosines, sines, scales,
    heads_in, rates_in, probs, mixed_in, sums_in, branch_f, middle_f, feed_f, ups, gates,
    hidden, expanded_low, back_in, heads_back_in,
    heads_out, rates_out, mixed_out, back_out, heads_back_out, sums_out, go_out, go_sib, go_in,
    outs, outs_in, key_rows, value_rows, query_grad, key_grad, value_grad,
    attn_own, attn_sib, attn_all, scale_own, scale_sib, scale_all,
    alpha_own, alpha_in, finals, finals_in,
    middle_cols, hidden_part, up_part, gate_part, stage_e, stage_r, raw,
    weight_sem, weight_send, send_sem, recv_sem, stage_sem, raw_sem,
):
    T, Z, S, part = sizes.tensors, sizes.places, sizes.local, sizes.part
    H, inner, units, D = sizes.heads, sizes.inner, sizes.units, sizes.width
    core, t, z = lax.axis_index("section"), lax.axis_index("tensor"), lax.axis_index("dp")
    sibling = (1 - core, t, z)
    side, row = lax.rem(t, 2), t // 2
    tensor_peers = [row * 2 + (1 - side), (1 - row) * 2 + side, (1 - row) * 2 + (1 - side)]
    place_peers = [lax.rem(z + k, Z) for k in range(1, Z)]
    tensor_ids = [(core, peer, z) for peer in tensor_peers]
    place_ids = [(core, t, peer) for peer in place_peers]
    slots = Slots(send_sem, recv_sem)
    pending = [[]]

    weights = [
        (wp_ref, lambda layer: wp.at[layer]),
        (wo_ref, lambda layer: wo.at[layer]),
        (we.at[core, 0], lambda layer: we.at[layer, 0]),
        (we.at[core, 1], lambda layer: we.at[layer, 1]),
        (wr_ref, lambda layer: wr.at[layer]),
        (qs_ref, lambda layer: qs.at[layer]),
        (us_ref, lambda layer: us.at[layer]),
        (al_ref, lambda layer: al.at[layer]),
    ]

    def weight_load(layer, piece):
        source, target = weights[piece]
        return pltpu.make_async_copy(source, target(layer), weight_sem.at[layer, piece])

    for piece in range(len(weights)):
        if piece not in (2, 3):
            weight_load(core, piece).start()

    raw_rows = raw.shape[1]

    def raw_load(block):
        return pltpu.make_async_copy(we_ref.at[pl.ds(block * raw_rows, raw_rows)], raw.at[block % 2], raw_sem.at[block % 2])

    for block in range(2):
        raw_load(block).start()

    def take_apart(blocks):
        for block in blocks:
            raw_load(block).wait()
            we[core, :, block * raw_rows : (block + 1) * raw_rows, :] = jnp.swapaxes(raw[block % 2], 0, 1)
            if (block + 2) * raw_rows < D:
                raw_load(block + 2).start()

    barrier = pltpu.get_barrier_semaphore()
    partners = [sibling] + tensor_ids + place_ids
    for partner in partners:
        pl.semaphore_signal(barrier, inc=1, device_id=partner, device_id_type=MESH_IDS)
    turn = HDIM // 2
    index_all = lax.broadcasted_iota(jnp.int32, (1, S * Z), 1)
    starts = sequence_starts(lengths_ref, core, index_all)
    rates = jnp.exp(lax.broadcasted_iota(jnp.int32, (turn, 1), 0).astype(F32) * (-2.0 * math.log(10000.0) / HDIM))
    angle = rates * (index_all - starts).astype(F32)
    cosine, sine = jnp.cos(angle), jnp.sin(angle)
    for place in range(Z):
        cosines[place] = cosine[:, place * S : (place + 1) * S]
        sines[place] = sine[:, place * S : (place + 1) * S]
    key_index = lax.broadcasted_iota(jnp.int32, (S * Z, S), 0)
    pl.semaphore_wait(barrier, len(partners))

    def weight_copy(piece):
        source, target = weights[piece]
        return pltpu.make_async_remote_copy(
            source, target(core), weight_send.at[piece], weight_sem.at[core, piece], device_id=sibling, device_id_type=MESH_IDS
        )

    def lend_weights(layer, pieces):
        @pl.when(core == layer)
        def _():
            for piece in pieces:
                weight_copy(piece).start()

    for piece in (5, 6, 7):
        weight_copy(piece).start()
    lend_weights(0, (0,))

    def await_weight(layer, piece):
        if piece in (2, 3):
            @pl.when(core != layer)
            def _():
                weight_load(layer, piece).wait()
        else:
            weight_load(layer, piece).wait()

    def send(name, source, target, device):
        copy = slots.copy(name, source, target, device)
        copy.start()
        pending[-1].append(copy)
        return copy

    def settle(keep=4):
        pending.append([])
        while len(pending) > keep:
            for copy in pending.pop(0):
                copy.wait_send()

    def arrive(copies):
        for copy in copies:
            copy.wait_recv()

    def rows_of(index):
        return pl.ds(pl.multiple_of(index * part, part), part)

    my_rows, far_rows = rows_of(t), rows_of(tensor_peers[2])

    def gather(name, target, half, value):
        count = value.shape[0]
        rows = pl.ds(pl.multiple_of(t * part + half * count, count), count)
        target[rows, :] = value
        mine = target.at[rows, :]
        return [send((name, half, k), mine, mine, device) for k, device in enumerate(tensor_ids)]

    def half_of(target, half):
        return jnp.concatenate([target[index * part + half * count : index * part + (half + 1) * count, :] for index in range(T)], axis=0)

    count = part // HALVES
    halves = range(HALVES)

    def piece_of(half):
        return slice(half * count, (half + 1) * count)

    class Line:
        def __init__(self, name, views, guard=None):
            self.name, self.views, self.guard = name, views, guard

        def copies(self, way, step, origin):
            device = (core, t, z + 1) if way == 0 else (core, t, z - 1)
            return [slots.copy((self.name, way, step, k), view, view, device) for k, view in enumerate(self.views(origin))]

        def when(self, condition):
            return pl.when(condition if self.guard is None else condition & self.guard)

        def origin(self, way, step):
            return z - step if way == 0 else z + step

        def sends(self, way, step):
            return (z >= step) & (z + 1 < Z) if way == 0 else (z + step < Z) & (z >= 1)

        def step(self, step):
            for way in range(2):
                if step > 0:
                    @self.when(z >= step if way == 0 else z + step < Z)
                    def _():
                        for copy in self.copies(way, step - 1, self.origin(way, step)):
                            copy.wait_recv()

                if step < Z - 1:
                    @self.when(self.sends(way, step))
                    def _():
                        for copy in self.copies(way, step, self.origin(way, step)):
                            copy.start()

        def finish(self):
            for way in range(2):
                for step in range(Z - 1):
                    @self.when(self.sends(way, step))
                    def _():
                        for copy in self.copies(way, step, self.origin(way, step)):
                            copy.wait_send()

    def row_line(name, layer, target, groups):
        return Line((name, len(groups)), lambda place: [target.at[layer, place, rows, :] for rows in groups])

    def pass_on(name, layer, target, count=2, indices=range(Z - 1)):
        passed = []
        for index in indices:
            got = target.at[layer, place_peers[index], my_rows, :]
            passed += [send((name, "pass", index, k), got, got, device) for k, device in enumerate(tensor_ids[:count])]
        return passed

    def scatter(number, half):
        return [
            send((number, half, k), sums_out.at[number, half, peer], sums_in.at[number, half, k], device)
            for k, (peer, device) in enumerate(zip(tensor_peers, tensor_ids))
        ]

    def scattered(number, half, copies):
        arrive(copies)
        total = sums_out[number, half, t].astype(F32)
        for k in range(T - 1):
            total = total + sums_in[number, half, k].astype(F32)
        return total

    def retire(copies):
        for copy in copies:
            for group in pending:
                if any(copy is other for other in group):
                    copy.wait_send()
                    group[:] = [other for other in group if other is not copy]

    def spread(name, source, target):
        target[z] = source[z]
        return [
            send((name, k), source.at[peer], target.at[z], device) for k, (peer, device) in enumerate(zip(place_peers, place_ids))
        ]

    def block(query, key):
        return query * (query + 1) // 2 + key

    used, waiting = {}, {}
    first_line = row_line("first line", 0, stream, [my_rows])
    stream_lines = [row_line("stream line", 0, stream, [far_rows]), row_line("stream line", 1, stream, [my_rows, far_rows])]
    middle_lines = [row_line("middle line", layer, middles, [my_rows, far_rows]) for layer in range(2)]
    feed_lines = [row_line(("feed line", layer), layer, feed_low, [my_rows]) for layer in range(2)]

    def free(name):
        retire(used.pop(name, []))

    first_stream = gather("stream", stream.at[0, z], 0, acts_ref[core, 0])
    first_line.step(0)

    def forward(layer, base_low, stream_copies, then):
        if layer == 0:
            take_apart(range(0, D // raw_rows // 2))
        await_weight(layer, 0)
        for piece in (5, 6, 7):
            await_weight(layer, piece)
        scale = jnp.broadcast_to(jnp.broadcast_to(qs[layer], (8, inner)).T[:, :1], (inner, 128)).reshape(H, HDIM, 128)
        scales[layer] = scale
        cosine_here, sine_here = cosines[z][None], sines[z][None]
        arrive(stream_copies)
        if layer == 0:
            first_line.step(1)
        free("heads")
        gathered = stream[layer, z]
        for third in range(3):
            piece = dot(gathered, wp[layer, third], NN).T.reshape(H, HDIM, S)
            if third < 2:
                front, back = piece[:, :turn], piece[:, turn:]
                piece = jnp.concatenate([front * cosine_here - back * sine_here, back * cosine_here + front * sine_here], axis=1)
                speed = lax.rsqrt(jnp.sum(piece * piece, axis=1, keepdims=True) + 1e-06)
                piece = piece * speed * scale[:, :, :1]
                for head in range(H):
                    rates_out[head, third : third + 1] = speed[head]
            heads_out[:, third] = piece.astype(BF16)
        copies = spread("heads", heads_out, heads_in.at[layer])
        rate_copies = spread("rates", rates_out, rates_in.at[layer])
        used["heads"] = copies + rate_copies
        if layer == 0:
            first_line.step(2)
            stream_lines[0].step(0)
            take_apart(range(D // raw_rows // 2, D // raw_rows))
        else:
            middle_lines[0].step(2)
        lend_weights(layer, (1, 2))
        settle()
        if layer:
            first_line.step(3)
            waiting["stream", 0] = pass_on("stream", 0, stream)
        arrive(copies + rate_copies)
        if layer:
            middle_lines[0].step(3)
            waiting["middle", 0] = pass_on("middle", 0, middles)
        for place in range(Z):
            key_rows[place] = heads_in[layer, place, 1].T
        free("mixed")
        for query in range(Z):
            raw = [dot(key_rows[key], heads_in[layer, query, 0], NN) * math.sqrt(HDIM) for key in range(query + 1)]
            first = starts[:, query * S : (query + 1) * S]
            last = index_all[:, query * S : (query + 1) * S]
            scores = []
            for key in range(query + 1):
                keys = key_index[key * S : (key + 1) * S]
                allowed = keys >= first
                if key == query:
                    allowed = allowed & (keys <= last)
                scores.append(jnp.where(allowed, raw[key], -1e30))
            highest = scores[0].max(axis=0, keepdims=True)
            for piece in scores[1:]:
                highest = jnp.maximum(highest, piece.max(axis=0, keepdims=True))
            lifted = [jnp.exp(piece - highest) for piece in scores]
            total = lifted[0].sum(axis=0, keepdims=True)
            for piece in lifted[1:]:
                total = total + piece.sum(axis=0, keepdims=True)
            shrink = 1.0 / total
            mixed = None
            for key in range(query + 1):
                low = (lifted[key] * shrink).astype(BF16)
                probs[layer, block(query, key)] = low
                term = dot(heads_in[layer, key, 2], low, NN)
                mixed = term if mixed is None else mixed + term
            mixed_out[query] = mixed.astype(BF16)
        copies = spread("mixed", mixed_out, mixed_in.at[layer])
        used["mixed"] = copies
        if layer == 0:
            stream_lines[0].step(1)
        settle()
        if layer:
            first_line.finish()
            stream_lines[0].step(3)
            stream_lines[0].finish()
            middle_lines[0].finish()
        await_weight(layer, 1)
        arrive(copies)
        attended = mixed_in[layer].reshape(inner, S).T
        free("branch")
        partial = dot(attended, wo[layer], NN).astype(BF16).reshape(T, HALVES, count, D)
        branch_copies = []
        for half in halves:
            sums_out[0, half] = partial[:, half]
            branch_copies.append(scatter(0, half))
        used["branch"] = sum(branch_copies, [])
        if layer:
            stream_lines[1].step(0)
        else:
            stream_lines[0].step(2)
        lend_weights(layer, (3,))
        settle()
        alpha = al[layer]
        middle_copies = []
        for half in halves:
            branch = scattered(0, half, branch_copies[half])
            base = base_low[piece_of(half)].astype(F32)
            middle = norm_parts(base + alpha[0:1] * (norm_parts(branch)[0] - base))[0]
            middle_copies.append(gather("middle", middles.at[layer, z], half, middle.astype(BF16)))
            branch_f[layer, piece_of(half)] = branch
            middle_f[layer, piece_of(half)] = middle
        if layer:
            stream_lines[1].step(1)
        lend_weights(layer, (4,))
        settle()
        if layer:
            arrive(waiting["stream", 0] + waiting["middle", 0])
        free("feed")
        for piece in (2, 3):
            await_weight(layer, piece)
        feed_copies = []
        for half in halves:
            arrive(middle_copies[half])
            middle_all = half_of(middles.at[layer, z], half)
            for begin in range(0, units, CHUNK):
                cols = slice(begin, begin + CHUNK)
                up = dot(middle_all, we[layer, 0, :, cols], NN)
                gate = dot(middle_all, we[layer, 1, :, cols], NN)
                ups[layer, half, :, cols] = up.astype(BF16)
                gates[layer, half, :, cols] = gate.astype(BF16)
                inside = us[layer, 1:2, cols] * gate
                hidden[:, cols] = (us[layer, 0:1, cols] * up * (inside / (1.0 + jnp.exp(-inside)))).astype(BF16)
            if half == 0:
                await_weight(layer, 4)
            acted = hidden[...]
            for begin in range(0, D, CHUNK):
                cols = slice(begin, begin + CHUNK)
                sums_out[1, half, :, :, cols] = dot(acted, wr[layer, :, cols], NN).astype(BF16).reshape(T, count, CHUNK)
            feed_copies.append(scatter(1, half))
        used["feed"] = sum(feed_copies, [])
        if layer:
            stream_lines[1].step(2)
        middle_lines[layer].step(0)
        settle()
        for half in halves:
            feed = scattered(1, half, feed_copies[half])
            feed_f[layer, piece_of(half)] = feed
            middle = middle_f[layer, piece_of(half)]
            result = norm_parts(middle + alpha[1:2] * (norm_parts(feed)[0] - middle))[0].astype(BF16)
            outs[0, layer, piece_of(half)] = result
            then(half, result)
        if layer == 0:
            middle_lines[0].step(1)
            lend_weights(1, (0,))

    def act_back(layer, cols, up, gate, slope_hidden):
        scale_up, scale_gate = us[layer, 0:1, cols], us[layer, 1:2, cols]
        inside = scale_gate * gate
        sigmoid = 1.0 / (1.0 + jnp.exp(-inside))
        silu = inside * sigmoid
        by_up = silu * slope_hidden
        by_gate = scale_up * up * (sigmoid + silu * (1.0 - sigmoid)) * slope_hidden
        return silu, by_up, by_gate

    def stage_copy(layer, chunk, which):
        buffer = (stage_e, stage_r)[which].at[chunk % 2]
        target = (ge_ref.at[0, chunk], gr_ref.at[0, chunk])[which]
        return pltpu.make_async_copy(buffer, target, stage_sem.at[layer, chunk, which])

    def stage_send(layer, chunk, which):
        buffer = (stage_e, stage_r)[which].at[chunk % 2]
        target = (ge_ref.at[1, chunk], gr_ref.at[1, chunk])[which]
        return slots.copy(("stage", chunk, which), buffer, target, sibling)

    def stage_wait(layer, chunk):
        @pl.when(core == layer)
        def _():
            for which in range(2):
                stage_copy(layer, chunk, which).wait()

        @pl.when(core != layer)
        def _():
            for which in range(2):
                stage_send(layer, chunk, which).wait_send()

    staged = []

    def feed_grads(layer, chunk):
        if chunk == 0:
            for place in range(Z):
                middle_cols[:, place * S : (place + 1) * S] = middles[layer, place].T
        cols = slice(chunk * CHUNK, (chunk + 1) * CHUNK)
        scale_up, scale_gate = us[layer, 0:1, cols], us[layer, 1:2, cols]
        sum_up = sum_gate = None
        for place in range(Z):
            rows = slice(place * S, (place + 1) * S)
            up = dot(middles[layer, place], we[layer, 0, :, cols], NN)
            gate = dot(middles[layer, place], we[layer, 1, :, cols], NN)
            slope_hidden = dot(feed_low[layer, place], wr[layer, cols, :], NT)
            silu, by_up, by_gate = act_back(layer, cols, up, gate, slope_hidden)
            hidden_part[:, rows] = (scale_up * up * silu).astype(BF16).T
            up_part[rows] = (by_up * scale_up).astype(BF16)
            gate_part[rows] = (by_gate * scale_gate).astype(BF16)
            term_up = jnp.sum(by_up * up, axis=0, keepdims=True)
            term_gate = jnp.sum(by_gate * gate, axis=0, keepdims=True)
            sum_up = term_up if sum_up is None else sum_up + term_up
            sum_gate = term_gate if sum_gate is None else sum_gate + term_gate
        finals[layer, 2:3, cols] = sum_up
        finals[layer, 3:4, cols] = sum_gate
        if len(staged) >= 2:
            stage_wait(*staged[-2])
        buffer = chunk % 2
        stage_e[buffer, 0] = dot(middle_cols[...], up_part[...], NN).astype(BF16)
        stage_e[buffer, 1] = dot(middle_cols[...], gate_part[...], NN).astype(BF16)
        stage_r[buffer] = dot(hidden_part[...], feed_low[layer].reshape(Z * S, D), NN).astype(BF16)

        @pl.when(core == layer)
        def _():
            for which in range(2):
                stage_copy(layer, chunk, which).start()

        @pl.when(core != layer)
        def _():
            for which in range(2):
                stage_send(layer, chunk, which).start()

        staged.append((layer, chunk))

    chunks = units // CHUNK
    projected = 3 * HDIM
    def attn_pair():
        return [slots.copy("head", attn_own, attn_sib, sibling), slots.copy("scale", scale_own, scale_sib, sibling)]

    def go_pair():
        return [slots.copy("go", go_out, go_sib, sibling)]

    def go_spread():
        return [
            slots.copy(("go", k), go_out.at[peer], go_in.at[k], device) for k, (peer, device) in enumerate(zip(place_peers, place_ids))
        ]

    def offer(layer, pair):
        @pl.when(core != layer)
        def _():
            for copy in pair():
                copy.start()

    def go_join(layer):
        @pl.when(core == layer)
        def _():
            for copy in go_pair():
                copy.wait_recv()
            go_out[...] = (go_out[...].astype(F32) + go_sib[...].astype(F32)).astype(BF16)
            for copy in go_spread():
                copy.start()

        @pl.when(core != layer)
        def _():
            for copy in go_pair():
                copy.wait_send()

    attn_lines = [Line("heads line", lambda place: [attn_all.at[place], scale_all.at[place]], core == layer) for layer in range(2)]

    def attn_join(layer):
        @pl.when(core == layer)
        def _():
            for copy in go_spread():
                copy.wait_recv()
            total = go_out[z].astype(F32)
            for k in range(Z - 1):
                total = total + go_in[k].astype(F32)
            attn_all[z, projected:] = total.astype(BF16)
            for copy in attn_pair():
                copy.wait_recv()
            attn_all[z, :projected] = (attn_own[...].astype(F32) + attn_sib[...].astype(F32)).astype(BF16)
            scale_all[z] = scale_own[...] + scale_sib[...]
            for copy in go_spread():
                copy.wait_send()

        @pl.when(core != layer)
        def _():
            for copy in attn_pair():
                copy.wait_send()

        attn_lines[layer].step(0)

    def head_grads(layer, scale_slope):
        if layer:
            arrive(waiting["stream", 1])
        grad = None
        for place in range(Z):
            term = dot(heads_back_out[place].reshape(3 * HDIM, S), stream[layer, place], NN)
            grad = term if grad is None else grad + term
        attn_own[...] = grad.astype(BF16)
        scale_rows = jnp.broadcast_to(scale_slope, (HDIM, 128)).T[:8]
        scale_own[...] = jnp.concatenate([scale_rows, scale_rows], axis=1)
        offer(layer, attn_pair)

    def enter(layer, half, slope):
        rows = piece_of(half)
        middle_slope, feed_slope, alpha_m = blend_back(slope, middle_f[layer, rows], feed_f[layer, rows], al[layer, 1:2])
        copies = gather("feed_low", feed_low.at[layer, z], half, feed_slope.astype(BF16))
        return middle_slope, alpha_m, copies

    def backward(layer, base_low, entered, then):
        alpha = al[layer]
        alpha_own[layer, 1:2] = entered[0][1] + entered[1][1]
        if layer:
            stream_lines[1].step(3)
            waiting["stream", 1] = pass_on("stream", 1, stream, 2, [0])
        else:
            waiting["feed", 1] += pass_on("feed", 1, feed_low, 3, [2])
        settle()
        if layer == 0:
            attn_join(1)
        free("middle_back")
        back_copies = []
        for half in halves:
            arrive(entered[half][2])
            feed_all = half_of(feed_low.at[layer, z], half)
            for begin in range(0, units, CHUNK):
                cols = slice(begin, begin + CHUNK)
                slope_hidden = dot(feed_all, wr[layer, cols, :], NT)
                up, gate = ups[layer, half, :, cols].astype(F32), gates[layer, half, :, cols].astype(F32)
                _, by_up, by_gate = act_back(layer, cols, up, gate, slope_hidden)
                expanded_low[0, :, cols] = (by_up * us[layer, 0:1, cols]).astype(BF16)
                expanded_low[1, :, cols] = (by_gate * us[layer, 1:2, cols]).astype(BF16)
            for begin in range(0, D, CHUNK):
                rows = slice(begin, begin + CHUNK)
                partial = dot(expanded_low[0], we[layer, 0, rows, :], NT) + dot(expanded_low[1], we[layer, 1, rows, :], NT)
                sums_out[2, half, :, :, rows] = partial.astype(BF16).reshape(T, count, CHUNK)
            back_copies.append(scatter(2, half))
        used["middle_back"] = sum(back_copies, [])
        if layer:
            waiting["stream", 1] += pass_on("stream", 1, stream, 2, [1])
            middle_lines[1].step(1)
        feed_lines[layer].step(0)
        settle()
        if layer == 0:
            attn_lines[1].step(1)
            arrive(waiting["feed", 1] + waiting["middle", 1])
            feed_grads(1, 0)
        free("branch_low")
        branch_copies, stream_slopes, alpha_a = [], [], None
        for half in halves:
            middle_total = entered[half][0] + scattered(2, half, back_copies[half])
            stream_slope, branch_slope, term = blend_back(
                middle_total, base_low[piece_of(half)].astype(F32), branch_f[layer, piece_of(half)], alpha[0:1]
            )
            branch_copies.append(gather("branch_low", branch_low, half, branch_slope.astype(BF16)))
            stream_slopes.append(stream_slope)
            alpha_a = term if alpha_a is None else alpha_a + term
        copies = sum(branch_copies, [])
        used["branch_low"] = copies
        alpha_own[layer, 0:1] = alpha_a
        if layer:
            waiting["stream", 1] += pass_on("stream", 1, stream, 2, [2])
            middle_lines[1].step(2)
        feed_lines[layer].step(1)
        if layer == 0:
            attn_lines[1].step(2)
            alpha_copies = [send(("alpha", k), alpha_own, alpha_in.at[k], device) for k, device in enumerate(tensor_ids)]
            feed_grads(1, 1)
        settle()
        arrive(copies)
        branch_all = branch_low[...]
        free("mixed_back")
        back_out[...] = dot(wo[layer], branch_all, NT).astype(BF16).reshape(H, HDIM, S)
        copies = spread("mixed_back", back_out, back_in)
        used["mixed_back"] = copies
        go_out[...] = dot(mixed_in[layer].reshape(inner, S), branch_all, NN).astype(BF16).reshape(H, HDIM, D)
        offer(layer, go_pair)
        feed_lines[layer].step(2)
        if layer:
            middle_lines[1].step(3)
            waiting["middle", 1] = pass_on("middle", 1, middles)
        else:
            stream_lines[1].finish()
            middle_lines[1].finish()
        settle()
        if layer == 0:
            feed_grads(1, 2)
        for place in range(Z):
            value_rows[place] = heads_in[layer, place, 2].T
        if layer == 0:
            arrive(alpha_copies)
            retire(alpha_copies)
            total = alpha_own[...]
            for k in range(T - 1):
                total = total + alpha_in[k]
            alpha_own[...] = total
            alpha_copies = [
                send(("alpha", T - 1 + k), alpha_own, alpha_in.at[T - 1 + k], device) for k, device in enumerate(place_ids)
            ]
        arrive(copies)
        if layer == 0:
            go_join(0)
            feed_lines[0].step(3)
            feed_passed = pass_on("feed", 0, feed_low, 3)
        for query in range(Z):
            slope_mixed = back_in[query]
            lows = [probs[layer, block(query, key)] for key in range(query + 1)]
            probs_slope = [dot(value_rows[key], slope_mixed, NN) for key in range(query + 1)]
            row_term = None
            for low, piece in zip(lows, probs_slope):
                term = jnp.sum(low.astype(F32) * piece, axis=0, keepdims=True)
                row_term = term if row_term is None else row_term + term
            query_slope = None
            for key in range(query + 1):
                low = lows[key]
                scores_low = (low.astype(F32) * (probs_slope[key] - row_term)).astype(BF16)
                term = dot(heads_in[layer, key, 1], scores_low, NN)
                query_slope = term if query_slope is None else query_slope + term
                key_term = dot(heads_in[layer, query, 0], scores_low, NT)
                value_term = dot(slope_mixed, low, NT)
                if key == query:
                    key_grad[key] = key_term
                    value_grad[key] = value_term
                else:
                    key_grad[key] += key_term
                    value_grad[key] += value_term
            query_grad[query] = query_slope
        free("heads_back")
        scale = scales[layer, z][:, :1]
        inverse = 1.0 / scale
        scale_slope = None
        for place in range(Z):
            cosine_there, sine_there = cosines[place], sines[place]
            for third, source in ((0, query_grad), (1, key_grad)):
                piece = source[place] * math.sqrt(HDIM)
                unit = heads_in[layer, place, third].astype(F32) * inverse
                term = jnp.sum(piece * unit, axis=1, keepdims=True)
                scale_slope = term if scale_slope is None else scale_slope + term
                piece = piece * scale
                piece = rates_in[layer, place, third : third + 1] * (piece - unit * jnp.sum(unit * piece, axis=0, keepdims=True))
                front, back = piece[:turn], piece[turn:]
                piece = jnp.concatenate([front * cosine_there + back * sine_there, back * cosine_there - front * sine_there], axis=0)
                heads_back_out[place, third] = piece.astype(BF16)
            heads_back_out[place, 2] = value_grad[place].astype(BF16)
        copies = spread("heads_back", heads_back_out, heads_back_in)
        used["heads_back"] = copies
        settle()
        if layer == 0:
            head_grads(layer, scale_slope)
            feed_grads(1, 3)
            attn_join(0)
            arrive(feed_passed)
            feed_grads(0, 0)
        arrive(copies)
        partial = None
        for third in range(3):
            term = dot(heads_back_in[:, third].reshape(inner, S).T, wp[layer, third], NT)
            partial = term if partial is None else partial + term
        free("stream_back")
        partial = partial.astype(BF16).reshape(T, HALVES, count, D)
        copies = []
        for half in halves:
            sums_out[3, half] = partial[:, half]
            copies.append(scatter(3, half))
        settle()
        if layer:
            feed_lines[1].step(3)
            waiting["feed", 1] = pass_on("feed", 1, feed_low, 3, [0, 1])
            head_grads(layer, scale_slope)
            go_join(1)
        else:
            attn_lines[0].step(1)
            feed_grads(0, 1)
            attn_lines[0].step(2)
        for half in halves:
            result = (stream_slopes[half] + scattered(3, half, copies[half])).astype(BF16)
            outs[1, layer, piece_of(half)] = result
            then(half, result)
        used["stream_back"] = sum(copies, [])
        if layer == 0:
            total = alpha_own[...]
            arrive(alpha_copies)
            for k in range(Z - 1):
                total = total + alpha_in[T - 1 + k]
            finals[0, 0:2] = total[0]
            finals[1, 0:2] = total[1]

    next_stream, entered_last, entered_first = [], [], []

    def to_second(half, result):
        next_stream.extend(gather("stream", stream.at[1, z], half, result))

    def to_backward(half, result):
        entered_last.append(enter(1, half, cot_ref[core, 0, piece_of(half)].astype(F32)))

    def to_first(half, result):
        entered_first.append(enter(0, half, result.astype(F32)))

    forward(0, acts_ref.at[core, 0], first_stream, to_second)
    forward(1, outs.at[0, 0], next_stream, to_backward)
    backward(1, outs.at[0, 0], entered_last, to_first)
    backward(0, acts_ref.at[core, 0], entered_first, lambda half, result: None)

    other = 1 - core
    last = [send("outs", outs.at[:, other], outs_in, sibling)]
    feed_grads(0, 2)
    for line in feed_lines:
        line.finish()
    attn_lines[1].step(3)
    attn_lines[1].finish()
    settle(2)
    feed_grads(0, 3)
    last += [send("finals", finals.at[other], finals_in, sibling)]
    for kind, target in enumerate((lo_ref, ig_ref)):
        target[core] = outs[kind, core]
    arrive(last)
    for kind, target in enumerate((lo_ref, ig_ref)):
        target[other] = outs_in[kind]
    small_ref[0:4] = finals[core] + finals_in[...]
    for layer, chunk in staged[-2:]:
        stage_wait(layer, chunk)
    for chunk in range(chunks):
        for which in range(2):
            stage_send(0, chunk, which).wait_recv()
    attn_lines[0].step(3)
    attn_out = pltpu.make_async_copy(attn_all, attn_ref, stage_sem.at[0, 0, 0])
    attn_out.start()
    for place in range(Z):
        small_ref[4:5, place * HDIM : (place + 1) * HDIM] = scale_all[place, :1, :HDIM]
    settle(0)
    for copy in [weight_copy(piece) for piece in range(len(weights))]:
        copy.wait_send()
    attn_lines[0].finish()
    attn_out.wait()
    assert len(slots.names) == COPIES, len(slots.names)


def relay(sizes, lengths, acts, cot, qs, us, al, wp, wo, we, wr):
    T, Z, S, part = sizes.tensors, sizes.places, sizes.local, sizes.part
    H, inner, units, D = sizes.heads, sizes.inner, sizes.units, sizes.width
    blocks, chunks = Z * (Z + 1) // 2, units // CHUNK
    vmem = pl.BlockSpec(memory_space=pltpu.VMEM)
    hbm = pl.BlockSpec(memory_space=pl.ANY)
    out_shape = (
        jax.ShapeDtypeStruct((2, part, D), BF16),
        jax.ShapeDtypeStruct((2, part, D), BF16),
        jax.ShapeDtypeStruct((8, D), F32),
        jax.ShapeDtypeStruct((Z, 4 * HDIM, D), BF16),
        jax.ShapeDtypeStruct((2, chunks, 2, D, CHUNK), BF16),
        jax.ShapeDtypeStruct((2, chunks, CHUNK, D), BF16),
    )
    DMA = pltpu.SemaphoreType.DMA
    V = pltpu.VMEM
    scratch = [
        V((2, 3, D, inner), BF16), V((2, inner, D), BF16), V((2, 2, D, units), BF16), V((2, units, D), BF16),
        V((2, 1, inner), F32), V((2, 2, units), F32), V((2, 2, D), F32),
        V((2, Z, S, D), BF16), V((2, Z, S, D), BF16), V((2, Z, S, D), BF16), V((S, D), BF16),
        V((Z, HDIM // 2, S), F32), V((Z, HDIM // 2, S), F32), V((2, H, HDIM, 128), F32),
        V((2, Z, 3, HDIM, S), BF16), V((2, Z, 2, S), F32),
        V((2, blocks, S, S), BF16), V((2, H, HDIM, S), BF16),
        V((4, HALVES, T - 1, part // HALVES, D), BF16),
        V((2, part, D), F32), V((2, part, D), F32), V((2, part, D), F32),
        V((2, HALVES, S // HALVES, units), BF16), V((2, HALVES, S // HALVES, units), BF16),
        V((S // HALVES, units), BF16), V((2, S // HALVES, units), BF16),
        V((Z, HDIM, S), BF16), V((H, 3, HDIM, S), BF16),
        V((H, 3, HDIM, S), BF16), V((H, 2, S), F32),
        V((Z, HDIM, S), BF16), V((H, HDIM, S), BF16), V((Z, 3, HDIM, S), BF16),
        V((4, HALVES, T, part // HALVES, D), BF16), V((H, HDIM, D), BF16), V((H, HDIM, D), BF16), V((Z - 1, HDIM, D), BF16),
        V((2, 2, part, D), BF16), V((2, part, D), BF16),
        V((Z, S, HDIM), BF16), V((Z, S, HDIM), BF16),
        V((Z, HDIM, S), F32), V((Z, HDIM, S), F32), V((Z, HDIM, S), F32),
        V((3 * HDIM, D), BF16), V((3 * HDIM, D), BF16), V((Z, 4 * HDIM, D), BF16),
        V((8, 128), F32), V((8, 128), F32), V((Z, 8, 128), F32),
        V((2, 2, D), F32), V((T + Z - 2, 2, 2, D), F32), V((2, 4, D), F32), V((4, D), F32),
        V((D, Z * S), BF16), V((CHUNK, Z * S), BF16), V((Z * S, CHUNK), BF16), V((Z * S, CHUNK), BF16),
        V((2, 2, D, CHUNK), BF16), V((2, CHUNK, D), BF16), V((2, D // 8, 2, units), BF16),
        DMA((2, 8)), DMA((8,)), DMA((COPIES,)), DMA((COPIES,)), DMA((2, chunks, 2)), DMA((2,)),
    ]
    return pl.pallas_call(
        functools.partial(relay_kernel, sizes),
        out_shape=out_shape,
        in_specs=[pl.BlockSpec(memory_space=pltpu.SMEM), vmem, vmem, vmem, vmem, vmem, hbm, hbm, hbm, hbm],
        out_specs=(vmem, vmem, vmem, hbm, hbm, hbm),
        scratch_shapes=scratch,
        compiler_params=pltpu.CompilerParams(collective_id=0, has_side_effects=True, vmem_limit_bytes=62 * 2**20),
        name="relay",
    )(lengths, acts, cot, qs, us, al, wp, wo, we, wr)


def finish_kernel(
    attn_ref, ge_ref, gr_ref, lo_in, ig_in, small_ref,
    projection_ref, output_ref, expansion_ref, reduction_ref, lo_ref, ig_ref, scale_ref, units_ref, alphas_ref,
):
    @pl.when(pl.program_id(0) == 0)
    def _():
        lo_ref[...] = lo_in[...]
        ig_ref[...] = ig_in[...]
        alphas_ref[...] = small_ref[0:2]
        units_ref[...] = small_ref[2:4, : units_ref.shape[1]]
        scale_ref[...] = small_ref[4:5, : scale_ref.shape[1]]

    places, chunks = attn_ref.shape[0], ge_ref.shape[1]
    for begin in range(0, ge_ref.shape[3], 16):
        rows = slice(begin, begin + 16)
        pieces = []
        for chunk in range(chunks):
            for lanes in (slice(0, 128), slice(128, 256)):
                for side in range(2):
                    total = ge_ref[0, chunk, side, rows, lanes].astype(F32) + ge_ref[1, chunk, side, rows, lanes].astype(F32)
                    pieces.append(total[None])
        expansion_ref[rows] = jnp.swapaxes(jnp.concatenate(pieces, axis=0), 0, 1)
    reduction_ref[...] = gr_ref[0].astype(F32) + gr_ref[1].astype(F32)
    for third in range(3):
        rows = attn_ref[:, third * HDIM : (third + 1) * HDIM, :].astype(F32)
        projection_ref[third] = rows.reshape(places * HDIM, rows.shape[2]).T
    output_ref[...] = attn_ref[:, 3 * HDIM :, :].astype(F32).reshape(output_ref.shape)


def finish(attn, ge, gr, lo, ig, small):
    places, _, D = attn.shape
    chunks, units, inner = ge.shape[1], ge.shape[1] * CHUNK, places * HDIM
    block = 256
    steps = D // block
    rows = units // steps

    def whole(shape):
        return pl.BlockSpec(shape, lambda i: (0,) * len(shape))

    return pl.pallas_call(
        finish_kernel,
        grid=(steps,),
        in_specs=[
            pl.BlockSpec((places, 4 * HDIM, block), lambda i: (0, 0, i)),
            pl.BlockSpec((2, chunks, 2, block, CHUNK), lambda i: (0, 0, 0, i, 0)),
            pl.BlockSpec((2, rows, D), lambda i: (0, i, 0)),
            whole(lo.shape),
            whole(ig.shape),
            whole(small.shape),
        ],
        out_specs=(
            pl.BlockSpec((3, block, inner), lambda i: (0, i, 0)),
            pl.BlockSpec((inner, block), lambda i: (0, i)),
            pl.BlockSpec((block, units // 64, 128), lambda i: (i, 0, 0)),
            pl.BlockSpec((rows, D), lambda i: (i, 0)),
            whole(lo.shape),
            whole(ig.shape),
            whole((1, inner)),
            whole((2, units)),
            whole((2, D)),
        ),
        out_shape=(
            jax.ShapeDtypeStruct((3, D, inner), F32),
            jax.ShapeDtypeStruct((inner, D), F32),
            jax.ShapeDtypeStruct((D, units // 64, 128), F32),
            jax.ShapeDtypeStruct((units, D), F32),
            jax.ShapeDtypeStruct(lo.shape, BF16),
            jax.ShapeDtypeStruct(ig.shape, BF16),
            jax.ShapeDtypeStruct((1, inner), F32),
            jax.ShapeDtypeStruct((2, units), F32),
            jax.ShapeDtypeStruct((2, D), F32),
        ),
        compiler_params=pltpu.CompilerParams(vmem_limit_bytes=60 * 2**20),
        name="finish",
    )(attn, ge, gr.reshape(2, units, D), lo, ig, small)


def fast_body(
    activations, lengths, projection, output_weight, expansion, reduction, query_scale, unit_scales, alphas, cotangent
):
    _, _, part, width = activations.shape
    inner, units = output_weight.shape[1], reduction.shape[1]
    places = lax.axis_size("dp")
    sizes = Sizes(lax.axis_size("tensor"), places, part, width, inner, units)
    lo, ig, small, attn, ge, gr = relay(
        sizes, lengths, activations, cotangent, query_scale, unit_scales[0], alphas[0],
        projection[0].transpose(1, 0, 2), output_weight[0], expansion[0], reduction[0],
    )
    projection_grad, output_grad, expansion_grad, reduction_grad, lo, ig, scale_grad, unit_grad, alpha_grad = finish(
        attn, ge, gr, lo, ig, small
    )
    columns = units // 128
    expansion_grad = expansion_grad.reshape(width, columns, 2, 128).transpose(0, 2, 1, 3).reshape(width, 2, units)
    projection_grad = projection_grad.transpose(1, 0, 2)
    return (
        lo[None, :, None],
        ig[None, :, None],
        projection_grad[None],
        output_grad[None],
        expansion_grad[None],
        reduction_grad[None],
        scale_grad,
        unit_grad[None],
        alpha_grad[None],
    )


def solution(mesh):
    in_specs = (
        P(None, None, ("dp", "tensor"), None),
        P(),
        P("section", None, None, "tensor"),
        P("section", "tensor", None),
        P("section", None, None, "tensor"),
        P("section", "tensor", None),
        P("section", "tensor"),
        P("section", None, "tensor"),
        P("section", None, None),
        P(None, None, ("dp", "tensor"), None),
    )
    out_specs = (
        P("section", None, None, ("dp", "tensor"), None),
        P("section", None, None, ("dp", "tensor"), None),
        P("section", None, None, "tensor"),
        P("section", "tensor", None),
        P("section", None, None, "tensor"),
        P("section", "tensor", None),
        P("section", "tensor"),
        P("section", None, "tensor"),
        P("section", None, None),
    )
    def chosen(*arrays):
        activations, output_weight = arrays[0], arrays[3]
        heads = output_weight.shape[1] // HDIM
        fits = (
            mesh.shape["section"] == 2
            and mesh.shape["tensor"] == 4
            and mesh.shape["dp"] == heads
            and activations.shape[:2] == (2, 1)
            and activations.shape[2] * mesh.shape["tensor"] == 256
        )
        return (fast_body if fits else body)(*arrays)

    return jax.shard_map(chosen, mesh=mesh, in_specs=in_specs, out_specs=out_specs, check_vma=False)
```

```python
import functools
import math

import jax
import jax.numpy as jnp
from jax import lax
from jax.experimental import pallas as pl
from jax.experimental.pallas import tpu as pltpu
from jax.sharding import PartitionSpec as P

HDIM = 64


def from_behind(value, axis, steps):
    count = lax.axis_size(axis)
    initial, last = (max(0, -steps), min(count, count - steps))
    return lax.ppermute(value, axis, [(source, source + steps) for source in range(initial, last)])


def normed(v):
    return v * lax.rsqrt(jnp.mean(v * v, axis=-1, keepdims=True) + 1e-06)


def unit_heads(v):
    return v * lax.rsqrt(jnp.sum(v * v, axis=-1, keepdims=True) + 1e-06)


def frequencies(half):
    return jnp.exp(jnp.arange(half, dtype=jnp.float32) * (-2.0 * math.log(10000.0) / (2 * half)))


def rotate(view, angle):
    half = view.shape[-1] // 2
    cosine = jnp.cos(angle)[..., None, :]
    sine = jnp.sin(angle)[..., None, :]
    front = view[..., :half]
    back = view[..., half:]
    return jnp.concatenate([front * cosine - back * sine, back * cosine + front * sine], axis=-1)


def shaped(projected, scale, angle, heads):
    inner = projected.shape[-1] // 3
    lead = projected.shape[:-1]

    def turned(piece):
        view = piece.reshape(lead + (heads, inner // heads))
        return unit_heads(rotate(view, angle)).reshape(lead + (inner,)) * scale

    return (
        turned(projected[..., :inner]),
        turned(projected[..., inner : 2 * inner]),
        projected[..., 2 * inner :],
    )


def layout(lengths_row, slots):
    ends = jnp.cumsum(lengths_row, dtype=jnp.int32)
    index = jnp.arange(slots, dtype=jnp.int32)
    after = index[:, None] >= ends[None, :]
    segment = jnp.sum(after.astype(jnp.int32), axis=1, dtype=jnp.int32)
    begin = jnp.sum(jnp.where(after, lengths_row[None, :], 0), axis=1, dtype=jnp.int32)
    inside = index < ends[-1]
    segment = jnp.where(inside, segment, lengths_row.shape[0] + index)
    position = jnp.where(inside, index - begin, 0)
    return (segment, position)


def blend(base, branch, alpha):
    return normed(base + alpha * (normed(branch) - base))


def activate(expanded, scales):
    half = expanded.shape[-1] // 2
    return expanded[..., :half] * scales[0] * jax.nn.silu(expanded[..., half:] * scales[1])


def placing(lengths_now, local):
    slots = local * lax.axis_size("dp")
    start_here = lax.axis_index("dp") * local
    segment_all, position_all = jax.vmap(lambda row: layout(row, slots))(lengths_now)
    segment_here = lax.dynamic_slice_in_dim(segment_all, start_here, local, 1)
    position_here = lax.dynamic_slice_in_dim(position_all, start_here, local, 1)
    index_here = start_here + jnp.arange(local, dtype=jnp.int32)
    every = jnp.arange(slots, dtype=jnp.int32)
    allowed = (segment_here[:, :, None] == segment_all[:, None, :]) & (
        every[None, None, :] <= index_here[None, :, None]
    )
    angle = position_here.astype(jnp.float32)[..., None] * frequencies(HDIM // 2)
    return (allowed, angle)


def scored(query, key_all, allowed, heads):
    rows, local, inner = query.shape
    depth = inner // heads
    query_heads = query.reshape(rows, local, heads, depth)
    key_heads = key_all.reshape(rows, key_all.shape[1], heads, depth)
    raw = jnp.einsum(
        "rqhe,rkhe->rhqk", query_heads, key_heads, preferred_element_type=jnp.float32
    ) * math.sqrt(depth)
    return jnp.where(allowed[:, None], raw, -1e30)


def forward(stream, lengths_now, weights):
    projection, output_weight, expansion, reduction, query_scale, unit_scales, alphas = weights
    rows, part, width = stream.shape
    inner = output_weight.shape[0]
    heads = inner // HDIM
    hidden_width = reduction.shape[0]
    gathered = lax.all_gather(stream.astype(jnp.bfloat16), "tensor", axis=1, tiled=True)
    local = gathered.shape[1]
    allowed, angle = placing(lengths_now, local)
    projected = jnp.einsum(
        "rsd,dc->rsc",
        gathered,
        projection.reshape(width, 3 * inner),
        preferred_element_type=jnp.float32,
    )
    query, key, value = shaped(projected, query_scale, angle, heads)
    query_low = query.astype(jnp.bfloat16)
    key_low = key.astype(jnp.bfloat16)
    value_low = value.astype(jnp.bfloat16)
    key_all, value_all = (
        lax.all_gather(key_low, "dp", axis=1, tiled=True),
        lax.all_gather(value_low, "dp", axis=1, tiled=True),
    )
    scores = scored(query_low, key_all, allowed, heads)
    highest = jnp.max(scores, axis=-1, keepdims=True)
    lifted = jnp.exp(scores - highest)
    total = jnp.sum(lifted, axis=-1, keepdims=True)
    log_total = highest + jnp.log(total)
    probs_low = (lifted / total).astype(jnp.bfloat16)
    value_heads = value_all.reshape(rows, value_all.shape[1], heads, HDIM)
    mixed = jnp.einsum(
        "rhqk,rkhe->rqhe", probs_low, value_heads, preferred_element_type=jnp.float32
    )
    attended = mixed.reshape(rows, local, inner).astype(jnp.bfloat16)
    partial_branch = jnp.einsum(
        "rsc,cd->rsd", attended, output_weight, preferred_element_type=jnp.float32
    )
    branch = lax.psum_scatter(partial_branch, "tensor", scatter_dimension=1, tiled=True)
    middle = blend(stream, branch, alphas[0])
    middle_all = lax.all_gather(middle.astype(jnp.bfloat16), "tensor", axis=1, tiled=True)
    expanded = jnp.einsum(
        "rsd,dc->rsc",
        middle_all,
        expansion.reshape(width, 2 * hidden_width),
        preferred_element_type=jnp.float32,
    )
    hidden = activate(expanded, unit_scales).astype(jnp.bfloat16)
    partial_feed = jnp.einsum("rsf,fd->rsd", hidden, reduction, preferred_element_type=jnp.float32)
    feed = lax.psum_scatter(partial_feed, "tensor", scatter_dimension=1, tiled=True)
    result = blend(middle, feed, alphas[1])
    kept = dict(
        stream=stream,
        gathered=gathered,
        projected=projected,
        query=query_low,
        key=key_low,
        value=value_low,
        log_total=log_total,
        attended=attended,
        branch=branch,
        middle=middle,
        middle_all=middle_all,
        expanded=expanded,
        hidden=hidden,
        feed=feed,
        lengths=lengths_now,
    )
    kept = dict(kept, key_all=key_all, value_all=value_all)
    return (result, kept)


def backward(slope, kept, weights):
    projection, output_weight, expansion, reduction, query_scale, unit_scales, alphas = weights
    rows, part, width = slope.shape
    inner = output_weight.shape[0]
    heads = inner // HDIM
    hidden_width = reduction.shape[0]
    _, pull_feed = jax.vjp(blend, kept["middle"], kept["feed"], alphas[1])
    middle_slope, feed_slope, alpha_feed = pull_feed(slope)
    feed_all = lax.all_gather(feed_slope.astype(jnp.bfloat16), "tensor", axis=1, tiled=True)
    reduction_grad = jnp.einsum(
        "rsf,rsd->fd", kept["hidden"], feed_all, preferred_element_type=jnp.float32
    )
    hidden_slope = jnp.einsum(
        "rsd,fd->rsf", feed_all, reduction, preferred_element_type=jnp.float32
    )
    _, pull_active = jax.vjp(activate, kept["expanded"], unit_scales)
    expanded_slope, unit_grad = pull_active(hidden_slope)
    expanded_low = expanded_slope.astype(jnp.bfloat16)
    expansion_grad = jnp.einsum(
        "rsd,rsc->dc", kept["middle_all"], expanded_low, preferred_element_type=jnp.float32
    ).reshape(width, 2, hidden_width)
    partial_middle = jnp.einsum(
        "rsc,dc->rsd",
        expanded_low,
        expansion.reshape(width, 2 * hidden_width),
        preferred_element_type=jnp.float32,
    )
    middle_total = middle_slope + lax.psum_scatter(
        partial_middle, "tensor", scatter_dimension=1, tiled=True
    )
    _, pull_branch = jax.vjp(blend, kept["stream"], kept["branch"], alphas[0])
    stream_slope, branch_slope, alpha_branch = pull_branch(middle_total)
    branch_all = lax.all_gather(branch_slope.astype(jnp.bfloat16), "tensor", axis=1, tiled=True)
    output_grad = jnp.einsum(
        "rsc,rsd->cd", kept["attended"], branch_all, preferred_element_type=jnp.float32
    )
    attended_low = jnp.einsum(
        "rsd,cd->rsc", branch_all, output_weight, preferred_element_type=jnp.float32
    ).astype(jnp.bfloat16)
    local = attended_low.shape[1]
    key_all = kept["key_all"]
    value_all = kept["value_all"]
    slots = key_all.shape[1]
    allowed, angle = placing(kept["lengths"], local)
    scores = scored(kept["query"], key_all, allowed, heads)
    probs = jnp.exp(scores - kept["log_total"])
    scale = math.sqrt(HDIM)
    back_heads = attended_low.reshape(rows, local, heads, HDIM)
    query_heads = kept["query"].reshape(rows, local, heads, HDIM)
    key_heads = key_all.reshape(rows, slots, heads, HDIM)
    value_heads = value_all.reshape(rows, slots, heads, HDIM)
    probs_slope = jnp.einsum(
        "rqhe,rkhe->rhqk", back_heads, value_heads, preferred_element_type=jnp.float32
    )
    row_term = jnp.sum(probs * probs_slope, axis=-1, keepdims=True)
    scores_low = (probs * (probs_slope - row_term)).astype(jnp.bfloat16)
    query_slope = (
        jnp.einsum("rhqk,rkhe->rqhe", scores_low, key_heads, preferred_element_type=jnp.float32)
        * scale
    )
    value_grad_all = jnp.einsum(
        "rhqk,rqhe->rkhe",
        probs.astype(jnp.bfloat16),
        back_heads,
        preferred_element_type=jnp.float32,
    )
    key_grad_all = (
        jnp.einsum("rhqk,rqhe->rkhe", scores_low, query_heads, preferred_element_type=jnp.float32)
        * scale
    )
    key_slope, value_slope = (
        lax.psum_scatter(
            key_grad_all.reshape(rows, slots, inner), "dp", scatter_dimension=1, tiled=True
        ),
        lax.psum_scatter(
            value_grad_all.reshape(rows, slots, inner), "dp", scatter_dimension=1, tiled=True
        ),
    )
    _, pull_shape = jax.vjp(
        lambda source, scale_now: shaped(source, scale_now, angle, heads),
        kept["projected"],
        query_scale,
    )
    projected_slope, query_scale_grad = pull_shape(
        (query_slope.reshape(rows, local, inner), key_slope, value_slope)
    )
    projected_low = projected_slope.astype(jnp.bfloat16)
    projection_grad = jnp.einsum(
        "rsd,rsc->dc", kept["gathered"], projected_low, preferred_element_type=jnp.float32
    ).reshape(width, 3, inner)
    partial_stream = jnp.einsum(
        "rsc,dc->rsd",
        projected_low,
        projection.reshape(width, 3 * inner),
        preferred_element_type=jnp.float32,
    )
    spread = jnp.broadcast_to(
        jnp.stack([alpha_branch, alpha_feed])[:, None, :], (2, lax.axis_size("tensor"), width)
    )
    stream_part, alpha_sum = (
        lax.psum_scatter(partial_stream, "tensor", scatter_dimension=1, tiled=True),
        lax.psum_scatter(spread, "tensor", scatter_dimension=1, tiled=True),
    )
    stream_total = stream_slope + stream_part
    return (
        stream_total,
        (
            projection_grad,
            output_grad,
            expansion_grad,
            reduction_grad,
            query_scale_grad,
            unit_grad,
            alpha_sum[:, 0],
        ),
    )


def body(
    activations,
    lengths,
    projection,
    output_weight,
    expansion,
    reduction,
    query_scale,
    unit_scales,
    alphas,
    cotangent,
):
    micro, rows, part, width = activations.shape
    section = lax.axis_index("section")
    first = section == 0
    weights = (
        projection[0],
        output_weight[0],
        expansion[0],
        reduction[0],
        query_scale[0],
        unit_scales[0],
        alphas[0],
    )
    steps = micro + 1
    received = jnp.zeros((rows, part, width), jnp.bfloat16)
    outputs = []
    keeps = []
    for step in range(steps):
        index_now = jnp.clip(step - section, 0, micro - 1)
        lengths_now = lax.dynamic_index_in_dim(lengths, index_now, 0, keepdims=False)
        stream = jnp.where(first, activations[min(step, micro - 1)], received).astype(jnp.float32)
        result, kept = forward(stream, lengths_now, weights)
        result_low = result.astype(jnp.bfloat16)
        outputs.append(result_low)
        keeps.append(kept)
        if step + 1 < steps:
            received = from_behind(result_low, "section", 1)
    stacked = jnp.stack(outputs)
    layer_output = jnp.where(first, stacked[:micro], stacked[1:])[None]
    back_received = jnp.zeros((rows, part, width), jnp.bfloat16)
    slopes = []
    summed = None
    for step in range(steps):
        batch_now = step - 1 + section
        valid = (batch_now >= 0) & (batch_now < micro)
        slope = jnp.where(first, back_received, cotangent[min(step, micro - 1)]).astype(jnp.float32)
        earlier = keeps[max(step - 1, 0)]
        later = keeps[min(step + 1, micro)]
        kept = jax.tree.map(lambda left, right: jnp.where(first, left, right), earlier, later)
        stream_total, layer_grads = backward(slope, kept, weights)
        stream_low = stream_total.astype(jnp.bfloat16)
        slopes.append(stream_low)
        masked = tuple((jnp.where(valid, piece, 0.0) for piece in layer_grads))
        summed = (
            masked
            if summed is None
            else tuple((left + right for left, right in zip(summed, masked)))
        )
        if step + 1 < steps:
            back_received = from_behind(stream_low, "section", -1)
    stacked_slopes = jnp.stack(slopes)
    input_gradient = jnp.where(first, stacked_slopes[1:], stacked_slopes[:micro])[None]
    (
        projection_grad,
        output_grad,
        expansion_grad,
        reduction_grad,
        query_scale_grad,
        unit_grad,
        alpha_grad,
    ) = summed
    totals = lax.psum(
        (
            projection_grad,
            output_grad,
            expansion_grad,
            reduction_grad,
            query_scale_grad,
            unit_grad,
            alpha_grad,
        ),
        "dp",
    )
    return (
        layer_output,
        input_gradient,
        totals[0][None],
        totals[1][None],
        totals[2][None],
        totals[3][None],
        totals[4][None],
        totals[5][None],
        totals[6][None],
    )


MESH_IDS = pl.DeviceIdType.MESH
F32, BF16 = jnp.float32, jnp.bfloat16
CHUNK = 256
NN = ((1,), (0,))
NT = ((1,), (1,))


def dot(left, right, dims):
    return lax.dot_general(left, right, (dims, ((), ())), preferred_element_type=F32)


def norm_parts(v):
    rate = lax.rsqrt(jnp.mean(v * v, axis=-1, keepdims=True) + 1e-06)
    return v * rate, rate


def norm_back(slope, unit, rate):
    return rate * (slope - unit * jnp.mean(unit * slope, axis=-1, keepdims=True))


def blend_back(slope, base, branch, alpha):
    unit_branch, rate_branch = norm_parts(branch)
    toward = unit_branch - base
    unit, rate = norm_parts(base + alpha * toward)
    inner_slope = norm_back(slope, unit, rate)
    alpha_slope = jnp.sum(inner_slope * toward, axis=0, keepdims=True)
    scaled = alpha * inner_slope
    return inner_slope - scaled, norm_back(scaled, unit_branch, rate_branch), alpha_slope


def sequence_starts(lengths_ref, row, index):
    begin = jnp.zeros_like(index)
    end = jnp.int32(0)
    for sequence in range(lengths_ref.shape[2]):
        end = end + lengths_ref[row, 0, sequence]
        begin = jnp.where(index >= end, end, begin)
    return jnp.where(index < end, begin, index)


class Sizes:
    def __init__(self, tensors, places, part, width, inner, units):
        self.tensors, self.places, self.part, self.width = tensors, places, part, width
        self.inner, self.units = inner, units
        self.local = part * tensors
        self.heads = inner // HDIM


class Slots:
    def __init__(self, send, recv):
        self.send, self.recv, self.names = send, recv, {}

    def copy(self, name, source, target, device):
        number = self.names.setdefault(name, len(self.names))
        return pltpu.make_async_remote_copy(
            source, target, self.send.at[number], self.recv.at[number], device_id=device, device_id_type=MESH_IDS
        )


HALVES = 2
COPIES = 199


def relay_kernel(
    sizes,
    lengths_ref, acts_ref, cot_ref, qs_ref, us_ref, al_ref, wp_ref, wo_ref, we_ref, wr_ref,
    lo_ref, ig_ref, small_ref, attn_ref, ge_ref, gr_ref,
    wp, wo, we, wr, qs, us, al,
    stream, middles, feed_low, branch_low,
    cosines, sines, scales,
    heads_in, rates_in, probs, mixed_in, sums_in, branch_f, middle_f, feed_f, ups, gates,
    hidden, expanded_low, back_in, heads_back_in,
    heads_out, rates_out, mixed_out, back_out, heads_back_out, sums_out, go_out, go_sib, go_in,
    outs, outs_in, key_rows, value_rows, query_grad, key_grad, value_grad,
    attn_own, attn_sib, attn_all, scale_own, scale_sib, scale_all,
    alpha_own, alpha_in, finals, finals_in,
    middle_cols, hidden_part, up_part, gate_part, stage_e, stage_r, raw,
    weight_sem, weight_send, send_sem, recv_sem, stage_sem, raw_sem,
):
    T, Z, S, part = sizes.tensors, sizes.places, sizes.local, sizes.part
    H, inner, units, D = sizes.heads, sizes.inner, sizes.units, sizes.width
    core, t, z = lax.axis_index("section"), lax.axis_index("tensor"), lax.axis_index("dp")
    sibling = (1 - core, t, z)
    side, row = lax.rem(t, 2), t // 2
    tensor_peers = [row * 2 + (1 - side), (1 - row) * 2 + side, (1 - row) * 2 + (1 - side)]
    place_peers = [lax.rem(z + k, Z) for k in range(1, Z)]
    tensor_ids = [(core, peer, z) for peer in tensor_peers]
    place_ids = [(core, t, peer) for peer in place_peers]
    slots = Slots(send_sem, recv_sem)
    pending = [[]]

    weights = [
        (wp_ref, lambda layer: wp.at[layer]),
        (wo_ref, lambda layer: wo.at[layer]),
        (we.at[core, 0], lambda layer: we.at[layer, 0]),
        (we.at[core, 1], lambda layer: we.at[layer, 1]),
        (wr_ref, lambda layer: wr.at[layer]),
        (qs_ref, lambda layer: qs.at[layer]),
        (us_ref, lambda layer: us.at[layer]),
        (al_ref, lambda layer: al.at[layer]),
    ]

    def weight_load(layer, piece):
        source, target = weights[piece]
        return pltpu.make_async_copy(source, target(layer), weight_sem.at[layer, piece])

    for piece in range(len(weights)):
        if piece not in (2, 3):
            weight_load(core, piece).start()

    raw_rows = raw.shape[1]

    def raw_load(block):
        return pltpu.make_async_copy(we_ref.at[pl.ds(block * raw_rows, raw_rows)], raw.at[block % 2], raw_sem.at[block % 2])

    for block in range(2):
        raw_load(block).start()

    def take_apart(blocks):
        for block in blocks:
            raw_load(block).wait()
            we[core, :, block * raw_rows : (block + 1) * raw_rows, :] = jnp.swapaxes(raw[block % 2], 0, 1)
            if (block + 2) * raw_rows < D:
                raw_load(block + 2).start()

    barrier = pltpu.get_barrier_semaphore()
    partners = [sibling] + tensor_ids + place_ids
    for partner in partners:
        pl.semaphore_signal(barrier, inc=1, device_id=partner, device_id_type=MESH_IDS)
    turn = HDIM // 2
    index_all = lax.broadcasted_iota(jnp.int32, (1, S * Z), 1)
    starts = sequence_starts(lengths_ref, core, index_all)
    rates = jnp.exp(lax.broadcasted_iota(jnp.int32, (turn, 1), 0).astype(F32) * (-2.0 * math.log(10000.0) / HDIM))
    angle = rates * (index_all - starts).astype(F32)
    cosine, sine = jnp.cos(angle), jnp.sin(angle)
    for place in range(Z):
        cosines[place] = cosine[:, place * S : (place + 1) * S]
        sines[place] = sine[:, place * S : (place + 1) * S]
    key_index = lax.broadcasted_iota(jnp.int32, (S * Z, S), 0)
    pl.semaphore_wait(barrier, len(partners))

    def weight_copy(piece):
        source, target = weights[piece]
        return pltpu.make_async_remote_copy(
            source, target(core), weight_send.at[piece], weight_sem.at[core, piece], device_id=sibling, device_id_type=MESH_IDS
        )

    def lend_weights(layer, pieces):
        @pl.when(core == layer)
        def _():
            for piece in pieces:
                weight_copy(piece).start()

    for piece in (5, 6, 7):
        weight_copy(piece).start()
    lend_weights(0, (0,))

    def await_weight(layer, piece):
        if piece in (2, 3):
            @pl.when(core != layer)
            def _():
                weight_load(layer, piece).wait()
        else:
            weight_load(layer, piece).wait()

    def send(name, source, target, device):
        copy = slots.copy(name, source, target, device)
        copy.start()
        pending[-1].append(copy)
        return copy

    def settle(keep=4):
        pending.append([])
        while len(pending) > keep:
            for copy in pending.pop(0):
                copy.wait_send()

    def arrive(copies):
        for copy in copies:
            copy.wait_recv()

    def rows_of(index):
        return pl.ds(pl.multiple_of(index * part, part), part)

    my_rows, far_rows = rows_of(t), rows_of(tensor_peers[2])

    def gather(name, target, half, value):
        count = value.shape[0]
        rows = pl.ds(pl.multiple_of(t * part + half * count, count), count)
        target[rows, :] = value
        mine = target.at[rows, :]
        return [send((name, half, k), mine, mine, device) for k, device in enumerate(tensor_ids)]

    def half_of(target, half):
        return jnp.concatenate([target[index * part + half * count : index * part + (half + 1) * count, :] for index in range(T)], axis=0)

    count = part // HALVES
    halves = range(HALVES)

    def piece_of(half):
        return slice(half * count, (half + 1) * count)

    class Line:
        def __init__(self, name, views, guard=None, passes=0):
            self.name, self.views, self.guard, self.passes = name, views, guard, passes

        def copies(self, way, step, origin):
            device = (core, t, z + 1) if way == 0 else (core, t, z - 1)
            return [slots.copy((self.name, way, step, k), view, view, device) for k, view in enumerate(self.views(origin))]

        def when(self, condition):
            return pl.when(condition if self.guard is None else condition & self.guard)

        def origin(self, way, step):
            return z - step if way == 0 else z + step

        def sends(self, way, step):
            return (z >= step) & (z + 1 < Z) if way == 0 else (z + step < Z) & (z >= 1)

        def comes(self, way, step):
            return z >= step if way == 0 else z + step < Z

        def passing(self, way, step):
            got = self.views(self.origin(way, step))[0]
            return [slots.copy((self.name, "pass", way, step, k), got, got, tensor_ids[k]) for k in range(self.passes)]

        def passed(self):
            for way in range(2):
                for step in range(1, Z):
                    @self.when(self.comes(way, step))
                    def _():
                        for copy in self.passing(way, step):
                            copy.wait_recv()

        def step(self, step):
            for way in range(2):
                if step > 0:
                    @self.when(self.comes(way, step))
                    def _():
                        for copy in self.copies(way, step - 1, self.origin(way, step)):
                            copy.wait_recv()
                        for copy in self.passing(way, step):
                            copy.start()

                if step < Z - 1:
                    @self.when(self.sends(way, step))
                    def _():
                        for copy in self.copies(way, step, self.origin(way, step)):
                            copy.start()

        def finish(self):
            for way in range(2):
                for step in range(Z - 1):
                    @self.when(self.sends(way, step))
                    def _():
                        for copy in self.copies(way, step, self.origin(way, step)):
                            copy.wait_send()

                    @self.when(self.comes(way, step + 1))
                    def _():
                        for copy in self.passing(way, step + 1):
                            copy.wait_send()

    def row_line(name, layer, target, groups, passes=0):
        return Line((name, len(groups)), lambda place: [target.at[layer, place, rows, :] for rows in groups], None, passes)

    def pass_on(name, layer, target, count=2, indices=range(Z - 1)):
        passed = []
        for index in indices:
            got = target.at[layer, place_peers[index], my_rows, :]
            passed += [send((name, "pass", index, k), got, got, device) for k, device in enumerate(tensor_ids[:count])]
        return passed

    def scatter(number, half):
        return [
            send((number, half, k), sums_out.at[number, half, peer], sums_in.at[number, half, k], device)
            for k, (peer, device) in enumerate(zip(tensor_peers, tensor_ids))
        ]

    def scattered(number, half, copies):
        arrive(copies)
        total = sums_out[number, half, t].astype(F32)
        for k in range(T - 1):
            total = total + sums_in[number, half, k].astype(F32)
        return total

    def retire(copies):
        for copy in copies:
            for group in pending:
                if any(copy is other for other in group):
                    copy.wait_send()
                    group[:] = [other for other in group if other is not copy]

    def spread(name, source, target):
        target[z] = source[z]
        return [
            send((name, k), source.at[peer], target.at[z], device) for k, (peer, device) in enumerate(zip(place_peers, place_ids))
        ]

    def block(query, key):
        return query * (query + 1) // 2 + key

    used, waiting = {}, {}
    first_line = row_line("first line", 0, stream, [my_rows])
    stream_lines = [row_line("stream line", 0, stream, [far_rows]), row_line("stream line", 1, stream, [my_rows, far_rows])]
    middle_lines = [row_line("middle line", layer, middles, [my_rows, far_rows]) for layer in range(2)]
    feed_lines = [row_line("feed line", layer, feed_low, [my_rows, far_rows][: layer + 1], 3 - layer) for layer in range(2)]

    def free(name):
        retire(used.pop(name, []))

    first_stream = gather("stream", stream.at[0, z], 0, acts_ref[core, 0])
    first_line.step(0)

    def forward(layer, base_low, stream_copies, then):
        if layer == 0:
            take_apart(range(0, D // raw_rows // 2))
        await_weight(layer, 0)
        for piece in (5, 6, 7):
            await_weight(layer, piece)
        scale = jnp.broadcast_to(jnp.broadcast_to(qs[layer], (8, inner)).T[:, :1], (inner, 128)).reshape(H, HDIM, 128)
        scales[layer] = scale
        cosine_here, sine_here = cosines[z][None], sines[z][None]
        arrive(stream_copies)
        if layer == 0:
            first_line.step(1)
        free("heads")
        gathered = stream[layer, z]
        for third in range(3):
            piece = dot(gathered, wp[layer, third], NN).T.reshape(H, HDIM, S)
            if third < 2:
                front, back = piece[:, :turn], piece[:, turn:]
                piece = jnp.concatenate([front * cosine_here - back * sine_here, back * cosine_here + front * sine_here], axis=1)
                speed = lax.rsqrt(jnp.sum(piece * piece, axis=1, keepdims=True) + 1e-06)
                piece = piece * speed * scale[:, :, :1]
                for head in range(H):
                    rates_out[head, third : third + 1] = speed[head]
            heads_out[:, third] = piece.astype(BF16)
        copies = spread("heads", heads_out, heads_in.at[layer])
        rate_copies = spread("rates", rates_out, rates_in.at[layer])
        used["heads"] = copies + rate_copies
        if layer == 0:
            first_line.step(2)
            stream_lines[0].step(0)
            take_apart(range(D // raw_rows // 2, D // raw_rows))
        else:
            middle_lines[0].step(2)
        lend_weights(layer, (1, 2))
        settle()
        if layer:
            first_line.step(3)
            waiting["stream", 0] = pass_on("stream", 0, stream)
        arrive(copies + rate_copies)
        if layer:
            middle_lines[0].step(3)
            waiting["middle", 0] = pass_on("middle", 0, middles)
        for place in range(Z):
            key_rows[place] = heads_in[layer, place, 1].T
        free("mixed")
        for query in range(Z):
            raw = [dot(key_rows[key], heads_in[layer, query, 0], NN) * math.sqrt(HDIM) for key in range(query + 1)]
            first = starts[:, query * S : (query + 1) * S]
            last = index_all[:, query * S : (query + 1) * S]
            scores = []
            for key in range(query + 1):
                keys = key_index[key * S : (key + 1) * S]
                allowed = keys >= first
                if key == query:
                    allowed = allowed & (keys <= last)
                scores.append(jnp.where(allowed, raw[key], -1e30))
            highest = scores[0].max(axis=0, keepdims=True)
            for piece in scores[1:]:
                highest = jnp.maximum(highest, piece.max(axis=0, keepdims=True))
            lifted = [jnp.exp(piece - highest) for piece in scores]
            total = lifted[0].sum(axis=0, keepdims=True)
            for piece in lifted[1:]:
                total = total + piece.sum(axis=0, keepdims=True)
            shrink = 1.0 / total
            mixed = None
            for key in range(query + 1):
                low = (lifted[key] * shrink).astype(BF16)
                probs[layer, block(query, key)] = low
                term = dot(heads_in[layer, key, 2], low, NN)
                mixed = term if mixed is None else mixed + term
            mixed_out[query] = mixed.astype(BF16)
        copies = spread("mixed", mixed_out, mixed_in.at[layer])
        used["mixed"] = copies
        if layer == 0:
            stream_lines[0].step(1)
        settle()
        if layer:
            first_line.finish()
            stream_lines[0].step(3)
            stream_lines[0].finish()
            middle_lines[0].finish()
        await_weight(layer, 1)
        arrive(copies)
        attended = mixed_in[layer].reshape(inner, S).T
        free("branch")
        partial = dot(attended, wo[layer], NN).astype(BF16).reshape(T, HALVES, count, D)
        branch_copies = []
        for half in halves:
            sums_out[0, half] = partial[:, half]
            branch_copies.append(scatter(0, half))
        used["branch"] = sum(branch_copies, [])
        if layer:
            stream_lines[1].step(0)
        else:
            stream_lines[0].step(2)
        lend_weights(layer, (3,))
        settle()
        alpha = al[layer]
        middle_copies = []
        for half in halves:
            branch = scattered(0, half, branch_copies[half])
            base = base_low[piece_of(half)].astype(F32)
            middle = norm_parts(base + alpha[0:1] * (norm_parts(branch)[0] - base))[0]
            middle_copies.append(gather("middle", middles.at[layer, z], half, middle.astype(BF16)))
            branch_f[layer, piece_of(half)] = branch
            middle_f[layer, piece_of(half)] = middle
        if layer:
            stream_lines[1].step(1)
        lend_weights(layer, (4,))
        settle()
        if layer:
            arrive(waiting["stream", 0] + waiting["middle", 0])
        free("feed")
        for piece in (2, 3):
            await_weight(layer, piece)
        feed_copies = []
        for half in halves:
            arrive(middle_copies[half])
            middle_all = half_of(middles.at[layer, z], half)
            for begin in range(0, units, CHUNK):
                cols = slice(begin, begin + CHUNK)
                up = dot(middle_all, we[layer, 0, :, cols], NN)
                gate = dot(middle_all, we[layer, 1, :, cols], NN)
                ups[layer, half, :, cols] = up.astype(BF16)
                gates[layer, half, :, cols] = gate.astype(BF16)
                inside = us[layer, 1:2, cols] * gate
                hidden[:, cols] = (us[layer, 0:1, cols] * up * (inside / (1.0 + jnp.exp(-inside)))).astype(BF16)
            if half == 0:
                await_weight(layer, 4)
            acted = hidden[...]
            for begin in range(0, D, CHUNK):
                cols = slice(begin, begin + CHUNK)
                sums_out[1, half, :, :, cols] = dot(acted, wr[layer, :, cols], NN).astype(BF16).reshape(T, count, CHUNK)
            feed_copies.append(scatter(1, half))
        used["feed"] = sum(feed_copies, [])
        if layer:
            stream_lines[1].step(2)
        middle_lines[layer].step(0)
        settle()
        for half in halves:
            feed = scattered(1, half, feed_copies[half])
            feed_f[layer, piece_of(half)] = feed
            middle = middle_f[layer, piece_of(half)]
            result = norm_parts(middle + alpha[1:2] * (norm_parts(feed)[0] - middle))[0].astype(BF16)
            outs[0, layer, piece_of(half)] = result
            then(half, result)
        if layer == 0:
            middle_lines[0].step(1)
            lend_weights(1, (0,))

    def act_back(layer, cols, up, gate, slope_hidden):
        scale_up, scale_gate = us[layer, 0:1, cols], us[layer, 1:2, cols]
        inside = scale_gate * gate
        sigmoid = 1.0 / (1.0 + jnp.exp(-inside))
        silu = inside * sigmoid
        by_up = silu * slope_hidden
        by_gate = scale_up * up * (sigmoid + silu * (1.0 - sigmoid)) * slope_hidden
        return silu, by_up, by_gate

    def stage_copy(layer, chunk, which):
        buffer = (stage_e, stage_r)[which].at[chunk % 2]
        target = (ge_ref.at[0, chunk], gr_ref.at[0, chunk])[which]
        return pltpu.make_async_copy(buffer, target, stage_sem.at[layer, chunk, which])

    def stage_send(layer, chunk, which):
        buffer = (stage_e, stage_r)[which].at[chunk % 2]
        target = (ge_ref.at[1, chunk], gr_ref.at[1, chunk])[which]
        return slots.copy(("stage", chunk, which), buffer, target, sibling)

    def stage_wait(layer, chunk):
        @pl.when(core == layer)
        def _():
            for which in range(2):
                stage_copy(layer, chunk, which).wait()

        @pl.when(core != layer)
        def _():
            for which in range(2):
                stage_send(layer, chunk, which).wait_send()

    def feed_ahead():
        @pl.when(core == 1)
        def _():
            for piece in (2, 3):
                weight_copy(piece).wait_send()

        for place in range(Z):
            rows = slice(place * S, (place + 1) * S)
            for begin in range(0, units, CHUNK):
                cols = slice(begin, begin + CHUNK)
                for side in range(2):
                    we[1, side, rows, cols] = dot(middles[0, place], we[0, side, :, cols], NN).astype(BF16)

    staged = []

    def feed_grads(layer, chunk):
        if chunk == 0:
            for place in range(Z):
                middle_cols[:, place * S : (place + 1) * S] = middles[layer, place].T
        cols = slice(chunk * CHUNK, (chunk + 1) * CHUNK)
        scale_up, scale_gate = us[layer, 0:1, cols], us[layer, 1:2, cols]
        sum_up = sum_gate = None
        for place in range(Z):
            rows = slice(place * S, (place + 1) * S)
            if layer:
                up = dot(middles[layer, place], we[layer, 0, :, cols], NN)
                gate = dot(middles[layer, place], we[layer, 1, :, cols], NN)
            else:
                up, gate = we[1, 0, rows, cols].astype(F32), we[1, 1, rows, cols].astype(F32)
            slope_hidden = dot(feed_low[layer, place], wr[layer, cols, :], NT)
            silu, by_up, by_gate = act_back(layer, cols, up, gate, slope_hidden)
            hidden_part[:, rows] = (scale_up * up * silu).astype(BF16).T
            up_part[rows] = (by_up * scale_up).astype(BF16)
            gate_part[rows] = (by_gate * scale_gate).astype(BF16)
            term_up = jnp.sum(by_up * up, axis=0, keepdims=True)
            term_gate = jnp.sum(by_gate * gate, axis=0, keepdims=True)
            sum_up = term_up if sum_up is None else sum_up + term_up
            sum_gate = term_gate if sum_gate is None else sum_gate + term_gate
        finals[layer, 2:3, cols] = sum_up
        finals[layer, 3:4, cols] = sum_gate
        if len(staged) >= 2:
            stage_wait(*staged[-2])
        buffer = chunk % 2
        stage_e[buffer, 0] = dot(middle_cols[...], up_part[...], NN).astype(BF16)
        stage_e[buffer, 1] = dot(middle_cols[...], gate_part[...], NN).astype(BF16)
        stage_r[buffer] = dot(hidden_part[...], feed_low[layer].reshape(Z * S, D), NN).astype(BF16)

        @pl.when(core == layer)
        def _():
            for which in range(2):
                stage_copy(layer, chunk, which).start()

        @pl.when(core != layer)
        def _():
            for which in range(2):
                stage_send(layer, chunk, which).start()

        staged.append((layer, chunk))

    chunks = units // CHUNK
    projected = 3 * HDIM
    def attn_pair():
        return [slots.copy("head", attn_own, attn_sib, sibling), slots.copy("scale", scale_own, scale_sib, sibling)]

    def go_pair():
        return [slots.copy("go", go_out, go_sib, sibling)]

    def go_spread():
        return [
            slots.copy(("go", k), go_out.at[peer], go_in.at[k], device) for k, (peer, device) in enumerate(zip(place_peers, place_ids))
        ]

    def offer(layer, pair):
        @pl.when(core != layer)
        def _():
            for copy in pair():
                copy.start()

    def go_join(layer):
        @pl.when(core == layer)
        def _():
            for copy in go_pair():
                copy.wait_recv()
            go_out[...] = (go_out[...].astype(F32) + go_sib[...].astype(F32)).astype(BF16)
            for copy in go_spread():
                copy.start()

        @pl.when(core != layer)
        def _():
            for copy in go_pair():
                copy.wait_send()

    attn_lines = [
        Line("heads line", lambda place: [attn_all.at[place, :projected], scale_all.at[place]], core == layer) for layer in range(2)
    ]
    go_lines = [Line("go line", lambda place: [attn_all.at[place, projected:]], core == layer) for layer in range(2)]

    def go_finish(layer):
        @pl.when(core == layer)
        def _():
            for copy in go_spread():
                copy.wait_recv()
            total = go_out[z].astype(F32)
            for k in range(Z - 1):
                total = total + go_in[k].astype(F32)
            attn_all[z, projected:] = total.astype(BF16)
            for copy in go_spread():
                copy.wait_send()

        go_lines[layer].step(0)

    def attn_join(layer):
        @pl.when(core == layer)
        def _():
            for copy in attn_pair():
                copy.wait_recv()
            attn_all[z, :projected] = (attn_own[...].astype(F32) + attn_sib[...].astype(F32)).astype(BF16)
            scale_all[z] = scale_own[...] + scale_sib[...]

        @pl.when(core != layer)
        def _():
            for copy in attn_pair():
                copy.wait_send()

        attn_lines[layer].step(0)

    def head_grads(layer, scale_slope):
        if layer:
            arrive(waiting["stream", 1])
        grad = None
        for place in range(Z):
            term = dot(heads_back_out[place].reshape(3 * HDIM, S), stream[layer, place], NN)
            grad = term if grad is None else grad + term
        attn_own[...] = grad.astype(BF16)
        scale_rows = jnp.broadcast_to(scale_slope, (HDIM, 128)).T[:8]
        scale_own[...] = jnp.concatenate([scale_rows, scale_rows], axis=1)
        offer(layer, attn_pair)

    def enter(layer, half, slope):
        rows = piece_of(half)
        middle_slope, feed_slope, alpha_m = blend_back(slope, middle_f[layer, rows], feed_f[layer, rows], al[layer, 1:2])
        copies = gather("feed_low", feed_low.at[layer, z], half, feed_slope.astype(BF16))
        return middle_slope, alpha_m, copies

    def backward(layer, base_low, entered, then):
        alpha = al[layer]
        alpha_own[layer, 1:2] = entered[0][1] + entered[1][1]
        if layer:
            stream_lines[1].step(3)
            waiting["stream", 1] = pass_on("stream", 1, stream, 2, [0])
        else:
            feed_lines[1].step(3)
        settle()
        if layer == 0:
            attn_join(1)
            go_finish(1)
        free("middle_back")
        back_copies = []
        for half in halves:
            arrive(entered[half][2])
            feed_all = half_of(feed_low.at[layer, z], half)
            for begin in range(0, units, CHUNK):
                cols = slice(begin, begin + CHUNK)
                slope_hidden = dot(feed_all, wr[layer, cols, :], NT)
                up, gate = ups[layer, half, :, cols].astype(F32), gates[layer, half, :, cols].astype(F32)
                _, by_up, by_gate = act_back(layer, cols, up, gate, slope_hidden)
                expanded_low[0, :, cols] = (by_up * us[layer, 0:1, cols]).astype(BF16)
                expanded_low[1, :, cols] = (by_gate * us[layer, 1:2, cols]).astype(BF16)
            for begin in range(0, D, CHUNK):
                rows = slice(begin, begin + CHUNK)
                partial = dot(expanded_low[0], we[layer, 0, rows, :], NT) + dot(expanded_low[1], we[layer, 1, rows, :], NT)
                sums_out[2, half, :, :, rows] = partial.astype(BF16).reshape(T, count, CHUNK)
            back_copies.append(scatter(2, half))
        used["middle_back"] = sum(back_copies, [])
        if layer:
            waiting["stream", 1] += pass_on("stream", 1, stream, 2, [1])
            middle_lines[1].step(1)
        feed_lines[layer].step(0)
        settle()
        if layer == 0:
            attn_lines[1].step(1)
            go_lines[1].step(1)
            feed_lines[1].passed()
            arrive(waiting["middle", 1])
            feed_grads(1, 0)
        free("branch_low")
        branch_copies, stream_slopes, alpha_a = [], [], None
        for half in halves:
            middle_total = entered[half][0] + scattered(2, half, back_copies[half])
            stream_slope, branch_slope, term = blend_back(
                middle_total, base_low[piece_of(half)].astype(F32), branch_f[layer, piece_of(half)], alpha[0:1]
            )
            branch_copies.append(gather("branch_low", branch_low, half, branch_slope.astype(BF16)))
            stream_slopes.append(stream_slope)
            alpha_a = term if alpha_a is None else alpha_a + term
        copies = sum(branch_copies, [])
        used["branch_low"] = copies
        alpha_own[layer, 0:1] = alpha_a
        if layer:
            waiting["stream", 1] += pass_on("stream", 1, stream, 2, [2])
            middle_lines[1].step(2)
        else:
            alpha_copies = [send(("alpha", k), alpha_own, alpha_in.at[k], device) for k, device in enumerate(tensor_ids)]
            feed_lines[0].step(1)
            attn_lines[1].step(2)
            go_lines[1].step(2)
            feed_grads(1, 1)
        settle()
        arrive(copies)
        branch_all = branch_low[...]
        free("mixed_back")
        back_out[...] = dot(wo[layer], branch_all, NT).astype(BF16).reshape(H, HDIM, S)
        copies = spread("mixed_back", back_out, back_in)
        used["mixed_back"] = copies
        go_out[...] = dot(mixed_in[layer].reshape(inner, S), branch_all, NN).astype(BF16).reshape(H, HDIM, D)
        offer(layer, go_pair)
        if layer:
            feed_lines[1].step(1)
        else:
            feed_lines[0].step(2)
        if layer:
            middle_lines[1].step(3)
            waiting["middle", 1] = pass_on("middle", 1, middles)
        else:
            stream_lines[1].finish()
            middle_lines[1].finish()
        settle()
        if layer == 0:
            feed_grads(1, 2)
        for place in range(Z):
            value_rows[place] = heads_in[layer, place, 2].T
        arrive(copies)
        if layer == 0:
            go_join(0)
            feed_lines[0].step(3)
        for query in range(Z):
            slope_mixed = back_in[query]
            lows = [probs[layer, block(query, key)] for key in range(query + 1)]
            probs_slope = [dot(value_rows[key], slope_mixed, NN) for key in range(query + 1)]
            row_term = None
            for low, piece in zip(lows, probs_slope):
                term = jnp.sum(low.astype(F32) * piece, axis=0, keepdims=True)
                row_term = term if row_term is None else row_term + term
            query_slope = None
            for key in range(query + 1):
                low = lows[key]
                scores_low = (low.astype(F32) * (probs_slope[key] - row_term)).astype(BF16)
                term = dot(heads_in[layer, key, 1], scores_low, NN)
                query_slope = term if query_slope is None else query_slope + term
                key_term = dot(heads_in[layer, query, 0], scores_low, NT)
                value_term = dot(slope_mixed, low, NT)
                if key == query:
                    key_grad[key] = key_term
                    value_grad[key] = value_term
                else:
                    key_grad[key] += key_term
                    value_grad[key] += value_term
            query_grad[query] = query_slope
        free("heads_back")
        scale = scales[layer, z][:, :1]
        inverse = 1.0 / scale
        scale_slope = None
        for place in range(Z):
            cosine_there, sine_there = cosines[place], sines[place]
            for third, source in ((0, query_grad), (1, key_grad)):
                piece = source[place] * math.sqrt(HDIM)
                unit = heads_in[layer, place, third].astype(F32) * inverse
                term = jnp.sum(piece * unit, axis=1, keepdims=True)
                scale_slope = term if scale_slope is None else scale_slope + term
                piece = piece * scale
                piece = rates_in[layer, place, third : third + 1] * (piece - unit * jnp.sum(unit * piece, axis=0, keepdims=True))
                front, back = piece[:turn], piece[turn:]
                piece = jnp.concatenate([front * cosine_there + back * sine_there, back * cosine_there - front * sine_there], axis=0)
                heads_back_out[place, third] = piece.astype(BF16)
            heads_back_out[place, 2] = value_grad[place].astype(BF16)
        copies = spread("heads_back", heads_back_out, heads_back_in)
        used["heads_back"] = copies
        settle()
        if layer:
            feed_lines[1].step(2)
        else:
            head_grads(layer, scale_slope)
            attn_join(0)
            feed_grads(1, 3)
            go_finish(0)
            arrive(alpha_copies)
            retire(alpha_copies)
            total = alpha_own[...]
            for k in range(T - 1):
                total = total + alpha_in[k]
            alpha_own[...] = total
            alpha_copies = [
                send(("alpha", T - 1 + k), alpha_own, alpha_in.at[T - 1 + k], device) for k, device in enumerate(place_ids)
            ]
            feed_ahead()
            attn_lines[0].step(1)
        arrive(copies)
        partial = None
        for third in range(3):
            term = dot(heads_back_in[:, third].reshape(inner, S).T, wp[layer, third], NT)
            partial = term if partial is None else partial + term
        free("stream_back")
        partial = partial.astype(BF16).reshape(T, HALVES, count, D)
        copies = []
        for half in halves:
            sums_out[3, half] = partial[:, half]
            copies.append(scatter(3, half))
        settle()
        if layer:
            head_grads(layer, scale_slope)
            go_join(1)
        else:
            feed_lines[0].passed()
            feed_grads(0, 0)
            go_lines[0].step(1)
            feed_grads(0, 1)
            attn_lines[0].step(2)
        for half in halves:
            result = (stream_slopes[half] + scattered(3, half, copies[half])).astype(BF16)
            outs[1, layer, piece_of(half)] = result
            then(half, result)
        used["stream_back"] = sum(copies, [])
        if layer == 0:
            waiting["alpha"] = alpha_copies

    next_stream, entered_last, entered_first = [], [], []

    def to_second(half, result):
        next_stream.extend(gather("stream", stream.at[1, z], half, result))

    def to_backward(half, result):
        entered_last.append(enter(1, half, cot_ref[core, 0, piece_of(half)].astype(F32)))

    def to_first(half, result):
        entered_first.append(enter(0, half, result.astype(F32)))

    forward(0, acts_ref.at[core, 0], first_stream, to_second)
    forward(1, outs.at[0, 0], next_stream, to_backward)
    backward(1, outs.at[0, 0], entered_last, to_first)
    backward(0, acts_ref.at[core, 0], entered_first, lambda half, result: None)

    other = 1 - core
    last = [send("outs", outs.at[:, other], outs_in, sibling)]
    feed_grads(0, 2)
    go_lines[0].step(2)
    for line in feed_lines:
        line.finish()
    for line in (attn_lines[1], go_lines[1]):
        line.step(3)
        line.finish()
    arrive(waiting["alpha"])
    total = alpha_own[...]
    for k in range(Z - 1):
        total = total + alpha_in[T - 1 + k]
    finals[0, 0:2] = total[0]
    finals[1, 0:2] = total[1]
    settle(2)
    feed_grads(0, 3)
    last += [send("finals", finals.at[other], finals_in, sibling)]
    for kind, target in enumerate((lo_ref, ig_ref)):
        target[core] = outs[kind, core]
    arrive(last)
    for kind, target in enumerate((lo_ref, ig_ref)):
        target[other] = outs_in[kind]
    small_ref[0:4] = finals[core] + finals_in[...]
    for layer, chunk in staged[-2:]:
        stage_wait(layer, chunk)
    for chunk in range(chunks):
        for which in range(2):
            stage_send(0, chunk, which).wait_recv()
    attn_lines[0].step(3)
    go_lines[0].step(3)
    attn_out = pltpu.make_async_copy(attn_all, attn_ref, stage_sem.at[0, 0, 0])
    attn_out.start()
    for place in range(Z):
        small_ref[4:5, place * HDIM : (place + 1) * HDIM] = scale_all[place, :1, :HDIM]
    settle(0)
    for piece in range(len(weights)):
        if piece not in (2, 3):
            weight_copy(piece).wait_send()

    @pl.when(core == 0)
    def _():
        for piece in (2, 3):
            weight_copy(piece).wait_send()

    attn_lines[0].finish()
    go_lines[0].finish()
    attn_out.wait()
    assert len(slots.names) == COPIES, len(slots.names)


def relay(sizes, lengths, acts, cot, qs, us, al, wp, wo, we, wr):
    T, Z, S, part = sizes.tensors, sizes.places, sizes.local, sizes.part
    H, inner, units, D = sizes.heads, sizes.inner, sizes.units, sizes.width
    blocks, chunks = Z * (Z + 1) // 2, units // CHUNK
    vmem = pl.BlockSpec(memory_space=pltpu.VMEM)
    hbm = pl.BlockSpec(memory_space=pl.ANY)
    out_shape = (
        jax.ShapeDtypeStruct((2, part, D), BF16),
        jax.ShapeDtypeStruct((2, part, D), BF16),
        jax.ShapeDtypeStruct((8, D), F32),
        jax.ShapeDtypeStruct((Z, 4 * HDIM, D), BF16),
        jax.ShapeDtypeStruct((2, chunks, 2, D, CHUNK), BF16),
        jax.ShapeDtypeStruct((2, chunks, CHUNK, D), BF16),
    )
    DMA = pltpu.SemaphoreType.DMA
    V = pltpu.VMEM
    scratch = [
        V((2, 3, D, inner), BF16), V((2, inner, D), BF16), V((2, 2, D, units), BF16), V((2, units, D), BF16),
        V((2, 1, inner), F32), V((2, 2, units), F32), V((2, 2, D), F32),
        V((2, Z, S, D), BF16), V((2, Z, S, D), BF16), V((2, Z, S, D), BF16), V((S, D), BF16),
        V((Z, HDIM // 2, S), F32), V((Z, HDIM // 2, S), F32), V((2, H, HDIM, 128), F32),
        V((2, Z, 3, HDIM, S), BF16), V((2, Z, 2, S), F32),
        V((2, blocks, S, S), BF16), V((2, H, HDIM, S), BF16),
        V((4, HALVES, T - 1, part // HALVES, D), BF16),
        V((2, part, D), F32), V((2, part, D), F32), V((2, part, D), F32),
        V((2, HALVES, S // HALVES, units), BF16), V((2, HALVES, S // HALVES, units), BF16),
        V((S // HALVES, units), BF16), V((2, S // HALVES, units), BF16),
        V((Z, HDIM, S), BF16), V((H, 3, HDIM, S), BF16),
        V((H, 3, HDIM, S), BF16), V((H, 2, S), F32),
        V((Z, HDIM, S), BF16), V((H, HDIM, S), BF16), V((Z, 3, HDIM, S), BF16),
        V((4, HALVES, T, part // HALVES, D), BF16), V((H, HDIM, D), BF16), V((H, HDIM, D), BF16), V((Z - 1, HDIM, D), BF16),
        V((2, 2, part, D), BF16), V((2, part, D), BF16),
        V((Z, S, HDIM), BF16), V((Z, S, HDIM), BF16),
        V((Z, HDIM, S), F32), V((Z, HDIM, S), F32), V((Z, HDIM, S), F32),
        V((3 * HDIM, D), BF16), V((3 * HDIM, D), BF16), V((Z, 4 * HDIM, D), BF16),
        V((8, 128), F32), V((8, 128), F32), V((Z, 8, 128), F32),
        V((2, 2, D), F32), V((T + Z - 2, 2, 2, D), F32), V((2, 4, D), F32), V((4, D), F32),
        V((D, Z * S), BF16), V((CHUNK, Z * S), BF16), V((Z * S, CHUNK), BF16), V((Z * S, CHUNK), BF16),
        V((2, 2, D, CHUNK), BF16), V((2, CHUNK, D), BF16), V((2, D // 8, 2, units), BF16),
        DMA((2, 8)), DMA((8,)), DMA((COPIES,)), DMA((COPIES,)), DMA((2, chunks, 2)), DMA((2,)),
    ]
    return pl.pallas_call(
        functools.partial(relay_kernel, sizes),
        out_shape=out_shape,
        in_specs=[pl.BlockSpec(memory_space=pltpu.SMEM), vmem, vmem, vmem, vmem, vmem, hbm, hbm, hbm, hbm],
        out_specs=(vmem, vmem, vmem, hbm, hbm, hbm),
        scratch_shapes=scratch,
        compiler_params=pltpu.CompilerParams(collective_id=0, has_side_effects=True, vmem_limit_bytes=62 * 2**20),
        name="relay",
    )(lengths, acts, cot, qs, us, al, wp, wo, we, wr)


def finish_kernel(
    attn_ref, ge_ref, gr_ref, lo_in, ig_in, small_ref,
    projection_ref, output_ref, expansion_ref, reduction_ref, lo_ref, ig_ref, scale_ref, units_ref, alphas_ref,
):
    @pl.when(pl.program_id(0) == 0)
    def _():
        lo_ref[...] = lo_in[...]
        ig_ref[...] = ig_in[...]
        alphas_ref[...] = small_ref[0:2]
        units_ref[...] = small_ref[2:4, : units_ref.shape[1]]
        scale_ref[...] = small_ref[4:5, : scale_ref.shape[1]]

    places, chunks = attn_ref.shape[0], ge_ref.shape[1]
    for begin in range(0, ge_ref.shape[3], 16):
        rows = slice(begin, begin + 16)
        pieces = []
        for chunk in range(chunks):
            for lanes in (slice(0, 128), slice(128, 256)):
                for side in range(2):
                    total = ge_ref[0, chunk, side, rows, lanes].astype(F32) + ge_ref[1, chunk, side, rows, lanes].astype(F32)
                    pieces.append(total[None])
        expansion_ref[rows] = jnp.swapaxes(jnp.concatenate(pieces, axis=0), 0, 1)
    reduction_ref[...] = gr_ref[0].astype(F32) + gr_ref[1].astype(F32)
    for third in range(3):
        rows = attn_ref[:, third * HDIM : (third + 1) * HDIM, :].astype(F32)
        projection_ref[third] = rows.reshape(places * HDIM, rows.shape[2]).T
    output_ref[...] = attn_ref[:, 3 * HDIM :, :].astype(F32).reshape(output_ref.shape)


def finish(attn, ge, gr, lo, ig, small):
    places, _, D = attn.shape
    chunks, units, inner = ge.shape[1], ge.shape[1] * CHUNK, places * HDIM
    block = 256
    steps = D // block
    rows = units // steps

    def whole(shape):
        return pl.BlockSpec(shape, lambda i: (0,) * len(shape))

    return pl.pallas_call(
        finish_kernel,
        grid=(steps,),
        in_specs=[
            pl.BlockSpec((places, 4 * HDIM, block), lambda i: (0, 0, i)),
            pl.BlockSpec((2, chunks, 2, block, CHUNK), lambda i: (0, 0, 0, i, 0)),
            pl.BlockSpec((2, rows, D), lambda i: (0, i, 0)),
            whole(lo.shape),
            whole(ig.shape),
            whole(small.shape),
        ],
        out_specs=(
            pl.BlockSpec((3, block, inner), lambda i: (0, i, 0)),
            pl.BlockSpec((inner, block), lambda i: (0, i)),
            pl.BlockSpec((block, units // 64, 128), lambda i: (i, 0, 0)),
            pl.BlockSpec((rows, D), lambda i: (i, 0)),
            whole(lo.shape),
            whole(ig.shape),
            whole((1, inner)),
            whole((2, units)),
            whole((2, D)),
        ),
        out_shape=(
            jax.ShapeDtypeStruct((3, D, inner), F32),
            jax.ShapeDtypeStruct((inner, D), F32),
            jax.ShapeDtypeStruct((D, units // 64, 128), F32),
            jax.ShapeDtypeStruct((units, D), F32),
            jax.ShapeDtypeStruct(lo.shape, BF16),
            jax.ShapeDtypeStruct(ig.shape, BF16),
            jax.ShapeDtypeStruct((1, inner), F32),
            jax.ShapeDtypeStruct((2, units), F32),
            jax.ShapeDtypeStruct((2, D), F32),
        ),
        compiler_params=pltpu.CompilerParams(vmem_limit_bytes=60 * 2**20),
        name="finish",
    )(attn, ge, gr.reshape(2, units, D), lo, ig, small)


def fast_body(
    activations, lengths, projection, output_weight, expansion, reduction, query_scale, unit_scales, alphas, cotangent
):
    _, _, part, width = activations.shape
    inner, units = output_weight.shape[1], reduction.shape[1]
    places = lax.axis_size("dp")
    sizes = Sizes(lax.axis_size("tensor"), places, part, width, inner, units)
    lo, ig, small, attn, ge, gr = relay(
        sizes, lengths, activations, cotangent, query_scale, unit_scales[0], alphas[0],
        projection[0].transpose(1, 0, 2), output_weight[0], expansion[0], reduction[0],
    )
    projection_grad, output_grad, expansion_grad, reduction_grad, lo, ig, scale_grad, unit_grad, alpha_grad = finish(
        attn, ge, gr, lo, ig, small
    )
    columns = units // 128
    expansion_grad = expansion_grad.reshape(width, columns, 2, 128).transpose(0, 2, 1, 3).reshape(width, 2, units)
    projection_grad = projection_grad.transpose(1, 0, 2)
    return (
        lo[None, :, None],
        ig[None, :, None],
        projection_grad[None],
        output_grad[None],
        expansion_grad[None],
        reduction_grad[None],
        scale_grad,
        unit_grad[None],
        alpha_grad[None],
    )


def solution(mesh):
    in_specs = (
        P(None, None, ("dp", "tensor"), None),
        P(),
        P("section", None, None, "tensor"),
        P("section", "tensor", None),
        P("section", None, None, "tensor"),
        P("section", "tensor", None),
        P("section", "tensor"),
        P("section", None, "tensor"),
        P("section", None, None),
        P(None, None, ("dp", "tensor"), None),
    )
    out_specs = (
        P("section", None, None, ("dp", "tensor"), None),
        P("section", None, None, ("dp", "tensor"), None),
        P("section", None, None, "tensor"),
        P("section", "tensor", None),
        P("section", None, None, "tensor"),
        P("section", "tensor", None),
        P("section", "tensor"),
        P("section", None, "tensor"),
        P("section", None, None),
    )
    def chosen(*arrays):
        activations, output_weight = arrays[0], arrays[3]
        heads = output_weight.shape[1] // HDIM
        fits = (
            mesh.shape["section"] == 2
            and mesh.shape["tensor"] == 4
            and mesh.shape["dp"] == heads
            and activations.shape[:2] == (2, 1)
            and activations.shape[2] * mesh.shape["tensor"] == 256
        )
        return (fast_body if fits else body)(*arrays)

    return jax.shard_map(chosen, mesh=mesh, in_specs=in_specs, out_specs=out_specs, check_vma=False)
```

```python
import functools
import math

import jax
import jax.numpy as jnp
from jax import lax
from jax.experimental import pallas as pl
from jax.experimental.pallas import tpu as pltpu
from jax.sharding import PartitionSpec as P

HDIM = 64


def from_behind(value, axis, steps):
    count = lax.axis_size(axis)
    initial, last = (max(0, -steps), min(count, count - steps))
    return lax.ppermute(value, axis, [(source, source + steps) for source in range(initial, last)])


def normed(v):
    return v * lax.rsqrt(jnp.mean(v * v, axis=-1, keepdims=True) + 1e-06)


def unit_heads(v):
    return v * lax.rsqrt(jnp.sum(v * v, axis=-1, keepdims=True) + 1e-06)


def frequencies(half):
    return jnp.exp(jnp.arange(half, dtype=jnp.float32) * (-2.0 * math.log(10000.0) / (2 * half)))


def rotate(view, angle):
    half = view.shape[-1] // 2
    cosine = jnp.cos(angle)[..., None, :]
    sine = jnp.sin(angle)[..., None, :]
    front = view[..., :half]
    back = view[..., half:]
    return jnp.concatenate([front * cosine - back * sine, back * cosine + front * sine], axis=-1)


def shaped(projected, scale, angle, heads):
    inner = projected.shape[-1] // 3
    lead = projected.shape[:-1]

    def turned(piece):
        view = piece.reshape(lead + (heads, inner // heads))
        return unit_heads(rotate(view, angle)).reshape(lead + (inner,)) * scale

    return (
        turned(projected[..., :inner]),
        turned(projected[..., inner : 2 * inner]),
        projected[..., 2 * inner :],
    )


def layout(lengths_row, slots):
    ends = jnp.cumsum(lengths_row, dtype=jnp.int32)
    index = jnp.arange(slots, dtype=jnp.int32)
    after = index[:, None] >= ends[None, :]
    segment = jnp.sum(after.astype(jnp.int32), axis=1, dtype=jnp.int32)
    begin = jnp.sum(jnp.where(after, lengths_row[None, :], 0), axis=1, dtype=jnp.int32)
    inside = index < ends[-1]
    segment = jnp.where(inside, segment, lengths_row.shape[0] + index)
    position = jnp.where(inside, index - begin, 0)
    return (segment, position)


def blend(base, branch, alpha):
    return normed(base + alpha * (normed(branch) - base))


def activate(expanded, scales):
    half = expanded.shape[-1] // 2
    return expanded[..., :half] * scales[0] * jax.nn.silu(expanded[..., half:] * scales[1])


def placing(lengths_now, local):
    slots = local * lax.axis_size("dp")
    start_here = lax.axis_index("dp") * local
    segment_all, position_all = jax.vmap(lambda row: layout(row, slots))(lengths_now)
    segment_here = lax.dynamic_slice_in_dim(segment_all, start_here, local, 1)
    position_here = lax.dynamic_slice_in_dim(position_all, start_here, local, 1)
    index_here = start_here + jnp.arange(local, dtype=jnp.int32)
    every = jnp.arange(slots, dtype=jnp.int32)
    allowed = (segment_here[:, :, None] == segment_all[:, None, :]) & (
        every[None, None, :] <= index_here[None, :, None]
    )
    angle = position_here.astype(jnp.float32)[..., None] * frequencies(HDIM // 2)
    return (allowed, angle)


def scored(query, key_all, allowed, heads):
    rows, local, inner = query.shape
    depth = inner // heads
    query_heads = query.reshape(rows, local, heads, depth)
    key_heads = key_all.reshape(rows, key_all.shape[1], heads, depth)
    raw = jnp.einsum(
        "rqhe,rkhe->rhqk", query_heads, key_heads, preferred_element_type=jnp.float32
    ) * math.sqrt(depth)
    return jnp.where(allowed[:, None], raw, -1e30)


def forward(stream, lengths_now, weights):
    projection, output_weight, expansion, reduction, query_scale, unit_scales, alphas = weights
    rows, part, width = stream.shape
    inner = output_weight.shape[0]
    heads = inner // HDIM
    hidden_width = reduction.shape[0]
    gathered = lax.all_gather(stream.astype(jnp.bfloat16), "tensor", axis=1, tiled=True)
    local = gathered.shape[1]
    allowed, angle = placing(lengths_now, local)
    projected = jnp.einsum(
        "rsd,dc->rsc",
        gathered,
        projection.reshape(width, 3 * inner),
        preferred_element_type=jnp.float32,
    )
    query, key, value = shaped(projected, query_scale, angle, heads)
    query_low = query.astype(jnp.bfloat16)
    key_low = key.astype(jnp.bfloat16)
    value_low = value.astype(jnp.bfloat16)
    key_all, value_all = (
        lax.all_gather(key_low, "dp", axis=1, tiled=True),
        lax.all_gather(value_low, "dp", axis=1, tiled=True),
    )
    scores = scored(query_low, key_all, allowed, heads)
    highest = jnp.max(scores, axis=-1, keepdims=True)
    lifted = jnp.exp(scores - highest)
    total = jnp.sum(lifted, axis=-1, keepdims=True)
    log_total = highest + jnp.log(total)
    probs_low = (lifted / total).astype(jnp.bfloat16)
    value_heads = value_all.reshape(rows, value_all.shape[1], heads, HDIM)
    mixed = jnp.einsum(
        "rhqk,rkhe->rqhe", probs_low, value_heads, preferred_element_type=jnp.float32
    )
    attended = mixed.reshape(rows, local, inner).astype(jnp.bfloat16)
    partial_branch = jnp.einsum(
        "rsc,cd->rsd", attended, output_weight, preferred_element_type=jnp.float32
    )
    branch = lax.psum_scatter(partial_branch, "tensor", scatter_dimension=1, tiled=True)
    middle = blend(stream, branch, alphas[0])
    middle_all = lax.all_gather(middle.astype(jnp.bfloat16), "tensor", axis=1, tiled=True)
    expanded = jnp.einsum(
        "rsd,dc->rsc",
        middle_all,
        expansion.reshape(width, 2 * hidden_width),
        preferred_element_type=jnp.float32,
    )
    hidden = activate(expanded, unit_scales).astype(jnp.bfloat16)
    partial_feed = jnp.einsum("rsf,fd->rsd", hidden, reduction, preferred_element_type=jnp.float32)
    feed = lax.psum_scatter(partial_feed, "tensor", scatter_dimension=1, tiled=True)
    result = blend(middle, feed, alphas[1])
    kept = dict(
        stream=stream,
        gathered=gathered,
        projected=projected,
        query=query_low,
        key=key_low,
        value=value_low,
        log_total=log_total,
        attended=attended,
        branch=branch,
        middle=middle,
        middle_all=middle_all,
        expanded=expanded,
        hidden=hidden,
        feed=feed,
        lengths=lengths_now,
    )
    kept = dict(kept, key_all=key_all, value_all=value_all)
    return (result, kept)


def backward(slope, kept, weights):
    projection, output_weight, expansion, reduction, query_scale, unit_scales, alphas = weights
    rows, part, width = slope.shape
    inner = output_weight.shape[0]
    heads = inner // HDIM
    hidden_width = reduction.shape[0]
    _, pull_feed = jax.vjp(blend, kept["middle"], kept["feed"], alphas[1])
    middle_slope, feed_slope, alpha_feed = pull_feed(slope)
    feed_all = lax.all_gather(feed_slope.astype(jnp.bfloat16), "tensor", axis=1, tiled=True)
    reduction_grad = jnp.einsum(
        "rsf,rsd->fd", kept["hidden"], feed_all, preferred_element_type=jnp.float32
    )
    hidden_slope = jnp.einsum(
        "rsd,fd->rsf", feed_all, reduction, preferred_element_type=jnp.float32
    )
    _, pull_active = jax.vjp(activate, kept["expanded"], unit_scales)
    expanded_slope, unit_grad = pull_active(hidden_slope)
    expanded_low = expanded_slope.astype(jnp.bfloat16)
    expansion_grad = jnp.einsum(
        "rsd,rsc->dc", kept["middle_all"], expanded_low, preferred_element_type=jnp.float32
    ).reshape(width, 2, hidden_width)
    partial_middle = jnp.einsum(
        "rsc,dc->rsd",
        expanded_low,
        expansion.reshape(width, 2 * hidden_width),
        preferred_element_type=jnp.float32,
    )
    middle_total = middle_slope + lax.psum_scatter(
        partial_middle, "tensor", scatter_dimension=1, tiled=True
    )
    _, pull_branch = jax.vjp(blend, kept["stream"], kept["branch"], alphas[0])
    stream_slope, branch_slope, alpha_branch = pull_branch(middle_total)
    branch_all = lax.all_gather(branch_slope.astype(jnp.bfloat16), "tensor", axis=1, tiled=True)
    output_grad = jnp.einsum(
        "rsc,rsd->cd", kept["attended"], branch_all, preferred_element_type=jnp.float32
    )
    attended_low = jnp.einsum(
        "rsd,cd->rsc", branch_all, output_weight, preferred_element_type=jnp.float32
    ).astype(jnp.bfloat16)
    local = attended_low.shape[1]
    key_all = kept["key_all"]
    value_all = kept["value_all"]
    slots = key_all.shape[1]
    allowed, angle = placing(kept["lengths"], local)
    scores = scored(kept["query"], key_all, allowed, heads)
    probs = jnp.exp(scores - kept["log_total"])
    scale = math.sqrt(HDIM)
    back_heads = attended_low.reshape(rows, local, heads, HDIM)
    query_heads = kept["query"].reshape(rows, local, heads, HDIM)
    key_heads = key_all.reshape(rows, slots, heads, HDIM)
    value_heads = value_all.reshape(rows, slots, heads, HDIM)
    probs_slope = jnp.einsum(
        "rqhe,rkhe->rhqk", back_heads, value_heads, preferred_element_type=jnp.float32
    )
    row_term = jnp.sum(probs * probs_slope, axis=-1, keepdims=True)
    scores_low = (probs * (probs_slope - row_term)).astype(jnp.bfloat16)
    query_slope = (
        jnp.einsum("rhqk,rkhe->rqhe", scores_low, key_heads, preferred_element_type=jnp.float32)
        * scale
    )
    value_grad_all = jnp.einsum(
        "rhqk,rqhe->rkhe",
        probs.astype(jnp.bfloat16),
        back_heads,
        preferred_element_type=jnp.float32,
    )
    key_grad_all = (
        jnp.einsum("rhqk,rqhe->rkhe", scores_low, query_heads, preferred_element_type=jnp.float32)
        * scale
    )
    key_slope, value_slope = (
        lax.psum_scatter(
            key_grad_all.reshape(rows, slots, inner), "dp", scatter_dimension=1, tiled=True
        ),
        lax.psum_scatter(
            value_grad_all.reshape(rows, slots, inner), "dp", scatter_dimension=1, tiled=True
        ),
    )
    _, pull_shape = jax.vjp(
        lambda source, scale_now: shaped(source, scale_now, angle, heads),
        kept["projected"],
        query_scale,
    )
    projected_slope, query_scale_grad = pull_shape(
        (query_slope.reshape(rows, local, inner), key_slope, value_slope)
    )
    projected_low = projected_slope.astype(jnp.bfloat16)
    projection_grad = jnp.einsum(
        "rsd,rsc->dc", kept["gathered"], projected_low, preferred_element_type=jnp.float32
    ).reshape(width, 3, inner)
    partial_stream = jnp.einsum(
        "rsc,dc->rsd",
        projected_low,
        projection.reshape(width, 3 * inner),
        preferred_element_type=jnp.float32,
    )
    spread = jnp.broadcast_to(
        jnp.stack([alpha_branch, alpha_feed])[:, None, :], (2, lax.axis_size("tensor"), width)
    )
    stream_part, alpha_sum = (
        lax.psum_scatter(partial_stream, "tensor", scatter_dimension=1, tiled=True),
        lax.psum_scatter(spread, "tensor", scatter_dimension=1, tiled=True),
    )
    stream_total = stream_slope + stream_part
    return (
        stream_total,
        (
            projection_grad,
            output_grad,
            expansion_grad,
            reduction_grad,
            query_scale_grad,
            unit_grad,
            alpha_sum[:, 0],
        ),
    )


def body(
    activations,
    lengths,
    projection,
    output_weight,
    expansion,
    reduction,
    query_scale,
    unit_scales,
    alphas,
    cotangent,
):
    micro, rows, part, width = activations.shape
    section = lax.axis_index("section")
    first = section == 0
    weights = (
        projection[0],
        output_weight[0],
        expansion[0],
        reduction[0],
        query_scale[0],
        unit_scales[0],
        alphas[0],
    )
    steps = micro + 1
    received = jnp.zeros((rows, part, width), jnp.bfloat16)
    outputs = []
    keeps = []
    for step in range(steps):
        index_now = jnp.clip(step - section, 0, micro - 1)
        lengths_now = lax.dynamic_index_in_dim(lengths, index_now, 0, keepdims=False)
        stream = jnp.where(first, activations[min(step, micro - 1)], received).astype(jnp.float32)
        result, kept = forward(stream, lengths_now, weights)
        result_low = result.astype(jnp.bfloat16)
        outputs.append(result_low)
        keeps.append(kept)
        if step + 1 < steps:
            received = from_behind(result_low, "section", 1)
    stacked = jnp.stack(outputs)
    layer_output = jnp.where(first, stacked[:micro], stacked[1:])[None]
    back_received = jnp.zeros((rows, part, width), jnp.bfloat16)
    slopes = []
    summed = None
    for step in range(steps):
        batch_now = step - 1 + section
        valid = (batch_now >= 0) & (batch_now < micro)
        slope = jnp.where(first, back_received, cotangent[min(step, micro - 1)]).astype(jnp.float32)
        earlier = keeps[max(step - 1, 0)]
        later = keeps[min(step + 1, micro)]
        kept = jax.tree.map(lambda left, right: jnp.where(first, left, right), earlier, later)
        stream_total, layer_grads = backward(slope, kept, weights)
        stream_low = stream_total.astype(jnp.bfloat16)
        slopes.append(stream_low)
        masked = tuple((jnp.where(valid, piece, 0.0) for piece in layer_grads))
        summed = (
            masked
            if summed is None
            else tuple((left + right for left, right in zip(summed, masked)))
        )
        if step + 1 < steps:
            back_received = from_behind(stream_low, "section", -1)
    stacked_slopes = jnp.stack(slopes)
    input_gradient = jnp.where(first, stacked_slopes[1:], stacked_slopes[:micro])[None]
    (
        projection_grad,
        output_grad,
        expansion_grad,
        reduction_grad,
        query_scale_grad,
        unit_grad,
        alpha_grad,
    ) = summed
    totals = lax.psum(
        (
            projection_grad,
            output_grad,
            expansion_grad,
            reduction_grad,
            query_scale_grad,
            unit_grad,
            alpha_grad,
        ),
        "dp",
    )
    return (
        layer_output,
        input_gradient,
        totals[0][None],
        totals[1][None],
        totals[2][None],
        totals[3][None],
        totals[4][None],
        totals[5][None],
        totals[6][None],
    )


MESH_IDS = pl.DeviceIdType.MESH
F32, BF16 = jnp.float32, jnp.bfloat16
CHUNK = 256
NN = ((1,), (0,))
NT = ((1,), (1,))


def dot(left, right, dims):
    return lax.dot_general(left, right, (dims, ((), ())), preferred_element_type=F32)


def sigmoid(v):
    return 0.5 + 0.5 * jnp.tanh(0.5 * v)


def norm_parts(v):
    rate = lax.rsqrt(jnp.mean(v * v, axis=-1, keepdims=True) + 1e-06)
    return v * rate, rate


def norm_back(slope, unit, rate):
    return rate * (slope - unit * jnp.mean(unit * slope, axis=-1, keepdims=True))


def blend_back(slope, base, branch, alpha):
    unit_branch, rate_branch = norm_parts(branch)
    toward = unit_branch - base
    unit, rate = norm_parts(base + alpha * toward)
    inner_slope = norm_back(slope, unit, rate)
    alpha_slope = jnp.sum(inner_slope * toward, axis=0, keepdims=True)
    scaled = alpha * inner_slope
    return inner_slope - scaled, norm_back(scaled, unit_branch, rate_branch), alpha_slope


def sequence_starts(lengths_ref, row, index):
    begin = jnp.zeros_like(index)
    end = jnp.int32(0)
    for sequence in range(lengths_ref.shape[2]):
        end = end + lengths_ref[row, 0, sequence]
        begin = jnp.where(index >= end, end, begin)
    return jnp.where(index < end, begin, index)


class Sizes:
    def __init__(self, tensors, places, part, width, inner, units):
        self.tensors, self.places, self.part, self.width = tensors, places, part, width
        self.inner, self.units = inner, units
        self.local = part * tensors
        self.heads = inner // HDIM


class Slots:
    def __init__(self, send, recv):
        self.send, self.recv, self.names = send, recv, {}

    def copy(self, name, source, target, device):
        number = self.names.setdefault(name, len(self.names))
        return pltpu.make_async_remote_copy(
            source, target, self.send.at[number], self.recv.at[number], device_id=device, device_id_type=MESH_IDS
        )


HALVES = 2
COPIES = 211


def relay_kernel(
    sizes,
    lengths_ref, acts_ref, cot_ref, qs_ref, us_ref, al_ref, wp_ref, wo_ref, we_ref, wr_ref,
    lo_ref, ig_ref, small_ref, attn_ref, ge_ref, gr_ref,
    wp, wo, we, wr, qs, us, al,
    stream, middles, feed_low, branch_low,
    cosines, sines, scales,
    heads_in, rates_in, probs, mixed_in, sums_in, branch_f, middle_f, feed_f, ups, gates,
    hidden, expanded_low, back_in, heads_back_in,
    heads_out, rates_out, mixed_out, sums_out, go_out, go_sib, go_in,
    outs, outs_in, turned_rows, query_grad, key_grad, value_grad,
    attn_own, attn_sib, attn_all, scale_own, scale_sib, scale_all,
    alpha_own, alpha_in, finals, finals_in,
    middle_cols, hidden_part, up_part, gate_part, stage_e, stage_r, raw, ahead,
    weight_sem, weight_send, send_sem, recv_sem, stage_sem, raw_sem,
):
    T, Z, S, part = sizes.tensors, sizes.places, sizes.local, sizes.part
    H, inner, units, D = sizes.heads, sizes.inner, sizes.units, sizes.width
    core, t, z = lax.axis_index("section"), lax.axis_index("tensor"), lax.axis_index("dp")
    sibling = (1 - core, t, z)
    side, row = lax.rem(t, 2), t // 2
    tensor_peers = [row * 2 + (1 - side), (1 - row) * 2 + side, (1 - row) * 2 + (1 - side)]
    place_peers = [lax.rem(z + k, Z) for k in range(1, Z)]
    tensor_ids = [(core, peer, z) for peer in tensor_peers]
    place_ids = [(core, t, peer) for peer in place_peers]
    slots = Slots(send_sem, recv_sem)
    pending = [[]]

    weights = [
        (wp_ref, lambda layer: wp.at[layer]),
        (wo_ref, lambda layer: wo.at[layer]),
        (we.at[core, 0], lambda layer: we.at[layer, 0]),
        (we.at[core, 1], lambda layer: we.at[layer, 1]),
        (wr_ref, lambda layer: wr.at[layer]),
        (qs_ref, lambda layer: qs.at[layer]),
        (us_ref, lambda layer: us.at[layer]),
        (al_ref, lambda layer: al.at[layer]),
    ]

    def weight_load(layer, piece):
        source, target = weights[piece]
        return pltpu.make_async_copy(source, target(layer), weight_sem.at[layer, piece])

    for piece in range(len(weights)):
        if piece not in (2, 3):
            weight_load(core, piece).start()

    raw_rows = raw.shape[1]

    def raw_load(block):
        return pltpu.make_async_copy(we_ref.at[pl.ds(block * raw_rows, raw_rows)], raw.at[block % 2], raw_sem.at[block % 2])

    for block in range(2):
        raw_load(block).start()

    def take_apart(blocks):
        for block in blocks:
            raw_load(block).wait()
            we[core, :, block * raw_rows : (block + 1) * raw_rows, :] = jnp.swapaxes(raw[block % 2], 0, 1)
            if (block + 2) * raw_rows < D:
                raw_load(block + 2).start()

    barrier = pltpu.get_barrier_semaphore()
    partners = [sibling] + tensor_ids + place_ids
    for partner in partners:
        pl.semaphore_signal(barrier, inc=1, device_id=partner, device_id_type=MESH_IDS)
    turn = HDIM // 2
    index_all = lax.broadcasted_iota(jnp.int32, (1, S * Z), 1)
    starts = sequence_starts(lengths_ref, core, index_all)
    rates = jnp.exp(lax.broadcasted_iota(jnp.int32, (turn, 1), 0).astype(F32) * (-2.0 * math.log(10000.0) / HDIM))
    angle = rates * (index_all - starts).astype(F32)
    cosine, sine = jnp.cos(angle), jnp.sin(angle)
    for place in range(Z):
        cosines[place] = cosine[:, place * S : (place + 1) * S]
        sines[place] = sine[:, place * S : (place + 1) * S]
    key_index = lax.broadcasted_iota(jnp.int32, (S * Z, S), 0)
    pl.semaphore_wait(barrier, len(partners))

    def weight_copy(piece):
        source, target = weights[piece]
        return pltpu.make_async_remote_copy(
            source, target(core), weight_send.at[piece], weight_sem.at[core, piece], device_id=sibling, device_id_type=MESH_IDS
        )

    def lend_weights(layer, pieces):
        @pl.when(core == layer)
        def _():
            for piece in pieces:
                weight_copy(piece).start()

    for piece in (5, 6, 7):
        weight_copy(piece).start()
    lend_weights(0, (0,))

    def await_weight(layer, piece):
        if piece in (2, 3):
            @pl.when(core != layer)
            def _():
                weight_load(layer, piece).wait()
        else:
            weight_load(layer, piece).wait()

    def send(name, source, target, device):
        copy = slots.copy(name, source, target, device)
        copy.start()
        pending[-1].append(copy)
        return copy

    def settle(keep=4):
        pending.append([])
        while len(pending) > keep:
            for copy in pending.pop(0):
                copy.wait_send()

    def arrive(copies):
        for copy in copies:
            copy.wait_recv()

    def rows_of(index):
        return pl.ds(pl.multiple_of(index * part, part), part)

    my_rows, far_rows = rows_of(t), rows_of(tensor_peers[2])

    def gather(name, target, half, value):
        count = value.shape[0]
        rows = pl.ds(pl.multiple_of(t * part + half * count, count), count)
        target[rows, :] = value
        mine = target.at[rows, :]
        return [send((name, half, k), mine, mine, device) for k, device in enumerate(tensor_ids)]

    def half_of(target, half):
        return jnp.concatenate([target[index * part + half * count : index * part + (half + 1) * count, :] for index in range(T)], axis=0)

    count = part // HALVES
    halves = range(HALVES)

    def piece_of(half):
        return slice(half * count, (half + 1) * count)

    class Line:
        def __init__(self, name, views, guard=None, passes=0):
            self.name, self.views, self.guard, self.passes = name, views, guard, passes

        def copies(self, way, step, origin):
            device = (core, t, z + 1) if way == 0 else (core, t, z - 1)
            return [slots.copy((self.name, way, step, k), view, view, device) for k, view in enumerate(self.views(origin))]

        def when(self, condition):
            return pl.when(condition if self.guard is None else condition & self.guard)

        def origin(self, way, step):
            return z - step if way == 0 else z + step

        def sends(self, way, step):
            return (z >= step) & (z + 1 < Z) if way == 0 else (z + step < Z) & (z >= 1)

        def comes(self, way, step):
            return z >= step if way == 0 else z + step < Z

        def passing(self, way, step):
            got = self.views(self.origin(way, step))[0]
            return [slots.copy((self.name, "pass", way, step, k), got, got, tensor_ids[k]) for k in range(self.passes)]

        def passed(self):
            for way in range(2):
                for step in range(1, Z):
                    @self.when(self.comes(way, step))
                    def _():
                        for copy in self.passing(way, step):
                            copy.wait_recv()

        def step(self, step):
            for way in range(2):
                if step > 0:
                    @self.when(self.comes(way, step))
                    def _():
                        for copy in self.copies(way, step - 1, self.origin(way, step)):
                            copy.wait_recv()
                        for copy in self.passing(way, step):
                            copy.start()

                if step < Z - 1:
                    @self.when(self.sends(way, step))
                    def _():
                        for copy in self.copies(way, step, self.origin(way, step)):
                            copy.start()

        def finish(self):
            for way in range(2):
                for step in range(Z - 1):
                    @self.when(self.sends(way, step))
                    def _():
                        for copy in self.copies(way, step, self.origin(way, step)):
                            copy.wait_send()

                    @self.when(self.comes(way, step + 1))
                    def _():
                        for copy in self.passing(way, step + 1):
                            copy.wait_send()

    def row_line(name, layer, target, groups, passes=0):
        return Line((name, len(groups)), lambda place: [target.at[layer, place, rows, :] for rows in groups], None, passes)

    def pass_on(name, layer, target, count=2, indices=range(Z - 1)):
        passed = []
        for index in indices:
            got = target.at[layer, place_peers[index], my_rows, :]
            passed += [send((name, "pass", index, k), got, got, device) for k, device in enumerate(tensor_ids[:count])]
        return passed

    def scatter(number, half):
        return [
            send((number % 2, half, k), sums_out.at[number % 2, half, peer], sums_in.at[number % 2, half, k], device)
            for k, (peer, device) in enumerate(zip(tensor_peers, tensor_ids))
        ]

    def scattered(number, half, copies):
        arrive(copies)
        total = sums_out[number % 2, half, t].astype(F32)
        for k in range(T - 1):
            total = total + sums_in[number % 2, half, k].astype(F32)
        return total

    def retire(copies):
        for copy in copies:
            for group in pending:
                if any(copy is other for other in group):
                    copy.wait_send()
                    group[:] = [other for other in group if other is not copy]

    def spread(name, source, target):
        target[z] = source[z]
        return [
            send((name, k), source.at[peer], target.at[z], device) for k, (peer, device) in enumerate(zip(place_peers, place_ids))
        ]

    def block(query, key):
        return query * (query + 1) // 2 + key

    used, waiting = {}, {}
    first_line = row_line("first line", 0, stream, [my_rows], 2)
    stream_lines = [row_line("stream line", 0, stream, [far_rows]), row_line("stream line", 1, stream, [my_rows, far_rows])]
    middle_lines = [row_line("middle line", layer, middles, [my_rows, far_rows], 2 - 2 * layer) for layer in range(2)]
    feed_lines = [row_line("feed line", layer, feed_low, [my_rows, far_rows][: layer + 1], 3 - layer) for layer in range(2)]

    def free(name):
        retire(used.pop(name, []))

    first_stream = gather("stream", stream.at[0, z], 0, acts_ref[core, 0])
    first_line.step(0)

    def forward(layer, base_low, stream_copies, then):
        if layer == 0:
            take_apart(range(0, D // raw_rows // 2))
        await_weight(layer, 0)
        for piece in (5, 6, 7):
            await_weight(layer, piece)
        scale = jnp.broadcast_to(jnp.broadcast_to(qs[layer], (8, inner)).T[:, :1], (inner, 128)).reshape(H, HDIM, 128)
        scales[layer] = scale
        cosine_here, sine_here = cosines[z][None], sines[z][None]
        arrive(stream_copies)
        if layer == 0:
            first_line.step(1)
        free("heads")
        gathered = stream[layer, z]
        for third in range(3):
            piece = dot(gathered, wp[layer, third], NN).T.reshape(H, HDIM, S)
            if third < 2:
                front, back = piece[:, :turn], piece[:, turn:]
                piece = jnp.concatenate([front * cosine_here - back * sine_here, back * cosine_here + front * sine_here], axis=1)
                speed = lax.rsqrt(jnp.sum(piece * piece, axis=1, keepdims=True) + 1e-06)
                piece = piece * speed * scale[:, :, :1]
                for head in range(H):
                    rates_out[head, third : third + 1] = speed[head]
            heads_out[:, third] = piece.astype(BF16)
        copies = spread("heads", heads_out, heads_in.at[layer])
        rate_copies = spread("rates", rates_out, rates_in.at[layer])
        used["heads"] = copies + rate_copies
        if layer == 0:
            take_apart(range(D // raw_rows // 2, D // raw_rows))
        else:
            middle_lines[0].step(2)
        lend_weights(layer, (1, 2))
        settle()
        if layer:
            first_line.step(3)
        arrive(copies + rate_copies)
        if layer:
            middle_lines[0].step(3)
        for place in range(Z):
            turned_rows[place] = heads_in[layer, place, 1].T
        free("mixed")
        for query in range(Z):
            raw = [dot(turned_rows[key], heads_in[layer, query, 0], NN) * math.sqrt(HDIM) for key in range(query + 1)]
            first = starts[:, query * S : (query + 1) * S]
            last = index_all[:, query * S : (query + 1) * S]
            scores = []
            for key in range(query + 1):
                keys = key_index[key * S : (key + 1) * S]
                allowed = keys >= first
                if key == query:
                    allowed = allowed & (keys <= last)
                scores.append(jnp.where(allowed, raw[key], -1e30))
            highest = scores[0].max(axis=0, keepdims=True)
            for piece in scores[1:]:
                highest = jnp.maximum(highest, piece.max(axis=0, keepdims=True))
            lifted = [jnp.exp(piece - highest) for piece in scores]
            total = lifted[0].sum(axis=0, keepdims=True)
            for piece in lifted[1:]:
                total = total + piece.sum(axis=0, keepdims=True)
            shrink = 1.0 / total
            mixed = None
            for key in range(query + 1):
                low = (lifted[key] * shrink).astype(BF16)
                probs[layer, block(query, key)] = low
                term = dot(heads_in[layer, key, 2], low, NN)
                mixed = term if mixed is None else mixed + term
            mixed_out[query] = mixed.astype(BF16)
        copies = spread("mixed", mixed_out, mixed_in.at[layer])
        used["mixed"] = copies
        if layer == 0:
            first_line.step(2)
            stream_lines[0].step(0)
        settle()
        if layer:
            stream_lines[0].step(3)
            stream_lines[0].finish()
        await_weight(layer, 1)
        arrive(copies)
        attended = mixed_in[layer].reshape(inner, S).T
        free("sums 0")
        partial = dot(attended, wo[layer], NN).astype(BF16).reshape(T, HALVES, count, D)
        branch_copies = []
        for half in halves:
            sums_out[0, half] = partial[:, half]
            branch_copies.append(scatter(0, half))
        used["sums 0"] = sum(branch_copies, [])
        if layer:
            stream_lines[1].step(0)
        else:
            stream_lines[0].step(1)
        lend_weights(layer, (3,))
        settle()
        alpha = al[layer]
        middle_copies = []
        for half in halves:
            branch = scattered(0, half, branch_copies[half])
            base = base_low[piece_of(half)].astype(F32)
            middle = norm_parts(base + alpha[0:1] * (norm_parts(branch)[0] - base))[0]
            middle_copies.append(gather("middle", middles.at[layer, z], half, middle.astype(BF16)))
            branch_f[layer, piece_of(half)] = branch
            middle_f[layer, piece_of(half)] = middle
        stream_lines[layer].step(1 + (layer == 0))
        lend_weights(layer, (4,))
        settle()
        if layer:
            for line in (first_line, middle_lines[0]):
                line.passed()
                line.finish()
        free("sums 1")
        for piece in (2, 3):
            await_weight(layer, piece)
        feed_copies = []
        for half in halves:
            arrive(middle_copies[half])
            middle_all = half_of(middles.at[layer, z], half)
            for begin in range(0, units, CHUNK):
                cols = slice(begin, begin + CHUNK)
                up = dot(middle_all, we[layer, 0, :, cols], NN)
                gate = dot(middle_all, we[layer, 1, :, cols], NN)
                if layer:
                    ups[half, :, cols] = up.astype(BF16)
                    gates[half, :, cols] = gate.astype(BF16)
                inside = us[layer, 1:2, cols] * gate
                hidden[:, cols] = (us[layer, 0:1, cols] * up * (inside * sigmoid(inside))).astype(BF16)
            if half == 0:
                await_weight(layer, 4)
            acted = hidden[...]
            for begin in range(0, D, CHUNK):
                cols = slice(begin, begin + CHUNK)
                sums_out[1, half, :, :, cols] = dot(acted, wr[layer, :, cols], NN).astype(BF16).reshape(T, count, CHUNK)
            feed_copies.append(scatter(1, half))
        used["sums 1"] = sum(feed_copies, [])
        if layer:
            stream_lines[1].step(2)
        middle_lines[layer].step(0)
        settle()
        for half in halves:
            feed = scattered(1, half, feed_copies[half])
            feed_f[layer, piece_of(half)] = feed
            middle = middle_f[layer, piece_of(half)]
            result = norm_parts(middle + alpha[1:2] * (norm_parts(feed)[0] - middle))[0].astype(BF16)
            outs[0, layer, piece_of(half)] = result
            then(half, result)
        if layer == 0:
            middle_lines[0].step(1)
            lend_weights(1, (0,))

    def act_back(layer, cols, up, gate, slope_hidden):
        scale_up, scale_gate = us[layer, 0:1, cols], us[layer, 1:2, cols]
        inside = scale_gate * gate
        gain = sigmoid(inside)
        silu = inside * gain
        by_up = silu * slope_hidden
        by_gate = scale_up * up * (gain + silu * (1.0 - gain)) * slope_hidden
        return silu, by_up, by_gate

    def stage_copy(layer, chunk, which):
        buffer = (stage_e, stage_r)[which].at[chunk % 2]
        target = (ge_ref.at[0, chunk], gr_ref.at[0, chunk])[which]
        return pltpu.make_async_copy(buffer, target, stage_sem.at[layer, chunk, which])

    def stage_send(layer, chunk, which):
        buffer = (stage_e, stage_r)[which].at[chunk % 2]
        target = (ge_ref.at[1, chunk], gr_ref.at[1, chunk])[which]
        return slots.copy(("stage", chunk, which), buffer, target, sibling)

    def stage_wait(layer, chunk):
        @pl.when(core == layer)
        def _():
            for which in range(2):
                stage_copy(layer, chunk, which).wait()

        @pl.when(core != layer)
        def _():
            for which in range(2):
                stage_send(layer, chunk, which).wait_send()

    def feed_ahead():
        def slots_of(place, carry):
            rows = pl.ds(pl.multiple_of(place * S, S), S)
            for begin in range(0, units, CHUNK):
                cols = slice(begin, begin + CHUNK)
                for side in range(2):
                    ahead[side, rows, cols] = dot(middles[0, place], we[0, side, :, cols], NN).astype(BF16)
            return carry

        lax.fori_loop(0, Z, slots_of, 0)

    staged = []

    def feed_grads(layer, chunk):
        if chunk == 0:
            for place in range(Z):
                middle_cols[:, place * S : (place + 1) * S] = middles[layer, place].T
        cols = slice(chunk * CHUNK, (chunk + 1) * CHUNK)
        scale_up, scale_gate = us[layer, 0:1, cols], us[layer, 1:2, cols]

        def slots_of(place, sums):
            rows = slice(place * S, (place + 1) * S) if layer else pl.ds(pl.multiple_of(place * S, S), S)
            if layer:
                up = dot(middles[layer, place], we[layer, 0, :, cols], NN)
                gate = dot(middles[layer, place], we[layer, 1, :, cols], NN)
            else:
                up, gate = ahead[0, rows, cols].astype(F32), ahead[1, rows, cols].astype(F32)
            slope_hidden = dot(feed_low[layer, place], wr[layer, cols, :], NT)
            silu, by_up, by_gate = act_back(layer, cols, up, gate, slope_hidden)
            hidden_part[:, rows] = (scale_up * up * silu).astype(BF16).T
            up_part[rows, :] = (by_up * scale_up).astype(BF16)
            gate_part[rows, :] = (by_gate * scale_gate).astype(BF16)
            return sums[0] + jnp.sum(by_up * up, axis=0, keepdims=True), sums[1] + jnp.sum(by_gate * gate, axis=0, keepdims=True)

        sums = (jnp.zeros((1, CHUNK), F32), jnp.zeros((1, CHUNK), F32))
        if layer:
            for place in range(Z):
                sums = slots_of(place, sums)
        else:
            sums = lax.fori_loop(0, Z, slots_of, sums)
        sum_up, sum_gate = sums
        finals[layer, 2:3, cols] = sum_up
        finals[layer, 3:4, cols] = sum_gate
        if len(staged) >= 2:
            stage_wait(*staged[-2])
        buffer = chunk % 2
        stage_e[buffer, 0] = dot(middle_cols[...], up_part[...], NN).astype(BF16)
        stage_e[buffer, 1] = dot(middle_cols[...], gate_part[...], NN).astype(BF16)
        stage_r[buffer] = dot(hidden_part[...], feed_low[layer].reshape(Z * S, D), NN).astype(BF16)

        @pl.when(core == layer)
        def _():
            for which in range(2):
                stage_copy(layer, chunk, which).start()

        @pl.when(core != layer)
        def _():
            for which in range(2):
                stage_send(layer, chunk, which).start()

        staged.append((layer, chunk))

    chunks = units // CHUNK
    projected = 3 * HDIM
    def attn_pair():
        return [slots.copy("head", attn_own, attn_sib, sibling), slots.copy("scale", scale_own, scale_sib, sibling)]

    def go_pair():
        return [slots.copy("go", go_out, go_sib, sibling)]

    def go_spread():
        return [
            slots.copy(("go", k), go_out.at[peer], go_in.at[k], device) for k, (peer, device) in enumerate(zip(place_peers, place_ids))
        ]

    def offer(layer, pair):
        @pl.when(core != layer)
        def _():
            for copy in pair():
                copy.start()

    def go_join(layer):
        @pl.when(core == layer)
        def _():
            for copy in go_pair():
                copy.wait_recv()
            go_out[...] = (go_out[...].astype(F32) + go_sib[...].astype(F32)).astype(BF16)
            for copy in go_spread():
                copy.start()

        @pl.when(core != layer)
        def _():
            for copy in go_pair():
                copy.wait_send()

    attn_lines = [
        Line("heads line", lambda place: [attn_all.at[place, :projected], scale_all.at[place]], core == layer) for layer in range(2)
    ]
    go_lines = [Line("go line", lambda place: [attn_all.at[place, projected:]], core == layer) for layer in range(2)]

    def go_finish(layer):
        @pl.when(core == layer)
        def _():
            for copy in go_spread():
                copy.wait_recv()
            total = go_out[z].astype(F32)
            for k in range(Z - 1):
                total = total + go_in[k].astype(F32)
            attn_all[z, projected:] = total.astype(BF16)
            for copy in go_spread():
                copy.wait_send()

        go_lines[layer].step(0)

    def attn_join(layer):
        @pl.when(core == layer)
        def _():
            for copy in attn_pair():
                copy.wait_recv()
            attn_all[z, :projected] = (attn_own[...].astype(F32) + attn_sib[...].astype(F32)).astype(BF16)
            scale_all[z] = scale_own[...] + scale_sib[...]

        @pl.when(core != layer)
        def _():
            for copy in attn_pair():
                copy.wait_send()

        attn_lines[layer].step(0)

    def head_grads(layer, scale_slope):
        if layer:
            arrive(waiting["stream", 1])
        grad = None
        for place in range(Z):
            term = dot(heads_out[place].reshape(3 * HDIM, S), stream[layer, place], NN)
            grad = term if grad is None else grad + term
        attn_own[...] = grad.astype(BF16)
        scale_rows = jnp.broadcast_to(scale_slope, (HDIM, 128)).T[:8]
        scale_own[...] = jnp.concatenate([scale_rows, scale_rows], axis=1)
        offer(layer, attn_pair)

    def enter(layer, half, slope):
        rows = piece_of(half)
        middle_slope, feed_slope, alpha_m = blend_back(slope, middle_f[layer, rows], feed_f[layer, rows], al[layer, 1:2])
        copies = gather("feed_low", feed_low.at[layer, z], half, feed_slope.astype(BF16))
        return middle_slope, alpha_m, copies

    def backward(layer, base_low, entered, then):
        alpha = al[layer]
        alpha_own[layer, 1:2] = entered[0][1] + entered[1][1]
        if layer:
            stream_lines[1].step(3)
            waiting["stream", 1] = pass_on("stream", 1, stream, 2, [0])
        else:
            feed_lines[1].step(3)
        settle()
        if layer == 0:
            attn_join(1)
            go_finish(1)
        free("sums 0")
        back_copies = []
        for half in halves:
            arrive(entered[half][2])
            feed_all = half_of(feed_low.at[layer, z], half)
            for begin in range(0, units, CHUNK):
                cols = slice(begin, begin + CHUNK)
                slope_hidden = dot(feed_all, wr[layer, cols, :], NT)
                if layer:
                    up, gate = ups[half, :, cols].astype(F32), gates[half, :, cols].astype(F32)
                else:
                    rows = [pl.ds(pl.multiple_of(z * S + index * part + half * count, count), count) for index in range(T)]
                    up, gate = (
                        jnp.concatenate([ahead[side, group, cols] for group in rows], axis=0).astype(F32) for side in range(2)
                    )
                _, by_up, by_gate = act_back(layer, cols, up, gate, slope_hidden)
                expanded_low[0, :, cols] = (by_up * us[layer, 0:1, cols]).astype(BF16)
                expanded_low[1, :, cols] = (by_gate * us[layer, 1:2, cols]).astype(BF16)
            for begin in range(0, D, CHUNK):
                rows = slice(begin, begin + CHUNK)
                partial = dot(expanded_low[0], we[layer, 0, rows, :], NT) + dot(expanded_low[1], we[layer, 1, rows, :], NT)
                sums_out[0, half, :, :, rows] = partial.astype(BF16).reshape(T, count, CHUNK)
            back_copies.append(scatter(2, half))
            if layer and half == 0:
                middle_lines[1].step(1)
        used["sums 0"] = sum(back_copies, [])
        if layer:
            waiting["stream", 1] += pass_on("stream", 1, stream, 2, [1])
        feed_lines[layer].step(0)
        settle()
        if layer == 0:
            attn_lines[1].step(1)
            go_lines[1].step(1)
            feed_lines[1].passed()
            arrive(waiting["middle", 1])
            feed_grads(1, 0)
        free("branch_low")
        branch_copies, stream_slopes, alpha_a = [], [], None
        for half in halves:
            middle_total = entered[half][0] + scattered(2, half, back_copies[half])
            stream_slope, branch_slope, term = blend_back(
                middle_total, base_low[piece_of(half)].astype(F32), branch_f[layer, piece_of(half)], alpha[0:1]
            )
            branch_copies.append(gather("branch_low", branch_low, half, branch_slope.astype(BF16)))
            stream_slopes.append(stream_slope)
            alpha_a = term if alpha_a is None else alpha_a + term
        copies = sum(branch_copies, [])
        used["branch_low"] = copies
        alpha_own[layer, 0:1] = alpha_a
        if layer:
            waiting["stream", 1] += pass_on("stream", 1, stream, 2, [2])
            middle_lines[1].step(2)
            feed_ahead()
        else:
            alpha_copies = [send(("alpha", k), alpha_own, alpha_in.at[k], device) for k, device in enumerate(tensor_ids)]
            feed_lines[0].step(1)
            attn_lines[1].step(2)
            go_lines[1].step(2)
            feed_grads(1, 1)
        settle()
        arrive(copies)
        branch_all = branch_low[...]
        free("mixed_back")
        free("mixed")
        mixed_out[...] = dot(wo[layer], branch_all, NT).astype(BF16).reshape(H, HDIM, S)
        copies = spread("mixed_back", mixed_out, back_in)
        used["mixed_back"] = copies
        go_out[...] = dot(mixed_in[layer].reshape(inner, S), branch_all, NN).astype(BF16).reshape(H, HDIM, D)
        offer(layer, go_pair)
        if layer:
            feed_lines[1].step(1)
        else:
            feed_lines[0].step(2)
        if layer:
            middle_lines[1].step(3)
            waiting["middle", 1] = pass_on("middle", 1, middles)
        else:
            stream_lines[1].finish()
            middle_lines[1].finish()
        settle()
        if layer == 0:
            feed_grads(1, 2)
        for place in range(Z):
            turned_rows[place] = heads_in[layer, place, 2].T
        arrive(copies)
        if layer == 0:
            go_join(0)
            feed_lines[0].step(3)
        for query in range(Z):
            slope_mixed = back_in[query]
            lows = [probs[layer, block(query, key)] for key in range(query + 1)]
            probs_slope = [dot(turned_rows[key], slope_mixed, NN) for key in range(query + 1)]
            row_term = None
            for low, piece in zip(lows, probs_slope):
                term = jnp.sum(low.astype(F32) * piece, axis=0, keepdims=True)
                row_term = term if row_term is None else row_term + term
            query_slope = None
            for key in range(query + 1):
                low = lows[key]
                scores_low = (low.astype(F32) * (probs_slope[key] - row_term)).astype(BF16)
                term = dot(heads_in[layer, key, 1], scores_low, NN)
                query_slope = term if query_slope is None else query_slope + term
                key_term = dot(heads_in[layer, query, 0], scores_low, NT)
                value_term = dot(slope_mixed, low, NT)
                if key == query:
                    key_grad[key] = key_term
                    value_grad[key] = value_term
                else:
                    key_grad[key] += key_term
                    value_grad[key] += value_term
            query_grad[query] = query_slope
        free("heads_back")
        free("heads")
        scale = scales[layer, z][:, :1]
        inverse = 1.0 / scale
        scale_slope = None
        for place in range(Z):
            cosine_there, sine_there = cosines[place], sines[place]
            for third, source in ((0, query_grad), (1, key_grad)):
                piece = source[place] * math.sqrt(HDIM)
                unit = heads_in[layer, place, third].astype(F32) * inverse
                term = jnp.sum(piece * unit, axis=1, keepdims=True)
                scale_slope = term if scale_slope is None else scale_slope + term
                piece = piece * scale
                piece = rates_in[layer, place, third : third + 1] * (piece - unit * jnp.sum(unit * piece, axis=0, keepdims=True))
                front, back = piece[:turn], piece[turn:]
                piece = jnp.concatenate([front * cosine_there + back * sine_there, back * cosine_there - front * sine_there], axis=0)
                heads_out[place, third] = piece.astype(BF16)
            heads_out[place, 2] = value_grad[place].astype(BF16)
        copies = spread("heads_back", heads_out, heads_back_in)
        used["heads_back"] = copies
        settle()
        if layer:
            feed_lines[1].step(2)
        else:
            head_grads(layer, scale_slope)
            attn_join(0)
            feed_grads(1, 3)
            go_finish(0)
            arrive(alpha_copies)
            retire(alpha_copies)
            total = alpha_own[...]
            for k in range(T - 1):
                total = total + alpha_in[k]
            alpha_own[...] = total
            alpha_copies = [
                send(("alpha", T - 1 + k), alpha_own, alpha_in.at[T - 1 + k], device) for k, device in enumerate(place_ids)
            ]
        if layer == 0:
            feed_lines[0].passed()
            feed_grads(0, 0)
            attn_lines[0].step(1)
        arrive(copies)
        partial = None
        for third in range(3):
            term = dot(heads_back_in[:, third].reshape(inner, S).T, wp[layer, third], NT)
            partial = term if partial is None else partial + term
        free("sums 1")
        partial = partial.astype(BF16).reshape(T, HALVES, count, D)
        copies = []
        for half in halves:
            sums_out[1, half] = partial[:, half]
            copies.append(scatter(3, half))
        settle()
        if layer:
            head_grads(layer, scale_slope)
            go_join(1)
        else:
            feed_grads(0, 1)
            go_lines[0].step(1)
        for half in halves:
            result = (stream_slopes[half] + scattered(3, half, copies[half])).astype(BF16)
            outs[1, layer, piece_of(half)] = result
            then(half, result)
        used["sums 1"] = sum(copies, [])
        if layer == 0:
            waiting["alpha"] = alpha_copies

    next_stream, entered_last, entered_first = [], [], []

    def to_second(half, result):
        next_stream.extend(gather("stream", stream.at[1, z], half, result))

    def to_backward(half, result):
        entered_last.append(enter(1, half, cot_ref[core, 0, piece_of(half)].astype(F32)))

    def to_first(half, result):
        entered_first.append(enter(0, half, result.astype(F32)))

    forward(0, acts_ref.at[core, 0], first_stream, to_second)
    forward(1, outs.at[0, 0], next_stream, to_backward)
    backward(1, outs.at[0, 0], entered_last, to_first)
    backward(0, acts_ref.at[core, 0], entered_first, lambda half, result: None)

    other = 1 - core
    last = [send("outs", outs.at[:, other], outs_in, sibling)]
    attn_lines[0].step(2)
    feed_grads(0, 2)
    go_lines[0].step(2)
    for line in feed_lines:
        line.finish()
    for line in (attn_lines[1], go_lines[1]):
        line.step(3)
        line.finish()
    arrive(waiting["alpha"])
    total = alpha_own[...]
    for k in range(Z - 1):
        total = total + alpha_in[T - 1 + k]
    finals[0, 0:2] = total[0]
    finals[1, 0:2] = total[1]
    settle(2)
    feed_grads(0, 3)
    last += [send("finals", finals.at[other], finals_in, sibling)]
    for kind, target in enumerate((lo_ref, ig_ref)):
        target[core] = outs[kind, core]
    arrive(last)
    for kind, target in enumerate((lo_ref, ig_ref)):
        target[other] = outs_in[kind]
    small_ref[0:4] = finals[core] + finals_in[...]
    for layer, chunk in staged[-2:]:
        stage_wait(layer, chunk)
    for chunk in range(chunks):
        for which in range(2):
            stage_send(0, chunk, which).wait_recv()
    attn_lines[0].step(3)
    go_lines[0].step(3)
    attn_out = pltpu.make_async_copy(attn_all, attn_ref, stage_sem.at[0, 0, 0])
    attn_out.start()
    for place in range(Z):
        small_ref[4:5, place * HDIM : (place + 1) * HDIM] = scale_all[place, :1, :HDIM]
    settle(0)
    for piece in range(len(weights)):
        weight_copy(piece).wait_send()
    attn_lines[0].finish()
    go_lines[0].finish()
    attn_out.wait()
    assert len(slots.names) == COPIES, len(slots.names)


def relay(sizes, lengths, acts, cot, qs, us, al, wp, wo, we, wr):
    T, Z, S, part = sizes.tensors, sizes.places, sizes.local, sizes.part
    H, inner, units, D = sizes.heads, sizes.inner, sizes.units, sizes.width
    blocks, chunks = Z * (Z + 1) // 2, units // CHUNK
    vmem = pl.BlockSpec(memory_space=pltpu.VMEM)
    hbm = pl.BlockSpec(memory_space=pl.ANY)
    out_shape = (
        jax.ShapeDtypeStruct((2, part, D), BF16),
        jax.ShapeDtypeStruct((2, part, D), BF16),
        jax.ShapeDtypeStruct((8, D), F32),
        jax.ShapeDtypeStruct((Z, 4 * HDIM, D), BF16),
        jax.ShapeDtypeStruct((2, chunks, 2, D, CHUNK), BF16),
        jax.ShapeDtypeStruct((2, chunks, CHUNK, D), BF16),
    )
    DMA = pltpu.SemaphoreType.DMA
    V = pltpu.VMEM
    scratch = [
        V((2, 3, D, inner), BF16), V((2, inner, D), BF16), V((2, 2, D, units), BF16), V((2, units, D), BF16),
        V((2, 1, inner), F32), V((2, 2, units), F32), V((2, 2, D), F32),
        V((2, Z, S, D), BF16), V((2, Z, S, D), BF16), V((2, Z, S, D), BF16), V((S, D), BF16),
        V((Z, HDIM // 2, S), F32), V((Z, HDIM // 2, S), F32), V((2, H, HDIM, 128), F32),
        V((2, Z, 3, HDIM, S), BF16), V((2, Z, 2, S), F32),
        V((2, blocks, S, S), BF16), V((2, H, HDIM, S), BF16),
        V((2, HALVES, T - 1, part // HALVES, D), BF16),
        V((2, part, D), F32), V((2, part, D), F32), V((2, part, D), F32),
        V((HALVES, S // HALVES, units), BF16), V((HALVES, S // HALVES, units), BF16),
        V((S // HALVES, units), BF16), V((2, S // HALVES, units), BF16),
        V((Z, HDIM, S), BF16), V((H, 3, HDIM, S), BF16),
        V((H, 3, HDIM, S), BF16), V((H, 2, S), F32),
        V((Z, HDIM, S), BF16),
        V((2, HALVES, T, part // HALVES, D), BF16), V((H, HDIM, D), BF16), V((H, HDIM, D), BF16), V((Z - 1, HDIM, D), BF16),
        V((2, 2, part, D), BF16), V((2, part, D), BF16),
        V((Z, S, HDIM), BF16),
        V((Z, HDIM, S), F32), V((Z, HDIM, S), F32), V((Z, HDIM, S), F32),
        V((3 * HDIM, D), BF16), V((3 * HDIM, D), BF16), V((Z, 4 * HDIM, D), BF16),
        V((8, 128), F32), V((8, 128), F32), V((Z, 8, 128), F32),
        V((2, 2, D), F32), V((T + Z - 2, 2, 2, D), F32), V((2, 4, D), F32), V((4, D), F32),
        V((D, Z * S), BF16), V((CHUNK, Z * S), BF16), V((Z * S, CHUNK), BF16), V((Z * S, CHUNK), BF16),
        V((2, 2, D, CHUNK), BF16), V((2, CHUNK, D), BF16), V((2, D // 16, 2, units), BF16),
        V((2, Z * S, units), BF16),
        DMA((2, 8)), DMA((8,)), DMA((COPIES,)), DMA((COPIES,)), DMA((2, chunks, 2)), DMA((2,)),
    ]
    return pl.pallas_call(
        functools.partial(relay_kernel, sizes),
        out_shape=out_shape,
        in_specs=[pl.BlockSpec(memory_space=pltpu.SMEM), vmem, vmem, vmem, vmem, vmem, hbm, hbm, hbm, hbm],
        out_specs=(vmem, vmem, vmem, hbm, hbm, hbm),
        scratch_shapes=scratch,
        compiler_params=pltpu.CompilerParams(collective_id=0, has_side_effects=True, vmem_limit_bytes=63 * 2**20),
        name="relay",
    )(lengths, acts, cot, qs, us, al, wp, wo, we, wr)


def finish_kernel(
    attn_ref, ge_ref, gr_ref, lo_in, ig_in, small_ref,
    projection_ref, output_ref, expansion_ref, reduction_ref, lo_ref, ig_ref, scale_ref, units_ref, alphas_ref,
):
    @pl.when(pl.program_id(0) == 0)
    def _():
        lo_ref[...] = lo_in[...]
        ig_ref[...] = ig_in[...]
        alphas_ref[...] = small_ref[0:2]
        units_ref[...] = small_ref[2:4, : units_ref.shape[1]]
        scale_ref[...] = small_ref[4:5, : scale_ref.shape[1]]

    places, chunks = attn_ref.shape[0], ge_ref.shape[1]
    for begin in range(0, ge_ref.shape[3], 16):
        rows = slice(begin, begin + 16)
        pieces = []
        for chunk in range(chunks):
            for lanes in (slice(0, 128), slice(128, 256)):
                for side in range(2):
                    total = ge_ref[0, chunk, side, rows, lanes].astype(F32) + ge_ref[1, chunk, side, rows, lanes].astype(F32)
                    pieces.append(total[None])
        expansion_ref[rows] = jnp.swapaxes(jnp.concatenate(pieces, axis=0), 0, 1)
    reduction_ref[...] = gr_ref[0].astype(F32) + gr_ref[1].astype(F32)
    for third in range(3):
        rows = attn_ref[:, third * HDIM : (third + 1) * HDIM, :].astype(F32)
        projection_ref[third] = rows.reshape(places * HDIM, rows.shape[2]).T
    output_ref[...] = attn_ref[:, 3 * HDIM :, :].astype(F32).reshape(output_ref.shape)


def finish(attn, ge, gr, lo, ig, small):
    places, _, D = attn.shape
    chunks, units, inner = ge.shape[1], ge.shape[1] * CHUNK, places * HDIM
    block = 256
    steps = D // block
    rows = units // steps

    def whole(shape):
        return pl.BlockSpec(shape, lambda i: (0,) * len(shape))

    return pl.pallas_call(
        finish_kernel,
        grid=(steps,),
        in_specs=[
            pl.BlockSpec((places, 4 * HDIM, block), lambda i: (0, 0, i)),
            pl.BlockSpec((2, chunks, 2, block, CHUNK), lambda i: (0, 0, 0, i, 0)),
            pl.BlockSpec((2, rows, D), lambda i: (0, i, 0)),
            whole(lo.shape),
            whole(ig.shape),
            whole(small.shape),
        ],
        out_specs=(
            pl.BlockSpec((3, block, inner), lambda i: (0, i, 0)),
            pl.BlockSpec((inner, block), lambda i: (0, i)),
            pl.BlockSpec((block, units // 64, 128), lambda i: (i, 0, 0)),
            pl.BlockSpec((rows, D), lambda i: (i, 0)),
            whole(lo.shape),
            whole(ig.shape),
            whole((1, inner)),
            whole((2, units)),
            whole((2, D)),
        ),
        out_shape=(
            jax.ShapeDtypeStruct((3, D, inner), F32),
            jax.ShapeDtypeStruct((inner, D), F32),
            jax.ShapeDtypeStruct((D, units // 64, 128), F32),
            jax.ShapeDtypeStruct((units, D), F32),
            jax.ShapeDtypeStruct(lo.shape, BF16),
            jax.ShapeDtypeStruct(ig.shape, BF16),
            jax.ShapeDtypeStruct((1, inner), F32),
            jax.ShapeDtypeStruct((2, units), F32),
            jax.ShapeDtypeStruct((2, D), F32),
        ),
        compiler_params=pltpu.CompilerParams(vmem_limit_bytes=60 * 2**20),
        name="finish",
    )(attn, ge, gr.reshape(2, units, D), lo, ig, small)


def fast_body(
    activations, lengths, projection, output_weight, expansion, reduction, query_scale, unit_scales, alphas, cotangent
):
    _, _, part, width = activations.shape
    inner, units = output_weight.shape[1], reduction.shape[1]
    places = lax.axis_size("dp")
    sizes = Sizes(lax.axis_size("tensor"), places, part, width, inner, units)
    lo, ig, small, attn, ge, gr = relay(
        sizes, lengths, activations, cotangent, query_scale, unit_scales[0], alphas[0],
        projection[0].transpose(1, 0, 2), output_weight[0], expansion[0], reduction[0],
    )
    projection_grad, output_grad, expansion_grad, reduction_grad, lo, ig, scale_grad, unit_grad, alpha_grad = finish(
        attn, ge, gr, lo, ig, small
    )
    columns = units // 128
    expansion_grad = expansion_grad.reshape(width, columns, 2, 128).transpose(0, 2, 1, 3).reshape(width, 2, units)
    projection_grad = projection_grad.transpose(1, 0, 2)
    return (
        lo[None, :, None],
        ig[None, :, None],
        projection_grad[None],
        output_grad[None],
        expansion_grad[None],
        reduction_grad[None],
        scale_grad,
        unit_grad[None],
        alpha_grad[None],
    )


def solution(mesh):
    in_specs = (
        P(None, None, ("dp", "tensor"), None),
        P(),
        P("section", None, None, "tensor"),
        P("section", "tensor", None),
        P("section", None, None, "tensor"),
        P("section", "tensor", None),
        P("section", "tensor"),
        P("section", None, "tensor"),
        P("section", None, None),
        P(None, None, ("dp", "tensor"), None),
    )
    out_specs = (
        P("section", None, None, ("dp", "tensor"), None),
        P("section", None, None, ("dp", "tensor"), None),
        P("section", None, None, "tensor"),
        P("section", "tensor", None),
        P("section", None, None, "tensor"),
        P("section", "tensor", None),
        P("section", "tensor"),
        P("section", None, "tensor"),
        P("section", None, None),
    )
    def chosen(*arrays):
        activations, output_weight = arrays[0], arrays[3]
        heads = output_weight.shape[1] // HDIM
        fits = (
            mesh.shape["section"] == 2
            and mesh.shape["tensor"] == 4
            and mesh.shape["dp"] == heads
            and activations.shape[:2] == (2, 1)
            and activations.shape[2] * mesh.shape["tensor"] == 256
        )
        return (fast_body if fits else body)(*arrays)

    return jax.shard_map(chosen, mesh=mesh, in_specs=in_specs, out_specs=out_specs, check_vma=False)
```

```python
import functools
import math

import jax
import jax.numpy as jnp
from jax import lax
from jax.experimental import pallas as pl
from jax.experimental.pallas import tpu as pltpu
from jax.sharding import PartitionSpec as P

HDIM = 64


def from_behind(value, axis, steps):
    count = lax.axis_size(axis)
    initial, last = (max(0, -steps), min(count, count - steps))
    return lax.ppermute(value, axis, [(source, source + steps) for source in range(initial, last)])


def normed(v):
    return v * lax.rsqrt(jnp.mean(v * v, axis=-1, keepdims=True) + 1e-06)


def unit_heads(v):
    return v * lax.rsqrt(jnp.sum(v * v, axis=-1, keepdims=True) + 1e-06)


def frequencies(half):
    return jnp.exp(jnp.arange(half, dtype=jnp.float32) * (-2.0 * math.log(10000.0) / (2 * half)))


def rotate(view, angle):
    half = view.shape[-1] // 2
    cosine = jnp.cos(angle)[..., None, :]
    sine = jnp.sin(angle)[..., None, :]
    front = view[..., :half]
    back = view[..., half:]
    return jnp.concatenate([front * cosine - back * sine, back * cosine + front * sine], axis=-1)


def shaped(projected, scale, angle, heads):
    inner = projected.shape[-1] // 3
    lead = projected.shape[:-1]

    def turned(piece):
        view = piece.reshape(lead + (heads, inner // heads))
        return unit_heads(rotate(view, angle)).reshape(lead + (inner,)) * scale

    return (
        turned(projected[..., :inner]),
        turned(projected[..., inner : 2 * inner]),
        projected[..., 2 * inner :],
    )


def layout(lengths_row, slots):
    ends = jnp.cumsum(lengths_row, dtype=jnp.int32)
    index = jnp.arange(slots, dtype=jnp.int32)
    after = index[:, None] >= ends[None, :]
    segment = jnp.sum(after.astype(jnp.int32), axis=1, dtype=jnp.int32)
    begin = jnp.sum(jnp.where(after, lengths_row[None, :], 0), axis=1, dtype=jnp.int32)
    inside = index < ends[-1]
    segment = jnp.where(inside, segment, lengths_row.shape[0] + index)
    position = jnp.where(inside, index - begin, 0)
    return (segment, position)


def blend(base, branch, alpha):
    return normed(base + alpha * (normed(branch) - base))


def activate(expanded, scales):
    half = expanded.shape[-1] // 2
    return expanded[..., :half] * scales[0] * jax.nn.silu(expanded[..., half:] * scales[1])


def placing(lengths_now, local):
    slots = local * lax.axis_size("dp")
    start_here = lax.axis_index("dp") * local
    segment_all, position_all = jax.vmap(lambda row: layout(row, slots))(lengths_now)
    segment_here = lax.dynamic_slice_in_dim(segment_all, start_here, local, 1)
    position_here = lax.dynamic_slice_in_dim(position_all, start_here, local, 1)
    index_here = start_here + jnp.arange(local, dtype=jnp.int32)
    every = jnp.arange(slots, dtype=jnp.int32)
    allowed = (segment_here[:, :, None] == segment_all[:, None, :]) & (
        every[None, None, :] <= index_here[None, :, None]
    )
    angle = position_here.astype(jnp.float32)[..., None] * frequencies(HDIM // 2)
    return (allowed, angle)


def scored(query, key_all, allowed, heads):
    rows, local, inner = query.shape
    depth = inner // heads
    query_heads = query.reshape(rows, local, heads, depth)
    key_heads = key_all.reshape(rows, key_all.shape[1], heads, depth)
    raw = jnp.einsum(
        "rqhe,rkhe->rhqk", query_heads, key_heads, preferred_element_type=jnp.float32
    ) * math.sqrt(depth)
    return jnp.where(allowed[:, None], raw, -1e30)


def forward(stream, lengths_now, weights):
    projection, output_weight, expansion, reduction, query_scale, unit_scales, alphas = weights
    rows, part, width = stream.shape
    inner = output_weight.shape[0]
    heads = inner // HDIM
    hidden_width = reduction.shape[0]
    gathered = lax.all_gather(stream.astype(jnp.bfloat16), "tensor", axis=1, tiled=True)
    local = gathered.shape[1]
    allowed, angle = placing(lengths_now, local)
    projected = jnp.einsum(
        "rsd,dc->rsc",
        gathered,
        projection.reshape(width, 3 * inner),
        preferred_element_type=jnp.float32,
    )
    query, key, value = shaped(projected, query_scale, angle, heads)
    query_low = query.astype(jnp.bfloat16)
    key_low = key.astype(jnp.bfloat16)
    value_low = value.astype(jnp.bfloat16)
    key_all, value_all = (
        lax.all_gather(key_low, "dp", axis=1, tiled=True),
        lax.all_gather(value_low, "dp", axis=1, tiled=True),
    )
    scores = scored(query_low, key_all, allowed, heads)
    highest = jnp.max(scores, axis=-1, keepdims=True)
    lifted = jnp.exp(scores - highest)
    total = jnp.sum(lifted, axis=-1, keepdims=True)
    log_total = highest + jnp.log(total)
    probs_low = (lifted / total).astype(jnp.bfloat16)
    value_heads = value_all.reshape(rows, value_all.shape[1], heads, HDIM)
    mixed = jnp.einsum(
        "rhqk,rkhe->rqhe", probs_low, value_heads, preferred_element_type=jnp.float32
    )
    attended = mixed.reshape(rows, local, inner).astype(jnp.bfloat16)
    partial_branch = jnp.einsum(
        "rsc,cd->rsd", attended, output_weight, preferred_element_type=jnp.float32
    )
    branch = lax.psum_scatter(partial_branch, "tensor", scatter_dimension=1, tiled=True)
    middle = blend(stream, branch, alphas[0])
    middle_all = lax.all_gather(middle.astype(jnp.bfloat16), "tensor", axis=1, tiled=True)
    expanded = jnp.einsum(
        "rsd,dc->rsc",
        middle_all,
        expansion.reshape(width, 2 * hidden_width),
        preferred_element_type=jnp.float32,
    )
    hidden = activate(expanded, unit_scales).astype(jnp.bfloat16)
    partial_feed = jnp.einsum("rsf,fd->rsd", hidden, reduction, preferred_element_type=jnp.float32)
    feed = lax.psum_scatter(partial_feed, "tensor", scatter_dimension=1, tiled=True)
    result = blend(middle, feed, alphas[1])
    kept = dict(
        stream=stream,
        gathered=gathered,
        projected=projected,
        query=query_low,
        key=key_low,
        value=value_low,
        log_total=log_total,
        attended=attended,
        branch=branch,
        middle=middle,
        middle_all=middle_all,
        expanded=expanded,
        hidden=hidden,
        feed=feed,
        lengths=lengths_now,
    )
    kept = dict(kept, key_all=key_all, value_all=value_all)
    return (result, kept)


def backward(slope, kept, weights):
    projection, output_weight, expansion, reduction, query_scale, unit_scales, alphas = weights
    rows, part, width = slope.shape
    inner = output_weight.shape[0]
    heads = inner // HDIM
    hidden_width = reduction.shape[0]
    _, pull_feed = jax.vjp(blend, kept["middle"], kept["feed"], alphas[1])
    middle_slope, feed_slope, alpha_feed = pull_feed(slope)
    feed_all = lax.all_gather(feed_slope.astype(jnp.bfloat16), "tensor", axis=1, tiled=True)
    reduction_grad = jnp.einsum(
        "rsf,rsd->fd", kept["hidden"], feed_all, preferred_element_type=jnp.float32
    )
    hidden_slope = jnp.einsum(
        "rsd,fd->rsf", feed_all, reduction, preferred_element_type=jnp.float32
    )
    _, pull_active = jax.vjp(activate, kept["expanded"], unit_scales)
    expanded_slope, unit_grad = pull_active(hidden_slope)
    expanded_low = expanded_slope.astype(jnp.bfloat16)
    expansion_grad = jnp.einsum(
        "rsd,rsc->dc", kept["middle_all"], expanded_low, preferred_element_type=jnp.float32
    ).reshape(width, 2, hidden_width)
    partial_middle = jnp.einsum(
        "rsc,dc->rsd",
        expanded_low,
        expansion.reshape(width, 2 * hidden_width),
        preferred_element_type=jnp.float32,
    )
    middle_total = middle_slope + lax.psum_scatter(
        partial_middle, "tensor", scatter_dimension=1, tiled=True
    )
    _, pull_branch = jax.vjp(blend, kept["stream"], kept["branch"], alphas[0])
    stream_slope, branch_slope, alpha_branch = pull_branch(middle_total)
    branch_all = lax.all_gather(branch_slope.astype(jnp.bfloat16), "tensor", axis=1, tiled=True)
    output_grad = jnp.einsum(
        "rsc,rsd->cd", kept["attended"], branch_all, preferred_element_type=jnp.float32
    )
    attended_low = jnp.einsum(
        "rsd,cd->rsc", branch_all, output_weight, preferred_element_type=jnp.float32
    ).astype(jnp.bfloat16)
    local = attended_low.shape[1]
    key_all = kept["key_all"]
    value_all = kept["value_all"]
    slots = key_all.shape[1]
    allowed, angle = placing(kept["lengths"], local)
    scores = scored(kept["query"], key_all, allowed, heads)
    probs = jnp.exp(scores - kept["log_total"])
    scale = math.sqrt(HDIM)
    back_heads = attended_low.reshape(rows, local, heads, HDIM)
    query_heads = kept["query"].reshape(rows, local, heads, HDIM)
    key_heads = key_all.reshape(rows, slots, heads, HDIM)
    value_heads = value_all.reshape(rows, slots, heads, HDIM)
    probs_slope = jnp.einsum(
        "rqhe,rkhe->rhqk", back_heads, value_heads, preferred_element_type=jnp.float32
    )
    row_term = jnp.sum(probs * probs_slope, axis=-1, keepdims=True)
    scores_low = (probs * (probs_slope - row_term)).astype(jnp.bfloat16)
    query_slope = (
        jnp.einsum("rhqk,rkhe->rqhe", scores_low, key_heads, preferred_element_type=jnp.float32)
        * scale
    )
    value_grad_all = jnp.einsum(
        "rhqk,rqhe->rkhe",
        probs.astype(jnp.bfloat16),
        back_heads,
        preferred_element_type=jnp.float32,
    )
    key_grad_all = (
        jnp.einsum("rhqk,rqhe->rkhe", scores_low, query_heads, preferred_element_type=jnp.float32)
        * scale
    )
    key_slope, value_slope = (
        lax.psum_scatter(
            key_grad_all.reshape(rows, slots, inner), "dp", scatter_dimension=1, tiled=True
        ),
        lax.psum_scatter(
            value_grad_all.reshape(rows, slots, inner), "dp", scatter_dimension=1, tiled=True
        ),
    )
    _, pull_shape = jax.vjp(
        lambda source, scale_now: shaped(source, scale_now, angle, heads),
        kept["projected"],
        query_scale,
    )
    projected_slope, query_scale_grad = pull_shape(
        (query_slope.reshape(rows, local, inner), key_slope, value_slope)
    )
    projected_low = projected_slope.astype(jnp.bfloat16)
    projection_grad = jnp.einsum(
        "rsd,rsc->dc", kept["gathered"], projected_low, preferred_element_type=jnp.float32
    ).reshape(width, 3, inner)
    partial_stream = jnp.einsum(
        "rsc,dc->rsd",
        projected_low,
        projection.reshape(width, 3 * inner),
        preferred_element_type=jnp.float32,
    )
    spread = jnp.broadcast_to(
        jnp.stack([alpha_branch, alpha_feed])[:, None, :], (2, lax.axis_size("tensor"), width)
    )
    stream_part, alpha_sum = (
        lax.psum_scatter(partial_stream, "tensor", scatter_dimension=1, tiled=True),
        lax.psum_scatter(spread, "tensor", scatter_dimension=1, tiled=True),
    )
    stream_total = stream_slope + stream_part
    return (
        stream_total,
        (
            projection_grad,
            output_grad,
            expansion_grad,
            reduction_grad,
            query_scale_grad,
            unit_grad,
            alpha_sum[:, 0],
        ),
    )


def body(
    activations,
    lengths,
    projection,
    output_weight,
    expansion,
    reduction,
    query_scale,
    unit_scales,
    alphas,
    cotangent,
):
    micro, rows, part, width = activations.shape
    section = lax.axis_index("section")
    first = section == 0
    weights = (
        projection[0],
        output_weight[0],
        expansion[0],
        reduction[0],
        query_scale[0],
        unit_scales[0],
        alphas[0],
    )
    steps = micro + 1
    received = jnp.zeros((rows, part, width), jnp.bfloat16)
    outputs = []
    keeps = []
    for step in range(steps):
        index_now = jnp.clip(step - section, 0, micro - 1)
        lengths_now = lax.dynamic_index_in_dim(lengths, index_now, 0, keepdims=False)
        stream = jnp.where(first, activations[min(step, micro - 1)], received).astype(jnp.float32)
        result, kept = forward(stream, lengths_now, weights)
        result_low = result.astype(jnp.bfloat16)
        outputs.append(result_low)
        keeps.append(kept)
        if step + 1 < steps:
            received = from_behind(result_low, "section", 1)
    stacked = jnp.stack(outputs)
    layer_output = jnp.where(first, stacked[:micro], stacked[1:])[None]
    back_received = jnp.zeros((rows, part, width), jnp.bfloat16)
    slopes = []
    summed = None
    for step in range(steps):
        batch_now = step - 1 + section
        valid = (batch_now >= 0) & (batch_now < micro)
        slope = jnp.where(first, back_received, cotangent[min(step, micro - 1)]).astype(jnp.float32)
        earlier = keeps[max(step - 1, 0)]
        later = keeps[min(step + 1, micro)]
        kept = jax.tree.map(lambda left, right: jnp.where(first, left, right), earlier, later)
        stream_total, layer_grads = backward(slope, kept, weights)
        stream_low = stream_total.astype(jnp.bfloat16)
        slopes.append(stream_low)
        masked = tuple((jnp.where(valid, piece, 0.0) for piece in layer_grads))
        summed = (
            masked
            if summed is None
            else tuple((left + right for left, right in zip(summed, masked)))
        )
        if step + 1 < steps:
            back_received = from_behind(stream_low, "section", -1)
    stacked_slopes = jnp.stack(slopes)
    input_gradient = jnp.where(first, stacked_slopes[1:], stacked_slopes[:micro])[None]
    (
        projection_grad,
        output_grad,
        expansion_grad,
        reduction_grad,
        query_scale_grad,
        unit_grad,
        alpha_grad,
    ) = summed
    totals = lax.psum(
        (
            projection_grad,
            output_grad,
            expansion_grad,
            reduction_grad,
            query_scale_grad,
            unit_grad,
            alpha_grad,
        ),
        "dp",
    )
    return (
        layer_output,
        input_gradient,
        totals[0][None],
        totals[1][None],
        totals[2][None],
        totals[3][None],
        totals[4][None],
        totals[5][None],
        totals[6][None],
    )


MESH_IDS = pl.DeviceIdType.MESH
F32, BF16 = jnp.float32, jnp.bfloat16
CHUNK = 256
NN = ((1,), (0,))
NT = ((1,), (1,))


def dot(left, right, dims):
    return lax.dot_general(left, right, (dims, ((), ())), preferred_element_type=F32)


def sigmoid(v):
    return 0.5 + 0.5 * jnp.tanh(0.5 * v)


def norm_parts(v):
    rate = lax.rsqrt(jnp.mean(v * v, axis=-1, keepdims=True) + 1e-06)
    return v * rate, rate


def norm_back(slope, unit, rate):
    return rate * (slope - unit * jnp.mean(unit * slope, axis=-1, keepdims=True))


def blend_back(slope, base, branch, alpha):
    unit_branch, rate_branch = norm_parts(branch)
    toward = unit_branch - base
    unit, rate = norm_parts(base + alpha * toward)
    inner_slope = norm_back(slope, unit, rate)
    alpha_slope = jnp.sum(inner_slope * toward, axis=0, keepdims=True)
    scaled = alpha * inner_slope
    return inner_slope - scaled, norm_back(scaled, unit_branch, rate_branch), alpha_slope


def sequence_starts(lengths_ref, row, index):
    begin = jnp.zeros_like(index)
    end = jnp.int32(0)
    for sequence in range(lengths_ref.shape[2]):
        end = end + lengths_ref[row, 0, sequence]
        begin = jnp.where(index >= end, end, begin)
    return jnp.where(index < end, begin, index)


class Sizes:
    def __init__(self, tensors, places, part, width, inner, units):
        self.tensors, self.places, self.part, self.width = tensors, places, part, width
        self.inner, self.units = inner, units
        self.local = part * tensors
        self.heads = inner // HDIM


class Slots:
    def __init__(self, send, recv):
        self.send, self.recv, self.names = send, recv, {}

    def copy(self, name, source, target, device):
        number = self.names.setdefault(name, len(self.names))
        return pltpu.make_async_remote_copy(
            source, target, self.send.at[number], self.recv.at[number], device_id=device, device_id_type=MESH_IDS
        )


HALVES = 2
COPIES = 211


def relay_kernel(
    sizes,
    lengths_ref, acts_ref, cot_ref, qs_ref, us_ref, al_ref, wp_ref, wo_ref, we_ref, wr_ref,
    lo_ref, ig_ref, small_ref, attn_ref, ge_ref, gr_ref,
    wp, wo, we, wr, qs, us, al,
    stream, middles, feed_low, branch_low,
    cosines, sines, scales,
    heads_in, rates_in, probs, mixed_in, sums_in, branch_f, middle_f, feed_f, ups, gates,
    hidden, expanded_low, back_in, heads_back_in,
    heads_out, rates_out, mixed_out, sums_out, go_out, go_sib, go_in,
    outs, outs_in, turned_rows, query_grad, key_grad, value_grad,
    attn_own, attn_sib, attn_all, scale_own, scale_sib, scale_all,
    alpha_own, alpha_in, finals, finals_in,
    middle_cols, hidden_part, up_part, gate_part, stage_e, stage_r, raw, ahead,
    weight_sem, weight_send, send_sem, recv_sem, stage_sem, raw_sem, out_sem,
):
    T, Z, S, part = sizes.tensors, sizes.places, sizes.local, sizes.part
    H, inner, units, D = sizes.heads, sizes.inner, sizes.units, sizes.width
    core, t, z = lax.axis_index("section"), lax.axis_index("tensor"), lax.axis_index("dp")
    sibling = (1 - core, t, z)
    side, row = lax.rem(t, 2), t // 2
    tensor_peers = [row * 2 + (1 - side), (1 - row) * 2 + side, (1 - row) * 2 + (1 - side)]
    place_peers = [lax.rem(z + k, Z) for k in range(1, Z)]
    tensor_ids = [(core, peer, z) for peer in tensor_peers]
    place_ids = [(core, t, peer) for peer in place_peers]
    slots = Slots(send_sem, recv_sem)
    pending = [[]]

    weights = [
        (wp_ref, lambda layer: wp.at[layer]),
        (wo_ref, lambda layer: wo.at[layer]),
        (we.at[core, 0], lambda layer: we.at[layer, 0]),
        (we.at[core, 1], lambda layer: we.at[layer, 1]),
        (wr_ref, lambda layer: wr.at[layer]),
        (qs_ref, lambda layer: qs.at[layer]),
        (us_ref, lambda layer: us.at[layer]),
        (al_ref, lambda layer: al.at[layer]),
    ]

    def weight_load(layer, piece):
        source, target = weights[piece]
        return pltpu.make_async_copy(source, target(layer), weight_sem.at[layer, piece])

    for piece in range(len(weights)):
        if piece not in (2, 3):
            weight_load(core, piece).start()

    raw_rows = raw.shape[1]

    def raw_load(block):
        return pltpu.make_async_copy(we_ref.at[pl.ds(block * raw_rows, raw_rows)], raw.at[block % 2], raw_sem.at[block % 2])

    for block in range(2):
        raw_load(block).start()

    def take_apart(blocks):
        for block in blocks:
            raw_load(block).wait()
            we[core, :, block * raw_rows : (block + 1) * raw_rows, :] = jnp.swapaxes(raw[block % 2], 0, 1)
            if (block + 2) * raw_rows < D:
                raw_load(block + 2).start()

    barrier = pltpu.get_barrier_semaphore()
    partners = [sibling] + tensor_ids + place_ids
    for partner in partners:
        pl.semaphore_signal(barrier, inc=1, device_id=partner, device_id_type=MESH_IDS)
    turn = HDIM // 2
    index_all = lax.broadcasted_iota(jnp.int32, (1, S * Z), 1)
    starts = sequence_starts(lengths_ref, core, index_all)
    rates = jnp.exp(lax.broadcasted_iota(jnp.int32, (turn, 1), 0).astype(F32) * (-2.0 * math.log(10000.0) / HDIM))
    angle = rates * (index_all - starts).astype(F32)
    cosine, sine = jnp.cos(angle), jnp.sin(angle)
    for place in range(Z):
        cosines[place] = cosine[:, place * S : (place + 1) * S]
        sines[place] = sine[:, place * S : (place + 1) * S]
    key_index = lax.broadcasted_iota(jnp.int32, (S * Z, S), 0)
    pl.semaphore_wait(barrier, len(partners))

    def weight_copy(piece):
        source, target = weights[piece]
        return pltpu.make_async_remote_copy(
            source, target(core), weight_send.at[piece], weight_sem.at[core, piece], device_id=sibling, device_id_type=MESH_IDS
        )

    def lend_weights(layer, pieces):
        @pl.when(core == layer)
        def _():
            for piece in pieces:
                weight_copy(piece).start()

    for piece in (5, 6, 7):
        weight_copy(piece).start()
    lend_weights(0, (0,))

    def await_weight(layer, piece):
        if piece in (2, 3):
            @pl.when(core != layer)
            def _():
                weight_load(layer, piece).wait()
        else:
            weight_load(layer, piece).wait()

    def send(name, source, target, device):
        copy = slots.copy(name, source, target, device)
        copy.start()
        pending[-1].append(copy)
        return copy

    def settle(keep=4):
        pending.append([])
        while len(pending) > keep:
            for copy in pending.pop(0):
                copy.wait_send()

    def arrive(copies):
        for copy in copies:
            copy.wait_recv()

    def rows_of(index):
        return pl.ds(pl.multiple_of(index * part, part), part)

    my_rows, far_rows = rows_of(t), rows_of(tensor_peers[2])

    def gather(name, target, half, value):
        count = value.shape[0]
        rows = pl.ds(pl.multiple_of(t * part + half * count, count), count)
        target[rows, :] = value
        mine = target.at[rows, :]
        return [send((name, half, k), mine, mine, device) for k, device in enumerate(tensor_ids)]

    def half_of(target, half):
        return jnp.concatenate([target[index * part + half * count : index * part + (half + 1) * count, :] for index in range(T)], axis=0)

    count = part // HALVES
    halves = range(HALVES)

    def piece_of(half):
        return slice(half * count, (half + 1) * count)

    class Line:
        def __init__(self, name, views, guard=None, passes=0):
            self.name, self.views, self.guard, self.passes = name, views, guard, passes

        def copies(self, way, step, origin):
            device = (core, t, z + 1) if way == 0 else (core, t, z - 1)
            return [slots.copy((self.name, way, step, k), view, view, device) for k, view in enumerate(self.views(origin))]

        def when(self, condition):
            return pl.when(condition if self.guard is None else condition & self.guard)

        def origin(self, way, step):
            return z - step if way == 0 else z + step

        def sends(self, way, step):
            return (z >= step) & (z + 1 < Z) if way == 0 else (z + step < Z) & (z >= 1)

        def comes(self, way, step):
            return z >= step if way == 0 else z + step < Z

        def passing(self, way, step):
            got = self.views(self.origin(way, step))[0]
            return [slots.copy((self.name, "pass", way, step, k), got, got, tensor_ids[k]) for k in range(self.passes)]

        def passed(self):
            for way in range(2):
                for step in range(1, Z):
                    @self.when(self.comes(way, step))
                    def _():
                        for copy in self.passing(way, step):
                            copy.wait_recv()

        def step(self, step):
            for way in range(2):
                if step > 0:
                    @self.when(self.comes(way, step))
                    def _():
                        for copy in self.copies(way, step - 1, self.origin(way, step)):
                            copy.wait_recv()
                        for copy in self.passing(way, step):
                            copy.start()

                if step < Z - 1:
                    @self.when(self.sends(way, step))
                    def _():
                        for copy in self.copies(way, step, self.origin(way, step)):
                            copy.start()

        def finish(self):
            for way in range(2):
                for step in range(Z - 1):
                    @self.when(self.sends(way, step))
                    def _():
                        for copy in self.copies(way, step, self.origin(way, step)):
                            copy.wait_send()

                    @self.when(self.comes(way, step + 1))
                    def _():
                        for copy in self.passing(way, step + 1):
                            copy.wait_send()

    def row_line(name, layer, target, groups, passes=0):
        return Line((name, len(groups)), lambda place: [target.at[layer, place, rows, :] for rows in groups], None, passes)

    def pass_on(name, layer, target, count=2, indices=range(Z - 1)):
        passed = []
        for index in indices:
            got = target.at[layer, place_peers[index], my_rows, :]
            passed += [send((name, "pass", index, k), got, got, device) for k, device in enumerate(tensor_ids[:count])]
        return passed

    def scatter(number, half):
        return [
            send((number % 2, half, k), sums_out.at[number % 2, half, peer], sums_in.at[number % 2, half, k], device)
            for k, (peer, device) in enumerate(zip(tensor_peers, tensor_ids))
        ]

    def scattered(number, half, copies):
        arrive(copies)
        total = sums_out[number % 2, half, t].astype(F32)
        for k in range(T - 1):
            total = total + sums_in[number % 2, half, k].astype(F32)
        return total

    def retire(copies):
        for copy in copies:
            for group in pending:
                if any(copy is other for other in group):
                    copy.wait_send()
                    group[:] = [other for other in group if other is not copy]

    def spread(name, source, target):
        target[z] = source[z]
        return [
            send((name, k), source.at[peer], target.at[z], device) for k, (peer, device) in enumerate(zip(place_peers, place_ids))
        ]

    def block(query, key):
        return query * (query + 1) // 2 + key

    used, waiting = {}, {}
    first_line = row_line("first line", 0, stream, [my_rows], 2)
    stream_lines = [row_line("stream line", 0, stream, [far_rows]), row_line("stream line", 1, stream, [my_rows, far_rows])]
    middle_lines = [row_line("middle line", layer, middles, [my_rows, far_rows], 2 - 2 * layer) for layer in range(2)]
    feed_lines = [row_line("feed line", layer, feed_low, [my_rows, far_rows][: layer + 1], 3 - layer) for layer in range(2)]

    def free(name):
        retire(used.pop(name, []))

    first_stream = gather("stream", stream.at[0, z], 0, acts_ref[core, 0])
    first_line.step(0)

    def forward(layer, base_low, stream_copies, then):
        if layer == 0:
            take_apart(range(0, D // raw_rows // 2))
        await_weight(layer, 0)
        for piece in (5, 6, 7):
            await_weight(layer, piece)
        scale = jnp.broadcast_to(jnp.broadcast_to(qs[layer], (8, inner)).T[:, :1], (inner, 128)).reshape(H, HDIM, 128)
        scales[layer] = scale
        cosine_here, sine_here = cosines[z][None], sines[z][None]
        arrive(stream_copies)
        free("heads")
        gathered = stream[layer, z]
        for third in range(3):
            piece = dot(gathered, wp[layer, third], NN).T.reshape(H, HDIM, S)
            if third < 2:
                front, back = piece[:, :turn], piece[:, turn:]
                piece = jnp.concatenate([front * cosine_here - back * sine_here, back * cosine_here + front * sine_here], axis=1)
                speed = lax.rsqrt(jnp.sum(piece * piece, axis=1, keepdims=True) + 1e-06)
                piece = piece * speed * scale[:, :, :1]
                for head in range(H):
                    rates_out[head, third : third + 1] = speed[head]
            heads_out[:, third] = piece.astype(BF16)
        copies = spread("heads", heads_out, heads_in.at[layer])
        rate_copies = spread("rates", rates_out, rates_in.at[layer])
        used["heads"] = copies + rate_copies
        if layer == 0:
            first_line.step(1)
            take_apart(range(D // raw_rows // 2, D // raw_rows))
        else:
            middle_lines[0].step(2)
        lend_weights(layer, (1, 2))
        settle()
        if layer:
            first_line.step(3)
        arrive(copies + rate_copies)
        if layer:
            middle_lines[0].step(3)
        for place in range(Z):
            turned_rows[place] = heads_in[layer, place, 1].T
        free("mixed")
        for query in range(Z):
            raw = [dot(turned_rows[key], heads_in[layer, query, 0], NN) * math.sqrt(HDIM) for key in range(query + 1)]
            first = starts[:, query * S : (query + 1) * S]
            last = index_all[:, query * S : (query + 1) * S]
            scores = []
            for key in range(query + 1):
                keys = key_index[key * S : (key + 1) * S]
                allowed = keys >= first
                if key == query:
                    allowed = allowed & (keys <= last)
                scores.append(jnp.where(allowed, raw[key], -1e30))
            highest = scores[0].max(axis=0, keepdims=True)
            for piece in scores[1:]:
                highest = jnp.maximum(highest, piece.max(axis=0, keepdims=True))
            lifted = [jnp.exp(piece - highest) for piece in scores]
            total = lifted[0].sum(axis=0, keepdims=True)
            for piece in lifted[1:]:
                total = total + piece.sum(axis=0, keepdims=True)
            shrink = 1.0 / total
            mixed = None
            for key in range(query + 1):
                low = (lifted[key] * shrink).astype(BF16)
                probs[layer, block(query, key)] = low
                term = dot(heads_in[layer, key, 2], low, NN)
                mixed = term if mixed is None else mixed + term
            mixed_out[query] = mixed.astype(BF16)
        copies = spread("mixed", mixed_out, mixed_in.at[layer])
        used["mixed"] = copies
        if layer == 0:
            first_line.step(2)
            stream_lines[0].step(0)
        settle()
        if layer:
            stream_lines[0].step(3)
            stream_lines[0].finish()
        await_weight(layer, 1)
        arrive(copies)
        attended = mixed_in[layer].reshape(inner, S).T
        free("sums 0")
        partial = dot(attended, wo[layer], NN).astype(BF16).reshape(T, HALVES, count, D)
        branch_copies = []
        for half in halves:
            sums_out[0, half] = partial[:, half]
            branch_copies.append(scatter(0, half))
        used["sums 0"] = sum(branch_copies, [])
        if layer:
            stream_lines[1].step(0)
        else:
            stream_lines[0].step(1)
        lend_weights(layer, (3,))
        settle()
        alpha = al[layer]
        middle_copies = []
        for half in halves:
            branch = scattered(0, half, branch_copies[half])
            base = base_low[piece_of(half)].astype(F32)
            middle = norm_parts(base + alpha[0:1] * (norm_parts(branch)[0] - base))[0]
            middle_copies.append(gather("middle", middles.at[layer, z], half, middle.astype(BF16)))
            branch_f[layer, piece_of(half)] = branch
            middle_f[layer, piece_of(half)] = middle
        stream_lines[layer].step(1 + (layer == 0))
        lend_weights(layer, (4,))
        settle()
        if layer:
            for line in (first_line, middle_lines[0]):
                line.passed()
                line.finish()
        free("sums 1")
        for piece in (2, 3):
            await_weight(layer, piece)
        feed_copies = []
        for half in halves:
            arrive(middle_copies[half])
            middle_all = half_of(middles.at[layer, z], half)
            for begin in range(0, units, CHUNK):
                cols = slice(begin, begin + CHUNK)
                up = dot(middle_all, we[layer, 0, :, cols], NN)
                gate = dot(middle_all, we[layer, 1, :, cols], NN)
                if layer:
                    ups[half, :, cols] = up.astype(BF16)
                    gates[half, :, cols] = gate.astype(BF16)
                inside = us[layer, 1:2, cols] * gate
                hidden[:, cols] = (us[layer, 0:1, cols] * up * (inside * sigmoid(inside))).astype(BF16)
            if half == 0:
                await_weight(layer, 4)
            acted = hidden[...]
            for begin in range(0, D, CHUNK):
                cols = slice(begin, begin + CHUNK)
                sums_out[1, half, :, :, cols] = dot(acted, wr[layer, :, cols], NN).astype(BF16).reshape(T, count, CHUNK)
            feed_copies.append(scatter(1, half))
        used["sums 1"] = sum(feed_copies, [])
        if layer:
            stream_lines[1].step(2)
        middle_lines[layer].step(0)
        settle()
        for half in halves:
            feed = scattered(1, half, feed_copies[half])
            feed_f[layer, piece_of(half)] = feed
            middle = middle_f[layer, piece_of(half)]
            result = norm_parts(middle + alpha[1:2] * (norm_parts(feed)[0] - middle))[0].astype(BF16)
            outs[0, layer, piece_of(half)] = result
            then(half, result)
        if layer == 0:
            middle_lines[0].step(1)
            lend_weights(1, (0,))

    def act_back(layer, cols, up, gate, slope_hidden):
        scale_up, scale_gate = us[layer, 0:1, cols], us[layer, 1:2, cols]
        inside = scale_gate * gate
        gain = sigmoid(inside)
        silu = inside * gain
        by_up = silu * slope_hidden
        by_gate = scale_up * up * (gain + silu * (1.0 - gain)) * slope_hidden
        return silu, by_up, by_gate

    def stage_copy(layer, chunk, which):
        buffer = (stage_e, stage_r)[which].at[chunk % 2]
        target = (ge_ref.at[0, chunk], gr_ref.at[0, chunk])[which]
        return pltpu.make_async_copy(buffer, target, stage_sem.at[layer, chunk, which])

    def stage_send(layer, chunk, which):
        buffer = (stage_e, stage_r)[which].at[chunk % 2]
        target = (ge_ref.at[1, chunk], gr_ref.at[1, chunk])[which]
        return slots.copy(("stage", chunk, which), buffer, target, sibling)

    def stage_wait(layer, chunk):
        @pl.when(core == layer)
        def _():
            for which in range(2):
                stage_copy(layer, chunk, which).wait()

        @pl.when(core != layer)
        def _():
            for which in range(2):
                stage_send(layer, chunk, which).wait_send()

    def feed_ahead():
        def slots_of(place, carry):
            rows = pl.ds(pl.multiple_of(place * S, S), S)
            for begin in range(0, units, CHUNK):
                cols = slice(begin, begin + CHUNK)
                for side in range(2):
                    ahead[side, rows, cols] = dot(middles[0, place], we[0, side, :, cols], NN).astype(BF16)
            return carry

        lax.fori_loop(0, Z, slots_of, 0)

    staged = []

    def feed_grads(layer, chunk):
        if chunk == 0:
            for place in range(Z):
                middle_cols[:, place * S : (place + 1) * S] = middles[layer, place].T
        cols = slice(chunk * CHUNK, (chunk + 1) * CHUNK)
        scale_up, scale_gate = us[layer, 0:1, cols], us[layer, 1:2, cols]

        def slots_of(place, sums):
            rows = slice(place * S, (place + 1) * S) if layer else pl.ds(pl.multiple_of(place * S, S), S)
            if layer:
                up = dot(middles[layer, place], we[layer, 0, :, cols], NN)
                gate = dot(middles[layer, place], we[layer, 1, :, cols], NN)
            else:
                up, gate = ahead[0, rows, cols].astype(F32), ahead[1, rows, cols].astype(F32)
            slope_hidden = dot(feed_low[layer, place], wr[layer, cols, :], NT)
            silu, by_up, by_gate = act_back(layer, cols, up, gate, slope_hidden)
            hidden_part[:, rows] = (scale_up * up * silu).astype(BF16).T
            up_part[rows, :] = (by_up * scale_up).astype(BF16)
            gate_part[rows, :] = (by_gate * scale_gate).astype(BF16)
            return sums[0] + jnp.sum(by_up * up, axis=0, keepdims=True), sums[1] + jnp.sum(by_gate * gate, axis=0, keepdims=True)

        sums = (jnp.zeros((1, CHUNK), F32), jnp.zeros((1, CHUNK), F32))
        if layer:
            for place in range(Z):
                sums = slots_of(place, sums)
        else:
            sums = lax.fori_loop(0, Z, slots_of, sums)
        sum_up, sum_gate = sums
        finals[layer, 2:3, cols] = sum_up
        finals[layer, 3:4, cols] = sum_gate
        if len(staged) >= 2:
            stage_wait(*staged[-2])
        buffer = chunk % 2
        stage_e[buffer, 0] = dot(middle_cols[...], up_part[...], NN).astype(BF16)
        stage_e[buffer, 1] = dot(middle_cols[...], gate_part[...], NN).astype(BF16)
        stage_r[buffer] = dot(hidden_part[...], feed_low[layer].reshape(Z * S, D), NN).astype(BF16)

        @pl.when(core == layer)
        def _():
            for which in range(2):
                stage_copy(layer, chunk, which).start()

        @pl.when(core != layer)
        def _():
            for which in range(2):
                stage_send(layer, chunk, which).start()

        staged.append((layer, chunk))

    chunks = units // CHUNK
    projected = 3 * HDIM
    def attn_pair():
        return [slots.copy("head", attn_own, attn_sib, sibling), slots.copy("scale", scale_own, scale_sib, sibling)]

    def go_pair():
        return [slots.copy("go", go_out, go_sib, sibling)]

    def go_spread():
        return [
            slots.copy(("go", k), go_out.at[peer], go_in.at[k], device) for k, (peer, device) in enumerate(zip(place_peers, place_ids))
        ]

    def offer(layer, pair):
        @pl.when(core != layer)
        def _():
            for copy in pair():
                copy.start()

    def go_join(layer):
        @pl.when(core == layer)
        def _():
            for copy in go_pair():
                copy.wait_recv()
            go_out[...] = (go_out[...].astype(F32) + go_sib[...].astype(F32)).astype(BF16)
            for copy in go_spread():
                copy.start()

        @pl.when(core != layer)
        def _():
            for copy in go_pair():
                copy.wait_send()

    attn_lines = [
        Line("heads line", lambda place: [attn_all.at[place, :projected], scale_all.at[place]], core == layer) for layer in range(2)
    ]
    go_lines = [Line("go line", lambda place: [attn_all.at[place, projected:]], core == layer) for layer in range(2)]

    def go_finish(layer):
        @pl.when(core == layer)
        def _():
            for copy in go_spread():
                copy.wait_recv()
            total = go_out[z].astype(F32)
            for k in range(Z - 1):
                total = total + go_in[k].astype(F32)
            attn_all[z, projected:] = total.astype(BF16)
            for copy in go_spread():
                copy.wait_send()

        go_lines[layer].step(0)

    def attn_join(layer):
        @pl.when(core == layer)
        def _():
            for copy in attn_pair():
                copy.wait_recv()
            attn_all[z, :projected] = (attn_own[...].astype(F32) + attn_sib[...].astype(F32)).astype(BF16)
            scale_all[z] = scale_own[...] + scale_sib[...]

        @pl.when(core != layer)
        def _():
            for copy in attn_pair():
                copy.wait_send()

        attn_lines[layer].step(0)

    def head_grads(layer, scale_slope):
        if layer:
            arrive(waiting["stream", 1])
        grad = None
        for place in range(Z):
            term = dot(heads_out[place].reshape(3 * HDIM, S), stream[layer, place], NN)
            grad = term if grad is None else grad + term
        attn_own[...] = grad.astype(BF16)
        scale_rows = jnp.broadcast_to(scale_slope, (HDIM, 128)).T[:8]
        scale_own[...] = jnp.concatenate([scale_rows, scale_rows], axis=1)
        offer(layer, attn_pair)

    def enter(layer, half, slope):
        rows = piece_of(half)
        middle_slope, feed_slope, alpha_m = blend_back(slope, middle_f[layer, rows], feed_f[layer, rows], al[layer, 1:2])
        copies = gather("feed_low", feed_low.at[layer, z], half, feed_slope.astype(BF16))
        return middle_slope, alpha_m, copies

    def backward(layer, base_low, entered, then):
        alpha = al[layer]
        alpha_own[layer, 1:2] = entered[0][1] + entered[1][1]
        if layer:
            stream_lines[1].step(3)
            waiting["stream", 1] = pass_on("stream", 1, stream, 2, [0])
        else:
            feed_lines[1].step(3)
        settle()
        if layer == 0:
            attn_join(1)
            go_finish(1)
        free("sums 0")
        back_copies = []
        for half in halves:
            arrive(entered[half][2])
            feed_all = half_of(feed_low.at[layer, z], half)
            for begin in range(0, units, CHUNK):
                cols = slice(begin, begin + CHUNK)
                slope_hidden = dot(feed_all, wr[layer, cols, :], NT)
                if layer:
                    up, gate = ups[half, :, cols].astype(F32), gates[half, :, cols].astype(F32)
                else:
                    rows = [pl.ds(pl.multiple_of(z * S + index * part + half * count, count), count) for index in range(T)]
                    up, gate = (
                        jnp.concatenate([ahead[side, group, cols] for group in rows], axis=0).astype(F32) for side in range(2)
                    )
                _, by_up, by_gate = act_back(layer, cols, up, gate, slope_hidden)
                expanded_low[0, :, cols] = (by_up * us[layer, 0:1, cols]).astype(BF16)
                expanded_low[1, :, cols] = (by_gate * us[layer, 1:2, cols]).astype(BF16)
            for begin in range(0, D, CHUNK):
                rows = slice(begin, begin + CHUNK)
                partial = dot(expanded_low[0], we[layer, 0, rows, :], NT) + dot(expanded_low[1], we[layer, 1, rows, :], NT)
                sums_out[0, half, :, :, rows] = partial.astype(BF16).reshape(T, count, CHUNK)
            back_copies.append(scatter(2, half))
            if layer and half == 0:
                middle_lines[1].step(1)
        used["sums 0"] = sum(back_copies, [])
        if layer:
            waiting["stream", 1] += pass_on("stream", 1, stream, 2, [1])
        feed_lines[layer].step(0)
        settle()
        if layer == 0:
            attn_lines[1].step(1)
            go_lines[1].step(1)
            feed_lines[1].passed()
            arrive(waiting["middle", 1])
            feed_grads(1, 0)
        free("branch_low")
        branch_copies, stream_slopes, alpha_a = [], [], None
        for half in halves:
            middle_total = entered[half][0] + scattered(2, half, back_copies[half])
            stream_slope, branch_slope, term = blend_back(
                middle_total, base_low[piece_of(half)].astype(F32), branch_f[layer, piece_of(half)], alpha[0:1]
            )
            branch_copies.append(gather("branch_low", branch_low, half, branch_slope.astype(BF16)))
            stream_slopes.append(stream_slope)
            alpha_a = term if alpha_a is None else alpha_a + term
        copies = sum(branch_copies, [])
        used["branch_low"] = copies
        alpha_own[layer, 0:1] = alpha_a
        if layer:
            waiting["stream", 1] += pass_on("stream", 1, stream, 2, [2])
            middle_lines[1].step(2)
            feed_ahead()
            feed_lines[1].step(1)
        else:
            alpha_copies = [send(("alpha", k), alpha_own, alpha_in.at[k], device) for k, device in enumerate(tensor_ids)]
            feed_lines[0].step(1)
            attn_lines[1].step(2)
            go_lines[1].step(2)
            feed_grads(1, 1)
        settle()
        arrive(copies)
        branch_all = branch_low[...]
        free("mixed_back")
        free("mixed")
        mixed_out[...] = dot(wo[layer], branch_all, NT).astype(BF16).reshape(H, HDIM, S)
        copies = spread("mixed_back", mixed_out, back_in)
        used["mixed_back"] = copies
        go_out[...] = dot(mixed_in[layer].reshape(inner, S), branch_all, NN).astype(BF16).reshape(H, HDIM, D)
        offer(layer, go_pair)
        if layer == 0:
            feed_lines[0].step(2)
        if layer:
            middle_lines[1].step(3)
            waiting["middle", 1] = pass_on("middle", 1, middles)
        else:
            stream_lines[1].finish()
            middle_lines[1].finish()
        settle()
        if layer == 0:
            feed_grads(1, 2)
        for place in range(Z):
            turned_rows[place] = heads_in[layer, place, 2].T
        arrive(copies)
        if layer == 0:
            go_join(0)
            feed_lines[0].step(3)
        for query in range(Z):
            slope_mixed = back_in[query]
            lows = [probs[layer, block(query, key)] for key in range(query + 1)]
            probs_slope = [dot(turned_rows[key], slope_mixed, NN) for key in range(query + 1)]
            row_term = None
            for low, piece in zip(lows, probs_slope):
                term = jnp.sum(low.astype(F32) * piece, axis=0, keepdims=True)
                row_term = term if row_term is None else row_term + term
            query_slope = None
            for key in range(query + 1):
                low = lows[key]
                scores_low = (low.astype(F32) * (probs_slope[key] - row_term)).astype(BF16)
                term = dot(heads_in[layer, key, 1], scores_low, NN)
                query_slope = term if query_slope is None else query_slope + term
                key_term = dot(heads_in[layer, query, 0], scores_low, NT)
                value_term = dot(slope_mixed, low, NT)
                if key == query:
                    key_grad[key] = key_term
                    value_grad[key] = value_term
                else:
                    key_grad[key] += key_term
                    value_grad[key] += value_term
            query_grad[query] = query_slope
        free("heads_back")
        free("heads")
        scale = scales[layer, z][:, :1]
        inverse = 1.0 / scale
        scale_slope = None
        for place in range(Z):
            cosine_there, sine_there = cosines[place], sines[place]
            for third, source in ((0, query_grad), (1, key_grad)):
                piece = source[place] * math.sqrt(HDIM)
                unit = heads_in[layer, place, third].astype(F32) * inverse
                term = jnp.sum(piece * unit, axis=1, keepdims=True)
                scale_slope = term if scale_slope is None else scale_slope + term
                piece = piece * scale
                piece = rates_in[layer, place, third : third + 1] * (piece - unit * jnp.sum(unit * piece, axis=0, keepdims=True))
                front, back = piece[:turn], piece[turn:]
                piece = jnp.concatenate([front * cosine_there + back * sine_there, back * cosine_there - front * sine_there], axis=0)
                heads_out[place, third] = piece.astype(BF16)
            heads_out[place, 2] = value_grad[place].astype(BF16)
        if layer == 0:
            head_grads(0, scale_slope)
            attn_join(0)
        copies = spread("heads_back", heads_out, heads_back_in)
        used["heads_back"] = copies
        settle()
        if layer:
            feed_lines[1].step(2)
        else:
            feed_grads(1, 3)
            go_finish(0)
            arrive(alpha_copies)
            retire(alpha_copies)
            total = alpha_own[...]
            for k in range(T - 1):
                total = total + alpha_in[k]
            alpha_own[...] = total
            alpha_copies = [
                send(("alpha", T - 1 + k), alpha_own, alpha_in.at[T - 1 + k], device) for k, device in enumerate(place_ids)
            ]
        if layer == 0:
            feed_lines[0].passed()
            feed_grads(0, 0)
            attn_lines[0].step(1)
        arrive(copies)
        partial = None
        for third in range(3):
            term = dot(heads_back_in[:, third].reshape(inner, S).T, wp[layer, third], NT)
            partial = term if partial is None else partial + term
        free("sums 1")
        partial = partial.astype(BF16).reshape(T, HALVES, count, D)
        copies = []
        for half in halves:
            sums_out[1, half] = partial[:, half]
            copies.append(scatter(3, half))
        settle()
        if layer:
            head_grads(layer, scale_slope)
            go_join(1)
        else:
            feed_grads(0, 1)
            go_lines[0].step(1)
        for half in halves:
            result = (stream_slopes[half] + scattered(3, half, copies[half])).astype(BF16)
            outs[1, layer, piece_of(half)] = result
            then(half, result)
        used["sums 1"] = sum(copies, [])
        if layer == 0:
            waiting["alpha"] = alpha_copies

    next_stream, entered_last, entered_first = [], [], []

    def to_second(half, result):
        next_stream.extend(gather("stream", stream.at[1, z], half, result))

    def to_backward(half, result):
        entered_last.append(enter(1, half, cot_ref[core, 0, piece_of(half)].astype(F32)))

    def to_first(half, result):
        entered_first.append(enter(0, half, result.astype(F32)))

    forward(0, acts_ref.at[core, 0], first_stream, to_second)
    forward(1, outs.at[0, 0], next_stream, to_backward)
    backward(1, outs.at[0, 0], entered_last, to_first)
    backward(0, acts_ref.at[core, 0], entered_first, lambda half, result: None)

    other = 1 - core
    last = [send("outs", outs.at[:, other], outs_in, sibling)]
    attn_lines[0].step(2)
    feed_grads(0, 2)
    go_lines[0].step(2)
    for line in feed_lines:
        line.finish()
    for line in (attn_lines[1], go_lines[1]):
        line.step(3)
        line.finish()
    arrive(waiting["alpha"])
    total = alpha_own[...]
    for k in range(Z - 1):
        total = total + alpha_in[T - 1 + k]
    finals[0, 0:2] = total[0]
    finals[1, 0:2] = total[1]
    settle(2)
    feed_grads(0, 3)
    last += [send("finals", finals.at[other], finals_in, sibling)]
    written = [
        pltpu.make_async_copy(outs.at[kind, core], target.at[core], out_sem.at[kind]) for kind, target in enumerate((lo_ref, ig_ref))
    ]
    for copy in written:
        copy.start()
    arrive(last)
    for kind, target in enumerate((lo_ref, ig_ref)):
        written.append(pltpu.make_async_copy(outs_in.at[kind], target.at[other], out_sem.at[2 + kind]))
        written[-1].start()
    small_ref[0:4] = finals[core] + finals_in[...]
    for layer, chunk in staged[-2:]:
        stage_wait(layer, chunk)
    for chunk in range(chunks):
        for which in range(2):
            stage_send(0, chunk, which).wait_recv()
    attn_lines[0].step(3)
    go_lines[0].step(3)
    attn_out = pltpu.make_async_copy(attn_all, attn_ref, stage_sem.at[0, 0, 0])
    attn_out.start()
    for place in range(Z):
        small_ref[4:5, place * HDIM : (place + 1) * HDIM] = scale_all[place, :1, :HDIM]
    settle(0)
    for piece in range(len(weights)):
        weight_copy(piece).wait_send()
    attn_lines[0].finish()
    go_lines[0].finish()
    for copy in written:
        copy.wait()
    attn_out.wait()
    assert len(slots.names) == COPIES, len(slots.names)


def relay(sizes, lengths, acts, cot, qs, us, al, wp, wo, we, wr):
    T, Z, S, part = sizes.tensors, sizes.places, sizes.local, sizes.part
    H, inner, units, D = sizes.heads, sizes.inner, sizes.units, sizes.width
    blocks, chunks = Z * (Z + 1) // 2, units // CHUNK
    vmem = pl.BlockSpec(memory_space=pltpu.VMEM)
    hbm = pl.BlockSpec(memory_space=pl.ANY)
    out_shape = (
        jax.ShapeDtypeStruct((2, part, D), BF16),
        jax.ShapeDtypeStruct((2, part, D), BF16),
        jax.ShapeDtypeStruct((8, D), F32),
        jax.ShapeDtypeStruct((Z, 4 * HDIM, D), BF16),
        jax.ShapeDtypeStruct((2, chunks, 2, D, CHUNK), BF16),
        jax.ShapeDtypeStruct((2, chunks, CHUNK, D), BF16),
    )
    DMA = pltpu.SemaphoreType.DMA
    V = pltpu.VMEM
    scratch = [
        V((2, 3, D, inner), BF16), V((2, inner, D), BF16), V((2, 2, D, units), BF16), V((2, units, D), BF16),
        V((2, 1, inner), F32), V((2, 2, units), F32), V((2, 2, D), F32),
        V((2, Z, S, D), BF16), V((2, Z, S, D), BF16), V((2, Z, S, D), BF16), V((S, D), BF16),
        V((Z, HDIM // 2, S), F32), V((Z, HDIM // 2, S), F32), V((2, H, HDIM, 128), F32),
        V((2, Z, 3, HDIM, S), BF16), V((2, Z, 2, S), F32),
        V((2, blocks, S, S), BF16), V((2, H, HDIM, S), BF16),
        V((2, HALVES, T - 1, part // HALVES, D), BF16),
        V((2, part, D), F32), V((2, part, D), F32), V((2, part, D), F32),
        V((HALVES, S // HALVES, units), BF16), V((HALVES, S // HALVES, units), BF16),
        V((S // HALVES, units), BF16), V((2, S // HALVES, units), BF16),
        V((Z, HDIM, S), BF16), V((H, 3, HDIM, S), BF16),
        V((H, 3, HDIM, S), BF16), V((H, 2, S), F32),
        V((Z, HDIM, S), BF16),
        V((2, HALVES, T, part // HALVES, D), BF16), V((H, HDIM, D), BF16), V((H, HDIM, D), BF16), V((Z - 1, HDIM, D), BF16),
        V((2, 2, part, D), BF16), V((2, part, D), BF16),
        V((Z, S, HDIM), BF16),
        V((Z, HDIM, S), F32), V((Z, HDIM, S), F32), V((Z, HDIM, S), F32),
        V((3 * HDIM, D), BF16), V((3 * HDIM, D), BF16), V((Z, 4 * HDIM, D), BF16),
        V((8, 128), F32), V((8, 128), F32), V((Z, 8, 128), F32),
        V((2, 2, D), F32), V((T + Z - 2, 2, 2, D), F32), V((2, 4, D), F32), V((4, D), F32),
        V((D, Z * S), BF16), V((CHUNK, Z * S), BF16), V((Z * S, CHUNK), BF16), V((Z * S, CHUNK), BF16),
        V((2, 2, D, CHUNK), BF16), V((2, CHUNK, D), BF16), V((2, D // 16, 2, units), BF16),
        V((2, Z * S, units), BF16),
        DMA((2, 8)), DMA((8,)), DMA((COPIES,)), DMA((COPIES,)), DMA((2, chunks, 2)), DMA((2,)), DMA((4,)),
    ]
    return pl.pallas_call(
        functools.partial(relay_kernel, sizes),
        out_shape=out_shape,
        in_specs=[pl.BlockSpec(memory_space=pltpu.SMEM), vmem, vmem, vmem, vmem, vmem, hbm, hbm, hbm, hbm],
        out_specs=(hbm, hbm, vmem, hbm, hbm, hbm),
        scratch_shapes=scratch,
        compiler_params=pltpu.CompilerParams(collective_id=0, has_side_effects=True, vmem_limit_bytes=63 * 2**20),
        name="relay",
    )(lengths, acts, cot, qs, us, al, wp, wo, we, wr)


def finish_kernel(
    attn_ref, ge_ref, gr_ref, lo_in, ig_in, small_ref,
    projection_ref, output_ref, expansion_ref, reduction_ref, lo_ref, ig_ref, scale_ref, units_ref, alphas_ref,
):
    @pl.when(pl.program_id(0) == 0)
    def _():
        lo_ref[...] = lo_in[...]
        ig_ref[...] = ig_in[...]
        alphas_ref[...] = small_ref[0:2]
        units_ref[...] = small_ref[2:4, : units_ref.shape[1]]
        scale_ref[...] = small_ref[4:5, : scale_ref.shape[1]]

    places, chunks = attn_ref.shape[0], ge_ref.shape[1]
    for begin in range(0, ge_ref.shape[3], 16):
        rows = slice(begin, begin + 16)
        pieces = []
        for chunk in range(chunks):
            for lanes in (slice(0, 128), slice(128, 256)):
                for side in range(2):
                    total = ge_ref[0, chunk, side, rows, lanes].astype(F32) + ge_ref[1, chunk, side, rows, lanes].astype(F32)
                    pieces.append(total[None])
        expansion_ref[rows] = jnp.swapaxes(jnp.concatenate(pieces, axis=0), 0, 1)
    reduction_ref[...] = gr_ref[0].astype(F32) + gr_ref[1].astype(F32)
    for third in range(3):
        rows = attn_ref[:, third * HDIM : (third + 1) * HDIM, :].astype(F32)
        projection_ref[third] = rows.reshape(places * HDIM, rows.shape[2]).T
    output_ref[...] = attn_ref[:, 3 * HDIM :, :].astype(F32).reshape(output_ref.shape)


def finish(attn, ge, gr, lo, ig, small):
    places, _, D = attn.shape
    chunks, units, inner = ge.shape[1], ge.shape[1] * CHUNK, places * HDIM
    block = D // 2
    steps = D // block
    rows = units // steps

    def whole(shape):
        return pl.BlockSpec(shape, lambda i: (0,) * len(shape))

    return pl.pallas_call(
        finish_kernel,
        grid=(steps,),
        in_specs=[
            pl.BlockSpec((places, 4 * HDIM, block), lambda i: (0, 0, i)),
            pl.BlockSpec((2, chunks, 2, block, CHUNK), lambda i: (0, 0, 0, i, 0)),
            pl.BlockSpec((2, rows, D), lambda i: (0, i, 0)),
            whole(lo.shape),
            whole(ig.shape),
            whole(small.shape),
        ],
        out_specs=(
            pl.BlockSpec((3, block, inner), lambda i: (0, i, 0)),
            pl.BlockSpec((inner, block), lambda i: (0, i)),
            pl.BlockSpec((block, units // 64, 128), lambda i: (i, 0, 0)),
            pl.BlockSpec((rows, D), lambda i: (i, 0)),
            whole(lo.shape),
            whole(ig.shape),
            whole((1, inner)),
            whole((2, units)),
            whole((2, D)),
        ),
        out_shape=(
            jax.ShapeDtypeStruct((3, D, inner), F32),
            jax.ShapeDtypeStruct((inner, D), F32),
            jax.ShapeDtypeStruct((D, units // 64, 128), F32),
            jax.ShapeDtypeStruct((units, D), F32),
            jax.ShapeDtypeStruct(lo.shape, BF16),
            jax.ShapeDtypeStruct(ig.shape, BF16),
            jax.ShapeDtypeStruct((1, inner), F32),
            jax.ShapeDtypeStruct((2, units), F32),
            jax.ShapeDtypeStruct((2, D), F32),
        ),
        compiler_params=pltpu.CompilerParams(vmem_limit_bytes=60 * 2**20),
        name="finish",
    )(attn, ge, gr.reshape(2, units, D), lo, ig, small)


def fast_body(
    activations, lengths, projection, output_weight, expansion, reduction, query_scale, unit_scales, alphas, cotangent
):
    _, _, part, width = activations.shape
    inner, units = output_weight.shape[1], reduction.shape[1]
    places = lax.axis_size("dp")
    sizes = Sizes(lax.axis_size("tensor"), places, part, width, inner, units)
    lo, ig, small, attn, ge, gr = relay(
        sizes, lengths, activations, cotangent, query_scale, unit_scales[0], alphas[0],
        projection[0].transpose(1, 0, 2), output_weight[0], expansion[0], reduction[0],
    )
    projection_grad, output_grad, expansion_grad, reduction_grad, lo, ig, scale_grad, unit_grad, alpha_grad = finish(
        attn, ge, gr, lo, ig, small
    )
    columns = units // 128
    expansion_grad = expansion_grad.reshape(width, columns, 2, 128).transpose(0, 2, 1, 3).reshape(width, 2, units)
    projection_grad = projection_grad.transpose(1, 0, 2)
    return (
        lo[None, :, None],
        ig[None, :, None],
        projection_grad[None],
        output_grad[None],
        expansion_grad[None],
        reduction_grad[None],
        scale_grad,
        unit_grad[None],
        alpha_grad[None],
    )


def solution(mesh):
    in_specs = (
        P(None, None, ("dp", "tensor"), None),
        P(),
        P("section", None, None, "tensor"),
        P("section", "tensor", None),
        P("section", None, None, "tensor"),
        P("section", "tensor", None),
        P("section", "tensor"),
        P("section", None, "tensor"),
        P("section", None, None),
        P(None, None, ("dp", "tensor"), None),
    )
    out_specs = (
        P("section", None, None, ("dp", "tensor"), None),
        P("section", None, None, ("dp", "tensor"), None),
        P("section", None, None, "tensor"),
        P("section", "tensor", None),
        P("section", None, None, "tensor"),
        P("section", "tensor", None),
        P("section", "tensor"),
        P("section", None, "tensor"),
        P("section", None, None),
    )
    def chosen(*arrays):
        activations, output_weight = arrays[0], arrays[3]
        heads = output_weight.shape[1] // HDIM
        fits = (
            mesh.shape["section"] == 2
            and mesh.shape["tensor"] == 4
            and mesh.shape["dp"] == heads
            and activations.shape[:2] == (2, 1)
            and activations.shape[2] * mesh.shape["tensor"] == 256
        )
        return (fast_body if fits else body)(*arrays)

    return jax.shard_map(chosen, mesh=mesh, in_specs=in_specs, out_specs=out_specs, check_vma=False)
```

```python
import functools
import math

import jax
import jax.numpy as jnp
from jax import lax
from jax.experimental import pallas as pl
from jax.experimental.pallas import tpu as pltpu
from jax.sharding import PartitionSpec as P

HDIM = 64


def from_behind(value, axis, steps):
    count = lax.axis_size(axis)
    initial, last = (max(0, -steps), min(count, count - steps))
    return lax.ppermute(value, axis, [(source, source + steps) for source in range(initial, last)])


def normed(v):
    return v * lax.rsqrt(jnp.mean(v * v, axis=-1, keepdims=True) + 1e-06)


def unit_heads(v):
    return v * lax.rsqrt(jnp.sum(v * v, axis=-1, keepdims=True) + 1e-06)


def frequencies(half):
    return jnp.exp(jnp.arange(half, dtype=jnp.float32) * (-2.0 * math.log(10000.0) / (2 * half)))


def rotate(view, angle):
    half = view.shape[-1] // 2
    cosine = jnp.cos(angle)[..., None, :]
    sine = jnp.sin(angle)[..., None, :]
    front = view[..., :half]
    back = view[..., half:]
    return jnp.concatenate([front * cosine - back * sine, back * cosine + front * sine], axis=-1)


def shaped(projected, scale, angle, heads):
    inner = projected.shape[-1] // 3
    lead = projected.shape[:-1]

    def turned(piece):
        view = piece.reshape(lead + (heads, inner // heads))
        return unit_heads(rotate(view, angle)).reshape(lead + (inner,)) * scale

    return (
        turned(projected[..., :inner]),
        turned(projected[..., inner : 2 * inner]),
        projected[..., 2 * inner :],
    )


def layout(lengths_row, slots):
    ends = jnp.cumsum(lengths_row, dtype=jnp.int32)
    index = jnp.arange(slots, dtype=jnp.int32)
    after = index[:, None] >= ends[None, :]
    segment = jnp.sum(after.astype(jnp.int32), axis=1, dtype=jnp.int32)
    begin = jnp.sum(jnp.where(after, lengths_row[None, :], 0), axis=1, dtype=jnp.int32)
    inside = index < ends[-1]
    segment = jnp.where(inside, segment, lengths_row.shape[0] + index)
    position = jnp.where(inside, index - begin, 0)
    return (segment, position)


def blend(base, branch, alpha):
    return normed(base + alpha * (normed(branch) - base))


def activate(expanded, scales):
    half = expanded.shape[-1] // 2
    return expanded[..., :half] * scales[0] * jax.nn.silu(expanded[..., half:] * scales[1])


def placing(lengths_now, local):
    slots = local * lax.axis_size("dp")
    start_here = lax.axis_index("dp") * local
    segment_all, position_all = jax.vmap(lambda row: layout(row, slots))(lengths_now)
    segment_here = lax.dynamic_slice_in_dim(segment_all, start_here, local, 1)
    position_here = lax.dynamic_slice_in_dim(position_all, start_here, local, 1)
    index_here = start_here + jnp.arange(local, dtype=jnp.int32)
    every = jnp.arange(slots, dtype=jnp.int32)
    allowed = (segment_here[:, :, None] == segment_all[:, None, :]) & (
        every[None, None, :] <= index_here[None, :, None]
    )
    angle = position_here.astype(jnp.float32)[..., None] * frequencies(HDIM // 2)
    return (allowed, angle)


def scored(query, key_all, allowed, heads):
    rows, local, inner = query.shape
    depth = inner // heads
    query_heads = query.reshape(rows, local, heads, depth)
    key_heads = key_all.reshape(rows, key_all.shape[1], heads, depth)
    raw = jnp.einsum(
        "rqhe,rkhe->rhqk", query_heads, key_heads, preferred_element_type=jnp.float32
    ) * math.sqrt(depth)
    return jnp.where(allowed[:, None], raw, -1e30)


def forward(stream, lengths_now, weights):
    projection, output_weight, expansion, reduction, query_scale, unit_scales, alphas = weights
    rows, part, width = stream.shape
    inner = output_weight.shape[0]
    heads = inner // HDIM
    hidden_width = reduction.shape[0]
    gathered = lax.all_gather(stream.astype(jnp.bfloat16), "tensor", axis=1, tiled=True)
    local = gathered.shape[1]
    allowed, angle = placing(lengths_now, local)
    projected = jnp.einsum(
        "rsd,dc->rsc",
        gathered,
        projection.reshape(width, 3 * inner),
        preferred_element_type=jnp.float32,
    )
    query, key, value = shaped(projected, query_scale, angle, heads)
    query_low = query.astype(jnp.bfloat16)
    key_low = key.astype(jnp.bfloat16)
    value_low = value.astype(jnp.bfloat16)
    key_all, value_all = (
        lax.all_gather(key_low, "dp", axis=1, tiled=True),
        lax.all_gather(value_low, "dp", axis=1, tiled=True),
    )
    scores = scored(query_low, key_all, allowed, heads)
    highest = jnp.max(scores, axis=-1, keepdims=True)
    lifted = jnp.exp(scores - highest)
    total = jnp.sum(lifted, axis=-1, keepdims=True)
    log_total = highest + jnp.log(total)
    probs_low = (lifted / total).astype(jnp.bfloat16)
    value_heads = value_all.reshape(rows, value_all.shape[1], heads, HDIM)
    mixed = jnp.einsum(
        "rhqk,rkhe->rqhe", probs_low, value_heads, preferred_element_type=jnp.float32
    )
    attended = mixed.reshape(rows, local, inner).astype(jnp.bfloat16)
    partial_branch = jnp.einsum(
        "rsc,cd->rsd", attended, output_weight, preferred_element_type=jnp.float32
    )
    branch = lax.psum_scatter(partial_branch, "tensor", scatter_dimension=1, tiled=True)
    middle = blend(stream, branch, alphas[0])
    middle_all = lax.all_gather(middle.astype(jnp.bfloat16), "tensor", axis=1, tiled=True)
    expanded = jnp.einsum(
        "rsd,dc->rsc",
        middle_all,
        expansion.reshape(width, 2 * hidden_width),
        preferred_element_type=jnp.float32,
    )
    hidden = activate(expanded, unit_scales).astype(jnp.bfloat16)
    partial_feed = jnp.einsum("rsf,fd->rsd", hidden, reduction, preferred_element_type=jnp.float32)
    feed = lax.psum_scatter(partial_feed, "tensor", scatter_dimension=1, tiled=True)
    result = blend(middle, feed, alphas[1])
    kept = dict(
        stream=stream,
        gathered=gathered,
        projected=projected,
        query=query_low,
        key=key_low,
        value=value_low,
        log_total=log_total,
        attended=attended,
        branch=branch,
        middle=middle,
        middle_all=middle_all,
        expanded=expanded,
        hidden=hidden,
        feed=feed,
        lengths=lengths_now,
    )
    kept = dict(kept, key_all=key_all, value_all=value_all)
    return (result, kept)


def backward(slope, kept, weights):
    projection, output_weight, expansion, reduction, query_scale, unit_scales, alphas = weights
    rows, part, width = slope.shape
    inner = output_weight.shape[0]
    heads = inner // HDIM
    hidden_width = reduction.shape[0]
    _, pull_feed = jax.vjp(blend, kept["middle"], kept["feed"], alphas[1])
    middle_slope, feed_slope, alpha_feed = pull_feed(slope)
    feed_all = lax.all_gather(feed_slope.astype(jnp.bfloat16), "tensor", axis=1, tiled=True)
    reduction_grad = jnp.einsum(
        "rsf,rsd->fd", kept["hidden"], feed_all, preferred_element_type=jnp.float32
    )
    hidden_slope = jnp.einsum(
        "rsd,fd->rsf", feed_all, reduction, preferred_element_type=jnp.float32
    )
    _, pull_active = jax.vjp(activate, kept["expanded"], unit_scales)
    expanded_slope, unit_grad = pull_active(hidden_slope)
    expanded_low = expanded_slope.astype(jnp.bfloat16)
    expansion_grad = jnp.einsum(
        "rsd,rsc->dc", kept["middle_all"], expanded_low, preferred_element_type=jnp.float32
    ).reshape(width, 2, hidden_width)
    partial_middle = jnp.einsum(
        "rsc,dc->rsd",
        expanded_low,
        expansion.reshape(width, 2 * hidden_width),
        preferred_element_type=jnp.float32,
    )
    middle_total = middle_slope + lax.psum_scatter(
        partial_middle, "tensor", scatter_dimension=1, tiled=True
    )
    _, pull_branch = jax.vjp(blend, kept["stream"], kept["branch"], alphas[0])
    stream_slope, branch_slope, alpha_branch = pull_branch(middle_total)
    branch_all = lax.all_gather(branch_slope.astype(jnp.bfloat16), "tensor", axis=1, tiled=True)
    output_grad = jnp.einsum(
        "rsc,rsd->cd", kept["attended"], branch_all, preferred_element_type=jnp.float32
    )
    attended_low = jnp.einsum(
        "rsd,cd->rsc", branch_all, output_weight, preferred_element_type=jnp.float32
    ).astype(jnp.bfloat16)
    local = attended_low.shape[1]
    key_all = kept["key_all"]
    value_all = kept["value_all"]
    slots = key_all.shape[1]
    allowed, angle = placing(kept["lengths"], local)
    scores = scored(kept["query"], key_all, allowed, heads)
    probs = jnp.exp(scores - kept["log_total"])
    scale = math.sqrt(HDIM)
    back_heads = attended_low.reshape(rows, local, heads, HDIM)
    query_heads = kept["query"].reshape(rows, local, heads, HDIM)
    key_heads = key_all.reshape(rows, slots, heads, HDIM)
    value_heads = value_all.reshape(rows, slots, heads, HDIM)
    probs_slope = jnp.einsum(
        "rqhe,rkhe->rhqk", back_heads, value_heads, preferred_element_type=jnp.float32
    )
    row_term = jnp.sum(probs * probs_slope, axis=-1, keepdims=True)
    scores_low = (probs * (probs_slope - row_term)).astype(jnp.bfloat16)
    query_slope = (
        jnp.einsum("rhqk,rkhe->rqhe", scores_low, key_heads, preferred_element_type=jnp.float32)
        * scale
    )
    value_grad_all = jnp.einsum(
        "rhqk,rqhe->rkhe",
        probs.astype(jnp.bfloat16),
        back_heads,
        preferred_element_type=jnp.float32,
    )
    key_grad_all = (
        jnp.einsum("rhqk,rqhe->rkhe", scores_low, query_heads, preferred_element_type=jnp.float32)
        * scale
    )
    key_slope, value_slope = (
        lax.psum_scatter(
            key_grad_all.reshape(rows, slots, inner), "dp", scatter_dimension=1, tiled=True
        ),
        lax.psum_scatter(
            value_grad_all.reshape(rows, slots, inner), "dp", scatter_dimension=1, tiled=True
        ),
    )
    _, pull_shape = jax.vjp(
        lambda source, scale_now: shaped(source, scale_now, angle, heads),
        kept["projected"],
        query_scale,
    )
    projected_slope, query_scale_grad = pull_shape(
        (query_slope.reshape(rows, local, inner), key_slope, value_slope)
    )
    projected_low = projected_slope.astype(jnp.bfloat16)
    projection_grad = jnp.einsum(
        "rsd,rsc->dc", kept["gathered"], projected_low, preferred_element_type=jnp.float32
    ).reshape(width, 3, inner)
    partial_stream = jnp.einsum(
        "rsc,dc->rsd",
        projected_low,
        projection.reshape(width, 3 * inner),
        preferred_element_type=jnp.float32,
    )
    spread = jnp.broadcast_to(
        jnp.stack([alpha_branch, alpha_feed])[:, None, :], (2, lax.axis_size("tensor"), width)
    )
    stream_part, alpha_sum = (
        lax.psum_scatter(partial_stream, "tensor", scatter_dimension=1, tiled=True),
        lax.psum_scatter(spread, "tensor", scatter_dimension=1, tiled=True),
    )
    stream_total = stream_slope + stream_part
    return (
        stream_total,
        (
            projection_grad,
            output_grad,
            expansion_grad,
            reduction_grad,
            query_scale_grad,
            unit_grad,
            alpha_sum[:, 0],
        ),
    )


def body(
    activations,
    lengths,
    projection,
    output_weight,
    expansion,
    reduction,
    query_scale,
    unit_scales,
    alphas,
    cotangent,
):
    micro, rows, part, width = activations.shape
    section = lax.axis_index("section")
    first = section == 0
    weights = (
        projection[0],
        output_weight[0],
        expansion[0],
        reduction[0],
        query_scale[0],
        unit_scales[0],
        alphas[0],
    )
    steps = micro + 1
    received = jnp.zeros((rows, part, width), jnp.bfloat16)
    outputs = []
    keeps = []
    for step in range(steps):
        index_now = jnp.clip(step - section, 0, micro - 1)
        lengths_now = lax.dynamic_index_in_dim(lengths, index_now, 0, keepdims=False)
        stream = jnp.where(first, activations[min(step, micro - 1)], received).astype(jnp.float32)
        result, kept = forward(stream, lengths_now, weights)
        result_low = result.astype(jnp.bfloat16)
        outputs.append(result_low)
        keeps.append(kept)
        if step + 1 < steps:
            received = from_behind(result_low, "section", 1)
    stacked = jnp.stack(outputs)
    layer_output = jnp.where(first, stacked[:micro], stacked[1:])[None]
    back_received = jnp.zeros((rows, part, width), jnp.bfloat16)
    slopes = []
    summed = None
    for step in range(steps):
        batch_now = step - 1 + section
        valid = (batch_now >= 0) & (batch_now < micro)
        slope = jnp.where(first, back_received, cotangent[min(step, micro - 1)]).astype(jnp.float32)
        earlier = keeps[max(step - 1, 0)]
        later = keeps[min(step + 1, micro)]
        kept = jax.tree.map(lambda left, right: jnp.where(first, left, right), earlier, later)
        stream_total, layer_grads = backward(slope, kept, weights)
        stream_low = stream_total.astype(jnp.bfloat16)
        slopes.append(stream_low)
        masked = tuple((jnp.where(valid, piece, 0.0) for piece in layer_grads))
        summed = (
            masked
            if summed is None
            else tuple((left + right for left, right in zip(summed, masked)))
        )
        if step + 1 < steps:
            back_received = from_behind(stream_low, "section", -1)
    stacked_slopes = jnp.stack(slopes)
    input_gradient = jnp.where(first, stacked_slopes[1:], stacked_slopes[:micro])[None]
    (
        projection_grad,
        output_grad,
        expansion_grad,
        reduction_grad,
        query_scale_grad,
        unit_grad,
        alpha_grad,
    ) = summed
    totals = lax.psum(
        (
            projection_grad,
            output_grad,
            expansion_grad,
            reduction_grad,
            query_scale_grad,
            unit_grad,
            alpha_grad,
        ),
        "dp",
    )
    return (
        layer_output,
        input_gradient,
        totals[0][None],
        totals[1][None],
        totals[2][None],
        totals[3][None],
        totals[4][None],
        totals[5][None],
        totals[6][None],
    )


MESH_IDS = pl.DeviceIdType.MESH
F32, BF16 = jnp.float32, jnp.bfloat16
CHUNK = 256
NN = ((1,), (0,))
NT = ((1,), (1,))


def dot(left, right, dims):
    return lax.dot_general(left, right, (dims, ((), ())), preferred_element_type=F32)


def sigmoid(v):
    return 0.5 + 0.5 * jnp.tanh(0.5 * v)


def norm_parts(v):
    rate = lax.rsqrt(jnp.mean(v * v, axis=-1, keepdims=True) + 1e-06)
    return v * rate, rate


def norm_back(slope, unit, rate):
    return rate * (slope - unit * jnp.mean(unit * slope, axis=-1, keepdims=True))


def blend_back(slope, base, branch, alpha):
    unit_branch, rate_branch = norm_parts(branch)
    toward = unit_branch - base
    unit, rate = norm_parts(base + alpha * toward)
    inner_slope = norm_back(slope, unit, rate)
    alpha_slope = jnp.sum(inner_slope * toward, axis=0, keepdims=True)
    scaled = alpha * inner_slope
    return inner_slope - scaled, norm_back(scaled, unit_branch, rate_branch), alpha_slope


def sequence_starts(lengths_ref, row, index):
    begin = jnp.zeros_like(index)
    end = jnp.int32(0)
    for sequence in range(lengths_ref.shape[2]):
        end = end + lengths_ref[row, 0, sequence]
        begin = jnp.where(index >= end, end, begin)
    return jnp.where(index < end, begin, index)


class Sizes:
    def __init__(self, tensors, places, part, width, inner, units):
        self.tensors, self.places, self.part, self.width = tensors, places, part, width
        self.inner, self.units = inner, units
        self.local = part * tensors
        self.heads = inner // HDIM


class Slots:
    def __init__(self, send, recv):
        self.send, self.recv, self.names = send, recv, {}

    def copy(self, name, source, target, device):
        number = self.names.setdefault(name, len(self.names))
        return pltpu.make_async_remote_copy(
            source, target, self.send.at[number], self.recv.at[number], device_id=device, device_id_type=MESH_IDS
        )


HALVES = 2
COPIES = 211


def relay_kernel(
    sizes,
    lengths_ref, acts_ref, cot_ref, qs_ref, us_ref, al_ref, wp_ref, wo_ref, we_ref, wr_ref,
    lo_ref, ig_ref, small_ref, attn_ref, ge_ref, gr_ref,
    wp, wo, we, wr, qs, us, al,
    stream, middles, feed_low, branch_low,
    cosines, sines, scales,
    heads_in, rates_in, probs, mixed_in, sums_in, branch_f, middle_f, feed_f, ups, gates,
    hidden, expanded_low, back_in, heads_back_in,
    heads_out, rates_out, mixed_out, sums_out, go_out, go_sib, go_in,
    outs, outs_in, turned_rows, query_grad, key_grad, value_grad,
    attn_own, attn_sib, attn_all, scale_own, scale_sib, scale_all,
    alpha_own, alpha_in, finals, finals_in,
    middle_cols, hidden_part, up_part, gate_part, stage_e, stage_r, raw, ahead,
    weight_sem, weight_send, send_sem, recv_sem, stage_sem, raw_sem, out_sem,
):
    T, Z, S, part = sizes.tensors, sizes.places, sizes.local, sizes.part
    H, inner, units, D = sizes.heads, sizes.inner, sizes.units, sizes.width
    core, t, z = lax.axis_index("section"), lax.axis_index("tensor"), lax.axis_index("dp")
    sibling = (1 - core, t, z)
    side, row = lax.rem(t, 2), t // 2
    tensor_peers = [row * 2 + (1 - side), (1 - row) * 2 + side, (1 - row) * 2 + (1 - side)]
    place_peers = [lax.rem(z + k, Z) for k in range(1, Z)]
    tensor_ids = [(core, peer, z) for peer in tensor_peers]
    place_ids = [(core, t, peer) for peer in place_peers]
    slots = Slots(send_sem, recv_sem)
    pending = [[]]

    weights = [
        (wp_ref, lambda layer: wp.at[layer]),
        (wo_ref, lambda layer: wo.at[layer]),
        (we.at[core, 0], lambda layer: we.at[layer, 0]),
        (we.at[core, 1], lambda layer: we.at[layer, 1]),
        (wr_ref, lambda layer: wr.at[layer]),
        (qs_ref, lambda layer: qs.at[layer]),
        (us_ref, lambda layer: us.at[layer]),
        (al_ref, lambda layer: al.at[layer]),
    ]

    def weight_load(layer, piece):
        source, target = weights[piece]
        return pltpu.make_async_copy(source, target(layer), weight_sem.at[layer, piece])

    for piece in range(len(weights)):
        if piece not in (2, 3):
            weight_load(core, piece).start()

    raw_rows = raw.shape[1]

    def raw_load(block):
        return pltpu.make_async_copy(we_ref.at[pl.ds(block * raw_rows, raw_rows)], raw.at[block % 2], raw_sem.at[block % 2])

    for block in range(2):
        raw_load(block).start()

    def take_apart(blocks):
        for block in blocks:
            raw_load(block).wait()
            we[core, :, block * raw_rows : (block + 1) * raw_rows, :] = jnp.swapaxes(raw[block % 2], 0, 1)
            if (block + 2) * raw_rows < D:
                raw_load(block + 2).start()

    barrier = pltpu.get_barrier_semaphore()
    partners = [sibling] + tensor_ids + place_ids
    for partner in partners:
        pl.semaphore_signal(barrier, inc=1, device_id=partner, device_id_type=MESH_IDS)
    turn = HDIM // 2
    index_all = lax.broadcasted_iota(jnp.int32, (1, S * Z), 1)
    starts = sequence_starts(lengths_ref, core, index_all)
    rates = jnp.exp(lax.broadcasted_iota(jnp.int32, (turn, 1), 0).astype(F32) * (-2.0 * math.log(10000.0) / HDIM))
    angle = rates * (index_all - starts).astype(F32)
    cosine, sine = jnp.cos(angle), jnp.sin(angle)
    for place in range(Z):
        cosines[place] = cosine[:, place * S : (place + 1) * S]
        sines[place] = sine[:, place * S : (place + 1) * S]
    key_index = lax.broadcasted_iota(jnp.int32, (S * Z, S), 0)
    pl.semaphore_wait(barrier, len(partners))

    def weight_copy(piece):
        source, target = weights[piece]
        return pltpu.make_async_remote_copy(
            source, target(core), weight_send.at[piece], weight_sem.at[core, piece], device_id=sibling, device_id_type=MESH_IDS
        )

    def lend_weights(layer, pieces):
        @pl.when(core == layer)
        def _():
            for piece in pieces:
                weight_copy(piece).start()

    for piece in (5, 6, 7):
        weight_copy(piece).start()
    lend_weights(0, (0,))

    def await_weight(layer, piece):
        if piece in (2, 3):
            @pl.when(core != layer)
            def _():
                weight_load(layer, piece).wait()
        else:
            weight_load(layer, piece).wait()

    def send(name, source, target, device):
        copy = slots.copy(name, source, target, device)
        copy.start()
        pending[-1].append(copy)
        return copy

    def settle(keep=4):
        pending.append([])
        while len(pending) > keep:
            for copy in pending.pop(0):
                copy.wait_send()

    def arrive(copies):
        for copy in copies:
            copy.wait_recv()

    def rows_of(index):
        return pl.ds(pl.multiple_of(index * part, part), part)

    my_rows, far_rows = rows_of(t), rows_of(tensor_peers[2])

    def gather(name, target, half, value):
        count = value.shape[0]
        rows = pl.ds(pl.multiple_of(t * part + half * count, count), count)
        target[rows, :] = value
        mine = target.at[rows, :]
        return [send((name, half, k), mine, mine, device) for k, device in enumerate(tensor_ids)]

    def half_of(target, half):
        return jnp.concatenate([target[index * part + half * count : index * part + (half + 1) * count, :] for index in range(T)], axis=0)

    count = part // HALVES
    halves = range(HALVES)

    def piece_of(half):
        return slice(half * count, (half + 1) * count)

    class Line:
        def __init__(self, name, views, guard=None, passes=0):
            self.name, self.views, self.guard, self.passes = name, views, guard, passes

        def copies(self, way, step, origin):
            device = (core, t, lax.rem(z + 1, Z)) if way == 0 else (core, t, lax.rem(z + Z - 1, Z))
            return [slots.copy((self.name, way, step, k), view, view, device) for k, view in enumerate(self.views(origin))]

        def when(self, condition):
            return pl.when(condition if self.guard is None else condition & self.guard)

        def origin(self, way, step):
            return z - step if way == 0 else z + step

        def sends(self, way, step):
            return (z >= step) & (z + 1 < Z) if way == 0 else (z + step < Z) & (z >= 1)

        def comes(self, way, step):
            return z >= step if way == 0 else z + step < Z

        def passing(self, way, step):
            got = self.views(self.origin(way, step))[0]
            return [slots.copy((self.name, "pass", way, step, k), got, got, tensor_ids[k]) for k in range(self.passes)]

        def passed(self):
            for way in range(2):
                for step in range(1, Z):
                    @self.when(self.comes(way, step))
                    def _():
                        for copy in self.passing(way, step):
                            copy.wait_recv()

        def step(self, step):
            for way in range(2):
                if step > 0:
                    @self.when(self.comes(way, step))
                    def _():
                        for copy in self.copies(way, step - 1, self.origin(way, step)):
                            copy.wait_recv()
                        for copy in self.passing(way, step):
                            copy.start()

                if step < Z - 1:
                    @self.when(self.sends(way, step))
                    def _():
                        for copy in self.copies(way, step, self.origin(way, step)):
                            copy.start()

        def finish(self):
            for way in range(2):
                for step in range(Z - 1):
                    @self.when(self.sends(way, step))
                    def _():
                        for copy in self.copies(way, step, self.origin(way, step)):
                            copy.wait_send()

                    @self.when(self.comes(way, step + 1))
                    def _():
                        for copy in self.passing(way, step + 1):
                            copy.wait_send()

    def row_line(name, layer, target, groups, passes=0):
        return Line((name, len(groups)), lambda place: [target.at[layer, place, rows, :] for rows in groups], None, passes)

    def pass_on(name, layer, target, count=2, indices=range(Z - 1)):
        passed = []
        for index in indices:
            got = target.at[layer, place_peers[index], my_rows, :]
            passed += [send((name, "pass", index, k), got, got, device) for k, device in enumerate(tensor_ids[:count])]
        return passed

    def scatter(number, half):
        return [
            send((number % 2, half, k), sums_out.at[number % 2, half, peer], sums_in.at[number % 2, half, k], device)
            for k, (peer, device) in enumerate(zip(tensor_peers, tensor_ids))
        ]

    def scattered(number, half, copies):
        arrive(copies)
        total = sums_out[number % 2, half, t].astype(F32)
        for k in range(T - 1):
            total = total + sums_in[number % 2, half, k].astype(F32)
        return total

    def retire(copies):
        for copy in copies:
            for group in pending:
                if any(copy is other for other in group):
                    copy.wait_send()
                    group[:] = [other for other in group if other is not copy]

    def spread(name, source, target):
        target[z] = source[z]
        return [
            send((name, k), source.at[peer], target.at[z], device) for k, (peer, device) in enumerate(zip(place_peers, place_ids))
        ]

    def block(query, key):
        return query * (query + 1) // 2 + key

    used, waiting = {}, {}
    first_line = row_line("first line", 0, stream, [my_rows], 2)
    stream_lines = [row_line("stream line", 0, stream, [far_rows]), row_line("stream line", 1, stream, [my_rows, far_rows])]
    middle_lines = [row_line("middle line", layer, middles, [my_rows, far_rows], 2 - 2 * layer) for layer in range(2)]
    feed_lines = [row_line("feed line", layer, feed_low, [my_rows, far_rows][: layer + 1], 3 - layer) for layer in range(2)]

    def free(name):
        retire(used.pop(name, []))

    first_stream = gather("stream", stream.at[0, z], 0, acts_ref[core, 0])
    first_line.step(0)

    def forward(layer, base_low, stream_copies, then):
        if layer == 0:
            take_apart(range(0, D // raw_rows // 2))
        await_weight(layer, 0)
        for piece in (5, 6, 7):
            await_weight(layer, piece)
        scale = jnp.broadcast_to(jnp.broadcast_to(qs[layer], (8, inner)).T[:, :1], (inner, 128)).reshape(H, HDIM, 128)
        scales[layer] = scale
        cosine_here, sine_here = cosines[z][None], sines[z][None]
        arrive(stream_copies)
        free("heads")
        gathered = stream[layer, z]
        for third in range(3):
            piece = dot(gathered, wp[layer, third], NN).T.reshape(H, HDIM, S)
            if third < 2:
                front, back = piece[:, :turn], piece[:, turn:]
                piece = jnp.concatenate([front * cosine_here - back * sine_here, back * cosine_here + front * sine_here], axis=1)
                speed = lax.rsqrt(jnp.sum(piece * piece, axis=1, keepdims=True) + 1e-06)
                piece = piece * speed * scale[:, :, :1]
                for head in range(H):
                    rates_out[head, third : third + 1] = speed[head]
            heads_out[:, third] = piece.astype(BF16)
        copies = spread("heads", heads_out, heads_in.at[layer])
        rate_copies = spread("rates", rates_out, rates_in.at[layer])
        used["heads"] = copies + rate_copies
        if layer == 0:
            first_line.step(1)
            take_apart(range(D // raw_rows // 2, D // raw_rows))
        else:
            middle_lines[0].step(2)
        lend_weights(layer, (1, 2))
        settle()
        if layer:
            first_line.step(3)
        arrive(copies + rate_copies)
        if layer:
            middle_lines[0].step(3)
        for place in range(Z):
            turned_rows[place] = heads_in[layer, place, 1].T
        free("mixed")
        for query in range(Z):
            raw = [dot(turned_rows[key], heads_in[layer, query, 0], NN) * math.sqrt(HDIM) for key in range(query + 1)]
            first = starts[:, query * S : (query + 1) * S]
            last = index_all[:, query * S : (query + 1) * S]
            scores = []
            for key in range(query + 1):
                keys = key_index[key * S : (key + 1) * S]
                allowed = keys >= first
                if key == query:
                    allowed = allowed & (keys <= last)
                scores.append(jnp.where(allowed, raw[key], -1e30))
            highest = scores[0].max(axis=0, keepdims=True)
            for piece in scores[1:]:
                highest = jnp.maximum(highest, piece.max(axis=0, keepdims=True))
            lifted = [jnp.exp(piece - highest) for piece in scores]
            total = lifted[0].sum(axis=0, keepdims=True)
            for piece in lifted[1:]:
                total = total + piece.sum(axis=0, keepdims=True)
            shrink = 1.0 / total
            mixed = None
            for key in range(query + 1):
                low = (lifted[key] * shrink).astype(BF16)
                probs[layer, block(query, key)] = low
                term = dot(heads_in[layer, key, 2], low, NN)
                mixed = term if mixed is None else mixed + term
            mixed_out[query] = mixed.astype(BF16)
        copies = spread("mixed", mixed_out, mixed_in.at[layer])
        used["mixed"] = copies
        if layer == 0:
            first_line.step(2)
            stream_lines[0].step(0)
        settle()
        if layer:
            stream_lines[0].step(3)
            stream_lines[0].finish()
        await_weight(layer, 1)
        arrive(copies)
        attended = mixed_in[layer].reshape(inner, S).T
        free("sums 0")
        partial = dot(attended, wo[layer], NN).astype(BF16).reshape(T, HALVES, count, D)
        branch_copies = []
        for half in halves:
            sums_out[0, half] = partial[:, half]
            branch_copies.append(scatter(0, half))
        used["sums 0"] = sum(branch_copies, [])
        if layer:
            stream_lines[1].step(0)
        else:
            stream_lines[0].step(1)
        lend_weights(layer, (3,))
        settle()
        alpha = al[layer]
        middle_copies = []
        for half in halves:
            branch = scattered(0, half, branch_copies[half])
            base = base_low[piece_of(half)].astype(F32)
            middle = norm_parts(base + alpha[0:1] * (norm_parts(branch)[0] - base))[0]
            middle_copies.append(gather("middle", middles.at[layer, z], half, middle.astype(BF16)))
            branch_f[layer, piece_of(half)] = branch
            middle_f[layer, piece_of(half)] = middle
        stream_lines[layer].step(1 + (layer == 0))
        lend_weights(layer, (4,))
        settle()
        if layer:
            for line in (first_line, middle_lines[0]):
                line.passed()
                line.finish()
        free("sums 1")
        for piece in (2, 3):
            await_weight(layer, piece)
        feed_copies = []
        for half in halves:
            arrive(middle_copies[half])
            middle_all = half_of(middles.at[layer, z], half)
            for begin in range(0, units, CHUNK):
                cols = slice(begin, begin + CHUNK)
                up = dot(middle_all, we[layer, 0, :, cols], NN)
                gate = dot(middle_all, we[layer, 1, :, cols], NN)
                if layer:
                    ups[half, :, cols] = up.astype(BF16)
                    gates[half, :, cols] = gate.astype(BF16)
                inside = us[layer, 1:2, cols] * gate
                hidden[:, cols] = (us[layer, 0:1, cols] * up * (inside * sigmoid(inside))).astype(BF16)
            if half == 0:
                await_weight(layer, 4)
            acted = hidden[...]
            for begin in range(0, D, CHUNK):
                cols = slice(begin, begin + CHUNK)
                sums_out[1, half, :, :, cols] = dot(acted, wr[layer, :, cols], NN).astype(BF16).reshape(T, count, CHUNK)
            feed_copies.append(scatter(1, half))
        used["sums 1"] = sum(feed_copies, [])
        if layer:
            stream_lines[1].step(2)
        middle_lines[layer].step(0)
        settle()
        for half in halves:
            feed = scattered(1, half, feed_copies[half])
            feed_f[layer, piece_of(half)] = feed
            middle = middle_f[layer, piece_of(half)]
            result = norm_parts(middle + alpha[1:2] * (norm_parts(feed)[0] - middle))[0].astype(BF16)
            outs[0, layer, piece_of(half)] = result
            then(half, result)
        if layer == 0:
            middle_lines[0].step(1)
            lend_weights(1, (0,))

    def act_back(layer, cols, up, gate, slope_hidden):
        scale_up, scale_gate = us[layer, 0:1, cols], us[layer, 1:2, cols]
        inside = scale_gate * gate
        gain = sigmoid(inside)
        silu = inside * gain
        by_up = silu * slope_hidden
        by_gate = scale_up * up * (gain + silu * (1.0 - gain)) * slope_hidden
        return silu, by_up, by_gate

    def stage_copy(layer, chunk, which):
        buffer = (stage_e, stage_r)[which].at[chunk % 2]
        target = (ge_ref.at[0, chunk], gr_ref.at[0, chunk])[which]
        return pltpu.make_async_copy(buffer, target, stage_sem.at[layer, chunk, which])

    def stage_send(layer, chunk, which):
        buffer = (stage_e, stage_r)[which].at[chunk % 2]
        target = (ge_ref.at[1, chunk], gr_ref.at[1, chunk])[which]
        return slots.copy(("stage", chunk, which), buffer, target, sibling)

    def stage_wait(layer, chunk):
        @pl.when(core == layer)
        def _():
            for which in range(2):
                stage_copy(layer, chunk, which).wait()

        @pl.when(core != layer)
        def _():
            for which in range(2):
                stage_send(layer, chunk, which).wait_send()

    def feed_ahead():
        def slots_of(place, carry):
            rows = pl.ds(pl.multiple_of(place * S, S), S)
            for begin in range(0, units, CHUNK):
                cols = slice(begin, begin + CHUNK)
                for side in range(2):
                    ahead[side, rows, cols] = dot(middles[0, place], we[0, side, :, cols], NN).astype(BF16)
            return carry

        lax.fori_loop(0, Z, slots_of, 0)

    staged = []

    def feed_grads(layer, chunk):
        if chunk == 0:
            for place in range(Z):
                middle_cols[:, place * S : (place + 1) * S] = middles[layer, place].T
        cols = slice(chunk * CHUNK, (chunk + 1) * CHUNK)
        scale_up, scale_gate = us[layer, 0:1, cols], us[layer, 1:2, cols]

        def slots_of(place, sums):
            rows = slice(place * S, (place + 1) * S) if layer else pl.ds(pl.multiple_of(place * S, S), S)
            if layer:
                up = dot(middles[layer, place], we[layer, 0, :, cols], NN)
                gate = dot(middles[layer, place], we[layer, 1, :, cols], NN)
            else:
                up, gate = ahead[0, rows, cols].astype(F32), ahead[1, rows, cols].astype(F32)
            slope_hidden = dot(feed_low[layer, place], wr[layer, cols, :], NT)
            silu, by_up, by_gate = act_back(layer, cols, up, gate, slope_hidden)
            hidden_part[:, rows] = (scale_up * up * silu).astype(BF16).T
            up_part[rows, :] = (by_up * scale_up).astype(BF16)
            gate_part[rows, :] = (by_gate * scale_gate).astype(BF16)
            return sums[0] + jnp.sum(by_up * up, axis=0, keepdims=True), sums[1] + jnp.sum(by_gate * gate, axis=0, keepdims=True)

        sums = (jnp.zeros((1, CHUNK), F32), jnp.zeros((1, CHUNK), F32))
        if layer:
            for place in range(Z):
                sums = slots_of(place, sums)
        else:
            sums = lax.fori_loop(0, Z, slots_of, sums)
        sum_up, sum_gate = sums
        finals[layer, 2:3, cols] = sum_up
        finals[layer, 3:4, cols] = sum_gate
        if len(staged) >= 2:
            stage_wait(*staged[-2])
        buffer = chunk % 2
        stage_e[buffer, 0] = dot(middle_cols[...], up_part[...], NN).astype(BF16)
        stage_e[buffer, 1] = dot(middle_cols[...], gate_part[...], NN).astype(BF16)
        stage_r[buffer] = dot(hidden_part[...], feed_low[layer].reshape(Z * S, D), NN).astype(BF16)

        @pl.when(core == layer)
        def _():
            for which in range(2):
                stage_copy(layer, chunk, which).start()

        @pl.when(core != layer)
        def _():
            for which in range(2):
                stage_send(layer, chunk, which).start()

        staged.append((layer, chunk))

    chunks = units // CHUNK
    projected = 3 * HDIM
    def attn_pair():
        return [slots.copy("head", attn_own, attn_sib, sibling), slots.copy("scale", scale_own, scale_sib, sibling)]

    def go_pair():
        return [slots.copy("go", go_out, go_sib, sibling)]

    def go_spread():
        return [
            slots.copy(("go", k), go_out.at[peer], go_in.at[k], device) for k, (peer, device) in enumerate(zip(place_peers, place_ids))
        ]

    def offer(layer, pair):
        @pl.when(core != layer)
        def _():
            for copy in pair():
                copy.start()

    def go_join(layer):
        @pl.when(core == layer)
        def _():
            for copy in go_pair():
                copy.wait_recv()
            go_out[...] = (go_out[...].astype(F32) + go_sib[...].astype(F32)).astype(BF16)
            for copy in go_spread():
                copy.start()

        @pl.when(core != layer)
        def _():
            for copy in go_pair():
                copy.wait_send()

    attn_lines = [
        Line("heads line", lambda place: [attn_all.at[place, :projected], scale_all.at[place]], core == layer) for layer in range(2)
    ]
    go_lines = [Line("go line", lambda place: [attn_all.at[place, projected:]], core == layer) for layer in range(2)]

    def go_finish(layer):
        @pl.when(core == layer)
        def _():
            for copy in go_spread():
                copy.wait_recv()
            total = go_out[z].astype(F32)
            for k in range(Z - 1):
                total = total + go_in[k].astype(F32)
            attn_all[z, projected:] = total.astype(BF16)
            for copy in go_spread():
                copy.wait_send()

        go_lines[layer].step(0)

    def attn_join(layer):
        @pl.when(core == layer)
        def _():
            for copy in attn_pair():
                copy.wait_recv()
            attn_all[z, :projected] = (attn_own[...].astype(F32) + attn_sib[...].astype(F32)).astype(BF16)
            scale_all[z] = scale_own[...] + scale_sib[...]

        @pl.when(core != layer)
        def _():
            for copy in attn_pair():
                copy.wait_send()

        attn_lines[layer].step(0)

    def head_grads(layer, scale_slope):
        if layer:
            arrive(waiting["stream", 1])
        grad = None
        for place in range(Z):
            term = dot(heads_out[place].reshape(3 * HDIM, S), stream[layer, place], NN)
            grad = term if grad is None else grad + term
        attn_own[...] = grad.astype(BF16)
        scale_rows = jnp.broadcast_to(scale_slope, (HDIM, 128)).T[:8]
        scale_own[...] = jnp.concatenate([scale_rows, scale_rows], axis=1)
        offer(layer, attn_pair)

    def enter(layer, half, slope):
        rows = piece_of(half)
        middle_slope, feed_slope, alpha_m = blend_back(slope, middle_f[layer, rows], feed_f[layer, rows], al[layer, 1:2])
        copies = gather("feed_low", feed_low.at[layer, z], half, feed_slope.astype(BF16))
        return middle_slope, alpha_m, copies

    def backward(layer, base_low, entered, then):
        alpha = al[layer]
        alpha_own[layer, 1:2] = entered[0][1] + entered[1][1]
        if layer:
            stream_lines[1].step(3)
            waiting["stream", 1] = pass_on("stream", 1, stream, 2, [0])
        else:
            feed_lines[1].step(3)
        settle()
        if layer == 0:
            attn_join(1)
            go_finish(1)
        free("sums 0")
        back_copies = []
        for half in halves:
            arrive(entered[half][2])
            feed_all = half_of(feed_low.at[layer, z], half)
            for begin in range(0, units, CHUNK):
                cols = slice(begin, begin + CHUNK)
                slope_hidden = dot(feed_all, wr[layer, cols, :], NT)
                if layer:
                    up, gate = ups[half, :, cols].astype(F32), gates[half, :, cols].astype(F32)
                else:
                    rows = [pl.ds(pl.multiple_of(z * S + index * part + half * count, count), count) for index in range(T)]
                    up, gate = (
                        jnp.concatenate([ahead[side, group, cols] for group in rows], axis=0).astype(F32) for side in range(2)
                    )
                _, by_up, by_gate = act_back(layer, cols, up, gate, slope_hidden)
                expanded_low[0, :, cols] = (by_up * us[layer, 0:1, cols]).astype(BF16)
                expanded_low[1, :, cols] = (by_gate * us[layer, 1:2, cols]).astype(BF16)
            for begin in range(0, D, CHUNK):
                rows = slice(begin, begin + CHUNK)
                partial = dot(expanded_low[0], we[layer, 0, rows, :], NT) + dot(expanded_low[1], we[layer, 1, rows, :], NT)
                sums_out[0, half, :, :, rows] = partial.astype(BF16).reshape(T, count, CHUNK)
            back_copies.append(scatter(2, half))
            if layer and half == 0:
                middle_lines[1].step(1)
        used["sums 0"] = sum(back_copies, [])
        if layer:
            waiting["stream", 1] += pass_on("stream", 1, stream, 2, [1])
        feed_lines[layer].step(0)
        settle()
        if layer == 0:
            attn_lines[1].step(1)
            go_lines[1].step(1)
            feed_lines[1].passed()
            arrive(waiting["middle", 1])
            feed_grads(1, 0)
        free("branch_low")
        branch_copies, stream_slopes, alpha_a = [], [], None
        for half in halves:
            middle_total = entered[half][0] + scattered(2, half, back_copies[half])
            stream_slope, branch_slope, term = blend_back(
                middle_total, base_low[piece_of(half)].astype(F32), branch_f[layer, piece_of(half)], alpha[0:1]
            )
            branch_copies.append(gather("branch_low", branch_low, half, branch_slope.astype(BF16)))
            stream_slopes.append(stream_slope)
            alpha_a = term if alpha_a is None else alpha_a + term
        copies = sum(branch_copies, [])
        used["branch_low"] = copies
        alpha_own[layer, 0:1] = alpha_a
        if layer:
            waiting["stream", 1] += pass_on("stream", 1, stream, 2, [2])
            middle_lines[1].step(2)
            feed_ahead()
            feed_lines[1].step(1)
        else:
            alpha_copies = [send(("alpha", k), alpha_own, alpha_in.at[k], device) for k, device in enumerate(tensor_ids)]
            feed_lines[0].step(1)
            attn_lines[1].step(2)
            go_lines[1].step(2)
            feed_grads(1, 1)
        settle()
        arrive(copies)
        branch_all = branch_low[...]
        free("mixed_back")
        free("mixed")
        mixed_out[...] = dot(wo[layer], branch_all, NT).astype(BF16).reshape(H, HDIM, S)
        copies = spread("mixed_back", mixed_out, back_in)
        used["mixed_back"] = copies
        go_out[...] = dot(mixed_in[layer].reshape(inner, S), branch_all, NN).astype(BF16).reshape(H, HDIM, D)
        offer(layer, go_pair)
        if layer == 0:
            feed_lines[0].step(2)
        if layer:
            middle_lines[1].step(3)
            waiting["middle", 1] = pass_on("middle", 1, middles)
        else:
            stream_lines[1].finish()
            middle_lines[1].finish()
        settle()
        if layer == 0:
            feed_grads(1, 2)
        for place in range(Z):
            turned_rows[place] = heads_in[layer, place, 2].T
        arrive(copies)
        if layer == 0:
            go_join(0)
            feed_lines[0].step(3)
        for query in range(Z):
            slope_mixed = back_in[query]
            lows = [probs[layer, block(query, key)] for key in range(query + 1)]
            probs_slope = [dot(turned_rows[key], slope_mixed, NN) for key in range(query + 1)]
            row_term = None
            for low, piece in zip(lows, probs_slope):
                term = jnp.sum(low.astype(F32) * piece, axis=0, keepdims=True)
                row_term = term if row_term is None else row_term + term
            query_slope = None
            for key in range(query + 1):
                low = lows[key]
                scores_low = (low.astype(F32) * (probs_slope[key] - row_term)).astype(BF16)
                term = dot(heads_in[layer, key, 1], scores_low, NN)
                query_slope = term if query_slope is None else query_slope + term
                key_term = dot(heads_in[layer, query, 0], scores_low, NT)
                value_term = dot(slope_mixed, low, NT)
                if key == query:
                    key_grad[key] = key_term
                    value_grad[key] = value_term
                else:
                    key_grad[key] += key_term
                    value_grad[key] += value_term
            query_grad[query] = query_slope
        free("heads_back")
        free("heads")
        scale = scales[layer, z][:, :1]
        inverse = 1.0 / scale
        scale_slope = None
        for place in range(Z):
            cosine_there, sine_there = cosines[place], sines[place]
            for third, source in ((0, query_grad), (1, key_grad)):
                piece = source[place] * math.sqrt(HDIM)
                unit = heads_in[layer, place, third].astype(F32) * inverse
                term = jnp.sum(piece * unit, axis=1, keepdims=True)
                scale_slope = term if scale_slope is None else scale_slope + term
                piece = piece * scale
                piece = rates_in[layer, place, third : third + 1] * (piece - unit * jnp.sum(unit * piece, axis=0, keepdims=True))
                front, back = piece[:turn], piece[turn:]
                piece = jnp.concatenate([front * cosine_there + back * sine_there, back * cosine_there - front * sine_there], axis=0)
                heads_out[place, third] = piece.astype(BF16)
            heads_out[place, 2] = value_grad[place].astype(BF16)
        if layer == 0:
            head_grads(0, scale_slope)
            attn_join(0)
        copies = spread("heads_back", heads_out, heads_back_in)
        used["heads_back"] = copies
        settle()
        if layer:
            feed_lines[1].step(2)
        else:
            feed_grads(1, 3)
            go_finish(0)
            arrive(alpha_copies)
            retire(alpha_copies)
            total = alpha_own[...]
            for k in range(T - 1):
                total = total + alpha_in[k]
            alpha_own[...] = total
            alpha_copies = [
                send(("alpha", T - 1 + k), alpha_own, alpha_in.at[T - 1 + k], device) for k, device in enumerate(place_ids)
            ]
        if layer == 0:
            feed_lines[0].passed()
            feed_grads(0, 0)
            attn_lines[0].step(1)
        arrive(copies)
        partial = None
        for third in range(3):
            term = dot(heads_back_in[:, third].reshape(inner, S).T, wp[layer, third], NT)
            partial = term if partial is None else partial + term
        free("sums 1")
        partial = partial.astype(BF16).reshape(T, HALVES, count, D)
        copies = []
        for half in halves:
            sums_out[1, half] = partial[:, half]
            copies.append(scatter(3, half))
        settle()
        if layer:
            head_grads(layer, scale_slope)
            go_join(1)
        else:
            feed_grads(0, 1)
            go_lines[0].step(1)
        for half in halves:
            result = (stream_slopes[half] + scattered(3, half, copies[half])).astype(BF16)
            outs[1, layer, piece_of(half)] = result
            then(half, result)
        used["sums 1"] = sum(copies, [])
        if layer == 0:
            waiting["alpha"] = alpha_copies

    next_stream, entered_last, entered_first = [], [], []

    def to_second(half, result):
        next_stream.extend(gather("stream", stream.at[1, z], half, result))

    def to_backward(half, result):
        entered_last.append(enter(1, half, cot_ref[core, 0, piece_of(half)].astype(F32)))

    def to_first(half, result):
        entered_first.append(enter(0, half, result.astype(F32)))

    forward(0, acts_ref.at[core, 0], first_stream, to_second)
    forward(1, outs.at[0, 0], next_stream, to_backward)
    backward(1, outs.at[0, 0], entered_last, to_first)
    backward(0, acts_ref.at[core, 0], entered_first, lambda half, result: None)

    other = 1 - core
    last = [send("outs", outs.at[:, other], outs_in, sibling)]
    attn_lines[0].step(2)
    feed_grads(0, 2)
    go_lines[0].step(2)
    for line in feed_lines:
        line.finish()
    for line in (attn_lines[1], go_lines[1]):
        line.step(3)
        line.finish()
    arrive(waiting["alpha"])
    total = alpha_own[...]
    for k in range(Z - 1):
        total = total + alpha_in[T - 1 + k]
    finals[0, 0:2] = total[0]
    finals[1, 0:2] = total[1]
    settle(2)
    feed_grads(0, 3)
    last += [send("finals", finals.at[other], finals_in, sibling)]
    written = [
        pltpu.make_async_copy(outs.at[kind, core], target.at[core], out_sem.at[kind]) for kind, target in enumerate((lo_ref, ig_ref))
    ]
    for copy in written:
        copy.start()
    arrive(last)
    for kind, target in enumerate((lo_ref, ig_ref)):
        written.append(pltpu.make_async_copy(outs_in.at[kind], target.at[other], out_sem.at[2 + kind]))
        written[-1].start()
    small_ref[0:4] = finals[core] + finals_in[...]
    for layer, chunk in staged[-2:]:
        stage_wait(layer, chunk)
    for chunk in range(chunks):
        for which in range(2):
            stage_send(0, chunk, which).wait_recv()
    attn_lines[0].step(3)
    go_lines[0].step(3)
    attn_out = pltpu.make_async_copy(attn_all, attn_ref, stage_sem.at[0, 0, 0])
    attn_out.start()
    for place in range(Z):
        small_ref[4:5, place * HDIM : (place + 1) * HDIM] = scale_all[place, :1, :HDIM]
    settle(0)
    for piece in range(len(weights)):
        weight_copy(piece).wait_send()
    attn_lines[0].finish()
    go_lines[0].finish()
    for copy in written:
        copy.wait()
    attn_out.wait()
    assert len(slots.names) == COPIES, len(slots.names)


def relay(sizes, lengths, acts, cot, qs, us, al, wp, wo, we, wr):
    T, Z, S, part = sizes.tensors, sizes.places, sizes.local, sizes.part
    H, inner, units, D = sizes.heads, sizes.inner, sizes.units, sizes.width
    blocks, chunks = Z * (Z + 1) // 2, units // CHUNK
    vmem = pl.BlockSpec(memory_space=pltpu.VMEM)
    hbm = pl.BlockSpec(memory_space=pl.ANY)
    out_shape = (
        jax.ShapeDtypeStruct((2, part, D), BF16),
        jax.ShapeDtypeStruct((2, part, D), BF16),
        jax.ShapeDtypeStruct((8, D), F32),
        jax.ShapeDtypeStruct((Z, 4 * HDIM, D), BF16),
        jax.ShapeDtypeStruct((2, chunks, 2, D, CHUNK), BF16),
        jax.ShapeDtypeStruct((2, chunks, CHUNK, D), BF16),
    )
    DMA = pltpu.SemaphoreType.DMA
    V = pltpu.VMEM
    scratch = [
        V((2, 3, D, inner), BF16), V((2, inner, D), BF16), V((2, 2, D, units), BF16), V((2, units, D), BF16),
        V((2, 1, inner), F32), V((2, 2, units), F32), V((2, 2, D), F32),
        V((2, Z, S, D), BF16), V((2, Z, S, D), BF16), V((2, Z, S, D), BF16), V((S, D), BF16),
        V((Z, HDIM // 2, S), F32), V((Z, HDIM // 2, S), F32), V((2, H, HDIM, 128), F32),
        V((2, Z, 3, HDIM, S), BF16), V((2, Z, 2, S), F32),
        V((2, blocks, S, S), BF16), V((2, H, HDIM, S), BF16),
        V((2, HALVES, T - 1, part // HALVES, D), BF16),
        V((2, part, D), F32), V((2, part, D), F32), V((2, part, D), F32),
        V((HALVES, S // HALVES, units), BF16), V((HALVES, S // HALVES, units), BF16),
        V((S // HALVES, units), BF16), V((2, S // HALVES, units), BF16),
        V((Z, HDIM, S), BF16), V((H, 3, HDIM, S), BF16),
        V((H, 3, HDIM, S), BF16), V((H, 2, S), F32),
        V((Z, HDIM, S), BF16),
        V((2, HALVES, T, part // HALVES, D), BF16), V((H, HDIM, D), BF16), V((H, HDIM, D), BF16), V((Z - 1, HDIM, D), BF16),
        V((2, 2, part, D), BF16), V((2, part, D), BF16),
        V((Z, S, HDIM), BF16),
        V((Z, HDIM, S), F32), V((Z, HDIM, S), F32), V((Z, HDIM, S), F32),
        V((3 * HDIM, D), BF16), V((3 * HDIM, D), BF16), V((Z, 4 * HDIM, D), BF16),
        V((8, 128), F32), V((8, 128), F32), V((Z, 8, 128), F32),
        V((2, 2, D), F32), V((T + Z - 2, 2, 2, D), F32), V((2, 4, D), F32), V((4, D), F32),
        V((D, Z * S), BF16), V((CHUNK, Z * S), BF16), V((Z * S, CHUNK), BF16), V((Z * S, CHUNK), BF16),
        V((2, 2, D, CHUNK), BF16), V((2, CHUNK, D), BF16), V((2, D // 16, 2, units), BF16),
        V((2, Z * S, units), BF16),
        DMA((2, 8)), DMA((8,)), DMA((COPIES,)), DMA((COPIES,)), DMA((2, chunks, 2)), DMA((2,)), DMA((4,)),
    ]
    return pl.pallas_call(
        functools.partial(relay_kernel, sizes),
        out_shape=out_shape,
        in_specs=[pl.BlockSpec(memory_space=pltpu.SMEM), vmem, vmem, vmem, vmem, vmem, hbm, hbm, hbm, hbm],
        out_specs=(hbm, hbm, vmem, hbm, hbm, hbm),
        scratch_shapes=scratch,
        compiler_params=pltpu.CompilerParams(collective_id=0, has_side_effects=True, vmem_limit_bytes=63 * 2**20),
        name="relay",
    )(lengths, acts, cot, qs, us, al, wp, wo, we, wr)


def finish_kernel(
    attn_ref, ge_ref, gr_ref, lo_in, ig_in, small_ref,
    projection_ref, output_ref, expansion_ref, reduction_ref, lo_ref, ig_ref, scale_ref, units_ref, alphas_ref,
):
    @pl.when(pl.program_id(0) == 0)
    def _():
        lo_ref[...] = lo_in[...]
        ig_ref[...] = ig_in[...]
        alphas_ref[...] = small_ref[0:2]
        units_ref[...] = small_ref[2:4, : units_ref.shape[1]]
        scale_ref[...] = small_ref[4:5, : scale_ref.shape[1]]

    places, chunks = attn_ref.shape[0], ge_ref.shape[1]
    for begin in range(0, ge_ref.shape[3], 16):
        rows = slice(begin, begin + 16)
        pieces = []
        for chunk in range(chunks):
            for lanes in (slice(0, 128), slice(128, 256)):
                for side in range(2):
                    total = ge_ref[0, chunk, side, rows, lanes].astype(F32) + ge_ref[1, chunk, side, rows, lanes].astype(F32)
                    pieces.append(total[None])
        expansion_ref[rows] = jnp.swapaxes(jnp.concatenate(pieces, axis=0), 0, 1)
    reduction_ref[...] = gr_ref[0].astype(F32) + gr_ref[1].astype(F32)
    for third in range(3):
        rows = attn_ref[:, third * HDIM : (third + 1) * HDIM, :].astype(F32)
        projection_ref[third] = rows.reshape(places * HDIM, rows.shape[2]).T
    output_ref[...] = attn_ref[:, 3 * HDIM :, :].astype(F32).reshape(output_ref.shape)


def finish(attn, ge, gr, lo, ig, small):
    places, _, D = attn.shape
    chunks, units, inner = ge.shape[1], ge.shape[1] * CHUNK, places * HDIM
    block = D // 2
    steps = D // block
    rows = units // steps

    def whole(shape):
        return pl.BlockSpec(shape, lambda i: (0,) * len(shape))

    return pl.pallas_call(
        finish_kernel,
        grid=(steps,),
        in_specs=[
            pl.BlockSpec((places, 4 * HDIM, block), lambda i: (0, 0, i)),
            pl.BlockSpec((2, chunks, 2, block, CHUNK), lambda i: (0, 0, 0, i, 0)),
            pl.BlockSpec((2, rows, D), lambda i: (0, i, 0)),
            whole(lo.shape),
            whole(ig.shape),
            whole(small.shape),
        ],
        out_specs=(
            pl.BlockSpec((3, block, inner), lambda i: (0, i, 0)),
            pl.BlockSpec((inner, block), lambda i: (0, i)),
            pl.BlockSpec((block, units // 64, 128), lambda i: (i, 0, 0)),
            pl.BlockSpec((rows, D), lambda i: (i, 0)),
            whole(lo.shape),
            whole(ig.shape),
            whole((1, inner)),
            whole((2, units)),
            whole((2, D)),
        ),
        out_shape=(
            jax.ShapeDtypeStruct((3, D, inner), F32),
            jax.ShapeDtypeStruct((inner, D), F32),
            jax.ShapeDtypeStruct((D, units // 64, 128), F32),
            jax.ShapeDtypeStruct((units, D), F32),
            jax.ShapeDtypeStruct(lo.shape, BF16),
            jax.ShapeDtypeStruct(ig.shape, BF16),
            jax.ShapeDtypeStruct((1, inner), F32),
            jax.ShapeDtypeStruct((2, units), F32),
            jax.ShapeDtypeStruct((2, D), F32),
        ),
        compiler_params=pltpu.CompilerParams(vmem_limit_bytes=60 * 2**20),
        name="finish",
    )(attn, ge, gr.reshape(2, units, D), lo, ig, small)


def fast_body(
    activations, lengths, projection, output_weight, expansion, reduction, query_scale, unit_scales, alphas, cotangent
):
    _, _, part, width = activations.shape
    inner, units = output_weight.shape[1], reduction.shape[1]
    places = lax.axis_size("dp")
    sizes = Sizes(lax.axis_size("tensor"), places, part, width, inner, units)
    lo, ig, small, attn, ge, gr = relay(
        sizes, lengths, activations, cotangent, query_scale, unit_scales[0], alphas[0],
        projection[0].transpose(1, 0, 2), output_weight[0], expansion[0], reduction[0],
    )
    projection_grad, output_grad, expansion_grad, reduction_grad, lo, ig, scale_grad, unit_grad, alpha_grad = finish(
        attn, ge, gr, lo, ig, small
    )
    columns = units // 128
    expansion_grad = expansion_grad.reshape(width, columns, 2, 128).transpose(0, 2, 1, 3).reshape(width, 2, units)
    projection_grad = projection_grad.transpose(1, 0, 2)
    return (
        lo[None, :, None],
        ig[None, :, None],
        projection_grad[None],
        output_grad[None],
        expansion_grad[None],
        reduction_grad[None],
        scale_grad,
        unit_grad[None],
        alpha_grad[None],
    )


def solution(mesh):
    in_specs = (
        P(None, None, ("dp", "tensor"), None),
        P(),
        P("section", None, None, "tensor"),
        P("section", "tensor", None),
        P("section", None, None, "tensor"),
        P("section", "tensor", None),
        P("section", "tensor"),
        P("section", None, "tensor"),
        P("section", None, None),
        P(None, None, ("dp", "tensor"), None),
    )
    out_specs = (
        P("section", None, None, ("dp", "tensor"), None),
        P("section", None, None, ("dp", "tensor"), None),
        P("section", None, None, "tensor"),
        P("section", "tensor", None),
        P("section", None, None, "tensor"),
        P("section", "tensor", None),
        P("section", "tensor"),
        P("section", None, "tensor"),
        P("section", None, None),
    )
    def chosen(*arrays):
        activations, output_weight = arrays[0], arrays[3]
        heads = output_weight.shape[1] // HDIM
        fits = (
            mesh.shape["section"] == 2
            and mesh.shape["tensor"] == 4
            and mesh.shape["dp"] == heads
            and activations.shape[:2] == (2, 1)
            and activations.shape[2] * mesh.shape["tensor"] == 256
        )
        return (fast_body if fits else body)(*arrays)

    return jax.shard_map(chosen, mesh=mesh, in_specs=in_specs, out_specs=out_specs, check_vma=False)
```
